32 devices in a mesh: seq: 4 (over y, x), head: 8 (over z, core).
Axes of the slice: x: 2, y: 2, z: 4, core: 2. Of those that a mesh axis runs over, the one named last changes fastest.
Arguments:
- layer_input: bfloat16 [16, 1024, 1024], P('seq', 'head'), may hold values from -6 to 6
- values_first: bfloat16 [16, 1024, 1024], P('seq', None, 'head'), may hold values from -6 to 6
- w_qkv: float32 [3, 1024, 1024], P(None, 'seq', 'head'), may hold values from -0.1875 to 0.1875
- w_gate_up: float32 [2, 1024, 2816], P(None, 'seq', 'head'), may hold values from -0.1875 to 0.1875
- w_out: float32 [1024, 1024], P('head', 'seq'), may hold values from -1.5 to 1.5
- w_down: float32 [2816, 1024], P('head', 'seq'), may hold values from -0.109375 to 0.109375
- norm_gains: float32 [2, 1024], replicated, may hold values from 0.5 to 1.5
- out_grad: bfloat16 [16, 1024, 1024], P('seq', 'head'), may hold values from -6 to 6
- segments: int32 [16, 1024], P('seq'), may hold values from 0 to 3, never falling along the last dimension, each value on 1 to 512 neighbouring positions
- counts: int32 [4], P('seq'), may hold values from 1 to 4, as said below
- stats_wide: float32 [7, 16, 1024, 1024], P(None, 'head', 'seq'), as said below
- roots_wide: float32 [7, 16, 1024, 1024], P(None, 'head', 'seq'), as said below
- stats_head: float32 [4, 16, 64, 64], P(None, 'head'), as said below
- roots_head: float32 [4, 16, 64, 64], P(None, 'head'), as said below
- stats_unit: float32 [3, 16, 176, 176], P(None, 'head'), as said below
- roots_unit: float32 [3, 16, 176, 176], P(None, 'head'), as said below
Outputs:
- block_out: float32 [16, 1024, 1024], P('seq', 'head')
- input_grad: float32 [16, 1024, 1024], P('seq', 'head')
- first_grad: float32 [16, 1024, 1024], P('seq', None, 'head')
- grad_qkv: float32 [3, 1024, 1024], P(None, 'seq', 'head')
- grad_gate_up: float32 [2, 1024, 2816], P(None, 'seq', 'head')
- grad_out: float32 [1024, 1024], P('head', 'seq')
- grad_down: float32 [2816, 1024], P('head', 'seq')
- grad_gains: float32 [2, 1024], replicated
- new_qkv: float32 [3, 1024, 1024], P(None, 'seq', 'head')
- new_gate_up: float32 [2, 1024, 2816], P(None, 'seq', 'head')
- new_out: float32 [1024, 1024], P('head', 'seq')
- new_down: float32 [2816, 1024], P('head', 'seq')
- new_gains: float32 [2, 1024], replicated
- new_stats_wide: float32 [6, 16, 1024, 1024], P(None, 'head', 'seq')
- new_out_right: float32 [16, 1024, 1024], P('head', 'seq')
- new_stats_head: float32 [4, 16, 64, 64], P(None, 'head')
- new_stats_unit: float32 [3, 16, 176, 176], P(None, 'head')
The draws below stay inside these ranges and needn't reach their ends.
Inputs may be any that keep to these rules, and one draw needn't show every extreme that they name: Slots 0 to counts - 1 of a group are live; at least one group has all 4 live. `segments`: along each sequence the numbers never fall; each of 0 to 3 covers 1 to 512 positions. `stats_wide`: symmetric in its last two dimensions. `roots_wide`: symmetric in its last two dimensions. `stats_head`: symmetric in its last two dimensions. `roots_head`: symmetric in its last two dimensions. `stats_unit`: symmetric in its last two dimensions. `roots_unit`: symmetric in its last two dimensions.
All inputs are finite; a program needn't handle non-finite values.
Results may differ from the reference program's by a relative error of at most 0.018.
Values may be sent and summed in bfloat16 or wider, within the bound.
A program may use at most 192 MiB of HBM per device.

```python
import math
import jax
import jax.numpy as jnp
import numpy as np
from jax import lax

D = 1024
H = 16
HD = 64
FF = 2816
MB = 4
DOCS = 4
HH = 1024
FFB = 176
LEN = 1024
NGROUPS = 4
NSEQS = 16
TOKENS = 16384


def symmetric_stack(key, members, dim, scales, spread, off_weight):
    key_diag, key_off = jax.random.split(key)
    level = jax.random.uniform(key_diag, (members, H, dim), jnp.float32)
    diagonal = jnp.exp(level * math.log(spread))
    noise = jax.random.normal(key_off, (members, H, dim, dim), jnp.float32) * (off_weight / math.sqrt(dim))
    matrix = 0.5 * (noise + jnp.swapaxes(noise, -1, -2)) + jnp.eye(dim, dtype=jnp.float32) * diagonal[..., None]
    return matrix * scales[:, None, None, None]


def draw_counts(key, part):
    key = jax.random.fold_in(key, 5)
    key_level, key_full = jax.random.split(key)
    loads = jax.random.randint(key_level, (NGROUPS,), 1, MB + 1)
    fullest = jax.random.randint(key_full, (), 0, NGROUPS)
    return loads.at[fullest].set(MB).astype(jnp.int32)


def draw_stats_wide(key, part):
    key = jax.random.fold_in(key, 11)
    scales = jnp.array([0.05 * HD, 0.05 * HD, 0.1 * HD, 0.15 * FFB, 0.15 * FFB, 0.02 * HD, 0.2 * FFB], jnp.float32) * TOKENS
    return symmetric_stack(key, 7, D, scales, 4.0, 0.7)


def draw_roots_wide(key, part):
    key = jax.random.fold_in(key, 12)
    scales = jnp.ones((7,), jnp.float32)
    return symmetric_stack(key, 7, D, scales, 4.0, 0.7)


def draw_stats_head(key, part):
    key = jax.random.fold_in(key, 13)
    scales = jnp.array([0.05, 0.05, 0.1, 0.02], jnp.float32) * (D * TOKENS)
    return symmetric_stack(key, 4, HD, scales, 4.0, 0.7)


def draw_roots_head(key, part):
    key = jax.random.fold_in(key, 14)
    scales = jnp.ones((4,), jnp.float32)
    return symmetric_stack(key, 4, HD, scales, 4.0, 0.7)


def draw_stats_unit(key, part):
    key = jax.random.fold_in(key, 15)
    scales = jnp.array([0.15, 0.15, 0.2], jnp.float32) * (D * TOKENS)
    return symmetric_stack(key, 3, FFB, scales, 4.0, 0.7)


def draw_roots_unit(key, part):
    key = jax.random.fold_in(key, 16)
    scales = jnp.ones((3,), jnp.float32)
    return symmetric_stack(key, 3, FFB, scales, 4.0, 0.7)


def steps_of(key, extent, pieces, low, top_value):
    def one(axis_at, blocks):
        heights = jax.random.uniform(jax.random.fold_in(jax.random.fold_in(key, 6), axis_at), (blocks,), jnp.float32, low / len(pieces), top_value / len(pieces))
        return jnp.repeat(jnp.exp(heights), extent[axis_at] // blocks).reshape((-1,) + (1,) * (len(extent) - axis_at - 1))

    loudness = one(*pieces[0])
    for cut in pieces[1:]:
        loudness = loudness * one(*cut)
    return loudness


def profile(number_of, total, bound, lean):
    weights = [(1 << 20) // math.isqrt(standing ** lean) + 1 for standing in range(2, number_of + 1)]
    surplus, holding = total - bound - (number_of - 1), [1] * (number_of - 1)
    while surplus > 0:
        candidates = [i for i in range(number_of - 1) if holding[i] < bound]
        whole, remaining = sum([weights[i] for i in candidates]), surplus
        for i in candidates:
            more = min(bound - holding[i], max(1, remaining * weights[i] // whole), surplus)
            holding[i] = holding[i] + more
            surplus = surplus - more
    return np.array([bound] + holding)


def uneven(stream_key, count, total, reach, slope):
    if count == 2:
        one = jax.random.randint(stream_key, (), max(1, total - reach), min(reach, total - 1) + 1)
        return jnp.stack([one, total - one])
    lengths = jnp.asarray(profile(count, total, reach, slope), jnp.int32)
    pairs = (count - 1) // 2
    source_of, receiver = lengths[1:1 + 2 * pairs:2], lengths[2:2 + 2 * pairs:2]
    margin = jnp.minimum(source_of - 1, reach - receiver)
    moved = jax.random.randint(jax.random.fold_in(stream_key, 1), (pairs,), 0, 1 << 20) % (margin + 1)
    lengths = lengths.at[1:1 + 2 * pairs:2].set(source_of - moved).at[2:2 + 2 * pairs:2].set(receiver + moved)
    return lengths[jax.random.permutation(jax.random.fold_in(stream_key, 2), count)]


def gaussian(own_key, dims, deviation, reach, shards=(), kind=jnp.bfloat16):
    entries = jax.random.normal(own_key, dims, jnp.float32) * deviation
    if len(shards) > 0:
        entries = steps_of(own_key, dims, shards, -0.22, 0.18) * entries
    return jnp.clip(entries, min=-reach, max=reach).astype(kind)


def setup_inputs(seed: int = 0) -> dict:
    keys = jax.random.split(jax.random.key(seed), 17)
    return {
        "layer_input": gaussian(keys[0], (NSEQS, LEN, D), 1.0, 6.0, ((0, 4), (1, 8))),
        "values_first": gaussian(keys[1], (NSEQS, LEN, HH), 1.0, 6.0, ((0, 4), (2, 8))),
        "w_qkv": gaussian(keys[2], (3, D, HH), D ** -0.5, 0.1875, ((1, 4), (2, 8)), jnp.float32),
        "w_gate_up": gaussian(keys[3], (2, D, FF), D ** -0.5, 0.1875, ((1, 4), (2, 8)), jnp.float32),
        "w_out": gaussian(keys[4], (HH, D), (max(HH // 64, 4)) ** -0.5, 1.5, ((0, 8), (1, 4)), jnp.float32),
        "w_down": gaussian(keys[5], (FF, D), FF ** -0.5, 0.109375, ((0, 8), (1, 4)), jnp.float32),
        "norm_gains": jnp.clip(1.0 + 0.1 * jax.random.normal(keys[6], (2, D), jnp.float32), 0.5, 1.5),
        "out_grad": gaussian(keys[7], (NSEQS, LEN, D), 1.0, 6.0, ((0, 4), (1, 8))),
        "segments": jax.vmap(lambda own: jnp.searchsorted(jnp.cumsum(uneven(own, DOCS, LEN, LEN // 2, 2)), jnp.arange(LEN), side="right"))(jax.random.split(keys[8], NSEQS)).reshape((NSEQS, LEN)).astype(jnp.int32),
        "counts": draw_counts(jax.random.fold_in(keys[16], 71), 0),
        "stats_wide": draw_stats_wide(jax.random.fold_in(keys[16], 71), 0),
        "roots_wide": draw_roots_wide(jax.random.fold_in(keys[16], 71), 0),
        "stats_head": draw_stats_head(jax.random.fold_in(keys[16], 71), 0),
        "roots_head": draw_roots_head(jax.random.fold_in(keys[16], 71), 0),
        "stats_unit": draw_stats_unit(jax.random.fold_in(keys[16], 71), 0),
        "roots_unit": draw_roots_unit(jax.random.fold_in(keys[16], 71), 0),
    }


EPSILON = 1e-06
STAT_DECAY = 0.5
STEP_RATE = 0.02
OUT_RATE = 0.1
GAIN_RATE = 0.25
HIGHEST = lax.Precision.HIGHEST

@jax.custom_vjp
def low(v):
    return lax.optimization_barrier(v.astype(jnp.bfloat16)).astype(jnp.float32)

@jax.custom_vjp
def low_back(v):
    return v

def low_keep(v):
    return (low(v), None)

def low_pass(kept, grad):
    return (grad,)

def back_keep(v):
    return (v, None)

def back_low(kept, grad):
    return (low(grad),)
low.defvjp(low_keep, low_pass)
low_back.defvjp(back_keep, back_low)

def rotary_tables(segment_ids, head_dim):
    length = segment_ids.shape[0]
    position = jnp.arange(length, dtype=jnp.int32)
    opens = jnp.concatenate([jnp.ones((1,), dtype=bool), segment_ids[1:] != segment_ids[:-1]])
    first_pos = lax.cummax(jnp.where(opens, position, 0), axis=0)
    offset = (position - first_pos).astype(jnp.float32)
    half_width = head_dim // 2
    frequency = jnp.exp(-jnp.log(10000.0) * jnp.arange(half_width, dtype=jnp.float32) / half_width)
    angle = offset[:, None] * frequency[None, :]
    return (jnp.cos(angle), jnp.sin(angle))

def rotate(values, cosine, sine_part):
    half_width = values.shape[-1] // 2
    front = values[..., :half_width]
    behind = values[..., half_width:]
    cos_wide = cosine[:, None, :]
    sin_wide = sine_part[:, None, :]
    return jnp.concatenate([front * cos_wide - behind * sin_wide, behind * cos_wide + front * sin_wide], axis=-1)

def normalize(values):
    return values * lax.rsqrt(lax.optimization_barrier(jnp.mean(values * values, axis=-1, keepdims=True)) + EPSILON)

def forward(x_seq, first_seq, w_qkv, w_gate_up, w_out, w_down, norm_gains, segment_ids, is_live):
    length = x_seq.shape[0]
    cosine, sine_part = rotary_tables(segment_ids, HD)
    normed = low(normalize(x_seq) * norm_gains[0])
    project = low_back(jnp.einsum('ld,idc->ilc', normed, low(w_qkv), precision=HIGHEST))
    split_heads = project.reshape(3, length, H, HD)
    q_rot = low(rotate(split_heads[0], cosine, sine_part) * 0.125)
    k_rot = low(rotate(split_heads[1], cosine, sine_part))
    v_mix = low(0.5 * split_heads[2] + 0.5 * first_seq.reshape(length, H, HD))
    position = jnp.arange(length)
    visible = (position[None, :] <= position[:, None]) & (segment_ids[None, :] == segment_ids[:, None])

    def one_head(operands):
        q_head, k_head, v_head = operands
        scores = low_back(jnp.dot(q_head, k_head.T, precision=HIGHEST))
        scores = jnp.where(visible, scores, -1e+30)
        chances = low(jax.nn.softmax(scores, axis=-1))
        return low(low_back(jnp.dot(chances, v_head, precision=HIGHEST)))
    mixed = lax.map(jax.checkpoint(one_head), (q_rot.transpose(1, 0, 2), k_rot.transpose(1, 0, 2), v_mix.transpose(1, 0, 2)))
    attended = mixed.transpose(1, 0, 2).reshape(length, H * HD)
    attn_out = low_back(jnp.dot(attended, low(w_out), precision=HIGHEST))
    middle = x_seq + attn_out
    normed_two = low(normalize(middle) * norm_gains[1])
    gate_up = low_back(jnp.einsum('ld,idf->ilf', normed_two, low(w_gate_up), precision=HIGHEST))
    hidden = low(jax.nn.silu(gate_up[0]) * gate_up[1])
    ffn_out = low_back(jnp.dot(hidden, low(w_down), precision=HIGHEST))
    return jnp.where(is_live, middle + ffn_out, x_seq)

def left_update(weight_blocks, grad_blocks, big_stat, big_root, small_stat, small_root):
    big_new = STAT_DECAY * big_stat + (1.0 - STAT_DECAY) * jnp.einsum('nhrk,nhsk->nhrs', grad_blocks, grad_blocks, precision=HIGHEST)
    small_new = STAT_DECAY * small_stat + (1.0 - STAT_DECAY) * jnp.einsum('nhrk,nhrl->nhkl', grad_blocks, grad_blocks, precision=HIGHEST)
    step_dir = jnp.einsum('nhrs,nhsk->nhrk', big_root, grad_blocks, precision=HIGHEST)
    step_dir = jnp.einsum('nhrk,nhkl->nhrl', step_dir, small_root, precision=HIGHEST)
    step_dir = step_dir * lax.rsqrt(lax.optimization_barrier(jnp.mean(step_dir * step_dir, axis=-1, keepdims=True)) + EPSILON)
    return (weight_blocks - STEP_RATE * step_dir, big_new, small_new)

def right_update(weight_blocks, grad_blocks, big_stat, big_root, small_stat, small_root, rate):
    small_new = STAT_DECAY * small_stat + (1.0 - STAT_DECAY) * jnp.einsum('hkr,hlr->hkl', grad_blocks, grad_blocks, precision=HIGHEST)
    big_new = STAT_DECAY * big_stat + (1.0 - STAT_DECAY) * jnp.einsum('hkr,hks->hrs', grad_blocks, grad_blocks, precision=HIGHEST)
    step_dir = jnp.einsum('hkl,hlr->hkr', small_root, grad_blocks, precision=HIGHEST)
    step_dir = jnp.einsum('hks,hsr->hkr', step_dir, big_root, precision=HIGHEST)
    step_dir = step_dir * lax.rsqrt(lax.optimization_barrier(jnp.mean(step_dir * step_dir, axis=1, keepdims=True)) + EPSILON)
    return (weight_blocks - rate * step_dir, big_new, small_new)

def reference(layer_input, values_first, w_qkv, w_gate_up, w_out, w_down, norm_gains, out_grad, segments, counts, stats_wide, roots_wide, stats_head, roots_head, stats_unit, roots_unit):
    slot_all = jnp.arange(layer_input.shape[0], dtype=jnp.int32)
    live_all = slot_all % MB < counts[slot_all // MB]
    weights = (w_qkv, w_gate_up, w_out, w_down, norm_gains)

    def seq_step(summed, item):
        x_seq, first_seq, grad_seq, segment_ids, is_live = item

        def local_fn(x_in, first_in, weight_a, weight_b, weight_c, weight_d, gain_in):
            return forward(x_in, first_in, weight_a, weight_b, weight_c, weight_d, gain_in, segment_ids, is_live)
        result, pull_back = jax.vjp(local_fn, x_seq.astype(jnp.float32), first_seq.astype(jnp.float32), *weights)
        grads = pull_back(grad_seq.astype(jnp.float32))
        summed = tuple((running + addend for running, addend in zip(summed, grads[2:])))
        return (summed, (result, grads[0], grads[1]))
    start_sums = tuple((jnp.zeros(weight.shape, jnp.float32) for weight in weights))
    summed, (block_out, input_grad, first_grad) = lax.scan(seq_step, start_sums, (layer_input, values_first, out_grad, segments, live_all))
    grad_qkv, grad_gate_up, grad_out, grad_down, grad_gains = summed
    qkv_blocks = w_qkv.reshape(3, D, H, HD).transpose(0, 2, 1, 3)
    qkv_grads = grad_qkv.reshape(3, D, H, HD).transpose(0, 2, 1, 3)
    new_qkv, wide_qkv, head_qkv = left_update(qkv_blocks, qkv_grads, stats_wide[0:3], roots_wide[0:3], stats_head[0:3], roots_head[0:3])
    new_qkv = new_qkv.transpose(0, 2, 1, 3).reshape(3, D, H * HD)
    gu_blocks = w_gate_up.reshape(2, D, H, FFB).transpose(0, 2, 1, 3)
    gu_grads = grad_gate_up.reshape(2, D, H, FFB).transpose(0, 2, 1, 3)
    new_gate_up, wide_gu, unit_gu = left_update(gu_blocks, gu_grads, stats_wide[3:5], roots_wide[3:5], stats_unit[0:2], roots_unit[0:2])
    new_gate_up = new_gate_up.transpose(0, 2, 1, 3).reshape(2, D, FF)
    new_out, wide_out, head_out = right_update(w_out.reshape(H, HD, D), grad_out.reshape(H, HD, D), stats_wide[5], roots_wide[5], stats_head[3], roots_head[3], OUT_RATE)
    new_out = new_out.reshape(H * HD, D)
    new_down, wide_down, unit_down = right_update(w_down.reshape(H, FFB, D), grad_down.reshape(H, FFB, D), stats_wide[6], roots_wide[6], stats_unit[2], roots_unit[2], STEP_RATE)
    new_down = new_down.reshape(FF, D)
    new_gains = norm_gains - GAIN_RATE * grad_gains * lax.rsqrt(lax.optimization_barrier(jnp.mean(grad_gains * grad_gains, axis=-1, keepdims=True)) + EPSILON)
    new_stats_wide = jnp.concatenate([wide_qkv, wide_gu, wide_down[None]], axis=0)
    new_stats_head = jnp.concatenate([head_qkv, head_out[None]], axis=0)
    new_stats_unit = jnp.concatenate([unit_gu, unit_down[None]], axis=0)
    return (block_out, input_grad, first_grad, grad_qkv, grad_gate_up, grad_out, grad_down, grad_gains, new_qkv, new_gate_up, new_out, new_down, new_gains, new_stats_wide, wide_out, new_stats_head, new_stats_unit)
```

```python
import functools

import jax
import jax.numpy as jnp
from jax import lax
from jax.experimental import pallas as pl
from jax.experimental.pallas import tpu as pltpu
from jax.sharding import PartitionSpec as P

EPSILON = 1e-06
STAT_DECAY = 0.5
STEP_RATE = 0.02
OUT_RATE = 0.1
GAIN_RATE = 0.25
AXES = ("seq", "head")
LANES = 128
BLOCK = 256
BF16 = jnp.bfloat16
F32 = jnp.float32


def dot_nt(matrix_a, matrix_b):
    return lax.dot_general(
        matrix_a, matrix_b, (((1,), (1,)), ((), ())), preferred_element_type=F32
    )


def dot_tn(matrix_a, matrix_b):
    return lax.dot_general(
        matrix_a, matrix_b, (((0,), (0,)), ((), ())), preferred_element_type=F32
    )


def dot_nn(matrix_a, matrix_b):
    return jnp.dot(matrix_a, matrix_b, preferred_element_type=F32)


def norm_back(d_normed, normed, inverse):
    return inverse * (d_normed - normed * jnp.mean(d_normed * normed, axis=-1, keepdims=True))


def position_tables(segment_ids, head_dim):
    length = segment_ids.shape[0]
    position = jnp.arange(length, dtype=jnp.int32)
    opens = jnp.concatenate([jnp.ones((1,), dtype=bool), segment_ids[1:] != segment_ids[:-1]])
    first_pos = lax.cummax(jnp.where(opens, position, 0), axis=0)
    offset = (position - first_pos).astype(F32)
    half_width = head_dim // 2
    frequency = jnp.exp(-jnp.log(10000.0) * jnp.arange(half_width, dtype=F32) / half_width)
    angle = offset[:, None] * frequency[None, :]
    cosine, sine_part = jnp.cos(angle), jnp.sin(angle)
    per_lane = LANES // head_dim
    cos_wide = jnp.concatenate([cosine, cosine] * per_lane, axis=1)
    sin_wide = jnp.concatenate([-sine_part, sine_part] * per_lane, axis=1)
    return first_pos, cos_wide, sin_wide


def swap_halves(values):
    lane = lax.broadcasted_iota(jnp.int32, values.shape, 1)
    return jnp.where((lane & 32) == 0, pltpu.roll(values, 96, 1), pltpu.roll(values, 32, 1))


def two_heads(block):
    lane = lax.broadcasted_iota(jnp.int32, block.shape, 1)
    zero = jnp.zeros_like(block)
    return jnp.concatenate(
        [jnp.where(lane < 64, block, zero), jnp.where(lane >= 64, block, zero)], axis=0
    )


def one_pair(transposed, width):
    kept = jnp.concatenate([transposed[:64, :width], transposed[64:, width:]], axis=0)
    return kept.T


def seen(first_ref, begin, key_count):
    first = first_ref[0:1, begin : begin + BLOCK]
    query = begin + lax.broadcasted_iota(jnp.int32, (1, BLOCK), 1)
    first = jnp.concatenate([first, first], axis=1)
    query = jnp.concatenate([query, query], axis=1)
    key = lax.broadcasted_iota(jnp.int32, (key_count, 2 * BLOCK), 0)
    return (key >= first) & (key <= query)


def attend_kernel(
    q_ref, k_ref, v_ref, vf_ref, cos_ref, sin_ref, first_ref, qr_ref, kr_ref, vm_ref, att_ref, lse_ref
):
    length = q_ref.shape[1]
    cosine, sine_part = cos_ref[...], sin_ref[...]
    q_raw, k_raw = q_ref[0], k_ref[0]
    qr_ref[0] = ((q_raw * cosine + swap_halves(q_raw) * sine_part) * 0.125).astype(BF16)
    kr_ref[0] = (k_raw * cosine + swap_halves(k_raw) * sine_part).astype(BF16)
    v_mix = (0.5 * v_ref[0] + 0.5 * vf_ref[0].astype(F32)).astype(BF16)
    vm_ref[0] = v_mix
    v_turned = v_mix.T
    for step in range(length // BLOCK):
        begin, keys = step * BLOCK, (step + 1) * BLOCK
        queries = two_heads(qr_ref[0, begin:keys, :])
        scores = dot_nt(kr_ref[0, :keys, :], queries)
        scores = jnp.where(seen(first_ref, begin, keys), scores, -1e30)
        top = jnp.max(scores, axis=0, keepdims=True)
        exps = jnp.exp(scores - top)
        total = jnp.sum(exps, axis=0, keepdims=True)
        chances = (exps * (1.0 / total)).astype(BF16)
        attended = dot_nn(v_turned[:, :keys], chances)
        att_ref[0, begin:keys, :] = one_pair(attended, BLOCK).astype(BF16)
        log_total = top + jnp.log(total)
        lse_ref[0, 0:1, begin:keys] = log_total[:, :BLOCK]
        lse_ref[0, 1:2, begin:keys] = log_total[:, BLOCK:]


def attend_back_kernel(
    qr_ref, kr_ref, vm_ref, att_ref, d_ref, lse_ref, cos_ref, sin_ref, first_ref,
    dq_ref, dk_ref, dv_ref, key_sum, value_sum,
):
    length = qr_ref.shape[1]
    key_sum[...] = jnp.zeros_like(key_sum)
    value_sum[...] = jnp.zeros_like(value_sum)
    k_turned = kr_ref[0].T
    cosine, sine_part = cos_ref[...], sin_ref[...]
    product = (d_ref[0].astype(F32) * att_ref[0].astype(F32)).T
    inner = [
        jnp.sum(product[:64], axis=0, keepdims=True),
        jnp.sum(product[64:], axis=0, keepdims=True),
    ]
    for step in range(length // BLOCK):
        begin, keys = step * BLOCK, (step + 1) * BLOCK
        queries = two_heads(qr_ref[0, begin:keys, :])
        d_out = two_heads(d_ref[0, begin:keys, :])
        scores = dot_nt(kr_ref[0, :keys, :], queries)
        log_total = jnp.concatenate(
            [lse_ref[0, 0:1, begin:keys], lse_ref[0, 1:2, begin:keys]], axis=1
        )
        chances = jnp.where(seen(first_ref, begin, keys), jnp.exp(scores - log_total), 0.0)
        d_chances = dot_nt(vm_ref[0, :keys, :], d_out)
        part = jnp.concatenate([inner[0][:, begin:keys], inner[1][:, begin:keys]], axis=1)
        d_scores = (chances * (d_chances - part)).astype(BF16)
        key_sum[:keys, :] += dot_nn(d_scores, queries)
        value_sum[:keys, :] += dot_nn(chances.astype(BF16), d_out)
        d_query = one_pair(dot_nn(k_turned[:, :keys], d_scores), BLOCK) * 0.125
        dq_ref[0, begin:keys, :] = (
            d_query * cosine[begin:keys] - swap_halves(d_query) * sine_part[begin:keys]
        ).astype(BF16)
    d_key = key_sum[...]
    dk_ref[0] = (d_key * cosine - swap_halves(d_key) * sine_part).astype(BF16)
    dv_ref[0] = (0.5 * value_sum[...]).astype(BF16)


def attend(project, first_values, cos_wide, sin_wide, first_pos):
    pairs, length, _ = project.shape
    part = lambda i: pl.BlockSpec((1, length, LANES), lambda p: (p, 0, i))
    table = pl.BlockSpec((length, LANES), lambda p: (0, 0))
    out = jax.ShapeDtypeStruct((pairs, length, LANES), BF16)
    return pl.pallas_call(
        attend_kernel,
        grid=(pairs,),
        in_specs=[part(0), part(1), part(2), part(0), table, table,
                  pl.BlockSpec((1, length), lambda p: (0, 0))],
        out_specs=[part(0)] * 4 + [pl.BlockSpec((1, 2, length), lambda p: (p, 0, 0))],
        out_shape=[out] * 4 + [jax.ShapeDtypeStruct((pairs, 2, length), F32)],
        compiler_params=pltpu.CompilerParams(vmem_limit_bytes=48 << 20),
        cost_estimate=pl.CostEstimate(
            flops=pairs * length * length * 128 * 8, bytes_accessed=pairs * length * 128 * 24,
            transcendentals=pairs * length * length),
    )(project, project, project, first_values, cos_wide, sin_wide, first_pos[None, :])


def attend_back(saved, d_attended, cos_wide, sin_wide, first_pos):
    q_rot, k_rot, v_mix, attended, log_total = saved
    pairs, length, _ = q_rot.shape
    part = pl.BlockSpec((1, length, LANES), lambda p: (p, 0, 0))
    table = pl.BlockSpec((length, LANES), lambda p: (0, 0))
    out = jax.ShapeDtypeStruct((pairs, length, LANES), BF16)
    return pl.pallas_call(
        attend_back_kernel,
        grid=(pairs,),
        in_specs=[part] * 5 + [pl.BlockSpec((1, 2, length), lambda p: (p, 0, 0)), table, table,
                               pl.BlockSpec((1, length), lambda p: (0, 0))],
        out_specs=[part] * 3,
        out_shape=[out] * 3,
        scratch_shapes=[pltpu.VMEM((length, LANES), F32)] * 2,
        compiler_params=pltpu.CompilerParams(vmem_limit_bytes=48 << 20),
        cost_estimate=pl.CostEstimate(
            flops=pairs * length * length * 128 * 20, bytes_accessed=pairs * length * 128 * 24,
            transcendentals=pairs * length * length),
    )(q_rot, k_rot, v_mix, attended, d_attended, log_total, cos_wide, sin_wide, first_pos[None, :])


class Links:
    def __init__(self, n_seq, n_head, slots):
        self.n_seq, self.n_head, self.slots = n_seq, n_head, slots
        self.ranks = n_head // slots
        self.slot = lax.axis_index("head") // self.ranks
        self.rank = lax.axis_index("head") % self.ranks
        self.alike = [
            [s * n_head + q * self.ranks + r for s in range(n_seq) for q in range(slots)]
            for r in range(self.ranks)
        ]

    def permute(self, value, partner):
        pairs = []
        for s in range(self.n_seq):
            for h in range(self.n_head):
                to_s, to_h = partner(s, h)
                pairs.append((s * self.n_head + h, to_s * self.n_head + to_h))
        return lax.ppermute(value, AXES, pairs)

    def swap_slots(self, value):
        got = [lax.dynamic_index_in_dim(value, self.slot, 0, keepdims=False)]
        for step in range(1, self.slots):
            piece = lax.dynamic_index_in_dim(value, self.slot ^ step, 0, keepdims=False)
            got.append(self.permute(piece, lambda s, h: (s, h ^ (step * self.ranks))))
        got = jnp.stack(got)
        return jnp.stack(
            [lax.dynamic_index_in_dim(got, self.slot ^ q, 0, keepdims=False) for q in range(self.slots)]
        )

    def gather_ranks(self, value):
        got = [value] + [
            self.permute(value, lambda s, h: (s, h ^ step)) for step in range(1, self.ranks)
        ]
        got = jnp.stack(got)
        return jnp.stack(
            [lax.dynamic_index_in_dim(got, self.rank ^ r, 0, keepdims=False) for r in range(self.ranks)]
        )

    def sum_ranks(self, value):
        total = lax.dynamic_index_in_dim(value, self.rank, 0, keepdims=False)
        for step in range(1, self.ranks):
            piece = lax.dynamic_index_in_dim(value, self.rank ^ step, 0, keepdims=False)
            got = self.permute(piece.astype(BF16), lambda s, h: (s, h ^ step))
            total = total + got.astype(F32)
        return total

    def gather_alike(self, value):
        out = lax.all_gather(value, AXES, axis=0, axis_index_groups=self.alike)
        return out.reshape((self.n_seq, self.slots) + value.shape)

    def sum_alike(self, value):
        flat = value.reshape((self.n_seq * self.slots,) + value.shape[2:])
        return lax.psum_scatter(flat, AXES, scatter_dimension=0, axis_index_groups=self.alike)

    def whole_sequence(self, own):
        both = self.gather_ranks(own)
        return jnp.swapaxes(both, 0, 1).reshape(-1, own.shape[-1])

    def own_sum(self, full):
        rows = full.shape[0] // (self.slots * self.ranks)
        parts = full.reshape(self.slots, self.ranks, rows, full.shape[-1])
        return self.sum_ranks(jnp.swapaxes(parts, 0, 1)).reshape(-1, full.shape[-1])


def left_update(weight_rows, grad, row_begin, big_stat, big_root, small_stat, small_root, width):
    members, row_part, columns = weight_rows.shape
    model_width = grad.shape[1]
    blocks = columns // width
    grad_blocks = grad.reshape(members, model_width, blocks, width)
    grad_rows = lax.dynamic_slice_in_dim(grad_blocks, row_begin, row_part, 1)
    ein = functools.partial(jnp.einsum, preferred_element_type=F32)
    big_new = STAT_DECAY * big_stat + (1.0 - STAT_DECAY) * ein(
        "nrbk,nsbk->nbrs", grad_rows, grad_blocks
    )
    small_new = STAT_DECAY * small_stat + (1.0 - STAT_DECAY) * ein(
        "nrbk,nrbl->nbkl", grad_blocks, grad_blocks
    )
    step_dir = ein("nbrs,nsbk->nrbk", big_root.astype(BF16), grad_blocks)
    step_dir = ein("nrbk,nbkl->nrbl", step_dir.astype(BF16), small_root.astype(BF16))
    step_dir = step_dir * lax.rsqrt(jnp.mean(step_dir * step_dir, axis=-1, keepdims=True) + EPSILON)
    return weight_rows - STEP_RATE * step_dir.reshape(members, row_part, columns), big_new, small_new


def right_update(weight_cols, grad, col_begin, big_stat, big_root, small_stat, small_root, width, rate):
    rows_all, col_part = weight_cols.shape
    model_width = grad.shape[1]
    blocks = rows_all // width
    grad_blocks = grad.reshape(blocks, width, model_width)
    grad_cols = lax.dynamic_slice_in_dim(grad_blocks, col_begin, col_part, 2)
    ein = functools.partial(jnp.einsum, preferred_element_type=F32)
    big_new = STAT_DECAY * big_stat + (1.0 - STAT_DECAY) * ein("bkr,bks->brs", grad_cols, grad_blocks)
    small_new = STAT_DECAY * small_stat + (1.0 - STAT_DECAY) * ein(
        "bkr,blr->bkl", grad_blocks, grad_blocks
    )
    step_dir = ein("bkl,bls->bks", small_root.astype(BF16), grad_blocks)
    step_dir = ein("bks,brs->bkr", step_dir.astype(BF16), big_root.astype(BF16))
    step_dir = step_dir * lax.rsqrt(jnp.mean(step_dir * step_dir, axis=1, keepdims=True) + EPSILON)
    return weight_cols - rate * step_dir.reshape(rows_all, col_part), big_new, small_new


def shards(
    n_seq,
    n_head,
    layer_input,
    values_first,
    w_qkv,
    w_gate_up,
    w_out,
    w_down,
    norm_gains,
    out_grad,
    segments,
    counts,
    stats_wide,
    roots_wide,
    stats_head,
    roots_head,
    stats_unit,
    roots_unit,
):
    slots, rows, width = layer_input.shape
    length = segments.shape[1]
    row_part, head_cols, ffn_cols = w_qkv.shape[1], w_qkv.shape[2], w_gate_up.shape[2]
    head_dim, unit_block = stats_head.shape[2], stats_unit.shape[2]
    links = Links(n_seq, n_head, slots)
    row_begin = lax.axis_index("seq") * row_part
    is_live = links.slot < counts[0]
    my_heads = slots * head_cols
    pairs = my_heads // LANES

    def pair_major(value):
        if head_cols == LANES:
            return value
        per = LANES // head_cols
        value = value.reshape(pairs, per, length, head_cols)
        return jnp.swapaxes(value, 1, 2).reshape(pairs, length, LANES)

    def slot_major(value):
        if head_cols == LANES:
            return value
        per = LANES // head_cols
        value = value.reshape(pairs, length, per, head_cols)
        return jnp.swapaxes(value, 1, 2).reshape(slots, length, head_cols)

    qkv_all = links.gather_alike(w_qkv.astype(BF16))
    x_own = links.swap_slots(layer_input).reshape(slots * rows, width).astype(F32)
    first_all = pair_major(links.swap_slots(values_first))
    out_all = links.gather_alike(w_out.astype(BF16))
    gate_up_all = links.gather_alike(w_gate_up.astype(BF16))
    down_all = links.gather_alike(w_down.astype(BF16))
    per = LANES // head_cols
    qkv_w = qkv_all.reshape(n_seq, pairs, per, 3, row_part, head_cols)
    qkv_w = qkv_w.transpose(1, 0, 4, 3, 2, 5).reshape(pairs, width, 3 * LANES)
    out_w = out_all.transpose(1, 2, 0, 3).reshape(my_heads, width)
    gate_up_w = gate_up_all.transpose(0, 3, 2, 1, 4).reshape(width, 2 * slots * ffn_cols)
    down_w = down_all.transpose(1, 2, 0, 3).reshape(slots * ffn_cols, width)
    units = slots * ffn_cols

    segment_ids = lax.dynamic_index_in_dim(segments, links.slot, 0, keepdims=False)
    first_pos, cos_wide, sin_wide = position_tables(segment_ids, head_dim)

    inverse_one = lax.rsqrt(jnp.mean(x_own * x_own, axis=-1, keepdims=True) + EPSILON)
    normed_one = x_own * inverse_one
    h_one = links.whole_sequence(
        (normed_one * norm_gains[0]).astype(BF16).reshape(slots, rows, width)
    )
    project = jnp.einsum("ld,pdc->plc", h_one, qkv_w, preferred_element_type=F32)
    saved = attend(project, first_all, cos_wide, sin_wide, first_pos)
    attended = jnp.swapaxes(saved[3], 0, 1).reshape(length, my_heads)
    attn_out = links.own_sum(dot_nn(attended, out_w))
    middle = x_own + attn_out
    inverse_two = lax.rsqrt(jnp.mean(middle * middle, axis=-1, keepdims=True) + EPSILON)
    normed_two = middle * inverse_two
    h_two = links.whole_sequence(
        (normed_two * norm_gains[1]).astype(BF16).reshape(slots, rows, width)
    )
    gate_up = dot_nn(h_two, gate_up_w)
    gate, up = gate_up[:, :units], gate_up[:, units:]
    sigmoid_gate = jax.nn.sigmoid(gate)
    activated = gate * sigmoid_gate
    hidden = (activated * up).astype(BF16)
    ffn_out = links.own_sum(dot_nn(hidden, down_w))
    block_delta = jnp.where(is_live, attn_out + ffn_out, 0.0).astype(BF16)
    block_out = layer_input.astype(F32) + links.swap_slots(
        block_delta.reshape(slots, rows, width)
    ).astype(F32)

    grad_own = links.swap_slots(out_grad)
    d_own = jnp.where(is_live, grad_own, jnp.zeros_like(grad_own))
    d_out = d_own.reshape(slots * rows, width).astype(F32)
    d_ffn = links.whole_sequence(d_own)
    g_down = dot_tn(hidden, d_ffn)
    sum_down = links.sum_alike(
        g_down.astype(BF16).reshape(slots, ffn_cols, n_seq, row_part).transpose(2, 0, 1, 3)
    )
    d_hidden = dot_nt(d_ffn, down_w)
    d_gate = (
        d_hidden * up * sigmoid_gate * (1.0 + gate * (1.0 - sigmoid_gate))
    ).astype(BF16)
    d_up = (d_hidden * activated).astype(BF16)
    d_gate_up = jnp.concatenate([d_gate, d_up], axis=1)
    d_normed_two = links.own_sum(dot_nt(d_gate_up, gate_up_w))
    g_gate_up = dot_tn(h_two, d_gate_up)
    sum_gate_up = links.sum_alike(
        g_gate_up.astype(BF16)
        .reshape(n_seq, row_part, 2, slots, ffn_cols)
        .transpose(0, 3, 2, 1, 4)
    )
    gain_two = jnp.sum(normed_two * d_normed_two, axis=0)
    middle_delta = norm_back(d_normed_two * norm_gains[1], normed_two, inverse_two)
    d_middle = d_out + middle_delta
    d_attn = links.whole_sequence(d_middle.astype(BF16).reshape(slots, rows, width))
    d_attended = dot_nt(d_attn, out_w).astype(BF16)
    d_query, d_key, d_value = attend_back(
        saved,
        jnp.swapaxes(d_attended.reshape(length, pairs, LANES), 0, 1),
        cos_wide,
        sin_wide,
        first_pos,
    )
    first_grad = links.swap_slots(slot_major(d_value)).astype(F32)
    g_out = dot_tn(attended, d_attn)
    sum_out = links.sum_alike(
        g_out.astype(BF16).reshape(slots, head_cols, n_seq, row_part).transpose(2, 0, 1, 3)
    )
    d_project = jnp.concatenate([d_query, d_key, d_value], axis=2)
    g_qkv = jnp.einsum("ld,plc->pdc", h_one, d_project, preferred_element_type=F32)
    sum_qkv = links.sum_alike(
        g_qkv.astype(BF16)
        .reshape(pairs, n_seq, row_part, 3, per, head_cols)
        .transpose(1, 0, 4, 3, 2, 5)
        .reshape(n_seq, slots, 3, row_part, head_cols)
    )
    d_normed_one = links.own_sum(
        jnp.einsum("plc,pdc->ld", d_project, qkv_w, preferred_element_type=F32)
    )
    gain_one = jnp.sum(normed_one * d_normed_one, axis=0)
    input_delta = middle_delta + norm_back(d_normed_one * norm_gains[0], normed_one, inverse_one)
    input_delta = jnp.where(is_live, input_delta, 0.0).astype(BF16)
    input_grad = out_grad.astype(F32) + links.swap_slots(
        input_delta.reshape(slots, rows, width)
    ).astype(F32)

    grad_gains = lax.psum(jnp.stack([gain_one, gain_two]), AXES)
    new_gains = norm_gains - GAIN_RATE * grad_gains * lax.rsqrt(
        jnp.mean(grad_gains * grad_gains, axis=-1, keepdims=True) + EPSILON
    )

    full_down = lax.all_gather(sum_down, "seq", axis=1, tiled=True)
    full_gate_up = lax.all_gather(sum_gate_up, "seq", axis=1, tiled=True)
    full_out = lax.all_gather(sum_out, "seq", axis=1, tiled=True)
    full_qkv = lax.all_gather(sum_qkv, "seq", axis=1, tiled=True)

    new_down, wide_down, unit_down = right_update(
        w_down, full_down, row_begin, stats_wide[6], roots_wide[6], stats_unit[2], roots_unit[2],
        unit_block, STEP_RATE,
    )
    new_gate_up, wide_gu, unit_gu = left_update(
        w_gate_up, full_gate_up, row_begin, stats_wide[3:5], roots_wide[3:5], stats_unit[0:2],
        roots_unit[0:2], unit_block,
    )
    new_out, wide_out, head_out = right_update(
        w_out, full_out, row_begin, stats_wide[5], roots_wide[5], stats_head[3], roots_head[3],
        head_dim, OUT_RATE,
    )
    new_qkv, wide_qkv, head_qkv = left_update(
        w_qkv, full_qkv, row_begin, stats_wide[0:3], roots_wide[0:3], stats_head[0:3],
        roots_head[0:3], head_dim,
    )
    return (
        block_out,
        input_grad,
        first_grad,
        sum_qkv.astype(F32),
        sum_gate_up.astype(F32),
        sum_out.astype(F32),
        sum_down.astype(F32),
        grad_gains,
        new_qkv,
        new_gate_up,
        new_out,
        new_down,
        new_gains,
        jnp.concatenate([wide_qkv, wide_gu, wide_down[None]], axis=0),
        wide_out,
        jnp.concatenate([head_qkv, head_out[None]], axis=0),
        jnp.concatenate([unit_gu, unit_down[None]], axis=0),
    )


def solution(mesh):
    return jax.shard_map(
        functools.partial(shards, mesh.shape["seq"], mesh.shape["head"]),
        mesh=mesh,
        in_specs=(
            P("seq", "head", None),
            P("seq", None, "head"),
            P(None, "seq", "head"),
            P(None, "seq", "head"),
            P("head", "seq"),
            P("head", "seq"),
            P(),
            P("seq", "head", None),
            P("seq", None),
            P("seq"),
            P(None, "head", "seq", None),
            P(None, "head", "seq", None),
            P(None, "head", None, None),
            P(None, "head", None, None),
            P(None, "head", None, None),
            P(None, "head", None, None),
        ),
        out_specs=(
            P("seq", "head", None),
            P("seq", "head", None),
            P("seq", None, "head"),
            P(None, "seq", "head"),
            P(None, "seq", "head"),
            P("head", "seq"),
            P("head", "seq"),
            P(),
            P(None, "seq", "head"),
            P(None, "seq", "head"),
            P("head", "seq"),
            P("head", "seq"),
            P(),
            P(None, "head", "seq", None),
            P("head", "seq", None),
            P(None, "head", None, None),
            P(None, "head", None, None),
        ),
        check_vma=False,
    )
```

```python
import functools

import jax
import jax.numpy as jnp
from jax import lax
from jax.experimental import pallas as pl
from jax.experimental.pallas import tpu as pltpu
from jax.sharding import PartitionSpec as P

EPSILON = 1e-06
STAT_DECAY = 0.5
STEP_RATE = 0.02
OUT_RATE = 0.1
GAIN_RATE = 0.25
AXES = ("seq", "head")
MESH = pl.DeviceIdType.MESH
LANES = 128
BLOCK = 256
BF16 = jnp.bfloat16
F32 = jnp.float32


def dot_nt(matrix_a, matrix_b):
    return lax.dot_general(
        matrix_a, matrix_b, (((1,), (1,)), ((), ())), preferred_element_type=F32
    )


def dot_tn(matrix_a, matrix_b):
    return lax.dot_general(
        matrix_a, matrix_b, (((0,), (0,)), ((), ())), preferred_element_type=F32
    )


def dot_nn(matrix_a, matrix_b):
    return jnp.dot(matrix_a, matrix_b, preferred_element_type=F32)


def norm_back(d_normed, normed, inverse):
    return inverse * (d_normed - normed * jnp.mean(d_normed * normed, axis=-1, keepdims=True))


def position_tables(segment_ids, head_dim):
    length = segment_ids.shape[0]
    position = jnp.arange(length, dtype=jnp.int32)
    opens = jnp.concatenate([jnp.ones((1,), dtype=bool), segment_ids[1:] != segment_ids[:-1]])
    first_pos = lax.cummax(jnp.where(opens, position, 0), axis=0)
    offset = (position - first_pos).astype(F32)
    half_width = head_dim // 2
    frequency = jnp.exp(-jnp.log(10000.0) * jnp.arange(half_width, dtype=F32) / half_width)
    angle = offset[:, None] * frequency[None, :]
    cosine, sine_part = jnp.cos(angle), jnp.sin(angle)
    per_lane = LANES // head_dim
    cos_wide = jnp.concatenate([cosine, cosine] * per_lane, axis=1)
    sin_wide = jnp.concatenate([-sine_part, sine_part] * per_lane, axis=1)
    return first_pos, cos_wide, sin_wide


def swap_halves(values):
    lane = lax.broadcasted_iota(jnp.int32, values.shape, 1)
    return jnp.where((lane & 32) == 0, pltpu.roll(values, 96, 1), pltpu.roll(values, 32, 1))


def two_heads(block):
    lane = lax.broadcasted_iota(jnp.int32, block.shape, 1)
    zero = jnp.zeros_like(block)
    return jnp.concatenate(
        [jnp.where(lane < 64, block, zero), jnp.where(lane >= 64, block, zero)], axis=0
    )


def one_pair(transposed, width):
    kept = jnp.concatenate([transposed[:64, :width], transposed[64:, width:]], axis=0)
    return kept.T


def seen(first_ref, begin, key_count):
    first = first_ref[0:1, begin : begin + BLOCK]
    query = begin + lax.broadcasted_iota(jnp.int32, (1, BLOCK), 1)
    first = jnp.concatenate([first, first], axis=1)
    query = jnp.concatenate([query, query], axis=1)
    key = lax.broadcasted_iota(jnp.int32, (key_count, 2 * BLOCK), 0)
    return (key >= first) & (key <= query)


def attend_kernel(
    q_ref, k_ref, v_ref, vf_ref, cos_ref, sin_ref, first_ref, qr_ref, kr_ref, vm_ref, att_ref, lse_ref
):
    length = q_ref.shape[1]
    cosine, sine_part = cos_ref[...], sin_ref[...]
    q_raw, k_raw = q_ref[0], k_ref[0]
    qr_ref[0] = ((q_raw * cosine + swap_halves(q_raw) * sine_part) * 0.125).astype(BF16)
    kr_ref[0] = (k_raw * cosine + swap_halves(k_raw) * sine_part).astype(BF16)
    v_mix = (0.5 * v_ref[0] + 0.5 * vf_ref[0].astype(F32)).astype(BF16)
    vm_ref[0] = v_mix
    v_turned = v_mix.T
    for step in range(length // BLOCK):
        begin, keys = step * BLOCK, (step + 1) * BLOCK
        queries = two_heads(qr_ref[0, begin:keys, :])
        scores = dot_nt(kr_ref[0, :keys, :], queries)
        scores = jnp.where(seen(first_ref, begin, keys), scores, -1e30)
        top = jnp.max(scores, axis=0, keepdims=True)
        exps = jnp.exp(scores - top)
        total = jnp.sum(exps, axis=0, keepdims=True)
        chances = (exps * (1.0 / total)).astype(BF16)
        attended = dot_nn(v_turned[:, :keys], chances)
        att_ref[0, begin:keys, :] = one_pair(attended, BLOCK).astype(BF16)
        log_total = top + jnp.log(total)
        lse_ref[0, 0:1, begin:keys] = log_total[:, :BLOCK]
        lse_ref[0, 1:2, begin:keys] = log_total[:, BLOCK:]


def attend_back_kernel(
    qr_ref, kr_ref, vm_ref, att_ref, d_ref, lse_ref, cos_ref, sin_ref, first_ref,
    dq_ref, dk_ref, dv_ref, key_sum, value_sum,
):
    length = qr_ref.shape[1]
    key_sum[...] = jnp.zeros_like(key_sum)
    value_sum[...] = jnp.zeros_like(value_sum)
    k_turned = kr_ref[0].T
    cosine, sine_part = cos_ref[...], sin_ref[...]
    product = (d_ref[0].astype(F32) * att_ref[0].astype(F32)).T
    inner = [
        jnp.sum(product[:64], axis=0, keepdims=True),
        jnp.sum(product[64:], axis=0, keepdims=True),
    ]
    for step in range(length // BLOCK):
        begin, keys = step * BLOCK, (step + 1) * BLOCK
        queries = two_heads(qr_ref[0, begin:keys, :])
        d_out = two_heads(d_ref[0, begin:keys, :])
        scores = dot_nt(kr_ref[0, :keys, :], queries)
        log_total = jnp.concatenate(
            [lse_ref[0, 0:1, begin:keys], lse_ref[0, 1:2, begin:keys]], axis=1
        )
        chances = jnp.where(seen(first_ref, begin, keys), jnp.exp(scores - log_total), 0.0)
        d_chances = dot_nt(vm_ref[0, :keys, :], d_out)
        part = jnp.concatenate([inner[0][:, begin:keys], inner[1][:, begin:keys]], axis=1)
        d_scores = (chances * (d_chances - part)).astype(BF16)
        key_sum[:keys, :] += dot_nn(d_scores, queries)
        value_sum[:keys, :] += dot_nn(chances.astype(BF16), d_out)
        d_query = one_pair(dot_nn(k_turned[:, :keys], d_scores), BLOCK) * 0.125
        dq_ref[0, begin:keys, :] = (
            d_query * cosine[begin:keys] - swap_halves(d_query) * sine_part[begin:keys]
        ).astype(BF16)
    d_key = key_sum[...]
    dk_ref[0] = (d_key * cosine - swap_halves(d_key) * sine_part).astype(BF16)
    dv_ref[0] = (0.5 * value_sum[...]).astype(BF16)


def attend(project, first_values, cos_wide, sin_wide, first_pos):
    pairs, length, _ = project.shape
    part = lambda i: pl.BlockSpec((1, length, LANES), lambda p: (p, 0, i))
    table = pl.BlockSpec((length, LANES), lambda p: (0, 0))
    out = jax.ShapeDtypeStruct((pairs, length, LANES), BF16)
    return pl.pallas_call(
        attend_kernel,
        grid=(pairs,),
        in_specs=[part(0), part(1), part(2), part(0), table, table,
                  pl.BlockSpec((1, length), lambda p: (0, 0))],
        out_specs=[part(0)] * 4 + [pl.BlockSpec((1, 2, length), lambda p: (p, 0, 0))],
        out_shape=[out] * 4 + [jax.ShapeDtypeStruct((pairs, 2, length), F32)],
        compiler_params=pltpu.CompilerParams(vmem_limit_bytes=48 << 20),
        cost_estimate=pl.CostEstimate(
            flops=pairs * length * length * 128 * 8, bytes_accessed=pairs * length * 128 * 24,
            transcendentals=pairs * length * length),
    )(project, project, project, first_values, cos_wide, sin_wide, first_pos[None, :])


def attend_back(saved, d_attended, cos_wide, sin_wide, first_pos):
    q_rot, k_rot, v_mix, attended, log_total = saved
    pairs, length, _ = q_rot.shape
    part = pl.BlockSpec((1, length, LANES), lambda p: (p, 0, 0))
    table = pl.BlockSpec((length, LANES), lambda p: (0, 0))
    out = jax.ShapeDtypeStruct((pairs, length, LANES), BF16)
    return pl.pallas_call(
        attend_back_kernel,
        grid=(pairs,),
        in_specs=[part] * 5 + [pl.BlockSpec((1, 2, length), lambda p: (p, 0, 0)), table, table,
                               pl.BlockSpec((1, length), lambda p: (0, 0))],
        out_specs=[part] * 3,
        out_shape=[out] * 3,
        scratch_shapes=[pltpu.VMEM((length, LANES), F32)] * 2,
        compiler_params=pltpu.CompilerParams(vmem_limit_bytes=48 << 20),
        cost_estimate=pl.CostEstimate(
            flops=pairs * length * length * 128 * 20, bytes_accessed=pairs * length * 128 * 24,
            transcendentals=pairs * length * length),
    )(q_rot, k_rot, v_mix, attended, d_attended, log_total, cos_wide, sin_wide, first_pos[None, :])


class Place:
    def __init__(self, n_seq, n_head, slots):
        self.n_seq, self.slots, self.ranks = n_seq, slots, n_head // slots
        self.seq = lax.axis_index("seq")
        head = lax.axis_index("head")
        self.slot, self.rank = head // self.ranks, head % self.ranks

    def at_slot(self, step):
        return (self.slot + step + self.slots) % self.slots

    def at_seq(self, step):
        return (self.seq + step + self.n_seq) % self.n_seq

    def device(self, seq=None, slot=None, rank=None):
        seq = self.seq if seq is None else seq
        slot = self.slot if slot is None else slot
        rank = self.rank if rank is None else rank
        return (seq, slot * self.ranks + rank)

    def greet(self, with_ranks):
        others = [self.device(slot=self.at_slot(k)) for k in range(1, self.slots)]
        others += [self.device(seq=self.at_seq(d)) for d in range(1, self.n_seq)]
        if with_ranks:
            others += [
                self.device(rank=(self.rank + j) % self.ranks) for j in range(1, self.ranks)
            ]
        barrier = pltpu.get_barrier_semaphore()
        for other in others:
            pl.semaphore_signal(barrier, inc=1, device_id=other, device_id_type=MESH)
        pl.semaphore_wait(barrier, len(others))


class Sender:
    def __init__(self, send_sems, recv_sems):
        self.send_sems, self.recv_sems, self.used = send_sems, recv_sems, 0

    def start(self, src, dst, device):
        copy = pltpu.make_async_remote_copy(
            src_ref=src,
            dst_ref=dst,
            send_sem=self.send_sems.at[self.used],
            recv_sem=self.recv_sems.at[self.used],
            device_id=device,
            device_id_type=MESH,
        )
        self.used += 1
        copy.start()
        return copy


def lanes(index, width):
    return pl.ds(pl.multiple_of(index * width, width), width)


def gather_kernel(
    n_seq, n_head, sections, x_ref, vf_ref, wt_ref, x_out, vf_out, w_out, send_sems, recv_sems, own_sems
):
    slots = x_ref.shape[0]
    part = wt_ref.shape[1]
    place = Place(n_seq, n_head, slots)
    place.greet(False)
    sender = Sender(send_sems, recv_sems)
    mine = lanes(place.seq, part)

    def swap(src, dst):
        return [
            sender.start(
                src.at[place.at_slot(k)], dst.at[place.slot], place.device(slot=place.at_slot(k))
            )
            for k in (2, 3, 1)
        ]

    def to_slots(section):
        rows = pl.ds(*section)
        return [
            sender.start(
                wt_ref.at[rows],
                w_out.at[place.slot, rows, mine],
                place.device(slot=place.at_slot(k)),
            )
            for k in range(1, slots)
        ]

    def to_seqs(section, step):
        rows = pl.ds(*section)
        slot = place.at_slot(-step)
        src = wt_ref.at[rows] if step == 0 else w_out.at[slot, rows, mine]
        return [
            sender.start(
                src, w_out.at[slot, rows, mine], place.device(seq=place.at_seq(d))
            )
            for d in range(1, n_seq)
        ]

    own = [
        pltpu.make_async_copy(x_ref.at[place.slot], x_out.at[place.slot], own_sems.at[0]),
        pltpu.make_async_copy(vf_ref.at[place.slot], vf_out.at[place.slot], own_sems.at[1]),
        pltpu.make_async_copy(wt_ref, w_out.at[place.slot, :, mine], own_sems.at[2]),
    ]
    x_copies = swap(x_ref, x_out)
    copies = list(x_copies)
    for copy in own:
        copy.start()
    near = to_slots(sections[0])
    copies += near
    copies += to_seqs(sections[0], 0)
    copies += to_seqs(sections[1], 0)
    received = []
    for step, copy in enumerate(near):
        copy.wait_recv()
        copies += to_seqs(sections[0], step + 1)
    received += near
    copies += swap(vf_ref, vf_out)
    near = to_slots(sections[1])
    copies += near
    for step, copy in enumerate(near):
        copy.wait_recv()
        copies += to_seqs(sections[1], step + 1)
    received += near
    for copy in copies:
        if all(copy is not other for other in received):
            copy.wait_recv()
    for copy in copies:
        copy.wait_send()
    for copy in own:
        copy.wait()


def gather_inputs(n_seq, n_head, sections, layer_input, values_first, weight_rows):
    slots = layer_input.shape[0]
    rows, part = weight_rows.shape
    count = 2 * (slots - 1) + len(sections) * ((slots - 1) + slots * (n_seq - 1))
    any_space = pl.BlockSpec(memory_space=pl.ANY)
    return pl.pallas_call(
        functools.partial(gather_kernel, n_seq, n_head, sections),
        in_specs=[any_space] * 3,
        out_specs=[any_space] * 3,
        out_shape=[
            jax.ShapeDtypeStruct(layer_input.shape, BF16),
            jax.ShapeDtypeStruct(values_first.shape, BF16),
            jax.ShapeDtypeStruct((slots, rows, part * n_seq), BF16),
        ],
        scratch_shapes=[
            pltpu.SemaphoreType.DMA((count,)),
            pltpu.SemaphoreType.DMA((count,)),
            pltpu.SemaphoreType.DMA((3,)),
        ],
        compiler_params=pltpu.CompilerParams(collective_id=0, has_side_effects=True),
    )(layer_input, values_first, weight_rows)


def reduce_kernel(
    n_seq, n_head, chunks,
    block_ref, input_ref, first_ref, gains_ref, grads_a, grads_b,
    block_out, input_out, first_out, gains_out, sum_a, sum_b, full_a, full_b,
    near_a, near_b, turn_a, turn_b, far_a, far_b, gain_seq, gain_slot, gain_rank,
    send_sems, recv_sems, own_sems,
):
    slots = block_ref.shape[0]
    place = Place(n_seq, n_head, slots)
    place.greet(True)
    sender = Sender(send_sems, recv_sems)
    part = sum_a.shape[1]
    mine = lanes(place.seq, part)
    order = [2, 3, 1, 0]
    parts = ((grads_b, sum_b, full_b, near_b, turn_b, far_b, chunks[1]),
             (grads_a, sum_a, full_a, near_a, turn_a, far_a, chunks[0]))
    copies, received = [], []

    def arrive(copy):
        copy.wait_recv()
        received.append(copy)

    def swap(src, dst):
        return [
            sender.start(
                src.at[place.at_slot(k)], dst.at[place.slot], place.device(slot=place.at_slot(k))
            )
            for k in (2, 3, 1)
        ]

    gain_seq[place.seq] = gains_ref[...]
    small = [
        sender.start(gain_seq.at[place.seq], gain_seq.at[place.seq],
                     place.device(seq=place.at_seq(d)))
        for d in range(1, n_seq)
    ]
    copies += small

    def to_seqs(grads, near, k):
        slot = place.at_slot(k)
        return [
            sender.start(
                grads.at[slot, :, lanes(place.at_seq(d), part)],
                near.at[k, d - 1],
                place.device(seq=place.at_seq(d)),
            )
            for d in range(1, n_seq)
        ]

    sent = {}
    units = [(which, k) for which in range(2) for k in order]

    def launch(unit):
        which, k = unit
        sent[unit] = to_seqs(parts[which][0], parts[which][3], k)
        copies.extend(sent[unit])

    own = [
        pltpu.make_async_copy(src.at[place.slot], dst.at[place.slot], own_sems.at[i])
        for i, (src, dst) in enumerate(
            ((block_ref, block_out), (input_ref, input_out), (first_ref, first_out))
        )
    ]
    for copy in own:
        copy.start()
    launch(units[0])
    launch(units[1])
    copies += swap(block_ref, block_out)
    for copy in small:
        arrive(copy)
    total = gain_seq[0]
    for i in range(1, n_seq):
        total = total + gain_seq[i]
    gain_slot[place.slot] = total
    small = [
        sender.start(gain_slot.at[place.slot], gain_slot.at[place.slot],
                     place.device(slot=place.at_slot(k)))
        for k in range(1, slots)
    ]
    copies += small
    far_copies = {0: [], 1: []}
    for index, unit in enumerate(units):
        which, k = unit
        grads, _, _, near, turn, far, chunk = parts[which]
        if index + 2 < len(units):
            launch(units[index + 2])
        for copy in sent[unit]:
            arrive(copy)
        slot = place.at_slot(k)

        def add(i, carry, grads=grads, near=near, turn=turn, slot=slot, k=k, chunk=chunk):
            rows = pl.ds(pl.multiple_of(i * chunk, chunk), chunk)
            value = grads[slot, rows, mine].astype(F32)
            for d in range(n_seq - 1):
                value = value + near[k, d, rows, :].astype(F32)
            turn[k, rows, :] = value.astype(BF16)
            return carry

        lax.fori_loop(0, grads.shape[1] // chunk, add, 0)
        if k != 0:
            copy = sender.start(turn.at[k], far.at[k - 1], place.device(slot=slot))
            copies.append(copy)
            far_copies[which].append(copy)
        if index == 1:
            copies += swap(first_ref, first_out)
        if index == 4:
            copies += swap(input_ref, input_out)
            for copy in small:
                arrive(copy)
            total = gain_slot[0]
            for i in range(1, slots):
                total = total + gain_slot[i]
            gain_rank[place.rank] = total
            small = [
                sender.start(gain_rank.at[place.rank], gain_rank.at[place.rank],
                             place.device(rank=(place.rank + j) % place.ranks))
                for j in range(1, place.ranks)
            ]
            copies += small
        if k == 0:
            for copy in far_copies[which]:
                arrive(copy)
            _, total_ref, full, _, _, _, _ = parts[which]

            def finish(i, carry, turn=turn, far=far, total_ref=total_ref, full=full, chunk=chunk):
                rows = pl.ds(pl.multiple_of(i * chunk, chunk), chunk)
                value = turn[0, rows, :].astype(F32)
                for j in range(slots - 1):
                    value = value + far[j, rows, :].astype(F32)
                value = value.astype(BF16)
                total_ref[rows, :] = value
                full[rows, mine] = value
                return carry

            lax.fori_loop(0, grads.shape[1] // chunk, finish, 0)
            copies += [
                sender.start(total_ref, full.at[:, mine], place.device(seq=place.at_seq(d)))
                for d in range(1, n_seq)
            ]
    for copy in small:
        arrive(copy)
    total = gain_rank[0]
    for i in range(1, place.ranks):
        total = total + gain_rank[i]
    gains_out[...] = total
    for copy in copies:
        if all(copy is not other for other in received):
            copy.wait_recv()
    for copy in copies:
        copy.wait_send()
    for copy in own:
        copy.wait()


def reduce_grads(n_seq, n_head, chunks, block_delta, input_delta, first_delta, gains, grads_a, grads_b):
    slots = block_delta.shape[0]
    part = grads_a.shape[2] // n_seq
    rows = (grads_a.shape[1], grads_b.shape[1])
    ranks = n_head // slots
    count = (
        3 * (slots - 1) + 2 * (slots * (n_seq - 1) + (slots - 1) + (n_seq - 1))
        + (n_seq - 1) + (slots - 1) + (ranks - 1)
    )
    any_space = pl.BlockSpec(memory_space=pl.ANY)
    vmem = pl.BlockSpec(memory_space=pltpu.VMEM)
    like = lambda value: jax.ShapeDtypeStruct(value.shape, value.dtype)
    return pl.pallas_call(
        functools.partial(reduce_kernel, n_seq, n_head, chunks),
        in_specs=[any_space] * 3 + [vmem] * 3,
        out_specs=[any_space] * 3 + [vmem] * 5,
        out_shape=[like(block_delta), like(input_delta), like(first_delta), like(gains)]
        + [jax.ShapeDtypeStruct((r, part), BF16) for r in rows]
        + [jax.ShapeDtypeStruct((r, part * n_seq), BF16) for r in rows],
        scratch_shapes=[pltpu.VMEM((slots, n_seq - 1, r, part), BF16) for r in rows]
        + [pltpu.VMEM((slots, r, part), BF16) for r in rows]
        + [pltpu.VMEM((slots - 1, r, part), BF16) for r in rows]
        + [pltpu.VMEM((n,) + gains.shape, F32) for n in (n_seq, slots, ranks)]
        + [
            pltpu.SemaphoreType.DMA((count,)),
            pltpu.SemaphoreType.DMA((count,)),
            pltpu.SemaphoreType.DMA((3,)),
        ],
        compiler_params=pltpu.CompilerParams(
            collective_id=1, has_side_effects=True, vmem_limit_bytes=56 << 20
        ),
    )(block_delta, input_delta, first_delta, gains, grads_a, grads_b)


def shampoo_kernel(
    stat_ref, root_ref, head_stat, head_root, unit_stat, unit_root, full_a, sum_a, full_b, sum_b,
    wide_ref, out_right_ref, new_head, new_unit, step_a, step_b,
):
    step = pl.program_id(0)
    blocks = stat_ref.shape[1]

    def one(member, width, small_stat, small_root, full, total, big_out, small_out, step_out):
        for b in range(blocks):
            rows = pl.ds(pl.multiple_of((member * blocks + b) * width, 16), width)
            grad, own = full[rows, :], total[rows, :]
            big_out[0, b] = STAT_DECAY * stat_ref[0, b] + (1.0 - STAT_DECAY) * dot_tn(own, grad)
            small_out[member, b] = STAT_DECAY * small_stat[member, b] + (
                1.0 - STAT_DECAY
            ) * dot_nt(grad, grad)
            turned = dot_nn(small_root[member, b].astype(BF16), grad).astype(BF16)
            turned = dot_nt(turned, root_ref[0, b].astype(BF16))
            scale = lax.rsqrt(jnp.mean(turned * turned, axis=0, keepdims=True) + EPSILON)
            step_out[rows, :] = turned * scale

    head_width, unit_width = head_stat.shape[2], unit_stat.shape[2]
    head_args = (head_width, head_stat, head_root, full_a, sum_a)
    unit_args = (unit_width, unit_stat, unit_root, full_b, sum_b)

    @pl.when(step < 3)
    def _():
        one(step, *head_args, wide_ref, new_head, step_a)

    @pl.when((step >= 3) & (step < 6))
    def _():
        one(step - 3, *unit_args, wide_ref, new_unit, step_b)

    @pl.when(step == 6)
    def _():
        one(3, *head_args, out_right_ref, new_head, step_a)


def shampoo(stats_wide, roots_wide, stats_head, roots_head, stats_unit, roots_unit, full_a, sum_a, full_b, sum_b):
    members, blocks, part, width = stats_wide.shape
    member = lambda i: (jnp.where(i == 5, 6, jnp.where(i == 6, 5, i)), 0, 0, 0)
    wide = pl.BlockSpec((1, blocks, part, width), member)
    vmem = pl.BlockSpec(memory_space=pltpu.VMEM)
    return pl.pallas_call(
        shampoo_kernel,
        grid=(members,),
        in_specs=[wide, wide] + [vmem] * 8,
        out_specs=[
            pl.BlockSpec((1, blocks, part, width), lambda i: (jnp.minimum(i, 5), 0, 0, 0)),
            pl.BlockSpec((1, blocks, part, width), lambda i: (0, 0, 0, 0)),
            vmem, vmem, vmem, vmem,
        ],
        out_shape=[
            jax.ShapeDtypeStruct((members - 1, blocks, part, width), F32),
            jax.ShapeDtypeStruct((1, blocks, part, width), F32),
            jax.ShapeDtypeStruct(stats_head.shape, F32),
            jax.ShapeDtypeStruct(stats_unit.shape, F32),
            jax.ShapeDtypeStruct(sum_a.shape, F32),
            jax.ShapeDtypeStruct(sum_b.shape, F32),
        ],
        compiler_params=pltpu.CompilerParams(vmem_limit_bytes=48 << 20),
    )(stats_wide, roots_wide, stats_head, roots_head, stats_unit, roots_unit, full_a, sum_a, full_b, sum_b)


class Links:
    def __init__(self, n_seq, n_head, slots):
        self.n_seq, self.n_head, self.slots = n_seq, n_head, slots
        self.ranks = n_head // slots
        self.slot = lax.axis_index("head") // self.ranks
        self.rank = lax.axis_index("head") % self.ranks

    def permute(self, value, partner):
        pairs = []
        for s in range(self.n_seq):
            for h in range(self.n_head):
                to_s, to_h = partner(s, h)
                pairs.append((s * self.n_head + h, to_s * self.n_head + to_h))
        return lax.ppermute(value, AXES, pairs)

    def swap_slots(self, value):
        got = [lax.dynamic_index_in_dim(value, self.slot, 0, keepdims=False)]
        for step in range(1, self.slots):
            piece = lax.dynamic_index_in_dim(value, self.slot ^ step, 0, keepdims=False)
            got.append(self.permute(piece, lambda s, h: (s, h ^ (step * self.ranks))))
        got = jnp.stack(got)
        return jnp.stack(
            [lax.dynamic_index_in_dim(got, self.slot ^ q, 0, keepdims=False) for q in range(self.slots)]
        )

    def gather_ranks(self, value):
        got = [value] + [
            self.permute(value, lambda s, h: (s, h ^ step)) for step in range(1, self.ranks)
        ]
        got = jnp.stack(got)
        return jnp.stack(
            [lax.dynamic_index_in_dim(got, self.rank ^ r, 0, keepdims=False) for r in range(self.ranks)]
        )

    def sum_ranks(self, value):
        total = lax.dynamic_index_in_dim(value, self.rank, 0, keepdims=False)
        for step in range(1, self.ranks):
            piece = lax.dynamic_index_in_dim(value, self.rank ^ step, 0, keepdims=False)
            got = self.permute(piece.astype(BF16), lambda s, h: (s, h ^ step))
            total = total + got.astype(F32)
        return total

    def whole_sequence(self, own):
        both = self.gather_ranks(own)
        return jnp.swapaxes(both, 0, 1).reshape(-1, own.shape[-1])

    def own_sum(self, full):
        rows = full.shape[0] // (self.slots * self.ranks)
        parts = full.reshape(self.slots, self.ranks, rows, full.shape[-1])
        return self.sum_ranks(jnp.swapaxes(parts, 0, 1)).reshape(-1, full.shape[-1])


def shards(
    n_seq,
    n_head,
    layer_input,
    values_first,
    w_qkv,
    w_gate_up,
    w_out,
    w_down,
    norm_gains,
    out_grad,
    segments,
    counts,
    stats_wide,
    roots_wide,
    stats_head,
    roots_head,
    stats_unit,
    roots_unit,
):
    slots, rows, width = layer_input.shape
    length = segments.shape[1]
    row_part, head_cols, ffn_cols = w_qkv.shape[1], w_qkv.shape[2], w_gate_up.shape[2]
    head_dim = stats_head.shape[2]
    links = Links(n_seq, n_head, slots)
    is_live = links.slot < counts[0]
    pairs = slots * head_cols // LANES
    per = LANES // head_cols
    rows_a, rows_b = 4 * head_cols, 3 * ffn_cols

    def pair_major(value):
        n = value.shape[2]
        value = value.reshape(pairs, per, length, n, head_cols)
        return value.transpose(0, 2, 3, 1, 4).reshape(pairs, length, n, LANES)

    def slot_major(value):
        n = value.shape[2]
        value = value.reshape(pairs, length, n, per, head_cols)
        return value.transpose(0, 3, 1, 2, 4).reshape(slots, length, n, head_cols)

    weight_rows = jnp.concatenate(
        [
            jnp.swapaxes(w_qkv.astype(BF16), 1, 2).reshape(3 * head_cols, row_part),
            w_out.astype(BF16),
            jnp.swapaxes(w_gate_up.astype(BF16), 1, 2).reshape(2 * ffn_cols, row_part),
            w_down.astype(BF16),
        ],
        axis=0,
    )
    x_bf16, first_all, weights = gather_inputs(
        n_seq, n_head, ((0, rows_a), (rows_a, rows_b)), layer_input, values_first, weight_rows
    )
    w_in, w_o = weights[:, : 3 * head_cols], weights[:, 3 * head_cols : rows_a]
    w_gu, w_d = weights[:, rows_a : rows_a + 2 * ffn_cols], weights[:, rows_a + 2 * ffn_cols :]
    x_own = x_bf16.reshape(slots * rows, width).astype(F32)
    ein = functools.partial(jnp.einsum, preferred_element_type=F32)

    segment_ids = lax.dynamic_index_in_dim(segments, links.slot, 0, keepdims=False)
    first_pos, cos_wide, sin_wide = position_tables(segment_ids, head_dim)

    inverse_one = lax.rsqrt(jnp.mean(x_own * x_own, axis=-1, keepdims=True) + EPSILON)
    normed_one = x_own * inverse_one
    h_one = links.whole_sequence(
        (normed_one * norm_gains[0]).astype(BF16).reshape(slots, rows, width)
    )
    project = ein("ld,qcd->qlc", h_one, w_in)
    if per > 1:
        project = pair_major(project.reshape(slots, length, 3, head_cols)).reshape(
            pairs, length, 3 * LANES
        )
        first_all = pair_major(first_all[:, :, None])[:, :, 0]
    saved = attend(project, first_all, cos_wide, sin_wide, first_pos)
    attended = saved[3]
    if per > 1:
        attended = slot_major(attended[:, :, None])[:, :, 0]
    attn_out = links.own_sum(ein("qlc,qcd->ld", attended, w_o))
    middle = x_own + attn_out
    inverse_two = lax.rsqrt(jnp.mean(middle * middle, axis=-1, keepdims=True) + EPSILON)
    normed_two = middle * inverse_two
    h_two = links.whole_sequence(
        (normed_two * norm_gains[1]).astype(BF16).reshape(slots, rows, width)
    )
    gate_up = ein("ld,qfd->qlf", h_two, w_gu)
    gate, up = gate_up[..., :ffn_cols], gate_up[..., ffn_cols:]
    sigmoid_gate = jax.nn.sigmoid(gate)
    activated = gate * sigmoid_gate
    hidden = (activated * up).astype(BF16)
    ffn_out = links.own_sum(ein("qlf,qfd->ld", hidden, w_d))
    block_delta = jnp.where(is_live, attn_out + ffn_out, 0.0).astype(BF16)

    grad_own = links.swap_slots(out_grad)
    d_own = jnp.where(is_live, grad_own, jnp.zeros_like(grad_own))
    d_out = d_own.reshape(slots * rows, width).astype(F32)
    d_ffn = links.whole_sequence(d_own)
    g_down = ein("qlf,ld->qfd", hidden, d_ffn)
    d_hidden = ein("ld,qfd->qlf", d_ffn, w_d)
    d_gate = (
        d_hidden * up * sigmoid_gate * (1.0 + gate * (1.0 - sigmoid_gate))
    ).astype(BF16)
    d_up = (d_hidden * activated).astype(BF16)
    d_gate_up = jnp.concatenate([d_gate, d_up], axis=2)
    d_normed_two = links.own_sum(ein("qlf,qfd->ld", d_gate_up, w_gu))
    g_gate_up = ein("qlf,ld->qfd", d_gate_up, h_two)
    grads_b = jnp.concatenate([g_gate_up.astype(BF16), g_down.astype(BF16)], axis=1)
    gain_two = jnp.sum(normed_two * d_normed_two, axis=0)
    middle_delta = norm_back(d_normed_two * norm_gains[1], normed_two, inverse_two)
    d_middle = d_out + middle_delta
    d_attn = links.whole_sequence(d_middle.astype(BF16).reshape(slots, rows, width))
    d_attended = ein("ld,qcd->qlc", d_attn, w_o).astype(BF16)
    if per > 1:
        d_attended = pair_major(d_attended[:, :, None])[:, :, 0]
    d_project = jnp.concatenate(
        attend_back(saved, d_attended, cos_wide, sin_wide, first_pos), axis=2
    )
    if per > 1:
        d_project = slot_major(d_project.reshape(pairs, length, 3, LANES)).reshape(
            slots, length, 3 * head_cols
        )
    d_value = d_project[:, :, 2 * head_cols :]
    g_out = ein("qlc,ld->qcd", attended, d_attn)
    g_qkv = ein("qlc,ld->qcd", d_project, h_one)
    grads_a = jnp.concatenate([g_qkv.astype(BF16), g_out.astype(BF16)], axis=1)
    d_normed_one = links.own_sum(ein("qlc,qcd->ld", d_project, w_in))
    gain_one = jnp.sum(normed_one * d_normed_one, axis=0)
    input_delta = middle_delta + norm_back(d_normed_one * norm_gains[0], normed_one, inverse_one)
    input_delta = jnp.where(is_live, input_delta, 0.0).astype(BF16)
    gains = jnp.concatenate([gain_one.reshape(8, -1), gain_two.reshape(8, -1)], axis=0)

    block_got, input_got, first_got, gains, sum_a, sum_b, full_a, full_b = reduce_grads(
        n_seq,
        n_head,
        (LANES, unit_chunk(rows_b)),
        block_delta.reshape(slots, rows, width),
        input_delta.reshape(slots, rows, width),
        d_value,
        gains,
        grads_a,
        grads_b,
    )
    block_out = layer_input.astype(F32) + block_got.astype(F32)
    input_grad = out_grad.astype(F32) + input_got.astype(F32)
    first_grad = first_got.astype(F32)
    grad_gains = gains.reshape(2, width)
    new_gains = norm_gains - GAIN_RATE * grad_gains * lax.rsqrt(
        jnp.mean(grad_gains * grad_gains, axis=-1, keepdims=True) + EPSILON
    )

    wide, out_right, new_head, new_unit, step_a, step_b = shampoo(
        stats_wide, roots_wide, stats_head, roots_head, stats_unit, roots_unit,
        full_a, sum_a, full_b, sum_b,
    )
    cut = 3 * head_cols
    turned = lambda value, n: jnp.swapaxes(value.reshape(n, -1, row_part), 1, 2)
    return (
        block_out,
        input_grad,
        first_grad,
        turned(sum_a[:cut], 3).astype(F32),
        turned(sum_b[: 2 * ffn_cols], 2).astype(F32),
        sum_a[cut:].astype(F32),
        sum_b[2 * ffn_cols :].astype(F32),
        grad_gains,
        w_qkv - STEP_RATE * turned(step_a[:cut], 3),
        w_gate_up - STEP_RATE * turned(step_b[: 2 * ffn_cols], 2),
        w_out - OUT_RATE * step_a[cut:],
        w_down - STEP_RATE * step_b[2 * ffn_cols :],
        new_gains,
        wide,
        out_right[0],
        new_head,
        new_unit,
    )


def unit_chunk(rows):
    return max(c for c in range(16, 177, 16) if rows % c == 0)


def solution(mesh):
    return jax.shard_map(
        functools.partial(shards, mesh.shape["seq"], mesh.shape["head"]),
        mesh=mesh,
        in_specs=(
            P("seq", "head", None),
            P("seq", None, "head"),
            P(None, "seq", "head"),
            P(None, "seq", "head"),
            P("head", "seq"),
            P("head", "seq"),
            P(),
            P("seq", "head", None),
            P("seq", None),
            P("seq"),
            P(None, "head", "seq", None),
            P(None, "head", "seq", None),
            P(None, "head", None, None),
            P(None, "head", None, None),
            P(None, "head", None, None),
            P(None, "head", None, None),
        ),
        out_specs=(
            P("seq", "head", None),
            P("seq", "head", None),
            P("seq", None, "head"),
            P(None, "seq", "head"),
            P(None, "seq", "head"),
            P("head", "seq"),
            P("head", "seq"),
            P(),
            P(None, "seq", "head"),
            P(None, "seq", "head"),
            P("head", "seq"),
            P("head", "seq"),
            P(),
            P(None, "head", "seq", None),
            P("head", "seq", None),
            P(None, "head", None, None),
            P(None, "head", None, None),
        ),
        check_vma=False,
    )
```

```python
import functools

import jax
import jax.numpy as jnp
from jax import lax
from jax.experimental import pallas as pl
from jax.experimental.pallas import tpu as pltpu
from jax.sharding import PartitionSpec as P

EPSILON = 1e-06
STAT_DECAY = 0.5
STEP_RATE = 0.02
OUT_RATE = 0.1
GAIN_RATE = 0.25
AXES = ("seq", "head")
MESH = pl.DeviceIdType.MESH
LANES = 128
BLOCK = 256
BF16 = jnp.bfloat16
F32 = jnp.float32


def dot_nt(matrix_a, matrix_b):
    return lax.dot_general(
        matrix_a, matrix_b, (((1,), (1,)), ((), ())), preferred_element_type=F32
    )


def dot_tn(matrix_a, matrix_b):
    return lax.dot_general(
        matrix_a, matrix_b, (((0,), (0,)), ((), ())), preferred_element_type=F32
    )


def dot_nn(matrix_a, matrix_b):
    return jnp.dot(matrix_a, matrix_b, preferred_element_type=F32)


def norm_back(d_normed, normed, inverse):
    return inverse * (d_normed - normed * jnp.mean(d_normed * normed, axis=-1, keepdims=True))


def position_tables(segment_ids, head_dim):
    length = segment_ids.shape[0]
    position = jnp.arange(length, dtype=jnp.int32)
    opens = jnp.concatenate([jnp.ones((1,), dtype=bool), segment_ids[1:] != segment_ids[:-1]])
    first_pos = lax.cummax(jnp.where(opens, position, 0), axis=0)
    offset = (position - first_pos).astype(F32)
    half_width = head_dim // 2
    frequency = jnp.exp(-jnp.log(10000.0) * jnp.arange(half_width, dtype=F32) / half_width)
    angle = offset[:, None] * frequency[None, :]
    cosine, sine_part = jnp.cos(angle), jnp.sin(angle)
    per_lane = LANES // head_dim
    cos_wide = jnp.concatenate([cosine, cosine] * per_lane, axis=1)
    sin_wide = jnp.concatenate([-sine_part, sine_part] * per_lane, axis=1)
    return first_pos, cos_wide, sin_wide


def swap_halves(values):
    lane = lax.broadcasted_iota(jnp.int32, values.shape, 1)
    return jnp.where((lane & 32) == 0, pltpu.roll(values, 96, 1), pltpu.roll(values, 32, 1))


def two_heads(block):
    lane = lax.broadcasted_iota(jnp.int32, block.shape, 1)
    zero = jnp.zeros_like(block)
    return jnp.concatenate(
        [jnp.where(lane < 64, block, zero), jnp.where(lane >= 64, block, zero)], axis=0
    )


def one_pair(transposed, width):
    kept = jnp.concatenate([transposed[:64, :width], transposed[64:, width:]], axis=0)
    return kept.T


def seen(first_ref, begin, key_count):
    first = first_ref[0:1, begin : begin + BLOCK]
    query = begin + lax.broadcasted_iota(jnp.int32, (1, BLOCK), 1)
    first = jnp.concatenate([first, first], axis=1)
    query = jnp.concatenate([query, query], axis=1)
    key = lax.broadcasted_iota(jnp.int32, (key_count, 2 * BLOCK), 0)
    return (key >= first) & (key <= query)


def attend_back_kernel(
    qr_ref, kr_ref, vm_ref, att_ref, d_ref, lse_ref, cos_ref, sin_ref, first_ref,
    dq_ref, dk_ref, dv_ref, key_sum, value_sum,
):
    length = qr_ref.shape[1]
    key_sum[...] = jnp.zeros_like(key_sum)
    value_sum[...] = jnp.zeros_like(value_sum)
    k_turned = kr_ref[0].T
    cosine, sine_part = cos_ref[...], sin_ref[...]
    product = (d_ref[0].astype(F32) * att_ref[...].astype(F32)).T
    inner = [
        jnp.sum(product[:64], axis=0, keepdims=True),
        jnp.sum(product[64:], axis=0, keepdims=True),
    ]
    for step in range(length // BLOCK):
        begin, keys = step * BLOCK, (step + 1) * BLOCK
        queries = two_heads(qr_ref[0, begin:keys, :])
        d_out = two_heads(d_ref[0, begin:keys, :])
        scores = dot_nt(kr_ref[0, :keys, :], queries)
        log_total = jnp.concatenate(
            [lse_ref[0, 0:1, begin:keys], lse_ref[0, 1:2, begin:keys]], axis=1
        )
        chances = jnp.where(seen(first_ref, begin, keys), jnp.exp(scores - log_total), 0.0)
        d_chances = dot_nt(vm_ref[0, :keys, :], d_out)
        part = jnp.concatenate([inner[0][:, begin:keys], inner[1][:, begin:keys]], axis=1)
        d_scores = (chances * (d_chances - part)).astype(BF16)
        key_sum[:keys, :] += dot_nn(d_scores, queries)
        value_sum[:keys, :] += dot_nn(chances.astype(BF16), d_out)
        d_query = one_pair(dot_nn(k_turned[:, :keys], d_scores), BLOCK) * 0.125
        dq_ref[0, begin:keys, :] = (
            d_query * cosine[begin:keys] - swap_halves(d_query) * sine_part[begin:keys]
        ).astype(BF16)
    d_key = key_sum[...]
    dk_ref[0] = (d_key * cosine - swap_halves(d_key) * sine_part).astype(BF16)
    dv_ref[0] = (0.5 * value_sum[...]).astype(BF16)


def attend_back(saved, d_attended, cos_wide, sin_wide, first_pos):
    q_rot, k_rot, v_mix, attended, log_total = saved
    pairs, length, _ = q_rot.shape
    part = pl.BlockSpec((1, length, LANES), lambda p: (p, 0, 0))
    table = pl.BlockSpec((length, LANES), lambda p: (0, 0))
    out = jax.ShapeDtypeStruct((pairs, length, LANES), BF16)
    return pl.pallas_call(
        attend_back_kernel,
        grid=(pairs,),
        in_specs=[part] * 3 + [pl.BlockSpec((length, LANES), lambda p: (0, p)), part,
                               pl.BlockSpec((1, 2, length), lambda p: (p, 0, 0)), table, table,
                               pl.BlockSpec((1, length), lambda p: (0, 0))],
        out_specs=[part] * 3,
        out_shape=[out] * 3,
        scratch_shapes=[pltpu.VMEM((length, LANES), F32)] * 2,
        compiler_params=pltpu.CompilerParams(vmem_limit_bytes=48 << 20),
        cost_estimate=pl.CostEstimate(
            flops=pairs * length * length * 128 * 20, bytes_accessed=pairs * length * 128 * 24,
            transcendentals=pairs * length * length),
    )(q_rot, k_rot, v_mix, attended, d_attended, log_total, cos_wide, sin_wide, first_pos[None, :])


class Place:
    def __init__(self, n_seq, n_head, slots):
        self.n_seq, self.slots, self.ranks = n_seq, slots, n_head // slots
        self.seq = lax.axis_index("seq")
        head = lax.axis_index("head")
        self.slot, self.rank = head // self.ranks, head % self.ranks

    def at_slot(self, step):
        return (self.slot + step + self.slots) % self.slots

    def at_seq(self, step):
        return (self.seq + step + self.n_seq) % self.n_seq

    @property
    def line(self):
        return self.slots == 4 and self.n_seq == 4

    def source(self, step):
        if not self.line:
            return self.at_slot(-step)
        upper = self.slot // 2
        inner = (self.slot + upper) % 2
        near = step + inner * (1 - 2 * step) * (1 - step // 2)
        return near + upper * (3 - 2 * near)

    @property
    def beside(self):
        return self.seq + 1 - 2 * (self.seq % 2)

    @property
    def across(self):
        return self.seq + 2 - 4 * (self.seq // 2)

    def device(self, seq=None, slot=None, rank=None):
        seq = self.seq if seq is None else seq
        slot = self.slot if slot is None else slot
        rank = self.rank if rank is None else rank
        return (seq, slot * self.ranks + rank)

    def greet(self, with_ranks):
        others = [self.device(slot=self.at_slot(k)) for k in range(1, self.slots)]
        others += [self.device(seq=self.at_seq(d)) for d in range(1, self.n_seq)]
        if with_ranks:
            others += [
                self.device(rank=(self.rank + j) % self.ranks) for j in range(1, self.ranks)
            ]
        barrier = pltpu.get_barrier_semaphore()
        for other in others:
            pl.semaphore_signal(barrier, inc=1, device_id=other, device_id_type=MESH)
        pl.semaphore_wait(barrier, len(others))


class Sender:
    def __init__(self, send_sems, recv_sems):
        self.send_sems, self.recv_sems, self.used = send_sems, recv_sems, 0

    def start(self, src, dst, device, recv=None):
        copy = pltpu.make_async_remote_copy(
            src_ref=src,
            dst_ref=dst,
            send_sem=self.send_sems.at[self.used],
            recv_sem=self.recv_sems.at[self.used] if recv is None else recv,
            device_id=device,
            device_id_type=MESH,
        )
        self.used += 1
        copy.start()
        return copy


def lanes(index, width):
    return pl.ds(pl.multiple_of(index * width, width), width)


def forward_kernel(
    n_seq, n_head, head_cols,
    x_ref, vf_ref, wt_ref, gains_ref, cos_ref, sin_ref, first_ref,
    x_out, h_one, q_out, k_out, v_out, att_out, lse_out, w_a, w_b, middle, h_two,
    vf_all, away, back, sems, z_recv, v_recv, own_sems,
):
    slots, rows, width = x_ref.shape
    part = wt_ref.shape[1]
    rows_a = w_a.shape[1]
    place = Place(n_seq, n_head, slots)
    ranks = place.ranks
    length = slots * ranks * rows
    per = LANES // head_cols
    pairs = slots // per
    mine = lanes(place.seq, part)
    sections = {"a": (w_a, pl.ds(0, rows_a)), "b": (w_b, pl.ds(rows_a, wt_ref.shape[0] - rows_a))}
    ids = {}
    elsewhere = place.device(seq=place.at_seq(1))

    def index(name):
        return ids.setdefault(name, len(ids))

    def remote(name, src, dst, device, recv=None):
        i = index(name)
        return pltpu.make_async_remote_copy(
            src_ref=src, dst_ref=dst, send_sem=sems.at[0, i],
            recv_sem=sems.at[1, i] if recv is None else recv,
            device_id=device, device_id_type=MESH,
        )

    def x_copy(k):
        to = place.at_slot(k)
        return remote(("x", k), x_ref.at[to], x_out.at[place.slot], place.device(slot=to))

    def v_copy(k):
        to = place.at_slot(k)
        return remote(("v", k), vf_ref.at[to], vf_all.at[place.slot], place.device(slot=to),
                      v_recv.at[place.slot])

    def v_wait(source):
        pltpu.make_async_remote_copy(
            src_ref=vf_ref.at[0], dst_ref=vf_all.at[source], send_sem=sems.at[0, 0],
            recv_sem=v_recv.at[source], device_id=elsewhere, device_id_type=MESH,
        ).wait_recv()

    def piece(sec, step):
        ref, at = sections[sec]
        return wt_ref.at[at] if step == 0 else ref.at[step, :, mine]

    def z_copy(name, sec, step, to, to_step):
        ref, _ = sections[sec]
        which = 0 if sec == "a" else 1
        return remote((name, sec, step), piece(sec, step), ref.at[to_step, :, mine],
                      place.device(slot=to), z_recv.at[which, to_step])

    def z_wait(sec, step):
        ref, _ = sections[sec]
        which = 0 if sec == "a" else 1
        pltpu.make_async_remote_copy(
            src_ref=piece(sec, 0), dst_ref=ref.at[step, :, mine], send_sem=sems.at[0, 0],
            recv_sem=z_recv.at[which, step], device_id=elsewhere, device_id_type=MESH,
        ).wait_recv()

    slot = place.slot
    upper = slot // 2
    inner = (slot + upper) % 2

    def z_start_own(sec):
        if not place.line:
            for k in range(1, slots):
                z_copy(("z", k), sec, 0, place.at_slot(k), k).start()
            return
        @pl.when(slot < 3)
        def _():
            to = slot + 1
            z_copy("up", sec, 0, to, 1 + (to == 2).astype(jnp.int32)).start()

        @pl.when(slot > 0)
        def _():
            to = slot - 1
            z_copy("down", sec, 0, to, 1 + (to == 1).astype(jnp.int32)).start()

    def z_own_sends(sec):
        if not place.line:
            for k in range(1, slots):
                z_copy(("z", k), sec, 0, place.at_slot(k), k).wait_send()
            return

        @pl.when(slot < 3)
        def _():
            z_copy("up", sec, 0, slot + 1, 1).wait_send()

        @pl.when(slot > 0)
        def _():
            z_copy("down", sec, 0, slot - 1, 1).wait_send()

    def z_relay(sec, step):
        if step == 1:
            return z_copy("on", sec, step, slot + 1 - 2 * upper, 3)
        return z_copy("on", sec, step, slot - 1 + 2 * upper, step)

    def near_copy(sec, step):
        ref, _ = sections[sec]
        dst = ref.at[step, :, mine]
        if not place.line:
            return [
                remote(("xy", d, sec, step), piece(sec, step), dst, place.device(seq=place.at_seq(d)))
                for d in range(1, n_seq)
            ]
        return [
            remote(("xy", 0, sec, step), piece(sec, step), dst, place.device(seq=place.beside)),
            remote(("xy", 1, sec, step), piece(sec, step), dst, place.device(seq=place.across)),
        ]

    def far_copy(sec, step, which):
        ref, at = sections[sec]
        half = at.size // 2
        cut = pl.ds(which * half, half)
        source = place.beside if which == 0 else place.across
        to = place.across if which == 0 else place.beside
        where = ref.at[step, cut, lanes(source, part)]
        return remote(("far", which, sec, step), where, where, place.device(seq=to))

    def z_event(sec, step):
        z_wait(sec, step)
        if place.line:
            @pl.when(inner == 1)
            def _():
                z_relay(sec, step).start()
        for copy in near_copy(sec, step):
            copy.start()

    def xy_event(sec, step):
        for which, copy in enumerate(near_copy(sec, step)):
            copy.wait_recv()
            if place.line:
                far_copy(sec, step, which).start()

    def done_event(sec, step):
        if place.line:
            for which in range(2):
                far_copy(sec, step, which).wait_recv()

    def position(p, rank):
        return pl.ds(pl.multiple_of((p * ranks + rank) * rows, rows), rows)

    def share(name, ref, p, j):
        where = ref.at[position(p, place.rank), :]
        return remote((name, p, j), where, where, place.device(rank=(place.rank + j) % ranks))

    place.greet(True)
    for k in (2, 3, 1):
        x_copy(k).start()
    own = [
        pltpu.make_async_copy(x_ref.at[slot], x_out.at[slot], own_sems.at[0]),
        pltpu.make_async_copy(wt_ref.at[sections["a"][1]], w_a.at[0, :, mine], own_sems.at[1]),
        pltpu.make_async_copy(wt_ref.at[sections["b"][1]], w_b.at[0, :, mine], own_sems.at[2]),
        pltpu.make_async_copy(vf_ref.at[slot], vf_all.at[slot], own_sems.at[3]),
    ]
    for copy in own:
        copy.start()
    z_start_own("a")
    for copy in near_copy("a", 0):
        copy.start()
    xy_event("a", 0)
    for copy in near_copy("b", 0):
        copy.start()
    z_event("a", 1)
    for k in range(1, slots):
        x_copy(k).wait_recv()
    own[0].wait()
    for k in range(1, slots):
        v_copy(k).start()

    for p in range(slots):
        x = x_out[p].astype(F32)
        normed = x * lax.rsqrt(jnp.mean(x * x, axis=-1, keepdims=True) + EPSILON)
        h_one[position(p, place.rank), :] = (normed * gains_ref[0:1, :]).astype(BF16)
        for j in range(1, ranks):
            share("h1", h_one, p, j).start()
    xy_event("a", 1)
    z_event("a", 2)
    z_start_own("b")
    own[1].wait()
    own[3].wait()
    done_event("a", 0)
    for p in range(slots):
        for j in range(1, ranks):
            share("h1", h_one, p, j).wait_recv()
    events = {
        (0, 1): [lambda: xy_event("a", 2)],
        (0, 3): [lambda: z_event("a", 3)],
        (1, 0): [lambda: done_event("a", 1)],
        (1, 1): [lambda: xy_event("b", 0)],
        (1, 2): [lambda: xy_event("a", 3)],
        (1, 3): [lambda: z_event("b", 1)],
        (2, 0): [lambda: done_event("a", 2)],
        (2, 1): [lambda: z_event("b", 2)],
        (2, 3): [lambda: xy_event("b", 1)],
        (3, 0): [lambda: done_event("a", 3)],
        (3, 1): [lambda: z_event("b", 3)],
        (3, 3): [lambda: xy_event("b", 2)],
    }
    if per > 1:
        xy_event("a", 2)
        z_event("a", 3)
        xy_event("a", 3)
        xy_event("b", 0)
        for step in range(1, slots):
            done_event("a", step)
            v_wait(place.source(step))
            z_event("b", step)
            xy_event("b", step)
        events = {}

    def one_pair_of_heads(j, carry):
        def pump(point):
            for (step, at), todo in events.items():
                if at == point:
                    @pl.when(j == step)
                    def _(todo=todo):
                        for act in todo:
                            act()

        pump(0)
        if per == 1:
            @pl.when(j > 0)
            def _():
                v_wait(place.source(j))
            w_in = w_a[j, : 3 * head_cols, :]
            first = vf_all[place.source(j)]
        else:
            w_in = jnp.concatenate(
                [
                    w_a[j * per + u, i * head_cols : (i + 1) * head_cols, :]
                    for i in range(3)
                    for u in range(per)
                ],
                axis=0,
            )
            first = jnp.concatenate([vf_all[place.source(j * per + u)] for u in range(per)], axis=1)
        half = length // 2
        for part_at in range(2):
            at = slice(part_at * half, (part_at + 1) * half)
            project = dot_nt(h_one[at, :], w_in)
            cosine, sine_part = cos_ref[at, :], sin_ref[at, :]
            q_raw, k_raw = project[:, :LANES], project[:, LANES : 2 * LANES]
            q_out[j, at, :] = ((q_raw * cosine + swap_halves(q_raw) * sine_part) * 0.125).astype(BF16)
            k_out[j, at, :] = (k_raw * cosine + swap_halves(k_raw) * sine_part).astype(BF16)
            v_out[j, at, :] = (0.5 * project[:, 2 * LANES :] + 0.5 * first[at].astype(F32)).astype(BF16)
        pump(1)
        v_turned = v_out[j].T
        for step in range(length // BLOCK):
            begin, keys = step * BLOCK, (step + 1) * BLOCK
            queries = two_heads(q_out[j, begin:keys, :])
            scores = dot_nt(k_out[j, :keys, :], queries)
            scores = jnp.where(seen(first_ref, begin, keys), scores, -1e30)
            top = jnp.max(scores, axis=0, keepdims=True)
            exps = jnp.exp(scores - top)
            total = jnp.sum(exps, axis=0, keepdims=True)
            chances = (exps * (1.0 / total)).astype(BF16)
            attended = dot_nn(v_turned[:, :keys], chances)
            att_out[begin:keys, lanes(j, LANES)] = one_pair(attended, BLOCK).astype(BF16)
            log_total = top + jnp.log(total)
            lse_out[j, 0:1, begin:keys] = log_total[:, :BLOCK]
            lse_out[j, 1:2, begin:keys] = log_total[:, BLOCK:]
            if step == length // BLOCK // 2 - 1:
                pump(2)
        pump(3)
        return carry

    lax.fori_loop(0, pairs, one_pair_of_heads, 0)

    w_o = w_a[:, 3 * head_cols :, :].reshape(slots * head_cols, width)

    def away_copy(p, j):
        return remote(("away", p, j), away.at[j - 1, p], back.at[j - 1, p],
                      place.device(rank=(place.rank + j) % ranks))

    for p in range(slots):
        for j in range(1, ranks):
            at = position(p, (place.rank + j) % ranks)
            away[j - 1, p] = dot_nn(att_out[at, :], w_o).astype(BF16)
            away_copy(p, j).start()
    if per == 1:
        xy_event("b", 3)
    for p in range(slots):
        middle[p] = x_out[p].astype(F32) + dot_nn(att_out[position(p, place.rank), :], w_o)
    for p in range(slots):
        value = middle[p]
        for j in range(1, ranks):
            away_copy(p, j).wait_recv()
            value = value + back[j - 1, p].astype(F32)
        middle[p] = value
        normed = value * lax.rsqrt(jnp.mean(value * value, axis=-1, keepdims=True) + EPSILON)
        h_two[position(p, place.rank), :] = (normed * gains_ref[1:2, :]).astype(BF16)
        for j in range(1, ranks):
            share("h2", h_two, p, j).start()
    for p in range(slots):
        for j in range(1, ranks):
            share("h2", h_two, p, j).wait_recv()
    for step in range(slots):
        done_event("b", step)
    for p in range(slots):
        for j in range(1, ranks):
            share("h1", h_one, p, j).wait_send()
            share("h2", h_two, p, j).wait_send()
            away_copy(p, j).wait_send()
    for k in range(1, slots):
        x_copy(k).wait_send()
        v_copy(k).wait_send()
    for sec in ("a", "b"):
        z_own_sends(sec)
        for step in range(slots):
            for copy in near_copy(sec, step):
                copy.wait_send()
            if place.line:
                for which in range(2):
                    far_copy(sec, step, which).wait_send()
                if step > 0:
                    @pl.when(inner == 1)
                    def _(sec=sec, step=step):
                        z_relay(sec, step).wait_send()
    own[2].wait()


def forward_part(n_seq, n_head, head_cols, layer_input, values_first, weight_rows, gains, cos_wide, sin_wide, first_pos):
    slots, rows, width = layer_input.shape
    all_rows, part = weight_rows.shape
    ranks = n_head // slots
    length = slots * ranks * rows
    rows_a = 4 * head_cols
    pairs = slots * head_cols // LANES
    count = 2 * (slots - 1) + 2 * (2 + 4 * slots + slots * n_seq) + 3 * slots * ranks
    any_space = pl.BlockSpec(memory_space=pl.ANY)
    vmem = pl.BlockSpec(memory_space=pltpu.VMEM)
    shape = jax.ShapeDtypeStruct
    heads = shape((pairs, length, LANES), BF16)
    return pl.pallas_call(
        functools.partial(forward_kernel, n_seq, n_head, head_cols),
        in_specs=[any_space] * 3 + [vmem] * 4,
        out_specs=[vmem] * 8 + [any_space] + [vmem] * 2,
        out_shape=[
            shape(layer_input.shape, BF16),
            shape((length, width), BF16),
            heads, heads, heads,
            shape((length, slots * head_cols), BF16),
            shape((pairs, 2, length), F32),
            shape((slots, rows_a, width), BF16),
            shape((slots, all_rows - rows_a, width), BF16),
            shape(layer_input.shape, F32),
            shape((length, width), BF16),
        ],
        scratch_shapes=[
            pltpu.VMEM(values_first.shape, BF16),
            pltpu.VMEM((ranks - 1, slots, rows, width), BF16),
            pltpu.VMEM((ranks - 1, slots, rows, width), BF16),
            pltpu.SemaphoreType.DMA((2, count)),
            pltpu.SemaphoreType.DMA((2, slots)),
            pltpu.SemaphoreType.DMA((slots,)),
            pltpu.SemaphoreType.DMA((4,)),
        ],
        compiler_params=pltpu.CompilerParams(
            collective_id=0, has_side_effects=True, vmem_limit_bytes=60 << 20
        ),
    )(layer_input, values_first, weight_rows, gains, cos_wide, sin_wide, first_pos[None, :])


def reduce_kernel(
    n_seq, n_head, chunks,
    block_ref, input_ref, first_ref, gains_ref, grads_a, grads_b,
    block_out, input_out, first_out, gains_out, sum_a, sum_b, full_a, full_b,
    near_a, near_b, turn_a, turn_b, far_a, far_b, gain_seq, gain_slot, gain_rank,
    send_sems, recv_sems, own_sems, far_recv, first_recv,
):
    slots = block_ref.shape[0]
    place = Place(n_seq, n_head, slots)
    place.greet(True)
    sender = Sender(send_sems, recv_sems)
    part = sum_a.shape[1]
    mine = lanes(place.seq, part)
    order = [2, 3, 1, 0]
    parts = ((grads_b, sum_b, full_b, near_b, turn_b, far_b, chunks[1]),
             (grads_a, sum_a, full_a, near_a, turn_a, far_a, chunks[0]))
    copies, received = [], []

    def arrive(copy):
        copy.wait_recv()
        received.append(copy)

    def swap(src, dst):
        return [
            sender.start(
                src.at[place.at_slot(k)], dst.at[place.slot], place.device(slot=place.at_slot(k))
            )
            for k in (2, 3, 1)
        ]

    gain_seq[place.seq] = gains_ref[...]
    small = [
        sender.start(gain_seq.at[place.seq], gain_seq.at[place.seq],
                     place.device(seq=place.at_seq(d)))
        for d in range(1, n_seq)
    ]
    copies += small

    def to_seqs(grads, near, k):
        return [
            sender.start(
                grads.at[k, :, lanes(place.at_seq(d), part)],
                near.at[k, d - 1],
                place.device(seq=place.at_seq(d)),
            )
            for d in range(1, n_seq)
        ]

    sent = {}
    units = [(which, k) for which in range(2) for k in order]

    def launch(unit):
        which, k = unit
        sent[unit] = to_seqs(parts[which][0], parts[which][3], k)
        copies.extend(sent[unit])

    own = [
        pltpu.make_async_copy(src, dst.at[place.slot], own_sems.at[i])
        for i, (src, dst) in enumerate(
            (
                (block_ref.at[place.slot], block_out),
                (input_ref.at[place.slot], input_out),
                (first_ref.at[0], first_out),
            )
        )
    ]
    for copy in own:
        copy.start()
    launch(units[0])
    launch(units[1])
    copies += swap(block_ref, block_out)
    for copy in small:
        arrive(copy)
    total = gain_seq[0]
    for i in range(1, n_seq):
        total = total + gain_seq[i]
    gain_slot[place.slot] = total
    small = [
        sender.start(gain_slot.at[place.slot], gain_slot.at[place.slot],
                     place.device(slot=place.at_slot(k)))
        for k in range(1, slots)
    ]
    copies += small
    elsewhere = place.device(seq=place.at_seq(1))
    for index, unit in enumerate(units):
        which, k = unit
        grads, _, _, near, turn, far, chunk = parts[which]
        if index + 2 < len(units):
            launch(units[index + 2])
        for copy in sent[unit]:
            arrive(copy)

        def add(i, carry, grads=grads, near=near, turn=turn, k=k, chunk=chunk):
            rows = pl.ds(pl.multiple_of(i * chunk, chunk), chunk)
            value = grads[k, rows, mine].astype(F32)
            for d in range(n_seq - 1):
                value = value + near[k, d, rows, :].astype(F32)
            turn[k, rows, :] = value.astype(BF16)
            return carry

        lax.fori_loop(0, grads.shape[1] // chunk, add, 0)
        if k != 0:
            copy = sender.start(
                turn.at[k], far.at[place.slot], place.device(slot=place.source(k)),
                far_recv.at[which, place.slot],
            )
            copies.append(copy)
            received.append(copy)
        if index == 1:
            for j in range(1, slots):
                copy = sender.start(
                    first_ref.at[j], first_out.at[place.slot],
                    place.device(slot=place.source(j)), first_recv.at[place.slot],
                )
                copies.append(copy)
                received.append(copy)
        if index == 4:
            copies += swap(input_ref, input_out)
            for copy in small:
                arrive(copy)
            total = gain_slot[0]
            for i in range(1, slots):
                total = total + gain_slot[i]
            gain_rank[place.rank] = total
            small = [
                sender.start(gain_rank.at[place.rank], gain_rank.at[place.rank],
                             place.device(rank=(place.rank + j) % place.ranks))
                for j in range(1, place.ranks)
            ]
            copies += small
        if k == 0:
            for j in range(1, slots):
                source = place.at_slot(j)
                pltpu.make_async_remote_copy(
                    src_ref=turn.at[0], dst_ref=far.at[source], send_sem=send_sems.at[0],
                    recv_sem=far_recv.at[which, source], device_id=elsewhere, device_id_type=MESH,
                ).wait_recv()
            _, total_ref, full, _, _, _, _ = parts[which]

            def finish(i, carry, turn=turn, far=far, total_ref=total_ref, full=full, chunk=chunk):
                rows = pl.ds(pl.multiple_of(i * chunk, chunk), chunk)
                value = turn[0, rows, :].astype(F32)
                for j in range(1, slots):
                    value = value + far[place.at_slot(j), rows, :].astype(F32)
                value = value.astype(BF16)
                total_ref[rows, :] = value
                full[rows, mine] = value
                return carry

            lax.fori_loop(0, grads.shape[1] // chunk, finish, 0)
            copies += [
                sender.start(total_ref, full.at[:, mine], place.device(seq=place.at_seq(d)))
                for d in range(1, n_seq)
            ]
    for copy in small:
        arrive(copy)
    total = gain_rank[0]
    for i in range(1, place.ranks):
        total = total + gain_rank[i]
    gains_out[...] = total
    for copy in copies:
        if all(copy is not other for other in received):
            copy.wait_recv()
    for j in range(1, slots):
        source = place.at_slot(j)
        pltpu.make_async_remote_copy(
            src_ref=first_ref.at[0], dst_ref=first_out.at[source], send_sem=send_sems.at[0],
            recv_sem=first_recv.at[source], device_id=elsewhere, device_id_type=MESH,
        ).wait_recv()
    for copy in copies:
        copy.wait_send()
    for copy in own:
        copy.wait()


def reduce_grads(n_seq, n_head, chunks, block_delta, input_delta, first_delta, gains, grads_a, grads_b):
    slots = block_delta.shape[0]
    part = grads_a.shape[2] // n_seq
    rows = (grads_a.shape[1], grads_b.shape[1])
    ranks = n_head // slots
    count = (
        3 * (slots - 1) + 2 * (slots * (n_seq - 1) + (slots - 1) + (n_seq - 1))
        + (n_seq - 1) + (slots - 1) + (ranks - 1)
    )
    any_space = pl.BlockSpec(memory_space=pl.ANY)
    vmem = pl.BlockSpec(memory_space=pltpu.VMEM)
    like = lambda value: jax.ShapeDtypeStruct(value.shape, value.dtype)
    return pl.pallas_call(
        functools.partial(reduce_kernel, n_seq, n_head, chunks),
        in_specs=[any_space] * 3 + [vmem] * 3,
        out_specs=[any_space] * 3 + [vmem] * 5,
        out_shape=[like(block_delta), like(input_delta), like(first_delta), like(gains)]
        + [jax.ShapeDtypeStruct((r, part), BF16) for r in rows]
        + [jax.ShapeDtypeStruct((r, part * n_seq), BF16) for r in rows],
        scratch_shapes=[pltpu.VMEM((slots, n_seq - 1, r, part), BF16) for r in rows]
        + [pltpu.VMEM((slots, r, part), BF16) for r in rows]
        + [pltpu.VMEM((slots, r, part), BF16) for r in rows]
        + [pltpu.VMEM((n,) + gains.shape, F32) for n in (n_seq, slots, ranks)]
        + [
            pltpu.SemaphoreType.DMA((count,)),
            pltpu.SemaphoreType.DMA((count,)),
            pltpu.SemaphoreType.DMA((3,)),
            pltpu.SemaphoreType.DMA((2, slots)),
            pltpu.SemaphoreType.DMA((slots,)),
        ],
        compiler_params=pltpu.CompilerParams(
            collective_id=1, has_side_effects=True, vmem_limit_bytes=56 << 20
        ),
    )(block_delta, input_delta, first_delta, gains, grads_a, grads_b)


def shampoo_kernel(
    stat_ref, root_ref, head_stat, head_root, unit_stat, unit_root, full_a, sum_a, full_b, sum_b,
    wide_ref, out_right_ref, new_head, new_unit, step_a, step_b,
):
    step = pl.program_id(0)
    blocks = stat_ref.shape[1]

    def one(member, width, small_stat, small_root, full, total, big_out, small_out, step_out):
        for b in range(blocks):
            rows = pl.ds(pl.multiple_of((member * blocks + b) * width, 16), width)
            grad, own = full[rows, :], total[rows, :]
            big_out[0, b] = STAT_DECAY * stat_ref[0, b] + (1.0 - STAT_DECAY) * dot_tn(own, grad)
            small_out[member, b] = STAT_DECAY * small_stat[member, b] + (
                1.0 - STAT_DECAY
            ) * dot_nt(grad, grad)
            turned = dot_nn(small_root[member, b].astype(BF16), grad).astype(BF16)
            turned = dot_nt(turned, root_ref[0, b].astype(BF16))
            scale = lax.rsqrt(jnp.mean(turned * turned, axis=0, keepdims=True) + EPSILON)
            step_out[rows, :] = turned * scale

    head_width, unit_width = head_stat.shape[2], unit_stat.shape[2]
    head_args = (head_width, head_stat, head_root, full_a, sum_a)
    unit_args = (unit_width, unit_stat, unit_root, full_b, sum_b)

    @pl.when(step < 3)
    def _():
        one(step, *head_args, wide_ref, new_head, step_a)

    @pl.when((step >= 3) & (step < 6))
    def _():
        one(step - 3, *unit_args, wide_ref, new_unit, step_b)

    @pl.when(step == 6)
    def _():
        one(3, *head_args, out_right_ref, new_head, step_a)


def shampoo(stats_wide, roots_wide, stats_head, roots_head, stats_unit, roots_unit, full_a, sum_a, full_b, sum_b):
    members, blocks, part, width = stats_wide.shape
    member = lambda i: (jnp.where(i == 5, 6, jnp.where(i == 6, 5, i)), 0, 0, 0)
    wide = pl.BlockSpec((1, blocks, part, width), member)
    vmem = pl.BlockSpec(memory_space=pltpu.VMEM)
    return pl.pallas_call(
        shampoo_kernel,
        grid=(members,),
        in_specs=[wide, wide] + [vmem] * 8,
        out_specs=[
            pl.BlockSpec((1, blocks, part, width), lambda i: (jnp.minimum(i, 5), 0, 0, 0)),
            pl.BlockSpec((1, blocks, part, width), lambda i: (0, 0, 0, 0)),
            vmem, vmem, vmem, vmem,
        ],
        out_shape=[
            jax.ShapeDtypeStruct((members - 1, blocks, part, width), F32),
            jax.ShapeDtypeStruct((1, blocks, part, width), F32),
            jax.ShapeDtypeStruct(stats_head.shape, F32),
            jax.ShapeDtypeStruct(stats_unit.shape, F32),
            jax.ShapeDtypeStruct(sum_a.shape, F32),
            jax.ShapeDtypeStruct(sum_b.shape, F32),
        ],
        compiler_params=pltpu.CompilerParams(vmem_limit_bytes=48 << 20),
    )(stats_wide, roots_wide, stats_head, roots_head, stats_unit, roots_unit, full_a, sum_a, full_b, sum_b)


class Links:
    def __init__(self, n_seq, n_head, slots):
        self.n_seq, self.n_head, self.slots = n_seq, n_head, slots
        self.ranks = n_head // slots
        self.slot = lax.axis_index("head") // self.ranks
        self.rank = lax.axis_index("head") % self.ranks

    def permute(self, value, partner):
        pairs = []
        for s in range(self.n_seq):
            for h in range(self.n_head):
                to_s, to_h = partner(s, h)
                pairs.append((s * self.n_head + h, to_s * self.n_head + to_h))
        return lax.ppermute(value, AXES, pairs)

    def swap_slots(self, value):
        got = [lax.dynamic_index_in_dim(value, self.slot, 0, keepdims=False)]
        for step in range(1, self.slots):
            piece = lax.dynamic_index_in_dim(value, self.slot ^ step, 0, keepdims=False)
            got.append(self.permute(piece, lambda s, h: (s, h ^ (step * self.ranks))))
        got = jnp.stack(got)
        return jnp.stack(
            [lax.dynamic_index_in_dim(got, self.slot ^ q, 0, keepdims=False) for q in range(self.slots)]
        )

    def gather_ranks(self, value):
        got = [value] + [
            self.permute(value, lambda s, h: (s, h ^ step)) for step in range(1, self.ranks)
        ]
        got = jnp.stack(got)
        return jnp.stack(
            [lax.dynamic_index_in_dim(got, self.rank ^ r, 0, keepdims=False) for r in range(self.ranks)]
        )

    def sum_ranks(self, value):
        total = lax.dynamic_index_in_dim(value, self.rank, 0, keepdims=False)
        for step in range(1, self.ranks):
            piece = lax.dynamic_index_in_dim(value, self.rank ^ step, 0, keepdims=False)
            got = self.permute(piece.astype(BF16), lambda s, h: (s, h ^ step))
            total = total + got.astype(F32)
        return total

    def whole_sequence(self, own):
        both = self.gather_ranks(own)
        return jnp.swapaxes(both, 0, 1).reshape(-1, own.shape[-1])

    def own_sum(self, full):
        rows = full.shape[0] // (self.slots * self.ranks)
        parts = full.reshape(self.slots, self.ranks, rows, full.shape[-1])
        return self.sum_ranks(jnp.swapaxes(parts, 0, 1)).reshape(-1, full.shape[-1])


def shards(
    n_seq,
    n_head,
    layer_input,
    values_first,
    w_qkv,
    w_gate_up,
    w_out,
    w_down,
    norm_gains,
    out_grad,
    segments,
    counts,
    stats_wide,
    roots_wide,
    stats_head,
    roots_head,
    stats_unit,
    roots_unit,
):
    slots, rows, width = layer_input.shape
    length = segments.shape[1]
    row_part, head_cols, ffn_cols = w_qkv.shape[1], w_qkv.shape[2], w_gate_up.shape[2]
    head_dim = stats_head.shape[2]
    links = Links(n_seq, n_head, slots)
    is_live = links.slot < counts[0]
    pairs = slots * head_cols // LANES
    per = LANES // head_cols
    rows_a, rows_b = 4 * head_cols, 3 * ffn_cols

    def pair_major(value):
        n = value.shape[2]
        value = value.reshape(pairs, per, length, n, head_cols)
        return value.transpose(0, 2, 3, 1, 4).reshape(pairs, length, n, LANES)

    def slot_major(value):
        n = value.shape[2]
        value = value.reshape(pairs, length, n, per, head_cols)
        return value.transpose(0, 3, 1, 2, 4).reshape(slots, length, n, head_cols)

    weight_rows = jnp.concatenate(
        [
            jnp.swapaxes(w_qkv.astype(BF16), 1, 2).reshape(3 * head_cols, row_part),
            w_out.astype(BF16),
            jnp.swapaxes(w_gate_up.astype(BF16), 1, 2).reshape(2 * ffn_cols, row_part),
            w_down.astype(BF16),
        ],
        axis=0,
    )
    segment_ids = lax.dynamic_index_in_dim(segments, links.slot, 0, keepdims=False)
    first_pos, cos_wide, sin_wide = position_tables(segment_ids, head_dim)
    x_bf16, h_one, q_rot, k_rot, v_mix, attended, log_total, weights_a, weights_b, middle, h_two = (
        forward_part(
            n_seq, n_head, head_cols, layer_input, values_first, weight_rows, norm_gains,
            cos_wide, sin_wide, first_pos,
        )
    )
    w_in, w_o = weights_a[:, : 3 * head_cols], weights_a[:, 3 * head_cols :]
    w_gu, w_d = weights_b[:, : 2 * ffn_cols], weights_b[:, 2 * ffn_cols :]
    x_own = x_bf16.reshape(slots * rows, width).astype(F32)
    middle = middle.reshape(slots * rows, width)
    ein = functools.partial(jnp.einsum, preferred_element_type=F32)
    inverse_one = lax.rsqrt(jnp.mean(x_own * x_own, axis=-1, keepdims=True) + EPSILON)
    normed_one = x_own * inverse_one
    inverse_two = lax.rsqrt(jnp.mean(middle * middle, axis=-1, keepdims=True) + EPSILON)
    normed_two = middle * inverse_two
    saved = (q_rot, k_rot, v_mix, attended, log_total)
    attended = jnp.swapaxes(attended.reshape(length, slots, head_cols), 0, 1)
    gate_up = ein("ld,qfd->qlf", h_two, w_gu)
    gate, up = gate_up[..., :ffn_cols], gate_up[..., ffn_cols:]
    sigmoid_gate = jax.nn.sigmoid(gate)
    activated = gate * sigmoid_gate
    hidden = (activated * up).astype(BF16)
    ffn_out = links.own_sum(ein("qlf,qfd->ld", hidden, w_d))
    block_delta = jnp.where(is_live, middle - x_own + ffn_out, 0.0).astype(BF16)

    grad_own = links.swap_slots(out_grad)
    d_own = jnp.where(is_live, grad_own, jnp.zeros_like(grad_own))
    d_out = d_own.reshape(slots * rows, width).astype(F32)
    d_ffn = links.whole_sequence(d_own)
    g_down = ein("qlf,ld->qfd", hidden, d_ffn)
    d_hidden = ein("ld,qfd->qlf", d_ffn, w_d)
    d_gate = (
        d_hidden * up * sigmoid_gate * (1.0 + gate * (1.0 - sigmoid_gate))
    ).astype(BF16)
    d_up = (d_hidden * activated).astype(BF16)
    d_gate_up = jnp.concatenate([d_gate, d_up], axis=2)
    d_normed_two = links.own_sum(ein("qlf,qfd->ld", d_gate_up, w_gu))
    g_gate_up = ein("qlf,ld->qfd", d_gate_up, h_two)
    grads_b = jnp.concatenate([g_gate_up.astype(BF16), g_down.astype(BF16)], axis=1)
    gain_two = jnp.sum(normed_two * d_normed_two, axis=0)
    middle_delta = norm_back(d_normed_two * norm_gains[1], normed_two, inverse_two)
    d_middle = d_out + middle_delta
    d_attn = links.whole_sequence(d_middle.astype(BF16).reshape(slots, rows, width))
    d_attended = ein("ld,qcd->qlc", d_attn, w_o).astype(BF16)
    if per > 1:
        d_attended = pair_major(d_attended[:, :, None])[:, :, 0]
    d_project = jnp.concatenate(
        attend_back(saved, d_attended, cos_wide, sin_wide, first_pos), axis=2
    )
    if per > 1:
        d_project = slot_major(d_project.reshape(pairs, length, 3, LANES)).reshape(
            slots, length, 3 * head_cols
        )
    d_value = d_project[:, :, 2 * head_cols :]
    g_out = ein("qlc,ld->qcd", attended, d_attn)
    g_qkv = ein("qlc,ld->qcd", d_project, h_one)
    grads_a = jnp.concatenate([g_qkv.astype(BF16), g_out.astype(BF16)], axis=1)
    d_normed_one = links.own_sum(ein("qlc,qcd->ld", d_project, w_in))
    gain_one = jnp.sum(normed_one * d_normed_one, axis=0)
    input_delta = middle_delta + norm_back(d_normed_one * norm_gains[0], normed_one, inverse_one)
    input_delta = jnp.where(is_live, input_delta, 0.0).astype(BF16)
    gains = jnp.concatenate([gain_one.reshape(8, -1), gain_two.reshape(8, -1)], axis=0)

    block_got, input_got, first_got, gains, sum_a, sum_b, full_a, full_b = reduce_grads(
        n_seq,
        n_head,
        (LANES, unit_chunk(rows_b)),
        block_delta.reshape(slots, rows, width),
        input_delta.reshape(slots, rows, width),
        d_value,
        gains,
        grads_a,
        grads_b,
    )
    block_out = layer_input.astype(F32) + block_got.astype(F32)
    input_grad = out_grad.astype(F32) + input_got.astype(F32)
    first_grad = first_got.astype(F32)
    grad_gains = gains.reshape(2, width)
    new_gains = norm_gains - GAIN_RATE * grad_gains * lax.rsqrt(
        jnp.mean(grad_gains * grad_gains, axis=-1, keepdims=True) + EPSILON
    )

    wide, out_right, new_head, new_unit, step_a, step_b = shampoo(
        stats_wide, roots_wide, stats_head, roots_head, stats_unit, roots_unit,
        full_a, sum_a, full_b, sum_b,
    )
    cut = 3 * head_cols
    turned = lambda value, n: jnp.swapaxes(value.reshape(n, -1, row_part), 1, 2)
    return (
        block_out,
        input_grad,
        first_grad,
        turned(sum_a[:cut], 3).astype(F32),
        turned(sum_b[: 2 * ffn_cols], 2).astype(F32),
        sum_a[cut:].astype(F32),
        sum_b[2 * ffn_cols :].astype(F32),
        grad_gains,
        w_qkv - STEP_RATE * turned(step_a[:cut], 3),
        w_gate_up - STEP_RATE * turned(step_b[: 2 * ffn_cols], 2),
        w_out - OUT_RATE * step_a[cut:],
        w_down - STEP_RATE * step_b[2 * ffn_cols :],
        new_gains,
        wide,
        out_right[0],
        new_head,
        new_unit,
    )


def unit_chunk(rows):
    return max(c for c in range(16, 177, 16) if rows % c == 0)


def solution(mesh):
    return jax.shard_map(
        functools.partial(shards, mesh.shape["seq"], mesh.shape["head"]),
        mesh=mesh,
        in_specs=(
            P("seq", "head", None),
            P("seq", None, "head"),
            P(None, "seq", "head"),
            P(None, "seq", "head"),
            P("head", "seq"),
            P("head", "seq"),
            P(),
            P("seq", "head", None),
            P("seq", None),
            P("seq"),
            P(None, "head", "seq", None),
            P(None, "head", "seq", None),
            P(None, "head", None, None),
            P(None, "head", None, None),
            P(None, "head", None, None),
            P(None, "head", None, None),
        ),
        out_specs=(
            P("seq", "head", None),
            P("seq", "head", None),
            P("seq", None, "head"),
            P(None, "seq", "head"),
            P(None, "seq", "head"),
            P("head", "seq"),
            P("head", "seq"),
            P(),
            P(None, "seq", "head"),
            P(None, "seq", "head"),
            P("head", "seq"),
            P("head", "seq"),
            P(),
            P(None, "head", "seq", None),
            P("head", "seq", None),
            P(None, "head", None, None),
            P(None, "head", None, None),
        ),
        check_vma=False,
    )
```

```python
import functools

import jax
import jax.numpy as jnp
from jax import lax
from jax.experimental import pallas as pl
from jax.experimental.pallas import tpu as pltpu
from jax.sharding import PartitionSpec as P

EPSILON = 1e-06
STAT_DECAY = 0.5
STEP_RATE = 0.02
OUT_RATE = 0.1
GAIN_RATE = 0.25
AXES = ("seq", "head")
MESH = pl.DeviceIdType.MESH
LANES = 128
BLOCK = 256
BF16 = jnp.bfloat16
F32 = jnp.float32


def dot_nt(matrix_a, matrix_b):
    return lax.dot_general(
        matrix_a, matrix_b, (((1,), (1,)), ((), ())), preferred_element_type=F32
    )


def dot_tn(matrix_a, matrix_b):
    return lax.dot_general(
        matrix_a, matrix_b, (((0,), (0,)), ((), ())), preferred_element_type=F32
    )


def dot_nn(matrix_a, matrix_b):
    return jnp.dot(matrix_a, matrix_b, preferred_element_type=F32)


def norm_back(d_normed, normed, inverse):
    return inverse * (d_normed - normed * jnp.mean(d_normed * normed, axis=-1, keepdims=True))


def position_tables(segment_ids, head_dim):
    length = segment_ids.shape[0]
    position = jnp.arange(length, dtype=jnp.int32)
    opens = jnp.concatenate([jnp.ones((1,), dtype=bool), segment_ids[1:] != segment_ids[:-1]])
    first_pos = lax.cummax(jnp.where(opens, position, 0), axis=0)
    offset = (position - first_pos).astype(F32)
    half_width = head_dim // 2
    frequency = jnp.exp(-jnp.log(10000.0) * jnp.arange(half_width, dtype=F32) / half_width)
    angle = offset[:, None] * frequency[None, :]
    cosine, sine_part = jnp.cos(angle), jnp.sin(angle)
    per_lane = LANES // head_dim
    cos_wide = jnp.concatenate([cosine, cosine] * per_lane, axis=1)
    sin_wide = jnp.concatenate([-sine_part, sine_part] * per_lane, axis=1)
    return first_pos, cos_wide, sin_wide


def swap_halves(values):
    lane = lax.broadcasted_iota(jnp.int32, values.shape, 1)
    return jnp.where((lane & 32) == 0, pltpu.roll(values, 96, 1), pltpu.roll(values, 32, 1))


def two_heads(block):
    lane = lax.broadcasted_iota(jnp.int32, block.shape, 1)
    zero = jnp.zeros_like(block)
    return jnp.concatenate(
        [jnp.where(lane < 64, block, zero), jnp.where(lane >= 64, block, zero)], axis=0
    )


def one_pair(transposed, width):
    kept = jnp.concatenate([transposed[:64, :width], transposed[64:, width:]], axis=0)
    return kept.T


def seen(first_ref, begin, key_count):
    first = first_ref[0:1, begin : begin + BLOCK]
    query = begin + lax.broadcasted_iota(jnp.int32, (1, BLOCK), 1)
    first = jnp.concatenate([first, first], axis=1)
    query = jnp.concatenate([query, query], axis=1)
    key = lax.broadcasted_iota(jnp.int32, (key_count, 2 * BLOCK), 0)
    return (key >= first) & (key <= query)


def attend_back_kernel(
    qr_ref, kr_ref, vm_ref, att_ref, d_ref, lse_ref, cos_ref, sin_ref, first_ref,
    dq_ref, dk_ref, dv_ref, key_sum, value_sum,
):
    length = qr_ref.shape[1]
    key_sum[...] = jnp.zeros_like(key_sum)
    value_sum[...] = jnp.zeros_like(value_sum)
    k_turned = kr_ref[0].T
    cosine, sine_part = cos_ref[...], sin_ref[...]
    product = (d_ref[0].astype(F32) * att_ref[...].astype(F32)).T
    inner = [
        jnp.sum(product[:64], axis=0, keepdims=True),
        jnp.sum(product[64:], axis=0, keepdims=True),
    ]
    for step in range(length // BLOCK):
        begin, keys = step * BLOCK, (step + 1) * BLOCK
        queries = two_heads(qr_ref[0, begin:keys, :])
        d_out = two_heads(d_ref[0, begin:keys, :])
        scores = dot_nt(kr_ref[0, :keys, :], queries)
        log_total = jnp.concatenate(
            [lse_ref[0, 0:1, begin:keys], lse_ref[0, 1:2, begin:keys]], axis=1
        )
        chances = jnp.where(seen(first_ref, begin, keys), jnp.exp(scores - log_total), 0.0)
        d_chances = dot_nt(vm_ref[0, :keys, :], d_out)
        part = jnp.concatenate([inner[0][:, begin:keys], inner[1][:, begin:keys]], axis=1)
        d_scores = (chances * (d_chances - part)).astype(BF16)
        key_sum[:keys, :] += dot_nn(d_scores, queries)
        value_sum[:keys, :] += dot_nn(chances.astype(BF16), d_out)
        d_query = one_pair(dot_nn(k_turned[:, :keys], d_scores), BLOCK) * 0.125
        dq_ref[0, begin:keys, :] = (
            d_query * cosine[begin:keys] - swap_halves(d_query) * sine_part[begin:keys]
        ).astype(BF16)
    d_key = key_sum[...]
    dk_ref[0] = (d_key * cosine - swap_halves(d_key) * sine_part).astype(BF16)
    dv_ref[0] = (0.5 * value_sum[...]).astype(BF16)


def attend_back(saved, d_attended, cos_wide, sin_wide, first_pos):
    q_rot, k_rot, v_mix, attended, log_total = saved
    pairs, length, _ = q_rot.shape
    part = pl.BlockSpec((1, length, LANES), lambda p: (p, 0, 0))
    table = pl.BlockSpec((length, LANES), lambda p: (0, 0))
    out = jax.ShapeDtypeStruct((pairs, length, LANES), BF16)
    return pl.pallas_call(
        attend_back_kernel,
        grid=(pairs,),
        in_specs=[part] * 3 + [pl.BlockSpec((length, LANES), lambda p: (0, p)), part,
                               pl.BlockSpec((1, 2, length), lambda p: (p, 0, 0)), table, table,
                               pl.BlockSpec((1, length), lambda p: (0, 0))],
        out_specs=[part] * 3,
        out_shape=[out] * 3,
        scratch_shapes=[pltpu.VMEM((length, LANES), F32)] * 2,
        compiler_params=pltpu.CompilerParams(vmem_limit_bytes=48 << 20),
        cost_estimate=pl.CostEstimate(
            flops=pairs * length * length * 128 * 20, bytes_accessed=pairs * length * 128 * 24,
            transcendentals=pairs * length * length),
    )(q_rot, k_rot, v_mix, attended, d_attended, log_total, cos_wide, sin_wide, first_pos[None, :])


class Place:
    def __init__(self, n_seq, n_head, slots):
        self.n_seq, self.slots, self.ranks = n_seq, slots, n_head // slots
        self.seq = lax.axis_index("seq")
        head = lax.axis_index("head")
        self.slot, self.rank = head // self.ranks, head % self.ranks

    def at_slot(self, step):
        return (self.slot + step + self.slots) % self.slots

    def at_seq(self, step):
        return (self.seq + step + self.n_seq) % self.n_seq

    @property
    def line(self):
        return self.slots == 4 and self.n_seq == 4

    def source(self, step):
        if not self.line:
            return self.at_slot(-step)
        upper = self.slot // 2
        inner = (self.slot + upper) % 2
        near = step + inner * (1 - 2 * step) * (1 - step // 2)
        return near + upper * (3 - 2 * near)

    @property
    def beside(self):
        return self.seq + 1 - 2 * (self.seq % 2)

    @property
    def across(self):
        return self.seq + 2 - 4 * (self.seq // 2)

    def device(self, seq=None, slot=None, rank=None):
        seq = self.seq if seq is None else seq
        slot = self.slot if slot is None else slot
        rank = self.rank if rank is None else rank
        return (seq, slot * self.ranks + rank)

    def greet(self, with_ranks):
        others = [self.device(slot=self.at_slot(k)) for k in range(1, self.slots)]
        others += [self.device(seq=self.at_seq(d)) for d in range(1, self.n_seq)]
        if with_ranks:
            others += [
                self.device(rank=(self.rank + j) % self.ranks) for j in range(1, self.ranks)
            ]
        barrier = pltpu.get_barrier_semaphore()
        for other in others:
            pl.semaphore_signal(barrier, inc=1, device_id=other, device_id_type=MESH)
        pl.semaphore_wait(barrier, len(others))


class Sender:
    def __init__(self, send_sems, recv_sems):
        self.send_sems, self.recv_sems, self.used = send_sems, recv_sems, 0

    def start(self, src, dst, device, recv=None):
        copy = pltpu.make_async_remote_copy(
            src_ref=src,
            dst_ref=dst,
            send_sem=self.send_sems.at[self.used],
            recv_sem=self.recv_sems.at[self.used] if recv is None else recv,
            device_id=device,
            device_id_type=MESH,
        )
        self.used += 1
        copy.start()
        return copy


def lanes(index, width):
    return pl.ds(pl.multiple_of(index * width, width), width)


def forward_kernel(
    n_seq, n_head, head_cols,
    x_ref, vf_ref, wt_ref, g_ref, gains_ref, cos_ref, sin_ref, first_ref, live_ref,
    x_res, h_one_res, q_res, k_res, v_res, att_res, lse_out, w_a_res, w_b, middle_res, h_two_res, g_res, e_res,
    x_out, h_one, q_out, k_out, v_out, att_out, w_a, middle, h_two, g_out, e_all,
    vf_all, away, back, sems, z_recv, v_recv, own_sems, res_sems,
):
    slots, rows, width = x_ref.shape
    part = wt_ref.shape[1]
    rows_a = w_a.shape[1]
    place = Place(n_seq, n_head, slots)
    ranks = place.ranks
    length = slots * ranks * rows
    per = LANES // head_cols
    pairs = slots // per
    mine = lanes(place.seq, part)
    sections = {"a": (w_a, pl.ds(0, rows_a)), "b": (w_b, pl.ds(rows_a, wt_ref.shape[0] - rows_a))}
    ids = {}
    elsewhere = place.device(seq=place.at_seq(1))

    def index(name):
        return ids.setdefault(name, len(ids))

    def remote(name, src, dst, device, recv=None):
        i = index(name)
        return pltpu.make_async_remote_copy(
            src_ref=src, dst_ref=dst, send_sem=sems.at[0, i],
            recv_sem=sems.at[1, i] if recv is None else recv,
            device_id=device, device_id_type=MESH,
        )

    def x_copy(k):
        to = place.at_slot(k)
        return remote(("x", k), x_ref.at[to], x_out.at[place.slot], place.device(slot=to))

    def g_copy(k):
        to = place.at_slot(k)
        return remote(("g", k), g_ref.at[to], g_out.at[place.slot], place.device(slot=to))

    def v_copy(k):
        to = place.at_slot(k)
        return remote(("v", k), vf_ref.at[to], vf_all.at[place.slot], place.device(slot=to),
                      v_recv.at[place.slot])

    def v_wait(source):
        pltpu.make_async_remote_copy(
            src_ref=vf_ref.at[0], dst_ref=vf_all.at[source], send_sem=sems.at[0, 0],
            recv_sem=v_recv.at[source], device_id=elsewhere, device_id_type=MESH,
        ).wait_recv()

    def piece(sec, step):
        ref, at = sections[sec]
        return wt_ref.at[at] if step == 0 else ref.at[step, :, mine]

    def z_copy(name, sec, step, to, to_step):
        ref, _ = sections[sec]
        which = 0 if sec == "a" else 1
        return remote((name, sec, step), piece(sec, step), ref.at[to_step, :, mine],
                      place.device(slot=to), z_recv.at[which, to_step])

    def z_wait(sec, step):
        ref, _ = sections[sec]
        which = 0 if sec == "a" else 1
        pltpu.make_async_remote_copy(
            src_ref=piece(sec, 0), dst_ref=ref.at[step, :, mine], send_sem=sems.at[0, 0],
            recv_sem=z_recv.at[which, step], device_id=elsewhere, device_id_type=MESH,
        ).wait_recv()

    slot = place.slot
    upper = slot // 2
    inner = (slot + upper) % 2

    def z_start_own(sec):
        if not place.line:
            for k in range(1, slots):
                z_copy(("z", k), sec, 0, place.at_slot(k), k).start()
            return
        @pl.when(slot < 3)
        def _():
            to = slot + 1
            z_copy("up", sec, 0, to, 1 + (to == 2).astype(jnp.int32)).start()

        @pl.when(slot > 0)
        def _():
            to = slot - 1
            z_copy("down", sec, 0, to, 1 + (to == 1).astype(jnp.int32)).start()

    def z_own_sends(sec):
        if not place.line:
            for k in range(1, slots):
                z_copy(("z", k), sec, 0, place.at_slot(k), k).wait_send()
            return

        @pl.when(slot < 3)
        def _():
            z_copy("up", sec, 0, slot + 1, 1).wait_send()

        @pl.when(slot > 0)
        def _():
            z_copy("down", sec, 0, slot - 1, 1).wait_send()

    def z_relay(sec, step):
        if step == 1:
            return z_copy("on", sec, step, slot + 1 - 2 * upper, 3)
        return z_copy("on", sec, step, slot - 1 + 2 * upper, step)

    def near_copy(sec, step):
        ref, _ = sections[sec]
        dst = ref.at[step, :, mine]
        if not place.line:
            return [
                remote(("xy", d, sec, step), piece(sec, step), dst, place.device(seq=place.at_seq(d)))
                for d in range(1, n_seq)
            ]
        return [
            remote(("xy", 0, sec, step), piece(sec, step), dst, place.device(seq=place.beside)),
            remote(("xy", 1, sec, step), piece(sec, step), dst, place.device(seq=place.across)),
        ]

    def far_copy(sec, step, which):
        ref, at = sections[sec]
        half = at.size // 2
        cut = pl.ds(which * half, half)
        source = place.beside if which == 0 else place.across
        to = place.across if which == 0 else place.beside
        where = ref.at[step, cut, lanes(source, part)]
        return remote(("far", which, sec, step), where, where, place.device(seq=to))

    def z_event(sec, step):
        z_wait(sec, step)
        if place.line:
            @pl.when(inner == 1)
            def _():
                z_relay(sec, step).start()
        for copy in near_copy(sec, step):
            copy.start()

    def xy_event(sec, step):
        for which, copy in enumerate(near_copy(sec, step)):
            copy.wait_recv()
            if place.line:
                far_copy(sec, step, which).start()

    def done_event(sec, step):
        if place.line:
            for which in range(2):
                far_copy(sec, step, which).wait_recv()

    def position(p, rank):
        return pl.ds(pl.multiple_of((p * ranks + rank) * rows, rows), rows)

    def share(name, ref, p, j):
        where = ref.at[position(p, place.rank), :]
        return remote((name, p, j), where, where, place.device(rank=(place.rank + j) % ranks))

    results = {
        "x": (x_out, x_res), "h1": (h_one, h_one_res), "q": (q_out, q_res), "k": (k_out, k_res),
        "v": (v_out, v_res), "att": (att_out, att_res), "a": (w_a, w_a_res),
        "mid": (middle, middle_res), "h2": (h_two, h_two_res), "g": (g_out, g_res),
        "e": (e_all, e_res),
    }

    def result(name):
        src, dst = results[name]
        return pltpu.make_async_copy(src, dst, res_sems.at[list(results).index(name)])

    place.greet(True)
    own = [
        pltpu.make_async_copy(x_ref.at[slot], x_out.at[slot], own_sems.at[0]),
        pltpu.make_async_copy(wt_ref.at[sections["a"][1]], w_a.at[0, :, mine], own_sems.at[1]),
        pltpu.make_async_copy(wt_ref.at[sections["b"][1]], w_b.at[0, :, mine], own_sems.at[2]),
        pltpu.make_async_copy(vf_ref.at[slot], vf_all.at[slot], own_sems.at[3]),
        pltpu.make_async_copy(g_ref.at[slot], g_out.at[slot], own_sems.at[4]),
    ]
    for sec in ("a", "b"):
        for copy in near_copy(sec, 0):
            copy.start()
        z_start_own(sec)
    for k in (2, 3, 1):
        x_copy(k).start()
    for copy in own:
        copy.start()
    xy_event("a", 0)
    z_event("a", 1)
    xy_event("b", 0)
    z_event("a", 2)
    xy_event("a", 1)
    z_event("b", 1)
    for k in range(1, slots):
        x_copy(k).wait_recv()
    own[0].wait()
    for k in range(1, slots):
        v_copy(k).start()

    for p in range(slots):
        x = x_out[p].astype(F32)
        normed = x * lax.rsqrt(jnp.mean(x * x, axis=-1, keepdims=True) + EPSILON)
        h_one[position(p, place.rank), :] = (normed * gains_ref[0:1, :]).astype(BF16)
        for j in range(1, ranks):
            share("h1", h_one, p, j).start()
    xy_event("a", 2)
    z_event("b", 2)
    xy_event("b", 1)
    z_event("a", 3)
    own[1].wait()
    own[3].wait()
    done_event("a", 0)
    for p in range(slots):
        for j in range(1, ranks):
            share("h1", h_one, p, j).wait_recv()
    result("x").start()
    result("h1").start()

    def g_event():
        for k in range(1, slots):
            g_copy(k).start()

    events = {
        (0, 1): [lambda: xy_event("a", 3)],
        (0, 3): [lambda: z_event("b", 3), g_event],
        (1, 0): [lambda: done_event("a", 1)],
        (1, 3): [lambda: xy_event("b", 2)],
        (2, 0): [lambda: done_event("a", 2)],
        (3, 0): [lambda: done_event("a", 3)],
    }
    if per > 1:
        xy_event("a", 3)
        z_event("b", 3)
        g_event()
        xy_event("b", 2)
        for step in range(1, slots):
            done_event("a", step)
            v_wait(place.source(step))
        events = {}

    def one_pair_of_heads(j, carry):
        def pump(point):
            for (step, at), todo in events.items():
                if at == point:
                    @pl.when(j == step)
                    def _(todo=todo):
                        for act in todo:
                            act()

        pump(0)
        if per == 1:
            @pl.when(j > 0)
            def _():
                v_wait(place.source(j))
            w_in = w_a[j, : 3 * head_cols, :]
            first = vf_all[place.source(j)]
        else:
            w_in = jnp.concatenate(
                [
                    w_a[j * per + u, i * head_cols : (i + 1) * head_cols, :]
                    for i in range(3)
                    for u in range(per)
                ],
                axis=0,
            )
            first = jnp.concatenate([vf_all[place.source(j * per + u)] for u in range(per)], axis=1)
        half = length // 2
        for part_at in range(2):
            at = slice(part_at * half, (part_at + 1) * half)
            project = dot_nt(h_one[at, :], w_in)
            cosine, sine_part = cos_ref[at, :], sin_ref[at, :]
            q_raw, k_raw = project[:, :LANES], project[:, LANES : 2 * LANES]
            q_out[j, at, :] = ((q_raw * cosine + swap_halves(q_raw) * sine_part) * 0.125).astype(BF16)
            k_out[j, at, :] = (k_raw * cosine + swap_halves(k_raw) * sine_part).astype(BF16)
            v_out[j, at, :] = (0.5 * project[:, 2 * LANES :] + 0.5 * first[at].astype(F32)).astype(BF16)
        pump(1)
        v_turned = v_out[j].T
        for step in range(length // BLOCK):
            begin, keys = step * BLOCK, (step + 1) * BLOCK
            queries = two_heads(q_out[j, begin:keys, :])
            scores = dot_nt(k_out[j, :keys, :], queries)
            scores = jnp.where(seen(first_ref, begin, keys), scores, -1e30)
            top = jnp.max(scores, axis=0, keepdims=True)
            exps = jnp.exp(scores - top)
            total = jnp.sum(exps, axis=0, keepdims=True)
            chances = (exps * (1.0 / total)).astype(BF16)
            attended = dot_nn(v_turned[:, :keys], chances)
            att_out[begin:keys, lanes(j, LANES)] = one_pair(attended, BLOCK).astype(BF16)
            log_total = top + jnp.log(total)
            lse_out[j, 0:1, begin:keys] = log_total[:, :BLOCK]
            lse_out[j, 1:2, begin:keys] = log_total[:, BLOCK:]
            if step == length // BLOCK // 2 - 1:
                pump(2)
        pump(3)
        return carry

    lax.fori_loop(0, pairs, one_pair_of_heads, 0)
    for name in ("q", "k", "v", "att", "a"):
        result(name).start()

    w_o = w_a[:, 3 * head_cols :, :].reshape(slots * head_cols, width)

    def away_copy(p, j):
        return remote(("away", p, j), away.at[j - 1, p], back.at[j - 1, p],
                      place.device(rank=(place.rank + j) % ranks))

    for p in range(slots):
        for j in range(1, ranks):
            at = position(p, (place.rank + j) % ranks)
            away[j - 1, p] = dot_nn(att_out[at, :], w_o).astype(BF16)
            away_copy(p, j).start()
    for p in range(slots):
        middle[p] = x_out[p].astype(F32) + dot_nn(att_out[position(p, place.rank), :], w_o)
    for p in range(slots):
        value = middle[p]
        for j in range(1, ranks):
            away_copy(p, j).wait_recv()
            value = value + back[j - 1, p].astype(F32)
        middle[p] = value
        normed = value * lax.rsqrt(jnp.mean(value * value, axis=-1, keepdims=True) + EPSILON)
        h_two[position(p, place.rank), :] = (normed * gains_ref[1:2, :]).astype(BF16)
        for j in range(1, ranks):
            share("h2", h_two, p, j).start()
    result("mid").start()
    own[4].wait()
    for k in range(1, slots):
        g_copy(k).wait_recv()
    result("g").start()
    for p in range(slots):
        e_all[position(p, place.rank), :] = (g_out[p].astype(F32) * live_ref[...]).astype(BF16)
        for j in range(1, ranks):
            share("e", e_all, p, j).start()
    for p in range(slots):
        for j in range(1, ranks):
            share("h2", h_two, p, j).wait_recv()
            share("e", e_all, p, j).wait_recv()
            share("e", e_all, p, j).wait_send()
    result("h2").start()
    result("e").start()
    xy_event("b", 3)
    for step in range(slots):
        done_event("b", step)
    for name in results:
        result(name).wait()
    for p in range(slots):
        for j in range(1, ranks):
            share("h1", h_one, p, j).wait_send()
            share("h2", h_two, p, j).wait_send()
            away_copy(p, j).wait_send()
    for k in range(1, slots):
        x_copy(k).wait_send()
        v_copy(k).wait_send()
        g_copy(k).wait_send()
    for sec in ("a", "b"):
        z_own_sends(sec)
        for step in range(slots):
            for copy in near_copy(sec, step):
                copy.wait_send()
            if place.line:
                for which in range(2):
                    far_copy(sec, step, which).wait_send()
                if step > 0:
                    @pl.when(inner == 1)
                    def _(sec=sec, step=step):
                        z_relay(sec, step).wait_send()
    own[2].wait()


def forward_part(
    n_seq, n_head, head_cols, layer_input, values_first, weight_rows, out_grad, gains,
    cos_wide, sin_wide, first_pos, live,
):
    slots, rows, width = layer_input.shape
    all_rows, part = weight_rows.shape
    ranks = n_head // slots
    length = slots * ranks * rows
    rows_a = 4 * head_cols
    pairs = slots * head_cols // LANES
    count = 3 * (slots - 1) + 2 * (2 + 4 * slots + slots * n_seq) + 4 * slots * ranks
    any_space = pl.BlockSpec(memory_space=pl.ANY)
    vmem = pl.BlockSpec(memory_space=pltpu.VMEM)
    shape = jax.ShapeDtypeStruct
    heads = shape((pairs, length, LANES), BF16)
    return pl.pallas_call(
        functools.partial(forward_kernel, n_seq, n_head, head_cols),
        in_specs=[any_space] * 4 + [vmem] * 5,
        out_specs=[any_space] * 6 + [vmem] + [any_space] * 6,
        out_shape=[
            shape(layer_input.shape, BF16),
            shape((length, width), BF16),
            heads, heads, heads,
            shape((length, slots * head_cols), BF16),
            shape((pairs, 2, length), F32),
            shape((slots, rows_a, width), BF16),
            shape((slots, all_rows - rows_a, width), BF16),
            shape(layer_input.shape, F32),
            shape((length, width), BF16),
            shape(layer_input.shape, BF16),
            shape((length, width), BF16),
        ],
        scratch_shapes=[
            pltpu.VMEM(layer_input.shape, BF16),
            pltpu.VMEM((length, width), BF16),
            pltpu.VMEM(heads.shape, BF16),
            pltpu.VMEM(heads.shape, BF16),
            pltpu.VMEM(heads.shape, BF16),
            pltpu.VMEM((length, slots * head_cols), BF16),
            pltpu.VMEM((slots, rows_a, width), BF16),
            pltpu.VMEM(layer_input.shape, F32),
            pltpu.VMEM((length, width), BF16),
            pltpu.VMEM(layer_input.shape, BF16),
            pltpu.VMEM((length, width), BF16),
            pltpu.VMEM(values_first.shape, BF16),
            pltpu.VMEM((ranks - 1, slots, rows, width), BF16),
            pltpu.VMEM((ranks - 1, slots, rows, width), BF16),
            pltpu.SemaphoreType.DMA((2, count)),
            pltpu.SemaphoreType.DMA((2, slots)),
            pltpu.SemaphoreType.DMA((slots,)),
            pltpu.SemaphoreType.DMA((5,)),
            pltpu.SemaphoreType.DMA((11,)),
        ],
        compiler_params=pltpu.CompilerParams(
            collective_id=0, has_side_effects=True, vmem_limit_bytes=60 << 20
        ),
    )(
        layer_input, values_first, weight_rows, out_grad, gains, cos_wide, sin_wide,
        first_pos[None, :], live,
    )


def backward_kernel(
    n_seq, n_head, head_cols,
    wa_ref, wb_ref, h_one_ref, h_two_ref, x_ref, mid_ref, g_ref, q_ref, k_ref, v_ref, att_ref, e_ref,
    lse_ref, gains_ref, cos_ref, sin_ref, first_ref, live_ref,
    block_out, input_out, first_out, gains_out, sum_a, sum_b, full_a, full_b,
    w_a, w_b, normed_all, e_all, x_own, middle, g_own, q_all, k_all, v_all, att_all,
    acc_one, acc_two, hidden, d_gate, d_project, away, back, delta_own,
    near_a, near_b, next_a, next_b, far_a, far_b,
    gain_sum, gain_seq, gain_slot, gain_rank,
    sems, near_sems, next_sems, far_sems, first_sems, load_sems, own_sems,
):
    slots, rows_b, width = w_b.shape
    rows_a = w_a.shape[1]
    ffn_cols = rows_b // 3
    ranks = n_head // slots
    rows = x_own.shape[1]
    length = slots * ranks * rows
    part = width // n_seq
    place = Place(n_seq, n_head, slots)
    slot = place.slot
    beside, across = place.beside, place.across
    corner = 3 - place.seq
    mine = lanes(place.seq, part)
    other = 1 - place.rank
    elsewhere = place.device(seq=beside)
    ids = {}
    sections = {
        "a": (0, w_a, near_a, next_a, far_a, sum_a, full_a, 128),
        "b": (1, w_b, near_b, next_b, far_b, sum_b, full_b, rows_b // 6),
    }

    def remote(name, src, dst, device, send=None, recv=None):
        if send is None:
            i = ids.setdefault(name, len(ids))
            send, recv = sems.at[0, i], sems.at[1, i]
        return pltpu.make_async_remote_copy(
            src_ref=src, dst_ref=dst, send_sem=send, recv_sem=recv,
            device_id=device, device_id_type=MESH,
        )

    def position(p, rank):
        return pl.ds(pl.multiple_of((p * ranks + rank) * rows, rows), rows)

    def halves(sec):
        half = sections[sec][1].shape[1] // 2
        return pl.ds(0, half), pl.ds(half, half)

    def near_copies(sec, k):
        i, grads, near = sections[sec][:3]
        upper, lower = halves(sec)
        plan = (
            (upper, beside, beside), (upper, corner, beside),
            (lower, across, across), (lower, corner, across),
        )
        return [
            remote(None, grads.at[k, cut, lanes(quarter, part)], near.at[k, n],
                   place.device(seq=to), near_sems.at[0, i, k, n], near_sems.at[1, i, k, n])
            for n, (cut, quarter, to) in enumerate(plan)
        ]

    def next_copies(sec, k):
        i, grads, _, then = sections[sec][:4]
        upper, lower = halves(sec)
        plan = ((upper, across), (lower, beside))
        return [
            remote(None, grads.at[k, cut, lanes(to, part)], then.at[k, n],
                   place.device(seq=to), next_sems.at[0, i, k, n], next_sems.at[1, i, k, n])
            for n, (cut, to) in enumerate(plan)
        ]

    def far_copy(sec, k):
        i, grads = sections[sec][:2]
        far = sections[sec][4]
        return remote(None, grads.at[k, :, mine], far.at[slot], place.device(slot=place.source(k)),
                      far_sems.at[0, i, k], far_sems.at[1, i, slot])

    def add_rows(sec, k, begin, where, addend):
        grads, strip = sections[sec][1], sections[sec][7]

        def one(i, carry):
            at = pl.ds(pl.multiple_of(begin + i * strip, 16), strip)
            value = grads[k, at, where].astype(F32)
            value = value + addend[pl.ds(pl.multiple_of(i * strip, 16), strip), :].astype(F32)
            grads[k, at, where] = value.astype(BF16)
            return carry

        lax.fori_loop(0, addend.shape[0] // strip, one, 0)

    def launch(sec, k):
        for copy in near_copies(sec, k):
            copy.start()

    def second(sec, k):
        near = sections[sec][2]
        half = near.shape[2]
        came = near_copies(sec, k)
        onward = next_copies(sec, k)
        came[1].wait_recv()
        add_rows(sec, k, 0, lanes(across, part), near.at[k, 1])
        onward[0].start()
        came[3].wait_recv()
        add_rows(sec, k, half, lanes(beside, part), near.at[k, 3])
        onward[1].start()
        came[0].wait_recv()
        add_rows(sec, k, 0, mine, near.at[k, 0])
        came[2].wait_recv()
        add_rows(sec, k, half, mine, near.at[k, 2])

    def third(sec, k, sends):
        then = sections[sec][3]
        half = then.shape[2]
        for n, copy in enumerate(next_copies(sec, k)):
            copy.wait_recv()
            add_rows(sec, k, n * half, mine, then.at[k, n])
        if sends:
            far_copy(sec, k).start()

    def gather_copies(sec):
        total, full = sections[sec][5:7]
        half = total.shape[0] // 2
        near = [
            remote(("full", sec, n), total, full.at[:, mine], place.device(seq=to))
            for n, to in enumerate((beside, across))
        ]
        far = []
        for n, (source, to) in enumerate(((beside, across), (across, beside))):
            where = full.at[pl.ds(n * half, half), lanes(source, part)]
            far.append(remote(("relay", sec, n), where, where, place.device(seq=to)))
        return near, far

    def own_copy(sec):
        i = sections[sec][0]
        return pltpu.make_async_copy(
            sections[sec][5], sections[sec][6].at[:, mine], own_sems.at[3 + i]
        )

    def finish(sec):
        i, grads = sections[sec][:2]
        far, total, _, strip = sections[sec][4:]
        for j in range(1, slots):
            source = place.at_slot(j)
            remote(None, grads.at[0, :, mine], far.at[source], elsewhere,
                   far_sems.at[0, i, 0], far_sems.at[1, i, source]).wait_recv()

        def one(r, carry):
            at = pl.ds(pl.multiple_of(r * strip, 16), strip)
            value = grads[0, at, mine].astype(F32)
            for j in range(1, slots):
                value = value + far[place.at_slot(j), at, :].astype(F32)
            total[at, :] = value.astype(BF16)
            return carry

        lax.fori_loop(0, total.shape[0] // strip, one, 0)
        own_copy(sec).start()
        for copy in gather_copies(sec)[0]:
            copy.start()

    def relay(sec):
        near, far = gather_copies(sec)
        for n in range(2):
            near[n].wait_recv()
            far[n].start()

    loads = {
        "h2": (h_two_ref, normed_all), "e": (e_ref, e_all), "h1": (h_one_ref, normed_all),
        "a": (wa_ref, w_a), "x": (x_ref, x_own), "mid": (mid_ref, middle),
        "g": (g_ref, g_own), "q": (q_ref, q_all), "k": (k_ref, k_all), "v": (v_ref, v_all),
        "att": (att_ref, att_all),
    }

    def load(name):
        src, dst = loads[name]
        return pltpu.make_async_copy(src, dst, load_sems.at[slots + list(loads).index(name)])

    def load_b(k):
        return pltpu.make_async_copy(wb_ref.at[k], w_b.at[k], load_sems.at[k])

    load_b(slots - 1).start()
    load("h2").start()
    load("e").start()
    for k in reversed(range(slots - 1)):
        load_b(k).start()
    for name in loads:
        if name not in ("h1", "h2", "e"):
            load(name).start()
    place.greet(True)
    load("h2").wait()
    load("e").wait()

    strip = length // 2
    key_sum, value_sum = acc_two.at[:, :LANES], acc_two.at[:, LANES : 2 * LANES]

    def units(i, carry):
        k = slots - 1 - i
        load_b(k).wait()

        def strips(n, carry):
            at = pl.ds(pl.multiple_of(n * strip, strip), strip)
            inner = normed_all[at, :]
            gate = dot_nt(inner, w_b[k, :ffn_cols, :])
            up = dot_nt(inner, w_b[k, ffn_cols : 2 * ffn_cols, :])
            sigmoid_gate = 1.0 / (1.0 + jnp.exp(-gate))
            activated = gate * sigmoid_gate
            hid = (activated * up).astype(BF16)
            hidden[at, :] = hid
            d_hidden = dot_nt(e_all[at, :], w_b[k, 2 * ffn_cols :, :])
            dg = (d_hidden * up * sigmoid_gate * (1.0 + gate * (1.0 - sigmoid_gate))).astype(BF16)
            du = (d_hidden * activated).astype(BF16)
            d_gate[at, :] = dg
            d_project[at, :ffn_cols] = du
            out = dot_nn(hid, w_b[k, 2 * ffn_cols :, :])
            d_in = dot_nn(dg, w_b[k, :ffn_cols, :]) + dot_nn(du, w_b[k, ffn_cols : 2 * ffn_cols, :])

            @pl.when(i == 0)
            def _():
                acc_one[at, :] = out
                acc_two[at, :] = d_in

            @pl.when(i > 0)
            def _():
                acc_one[at, :] += out
                acc_two[at, :] += d_in

            return carry

        lax.fori_loop(0, length // strip, strips, 0)
        w_b[k, 2 * ffn_cols :, :] = dot_tn(hidden[...], e_all[...]).astype(BF16)
        w_b[k, :ffn_cols, :] = dot_tn(d_gate[...], normed_all[...]).astype(BF16)
        w_b[k, ffn_cols : 2 * ffn_cols, :] = dot_tn(d_project[:, :ffn_cols], normed_all[...]).astype(BF16)
        launch("b", k)

        @pl.when(i > 0)
        def _():
            second("b", k + 1)

        @pl.when(i > 1)
        def _():
            third("b", k + 2, True)

        return carry

    lax.fori_loop(0, slots, units, 0)
    load("h1").start()

    def away_copy(n, p):
        return remote(("away", n, p), away.at[n, p], back.at[n, p], place.device(rank=other))

    def share(p):
        where = e_all.at[position(p, place.rank), :]
        return remote(("share", p), where, where, place.device(rank=other))

    for n, acc in ((1, acc_two), (0, acc_one)):
        for p in range(slots):
            away[n, p] = acc[position(p, other), :].astype(BF16)
            away_copy(n, p).start()
    for name in ("x", "mid", "g"):
        load(name).wait()
    live = live_ref[...]
    gain_sum[...] = jnp.zeros_like(gain_sum)
    for p in range(slots):
        value = middle[p]
        inverse = lax.rsqrt(jnp.mean(value * value, axis=-1, keepdims=True) + EPSILON)
        normed = value * inverse
        away_copy(1, p).wait_recv()
        d_normed = acc_two[position(p, place.rank), :] + back[1, p].astype(F32)
        gain_sum[1:2, :] += jnp.sum(normed * d_normed, axis=0, keepdims=True)
        delta = norm_back(d_normed * gains_ref[1:2, :], normed, inverse)
        away_copy(0, p).wait_recv()
        out = acc_one[position(p, place.rank), :] + back[0, p].astype(F32)
        delta_own[p] = ((value - x_own[p].astype(F32) + out) * live).astype(BF16)
        middle[p] = delta
        e_all[position(p, place.rank), :] = (g_own[p].astype(F32) * live + delta).astype(BF16)
        share(p).start()

    def swap(name, src, dst):
        return [
            remote((name, j), src.at[place.at_slot(j)], dst.at[slot],
                   place.device(slot=place.at_slot(j)))
            for j in (2, 3, 1)
        ]

    def keep(n, src, dst):
        return pltpu.make_async_copy(src, dst.at[slot], own_sems.at[n])

    for copy in swap("block", delta_own, block_out):
        copy.start()
    keep(0, delta_own.at[slot], block_out).start()
    for name in ("a", "h1", "q", "k", "v", "att"):
        load(name).wait()
    for p in range(slots):
        share(p).wait_recv()

    def first_copy(k):
        return remote(None, v_all.at[k], first_out.at[slot],
                      place.device(slot=place.source(k)),
                      first_sems.at[0, k], first_sems.at[1, slot])

    def heads(i, carry):
        k = slots - 1 - i
        lane = lanes(k, LANES)
        d_att = dot_nt(e_all[...], w_a[k, 3 * head_cols :, :]).astype(BF16)
        product = (d_att.astype(F32) * att_all[:, lane].astype(F32)).T
        inner = [
            jnp.sum(product[:64], axis=0, keepdims=True),
            jnp.sum(product[64:], axis=0, keepdims=True),
        ]
        key_sum[...] = jnp.zeros_like(key_sum)
        value_sum[...] = jnp.zeros_like(value_sum)
        k_turned = k_all[k].T
        for step in range(length // BLOCK):
            begin, keys = step * BLOCK, (step + 1) * BLOCK
            queries = two_heads(q_all[k, begin:keys, :])
            d_out = two_heads(d_att[begin:keys, :])
            scores = dot_nt(k_all[k, :keys, :], queries)
            log_total = jnp.concatenate(
                [lse_ref[k, 0:1, begin:keys], lse_ref[k, 1:2, begin:keys]], axis=1
            )
            chances = jnp.where(seen(first_ref, begin, keys), jnp.exp(scores - log_total), 0.0)
            d_chances = dot_nt(v_all[k, :keys, :], d_out)
            rest = jnp.concatenate([inner[0][:, begin:keys], inner[1][:, begin:keys]], axis=1)
            d_scores = (chances * (d_chances - rest)).astype(BF16)
            key_sum[:keys, :] += dot_nn(d_scores, queries)
            value_sum[:keys, :] += dot_nn(chances.astype(BF16), d_out)
            d_query = one_pair(dot_nn(k_turned[:, :keys], d_scores), BLOCK) * 0.125
            d_project[begin:keys, :LANES] = (
                d_query * cos_ref[begin:keys, :] - swap_halves(d_query) * sin_ref[begin:keys, :]
            ).astype(BF16)
        d_key = key_sum[...]
        d_project[:, LANES : 2 * LANES] = (
            d_key * cos_ref[...] - swap_halves(d_key) * sin_ref[...]
        ).astype(BF16)
        d_value = (0.5 * value_sum[...]).astype(BF16)
        d_project[:, 2 * LANES :] = d_value
        v_all[k] = d_value

        @pl.when(k > 0)
        def _():
            first_copy(k).start()

        @pl.when(k == 0)
        def _():
            keep(2, v_all.at[0], first_out).start()

        for n in range(2):
            at = pl.ds(n * strip, strip)
            d_in = dot_nn(d_project[at, :], w_a[k, : 3 * head_cols, :])

            @pl.when(i == 0)
            def _():
                acc_one[at, :] = d_in

            @pl.when(i > 0)
            def _():
                acc_one[at, :] += d_in

        w_a[k, : 3 * head_cols, :] = dot_tn(d_project[...], normed_all[...]).astype(BF16)
        w_a[k, 3 * head_cols :, :] = dot_tn(att_all[:, lane], e_all[...]).astype(BF16)
        launch("a", k)

        @pl.when(i == 0)
        def _():
            second("b", 0)
            third("b", 1, True)

        @pl.when(i == 1)
        def _():
            third("b", 0, False)
            second("a", 3)

        @pl.when(i == 2)
        def _():
            second("a", 2)
            third("a", 3, True)

        @pl.when(i == 3)
        def _():
            finish("b")
            second("a", 1)
            third("a", 2, True)

        return carry

    lax.fori_loop(0, slots, heads, 0)

    for copy in swap("block", delta_own, block_out):
        copy.wait_send()
    keep(0, delta_own.at[slot], block_out).wait()
    for p in range(slots):
        away_copy(0, p).wait_send()
        away[0, p] = acc_one[position(p, other), :].astype(BF16)
        remote(("again", p), away.at[0, p], back.at[0, p], place.device(rank=other)).start()
    for p in range(slots):
        value = x_own[p].astype(F32)
        inverse = lax.rsqrt(jnp.mean(value * value, axis=-1, keepdims=True) + EPSILON)
        normed = value * inverse
        remote(("again", p), away.at[0, p], back.at[0, p], place.device(rank=other)).wait_recv()
        d_normed = acc_one[position(p, place.rank), :] + back[0, p].astype(F32)
        gain_sum[0:1, :] += jnp.sum(normed * d_normed, axis=0, keepdims=True)
        delta = norm_back(d_normed * gains_ref[0:1, :], normed, inverse)
        delta_own[p] = ((middle[p] + delta) * live).astype(BF16)
    for copy in swap("input", delta_own, input_out):
        copy.start()
    keep(1, delta_own.at[slot], input_out).start()

    def gain_copies(level):
        if level == 0:
            return [
                remote(("gain", 0, d), gain_seq.at[place.seq], gain_seq.at[place.seq],
                       place.device(seq=place.at_seq(d)))
                for d in range(1, n_seq)
            ]
        if level == 1:
            return [
                remote(("gain", 1, j), gain_slot.at[slot], gain_slot.at[slot],
                       place.device(slot=place.at_slot(j)))
                for j in range(1, slots)
            ]
        return [
            remote(("gain", 2, 0), gain_rank.at[place.rank], gain_rank.at[place.rank],
                   place.device(rank=other))
        ]

    def gain_step(level):
        value = gain_sum[...]
        if level > 0:
            for copy in gain_copies(level - 1):
                copy.wait_recv()
            held = (gain_seq, gain_slot, gain_rank)[level - 1]
            value = held[0]
            for j in range(1, held.shape[0]):
                value = value + held[j]
        if level == 3:
            gains_out[...] = value
            return
        target = (gain_seq, gain_slot, gain_rank)[level]
        target[(place.seq, slot, place.rank)[level]] = value
        for copy in gain_copies(level):
            copy.start()

    gain_step(0)
    relay("b")
    second("a", 0)
    gain_step(1)
    third("a", 1, True)
    gain_step(2)
    third("a", 0, False)
    gain_step(3)
    finish("a")
    relay("a")
    for sec in ("b", "a"):
        near, far = gather_copies(sec)
        for copy in far:
            copy.wait_recv()
            copy.wait_send()
        for copy in near:
            copy.wait_send()
        own_copy(sec).wait()
        for k in range(slots):
            for copy in near_copies(sec, k) + next_copies(sec, k):
                copy.wait_send()
            if k > 0:
                far_copy(sec, k).wait_send()
    for copy in swap("block", delta_own, block_out):
        copy.wait_recv()
    for copy in swap("input", delta_own, input_out):
        copy.wait()
    for j in range(1, slots):
        source = place.at_slot(j)
        remote(None, v_all.at[0], first_out.at[source], elsewhere,
               first_sems.at[0, 0], first_sems.at[1, source]).wait_recv()
        first_copy(j).wait_send()
    for p in range(slots):
        away_copy(1, p).wait_send()
        remote(("again", p), away.at[0, p], back.at[0, p], place.device(rank=other)).wait_send()
        share(p).wait_send()
    for level in range(3):
        for copy in gain_copies(level):
            copy.wait_send()
    keep(1, delta_own.at[slot], input_out).wait()
    keep(2, v_all.at[0], first_out).wait()


def backward_part(n_seq, n_head, head_cols, saved, gains, tables, live):
    (
        x_own, h_one, q_rot, k_rot, v_mix, attended, log_total, weights_a, weights_b, middle, h_two,
        grad_own, e_all,
    ) = saved
    cos_wide, sin_wide, first_pos = tables
    slots, rows, width = x_own.shape
    length = h_one.shape[0]
    rows_a, rows_b = weights_a.shape[1], weights_b.shape[1]
    part = width // n_seq
    ranks = n_head // slots
    any_space = pl.BlockSpec(memory_space=pl.ANY)
    vmem = pl.BlockSpec(memory_space=pltpu.VMEM)
    shape = jax.ShapeDtypeStruct
    like = lambda value: pltpu.VMEM(value.shape, value.dtype)
    count = 2 * 4 + 2 * slots + slots + 2 * (slots - 1) + n_seq + slots + 4
    sem = pltpu.SemaphoreType.DMA
    return pl.pallas_call(
        functools.partial(backward_kernel, n_seq, n_head, head_cols),
        in_specs=[any_space] * 12 + [vmem] * 6,
        out_specs=[any_space] * 3 + [vmem] * 3 + [any_space] * 2,
        out_shape=[
            shape(x_own.shape, BF16),
            shape(x_own.shape, BF16),
            shape((slots, length, head_cols), BF16),
            shape((8, width), F32),
            shape((rows_a, part), BF16),
            shape((rows_b, part), BF16),
            shape((rows_a, width), BF16),
            shape((rows_b, width), BF16),
        ],
        scratch_shapes=[
            like(weights_a), like(weights_b), like(h_two), like(e_all), like(x_own), like(middle),
            like(grad_own),
            like(q_rot), like(k_rot), like(v_mix), like(attended),
            pltpu.VMEM((length, width), F32),
            pltpu.VMEM((length, width), F32),
            pltpu.VMEM((length, rows_b // 3), BF16),
            pltpu.VMEM((length, rows_b // 3), BF16),
            pltpu.VMEM((length, 3 * LANES), BF16),
            pltpu.VMEM((2, slots, rows, width), BF16),
            pltpu.VMEM((2, slots, rows, width), BF16),
            like(x_own),
            pltpu.VMEM((slots, 4, rows_a // 2, part), BF16),
            pltpu.VMEM((slots, 4, rows_b // 2, part), BF16),
            pltpu.VMEM((slots, 2, rows_a // 2, part), BF16),
            pltpu.VMEM((slots, 2, rows_b // 2, part), BF16),
            pltpu.VMEM((slots, rows_a, part), BF16),
            pltpu.VMEM((slots, rows_b, part), BF16),
            pltpu.VMEM((8, width), F32),
            pltpu.VMEM((n_seq, 8, width), F32),
            pltpu.VMEM((slots, 8, width), F32),
            pltpu.VMEM((ranks, 8, width), F32),
            sem((2, count)),
            sem((2, 2, slots, 4)),
            sem((2, 2, slots, 2)),
            sem((2, 2, slots)),
            sem((2, slots)),
            sem((slots + 11,)),
            sem((5,)),
        ],
        compiler_params=pltpu.CompilerParams(
            collective_id=2, has_side_effects=True, vmem_limit_bytes=64 << 20
        ),
    )(
        weights_a, weights_b, h_one, h_two, x_own, middle, grad_own, q_rot, k_rot, v_mix, attended,
        e_all, log_total, gains, cos_wide, sin_wide, first_pos[None, :], live,
    )


def reduce_kernel(
    n_seq, n_head, chunks,
    block_ref, input_ref, first_ref, gains_ref, grads_a, grads_b,
    block_out, input_out, first_out, gains_out, sum_a, sum_b, full_a, full_b,
    near_a, near_b, turn_a, turn_b, far_a, far_b, gain_seq, gain_slot, gain_rank,
    send_sems, recv_sems, own_sems, far_recv, first_recv,
):
    slots = block_ref.shape[0]
    place = Place(n_seq, n_head, slots)
    place.greet(True)
    sender = Sender(send_sems, recv_sems)
    part = sum_a.shape[1]
    mine = lanes(place.seq, part)
    order = [2, 3, 1, 0]
    parts = ((grads_b, sum_b, full_b, near_b, turn_b, far_b, chunks[1]),
             (grads_a, sum_a, full_a, near_a, turn_a, far_a, chunks[0]))
    copies, received = [], []

    def arrive(copy):
        copy.wait_recv()
        received.append(copy)

    def swap(src, dst):
        return [
            sender.start(
                src.at[place.at_slot(k)], dst.at[place.slot], place.device(slot=place.at_slot(k))
            )
            for k in (2, 3, 1)
        ]

    gain_seq[place.seq] = gains_ref[...]
    small = [
        sender.start(gain_seq.at[place.seq], gain_seq.at[place.seq],
                     place.device(seq=place.at_seq(d)))
        for d in range(1, n_seq)
    ]
    copies += small

    def to_seqs(grads, near, k):
        return [
            sender.start(
                grads.at[k, :, lanes(place.at_seq(d), part)],
                near.at[k, d - 1],
                place.device(seq=place.at_seq(d)),
            )
            for d in range(1, n_seq)
        ]

    sent = {}
    units = [(which, k) for which in range(2) for k in order]

    def launch(unit):
        which, k = unit
        sent[unit] = to_seqs(parts[which][0], parts[which][3], k)
        copies.extend(sent[unit])

    own = [
        pltpu.make_async_copy(src, dst.at[place.slot], own_sems.at[i])
        for i, (src, dst) in enumerate(
            (
                (block_ref.at[place.slot], block_out),
                (input_ref.at[place.slot], input_out),
                (first_ref.at[0], first_out),
            )
        )
    ]
    for copy in own:
        copy.start()
    launch(units[0])
    launch(units[1])
    copies += swap(block_ref, block_out)
    for copy in small:
        arrive(copy)
    total = gain_seq[0]
    for i in range(1, n_seq):
        total = total + gain_seq[i]
    gain_slot[place.slot] = total
    small = [
        sender.start(gain_slot.at[place.slot], gain_slot.at[place.slot],
                     place.device(slot=place.at_slot(k)))
        for k in range(1, slots)
    ]
    copies += small
    elsewhere = place.device(seq=place.at_seq(1))
    for index, unit in enumerate(units):
        which, k = unit
        grads, _, _, near, turn, far, chunk = parts[which]
        if index + 2 < len(units):
            launch(units[index + 2])
        for copy in sent[unit]:
            arrive(copy)

        def add(i, carry, grads=grads, near=near, turn=turn, k=k, chunk=chunk):
            rows = pl.ds(pl.multiple_of(i * chunk, chunk), chunk)
            value = grads[k, rows, mine].astype(F32)
            for d in range(n_seq - 1):
                value = value + near[k, d, rows, :].astype(F32)
            turn[k, rows, :] = value.astype(BF16)
            return carry

        lax.fori_loop(0, grads.shape[1] // chunk, add, 0)
        if k != 0:
            copy = sender.start(
                turn.at[k], far.at[place.slot], place.device(slot=place.source(k)),
                far_recv.at[which, place.slot],
            )
            copies.append(copy)
            received.append(copy)
        if index == 1:
            for j in range(1, slots):
                copy = sender.start(
                    first_ref.at[j], first_out.at[place.slot],
                    place.device(slot=place.source(j)), first_recv.at[place.slot],
                )
                copies.append(copy)
                received.append(copy)
        if index == 4:
            copies += swap(input_ref, input_out)
            for copy in small:
                arrive(copy)
            total = gain_slot[0]
            for i in range(1, slots):
                total = total + gain_slot[i]
            gain_rank[place.rank] = total
            small = [
                sender.start(gain_rank.at[place.rank], gain_rank.at[place.rank],
                             place.device(rank=(place.rank + j) % place.ranks))
                for j in range(1, place.ranks)
            ]
            copies += small
        if k == 0:
            for j in range(1, slots):
                source = place.at_slot(j)
                pltpu.make_async_remote_copy(
                    src_ref=turn.at[0], dst_ref=far.at[source], send_sem=send_sems.at[0],
                    recv_sem=far_recv.at[which, source], device_id=elsewhere, device_id_type=MESH,
                ).wait_recv()
            _, total_ref, full, _, _, _, _ = parts[which]

            def finish(i, carry, turn=turn, far=far, total_ref=total_ref, full=full, chunk=chunk):
                rows = pl.ds(pl.multiple_of(i * chunk, chunk), chunk)
                value = turn[0, rows, :].astype(F32)
                for j in range(1, slots):
                    value = value + far[place.at_slot(j), rows, :].astype(F32)
                value = value.astype(BF16)
                total_ref[rows, :] = value
                full[rows, mine] = value
                return carry

            lax.fori_loop(0, grads.shape[1] // chunk, finish, 0)
            copies += [
                sender.start(total_ref, full.at[:, mine], place.device(seq=place.at_seq(d)))
                for d in range(1, n_seq)
            ]
    for copy in small:
        arrive(copy)
    total = gain_rank[0]
    for i in range(1, place.ranks):
        total = total + gain_rank[i]
    gains_out[...] = total
    for copy in copies:
        if all(copy is not other for other in received):
            copy.wait_recv()
    for j in range(1, slots):
        source = place.at_slot(j)
        pltpu.make_async_remote_copy(
            src_ref=first_ref.at[0], dst_ref=first_out.at[source], send_sem=send_sems.at[0],
            recv_sem=first_recv.at[source], device_id=elsewhere, device_id_type=MESH,
        ).wait_recv()
    for copy in copies:
        copy.wait_send()
    for copy in own:
        copy.wait()


def reduce_grads(n_seq, n_head, chunks, block_delta, input_delta, first_delta, gains, grads_a, grads_b):
    slots = block_delta.shape[0]
    part = grads_a.shape[2] // n_seq
    rows = (grads_a.shape[1], grads_b.shape[1])
    ranks = n_head // slots
    count = (
        3 * (slots - 1) + 2 * (slots * (n_seq - 1) + (slots - 1) + (n_seq - 1))
        + (n_seq - 1) + (slots - 1) + (ranks - 1)
    )
    any_space = pl.BlockSpec(memory_space=pl.ANY)
    vmem = pl.BlockSpec(memory_space=pltpu.VMEM)
    like = lambda value: jax.ShapeDtypeStruct(value.shape, value.dtype)
    return pl.pallas_call(
        functools.partial(reduce_kernel, n_seq, n_head, chunks),
        in_specs=[any_space] * 3 + [vmem] * 3,
        out_specs=[any_space] * 3 + [vmem] * 5,
        out_shape=[like(block_delta), like(input_delta), like(first_delta), like(gains)]
        + [jax.ShapeDtypeStruct((r, part), BF16) for r in rows]
        + [jax.ShapeDtypeStruct((r, part * n_seq), BF16) for r in rows],
        scratch_shapes=[pltpu.VMEM((slots, n_seq - 1, r, part), BF16) for r in rows]
        + [pltpu.VMEM((slots, r, part), BF16) for r in rows]
        + [pltpu.VMEM((slots, r, part), BF16) for r in rows]
        + [pltpu.VMEM((n,) + gains.shape, F32) for n in (n_seq, slots, ranks)]
        + [
            pltpu.SemaphoreType.DMA((count,)),
            pltpu.SemaphoreType.DMA((count,)),
            pltpu.SemaphoreType.DMA((3,)),
            pltpu.SemaphoreType.DMA((2, slots)),
            pltpu.SemaphoreType.DMA((slots,)),
        ],
        compiler_params=pltpu.CompilerParams(
            collective_id=1, has_side_effects=True, vmem_limit_bytes=56 << 20
        ),
    )(block_delta, input_delta, first_delta, gains, grads_a, grads_b)


def shampoo_kernel(
    stat_ref, root_ref, head_stat, head_root, unit_stat, unit_root, full_a, sum_a, full_b, sum_b,
    wide_ref, out_right_ref, new_head, new_unit, step_a, step_b,
):
    step = pl.program_id(0)
    blocks = stat_ref.shape[1]

    def one(member, width, small_stat, small_root, full, total, big_out, small_out, step_out):
        for b in range(blocks):
            rows = pl.ds(pl.multiple_of((member * blocks + b) * width, 16), width)
            grad, own = full[rows, :], total[rows, :]
            big_out[0, b] = STAT_DECAY * stat_ref[0, b] + (1.0 - STAT_DECAY) * dot_tn(own, grad)
            small_out[member, b] = STAT_DECAY * small_stat[member, b] + (
                1.0 - STAT_DECAY
            ) * dot_nt(grad, grad)
            turned = dot_nn(small_root[member, b].astype(BF16), grad).astype(BF16)
            turned = dot_nt(turned, root_ref[0, b].astype(BF16))
            scale = lax.rsqrt(jnp.mean(turned * turned, axis=0, keepdims=True) + EPSILON)
            step_out[rows, :] = turned * scale

    head_width, unit_width = head_stat.shape[2], unit_stat.shape[2]
    head_args = (head_width, head_stat, head_root, full_a, sum_a)
    unit_args = (unit_width, unit_stat, unit_root, full_b, sum_b)

    @pl.when(step < 3)
    def _():
        one(step, *head_args, wide_ref, new_head, step_a)

    @pl.when((step >= 3) & (step < 6))
    def _():
        one(step - 3, *unit_args, wide_ref, new_unit, step_b)

    @pl.when(step == 6)
    def _():
        one(3, *head_args, out_right_ref, new_head, step_a)


def shampoo(stats_wide, roots_wide, stats_head, roots_head, stats_unit, roots_unit, full_a, sum_a, full_b, sum_b):
    members, blocks, part, width = stats_wide.shape
    member = lambda i: (jnp.where(i == 5, 6, jnp.where(i == 6, 5, i)), 0, 0, 0)
    wide = pl.BlockSpec((1, blocks, part, width), member)
    vmem = pl.BlockSpec(memory_space=pltpu.VMEM)
    return pl.pallas_call(
        shampoo_kernel,
        grid=(members,),
        in_specs=[wide, wide] + [vmem] * 8,
        out_specs=[
            pl.BlockSpec((1, blocks, part, width), lambda i: (jnp.minimum(i, 5), 0, 0, 0)),
            pl.BlockSpec((1, blocks, part, width), lambda i: (0, 0, 0, 0)),
            vmem, vmem, vmem, vmem,
        ],
        out_shape=[
            jax.ShapeDtypeStruct((members - 1, blocks, part, width), F32),
            jax.ShapeDtypeStruct((1, blocks, part, width), F32),
            jax.ShapeDtypeStruct(stats_head.shape, F32),
            jax.ShapeDtypeStruct(stats_unit.shape, F32),
            jax.ShapeDtypeStruct(sum_a.shape, F32),
            jax.ShapeDtypeStruct(sum_b.shape, F32),
        ],
        compiler_params=pltpu.CompilerParams(vmem_limit_bytes=48 << 20),
    )(stats_wide, roots_wide, stats_head, roots_head, stats_unit, roots_unit, full_a, sum_a, full_b, sum_b)


class Links:
    def __init__(self, n_seq, n_head, slots):
        self.n_seq, self.n_head, self.slots = n_seq, n_head, slots
        self.ranks = n_head // slots
        self.slot = lax.axis_index("head") // self.ranks
        self.rank = lax.axis_index("head") % self.ranks

    def permute(self, value, partner):
        pairs = []
        for s in range(self.n_seq):
            for h in range(self.n_head):
                to_s, to_h = partner(s, h)
                pairs.append((s * self.n_head + h, to_s * self.n_head + to_h))
        return lax.ppermute(value, AXES, pairs)

    def swap_slots(self, value):
        got = [lax.dynamic_index_in_dim(value, self.slot, 0, keepdims=False)]
        for step in range(1, self.slots):
            piece = lax.dynamic_index_in_dim(value, self.slot ^ step, 0, keepdims=False)
            got.append(self.permute(piece, lambda s, h: (s, h ^ (step * self.ranks))))
        got = jnp.stack(got)
        return jnp.stack(
            [lax.dynamic_index_in_dim(got, self.slot ^ q, 0, keepdims=False) for q in range(self.slots)]
        )

    def gather_ranks(self, value):
        got = [value] + [
            self.permute(value, lambda s, h: (s, h ^ step)) for step in range(1, self.ranks)
        ]
        got = jnp.stack(got)
        return jnp.stack(
            [lax.dynamic_index_in_dim(got, self.rank ^ r, 0, keepdims=False) for r in range(self.ranks)]
        )

    def sum_ranks(self, value):
        total = lax.dynamic_index_in_dim(value, self.rank, 0, keepdims=False)
        for step in range(1, self.ranks):
            piece = lax.dynamic_index_in_dim(value, self.rank ^ step, 0, keepdims=False)
            got = self.permute(piece.astype(BF16), lambda s, h: (s, h ^ step))
            total = total + got.astype(F32)
        return total

    def whole_sequence(self, own):
        both = self.gather_ranks(own)
        return jnp.swapaxes(both, 0, 1).reshape(-1, own.shape[-1])

    def own_sum(self, full):
        rows = full.shape[0] // (self.slots * self.ranks)
        parts = full.reshape(self.slots, self.ranks, rows, full.shape[-1])
        return self.sum_ranks(jnp.swapaxes(parts, 0, 1)).reshape(-1, full.shape[-1])


def backward_plain(n_seq, n_head, head_cols, ffn_cols, links, saved, gains, tables, is_live):
    (
        x_bf16, h_one, q_rot, k_rot, v_mix, attended, log_total, weights_a, weights_b, middle,
        h_two, grad_own, d_ffn,
    ) = saved
    cos_wide, sin_wide, first_pos = tables
    slots, rows, width = x_bf16.shape
    length = h_one.shape[0]
    rows_a, rows_b = weights_a.shape[1], weights_b.shape[1]
    pairs = slots * head_cols // LANES
    per = LANES // head_cols

    def pair_major(value):
        n = value.shape[2]
        value = value.reshape(pairs, per, length, n, head_cols)
        return value.transpose(0, 2, 3, 1, 4).reshape(pairs, length, n, LANES)

    def slot_major(value):
        n = value.shape[2]
        value = value.reshape(pairs, length, n, per, head_cols)
        return value.transpose(0, 3, 1, 2, 4).reshape(slots, length, n, head_cols)

    w_in, w_o = weights_a[:, : 3 * head_cols], weights_a[:, 3 * head_cols :]
    w_gu, w_d = weights_b[:, : 2 * ffn_cols], weights_b[:, 2 * ffn_cols :]
    x_own = x_bf16.reshape(slots * rows, width).astype(F32)
    middle = middle.reshape(slots * rows, width)
    ein = functools.partial(jnp.einsum, preferred_element_type=F32)
    inverse_one = lax.rsqrt(jnp.mean(x_own * x_own, axis=-1, keepdims=True) + EPSILON)
    normed_one = x_own * inverse_one
    inverse_two = lax.rsqrt(jnp.mean(middle * middle, axis=-1, keepdims=True) + EPSILON)
    normed_two = middle * inverse_two
    saved = (q_rot, k_rot, v_mix, attended, log_total)
    attended = jnp.swapaxes(attended.reshape(length, slots, head_cols), 0, 1)
    gate_up = ein("ld,qfd->qlf", h_two, w_gu)
    gate, up = gate_up[..., :ffn_cols], gate_up[..., ffn_cols:]
    sigmoid_gate = jax.nn.sigmoid(gate)
    activated = gate * sigmoid_gate
    hidden = (activated * up).astype(BF16)
    ffn_out = links.own_sum(ein("qlf,qfd->ld", hidden, w_d))
    block_delta = jnp.where(is_live, middle - x_own + ffn_out, 0.0).astype(BF16)

    d_own = jnp.where(is_live, grad_own, jnp.zeros_like(grad_own))
    d_out = d_own.reshape(slots * rows, width).astype(F32)
    g_down = ein("qlf,ld->qfd", hidden, d_ffn)
    d_hidden = ein("ld,qfd->qlf", d_ffn, w_d)
    d_gate = (
        d_hidden * up * sigmoid_gate * (1.0 + gate * (1.0 - sigmoid_gate))
    ).astype(BF16)
    d_up = (d_hidden * activated).astype(BF16)
    d_gate_up = jnp.concatenate([d_gate, d_up], axis=2)
    d_normed_two = links.own_sum(ein("qlf,qfd->ld", d_gate_up, w_gu))
    g_gate_up = ein("qlf,ld->qfd", d_gate_up, h_two)
    grads_b = jnp.concatenate([g_gate_up.astype(BF16), g_down.astype(BF16)], axis=1)
    gain_two = jnp.sum(normed_two * d_normed_two, axis=0)
    middle_delta = norm_back(d_normed_two * gains[1], normed_two, inverse_two)
    d_middle = d_out + middle_delta
    d_attn = links.whole_sequence(d_middle.astype(BF16).reshape(slots, rows, width))
    d_attended = ein("ld,qcd->qlc", d_attn, w_o).astype(BF16)
    if per > 1:
        d_attended = pair_major(d_attended[:, :, None])[:, :, 0]
    d_project = jnp.concatenate(
        attend_back(saved, d_attended, cos_wide, sin_wide, first_pos), axis=2
    )
    if per > 1:
        d_project = slot_major(d_project.reshape(pairs, length, 3, LANES)).reshape(
            slots, length, 3 * head_cols
        )
    d_value = d_project[:, :, 2 * head_cols :]
    g_out = ein("qlc,ld->qcd", attended, d_attn)
    g_qkv = ein("qlc,ld->qcd", d_project, h_one)
    grads_a = jnp.concatenate([g_qkv.astype(BF16), g_out.astype(BF16)], axis=1)
    d_normed_one = links.own_sum(ein("qlc,qcd->ld", d_project, w_in))
    gain_one = jnp.sum(normed_one * d_normed_one, axis=0)
    input_delta = middle_delta + norm_back(d_normed_one * gains[0], normed_one, inverse_one)
    input_delta = jnp.where(is_live, input_delta, 0.0).astype(BF16)
    gain_rows = jnp.concatenate([gain_one.reshape(8, -1), gain_two.reshape(8, -1)], axis=0)

    return reduce_grads(
        n_seq,
        n_head,
        (LANES, unit_chunk(rows_b)),
        block_delta.reshape(slots, rows, width),
        input_delta.reshape(slots, rows, width),
        d_value,
        gain_rows,
        grads_a,
        grads_b,
    )


def shards(
    n_seq,
    n_head,
    layer_input,
    values_first,
    w_qkv,
    w_gate_up,
    w_out,
    w_down,
    norm_gains,
    out_grad,
    segments,
    counts,
    stats_wide,
    roots_wide,
    stats_head,
    roots_head,
    stats_unit,
    roots_unit,
):
    slots, rows, width = layer_input.shape
    length = segments.shape[1]
    row_part, head_cols, ffn_cols = w_qkv.shape[1], w_qkv.shape[2], w_gate_up.shape[2]
    head_dim = stats_head.shape[2]
    links = Links(n_seq, n_head, slots)
    is_live = links.slot < counts[0]
    pairs = slots * head_cols // LANES
    per = LANES // head_cols
    rows_a, rows_b = 4 * head_cols, 3 * ffn_cols

    weight_rows = jnp.concatenate(
        [
            jnp.swapaxes(w_qkv.astype(BF16), 1, 2).reshape(3 * head_cols, row_part),
            w_out.astype(BF16),
            jnp.swapaxes(w_gate_up.astype(BF16), 1, 2).reshape(2 * ffn_cols, row_part),
            w_down.astype(BF16),
        ],
        axis=0,
    )
    segment_ids = lax.dynamic_index_in_dim(segments, links.slot, 0, keepdims=False)
    first_pos, cos_wide, sin_wide = position_tables(segment_ids, head_dim)
    live = jnp.full((1, width), is_live, F32)
    saved = forward_part(
        n_seq, n_head, head_cols, layer_input, values_first, weight_rows, out_grad, norm_gains,
        cos_wide, sin_wide, first_pos, live,
    )
    tables = (cos_wide, sin_wide, first_pos)
    if n_seq == 4 and slots == 4 and links.ranks == 2 and per == 1:
        block_got, input_got, first_got, gains, sum_a, sum_b, full_a, full_b = backward_part(
            n_seq, n_head, head_cols, saved, norm_gains, tables, live
        )
        gains = gains[:2]
    else:
        block_got, input_got, first_got, gains, sum_a, sum_b, full_a, full_b = backward_plain(
            n_seq, n_head, head_cols, ffn_cols, links, saved, norm_gains, tables, is_live
        )
        gains = gains.reshape(2, width)
    block_out = layer_input.astype(F32) + block_got.astype(F32)
    input_grad = out_grad.astype(F32) + input_got.astype(F32)
    first_grad = first_got.astype(F32)
    grad_gains = gains
    new_gains = norm_gains - GAIN_RATE * grad_gains * lax.rsqrt(
        jnp.mean(grad_gains * grad_gains, axis=-1, keepdims=True) + EPSILON
    )

    wide, out_right, new_head, new_unit, step_a, step_b = shampoo(
        stats_wide, roots_wide, stats_head, roots_head, stats_unit, roots_unit,
        full_a, sum_a, full_b, sum_b,
    )
    cut = 3 * head_cols
    turned = lambda value, n: jnp.swapaxes(value.reshape(n, -1, row_part), 1, 2)
    return (
        block_out,
        input_grad,
        first_grad,
        turned(sum_a[:cut], 3).astype(F32),
        turned(sum_b[: 2 * ffn_cols], 2).astype(F32),
        sum_a[cut:].astype(F32),
        sum_b[2 * ffn_cols :].astype(F32),
        grad_gains,
        w_qkv - STEP_RATE * turned(step_a[:cut], 3),
        w_gate_up - STEP_RATE * turned(step_b[: 2 * ffn_cols], 2),
        w_out - OUT_RATE * step_a[cut:],
        w_down - STEP_RATE * step_b[2 * ffn_cols :],
        new_gains,
        wide,
        out_right[0],
        new_head,
        new_unit,
    )


def unit_chunk(rows):
    return max(c for c in range(16, 177, 16) if rows % c == 0)


def solution(mesh):
    return jax.shard_map(
        functools.partial(shards, mesh.shape["seq"], mesh.shape["head"]),
        mesh=mesh,
        in_specs=(
            P("seq", "head", None),
            P("seq", None, "head"),
            P(None, "seq", "head"),
            P(None, "seq", "head"),
            P("head", "seq"),
            P("head", "seq"),
            P(),
            P("seq", "head", None),
            P("seq", None),
            P("seq"),
            P(None, "head", "seq", None),
            P(None, "head", "seq", None),
            P(None, "head", None, None),
            P(None, "head", None, None),
            P(None, "head", None, None),
            P(None, "head", None, None),
        ),
        out_specs=(
            P("seq", "head", None),
            P("seq", "head", None),
            P("seq", None, "head"),
            P(None, "seq", "head"),
            P(None, "seq", "head"),
            P("head", "seq"),
            P("head", "seq"),
            P(),
            P(None, "seq", "head"),
            P(None, "seq", "head"),
            P("head", "seq"),
            P("head", "seq"),
            P(),
            P(None, "head", "seq", None),
            P("head", "seq", None),
            P(None, "head", None, None),
            P(None, "head", None, None),
        ),
        check_vma=False,
    )
```

```python
import functools

import jax
import jax.numpy as jnp
from jax import lax
from jax.experimental import pallas as pl
from jax.experimental.pallas import tpu as pltpu
from jax.sharding import PartitionSpec as P

EPSILON = 1e-06
STAT_DECAY = 0.5
STEP_RATE = 0.02
OUT_RATE = 0.1
GAIN_RATE = 0.25
AXES = ("seq", "head")
MESH = pl.DeviceIdType.MESH
LANES = 128
BLOCK = 128
BF16 = jnp.bfloat16
F32 = jnp.float32


def dot_nt(matrix_a, matrix_b):
    return lax.dot_general(
        matrix_a, matrix_b, (((1,), (1,)), ((), ())), preferred_element_type=F32
    )


def dot_tn(matrix_a, matrix_b):
    return lax.dot_general(
        matrix_a, matrix_b, (((0,), (0,)), ((), ())), preferred_element_type=F32
    )


def dot_nn(matrix_a, matrix_b):
    return jnp.dot(matrix_a, matrix_b, preferred_element_type=F32)


def norm_back(d_normed, normed, inverse):
    return inverse * (d_normed - normed * jnp.mean(d_normed * normed, axis=-1, keepdims=True))


def position_tables(segment_ids, head_dim):
    length = segment_ids.shape[0]
    position = jnp.arange(length, dtype=jnp.int32)
    opens = jnp.concatenate([jnp.ones((1,), dtype=bool), segment_ids[1:] != segment_ids[:-1]])
    first_pos = lax.cummax(jnp.where(opens, position, 0), axis=0)
    offset = (position - first_pos).astype(F32)
    half_width = head_dim // 2
    frequency = jnp.exp(-jnp.log(10000.0) * jnp.arange(half_width, dtype=F32) / half_width)
    angle = offset[:, None] * frequency[None, :]
    cosine, sine_part = jnp.cos(angle), jnp.sin(angle)
    per_lane = LANES // head_dim
    cos_wide = jnp.concatenate([cosine, cosine] * per_lane, axis=1)
    sin_wide = jnp.concatenate([-sine_part, sine_part] * per_lane, axis=1)
    return first_pos, cos_wide, sin_wide


def swap_halves(values):
    lane = lax.broadcasted_iota(jnp.int32, values.shape, 1)
    return jnp.where((lane & 32) == 0, pltpu.roll(values, 96, 1), pltpu.roll(values, 32, 1))


def two_heads(block):
    lane = lax.broadcasted_iota(jnp.int32, block.shape, 1)
    zero = jnp.zeros_like(block)
    return jnp.concatenate(
        [jnp.where(lane < 64, block, zero), jnp.where(lane >= 64, block, zero)], axis=0
    )


def one_pair(transposed, width):
    kept = jnp.concatenate([transposed[:64, :width], transposed[64:, width:]], axis=0)
    return kept.T


def first_key(begin, length):
    return max(0, (begin - length // 2 + 1) // BLOCK * BLOCK)


def seen(first_ref, begin, low, key_count):
    first = first_ref[0:1, begin : begin + BLOCK]
    query = begin + lax.broadcasted_iota(jnp.int32, (1, BLOCK), 1)
    first = jnp.concatenate([first, first], axis=1)
    query = jnp.concatenate([query, query], axis=1)
    key = low + lax.broadcasted_iota(jnp.int32, (key_count, 2 * BLOCK), 0)
    return (key >= first) & (key <= query)


def attend_back_kernel(
    qr_ref, kr_ref, vm_ref, att_ref, d_ref, lse_ref, cos_ref, sin_ref, first_ref,
    dq_ref, dk_ref, dv_ref, key_sum, value_sum,
):
    length = qr_ref.shape[1]
    key_sum[...] = jnp.zeros_like(key_sum)
    value_sum[...] = jnp.zeros_like(value_sum)
    k_turned = kr_ref[0].T
    cosine, sine_part = cos_ref[...], sin_ref[...]
    product = (d_ref[0].astype(F32) * att_ref[...].astype(F32)).T
    inner = [
        jnp.sum(product[:64], axis=0, keepdims=True),
        jnp.sum(product[64:], axis=0, keepdims=True),
    ]
    for step in range(length // BLOCK):
        begin, keys = step * BLOCK, (step + 1) * BLOCK
        low = first_key(begin, length)
        queries = two_heads(qr_ref[0, begin:keys, :])
        d_out = two_heads(d_ref[0, begin:keys, :])
        scores = dot_nt(kr_ref[0, low:keys, :], queries)
        log_total = jnp.concatenate(
            [lse_ref[0, 0:1, begin:keys], lse_ref[0, 1:2, begin:keys]], axis=1
        )
        chances = jnp.where(seen(first_ref, begin, low, keys - low), jnp.exp(scores - log_total), 0.0)
        d_chances = dot_nt(vm_ref[0, low:keys, :], d_out)
        part = jnp.concatenate([inner[0][:, begin:keys], inner[1][:, begin:keys]], axis=1)
        d_scores = (chances * (d_chances - part)).astype(BF16)
        key_sum[low:keys, :] += dot_nn(d_scores, queries)
        value_sum[low:keys, :] += dot_nn(chances.astype(BF16), d_out)
        d_query = one_pair(dot_nn(k_turned[:, low:keys], d_scores), BLOCK) * 0.125
        dq_ref[0, begin:keys, :] = (
            d_query * cosine[begin:keys] - swap_halves(d_query) * sine_part[begin:keys]
        ).astype(BF16)
    d_key = key_sum[...]
    dk_ref[0] = (d_key * cosine - swap_halves(d_key) * sine_part).astype(BF16)
    dv_ref[0] = (0.5 * value_sum[...]).astype(BF16)


def attend_back(saved, d_attended, cos_wide, sin_wide, first_pos):
    q_rot, k_rot, v_mix, attended, log_total = saved
    pairs, length, _ = q_rot.shape
    part = pl.BlockSpec((1, length, LANES), lambda p: (p, 0, 0))
    table = pl.BlockSpec((length, LANES), lambda p: (0, 0))
    out = jax.ShapeDtypeStruct((pairs, length, LANES), BF16)
    return pl.pallas_call(
        attend_back_kernel,
        grid=(pairs,),
        in_specs=[part] * 3 + [pl.BlockSpec((length, LANES), lambda p: (0, p)), part,
                               pl.BlockSpec((1, 2, length), lambda p: (p, 0, 0)), table, table,
                               pl.BlockSpec((1, length), lambda p: (0, 0))],
        out_specs=[part] * 3,
        out_shape=[out] * 3,
        scratch_shapes=[pltpu.VMEM((length, LANES), F32)] * 2,
        compiler_params=pltpu.CompilerParams(vmem_limit_bytes=48 << 20),
        cost_estimate=pl.CostEstimate(
            flops=pairs * length * length * 128 * 20, bytes_accessed=pairs * length * 128 * 24,
            transcendentals=pairs * length * length),
    )(q_rot, k_rot, v_mix, attended, d_attended, log_total, cos_wide, sin_wide, first_pos[None, :])


class Place:
    def __init__(self, n_seq, n_head, slots):
        self.n_seq, self.slots, self.ranks = n_seq, slots, n_head // slots
        self.seq = lax.axis_index("seq")
        head = lax.axis_index("head")
        self.slot, self.rank = head // self.ranks, head % self.ranks

    def at_slot(self, step):
        return (self.slot + step + self.slots) % self.slots

    def at_seq(self, step):
        return (self.seq + step + self.n_seq) % self.n_seq

    @property
    def line(self):
        return self.slots == 4 and self.n_seq == 4

    def source(self, step):
        if not self.line:
            return self.at_slot(-step)
        upper = self.slot // 2
        inner = (self.slot + upper) % 2
        near = step + inner * (1 - 2 * step) * (1 - step // 2)
        return near + upper * (3 - 2 * near)

    @property
    def beside(self):
        return self.seq + 1 - 2 * (self.seq % 2)

    @property
    def across(self):
        return self.seq + 2 - 4 * (self.seq // 2)

    def device(self, seq=None, slot=None, rank=None):
        seq = self.seq if seq is None else seq
        slot = self.slot if slot is None else slot
        rank = self.rank if rank is None else rank
        return (seq, slot * self.ranks + rank)

    def greet(self, with_ranks):
        others = [self.device(slot=self.at_slot(k)) for k in range(1, self.slots)]
        others += [self.device(seq=self.at_seq(d)) for d in range(1, self.n_seq)]
        if with_ranks:
            others += [
                self.device(rank=(self.rank + j) % self.ranks) for j in range(1, self.ranks)
            ]
        barrier = pltpu.get_barrier_semaphore()
        for other in others:
            pl.semaphore_signal(barrier, inc=1, device_id=other, device_id_type=MESH)
        pl.semaphore_wait(barrier, len(others))


class Sender:
    def __init__(self, send_sems, recv_sems):
        self.send_sems, self.recv_sems, self.used = send_sems, recv_sems, 0

    def start(self, src, dst, device, recv=None):
        copy = pltpu.make_async_remote_copy(
            src_ref=src,
            dst_ref=dst,
            send_sem=self.send_sems.at[self.used],
            recv_sem=self.recv_sems.at[self.used] if recv is None else recv,
            device_id=device,
            device_id_type=MESH,
        )
        self.used += 1
        copy.start()
        return copy


def lanes(index, width):
    return pl.ds(pl.multiple_of(index * width, width), width)


def forward_kernel(
    n_seq, n_head, head_cols, early,
    x_ref, vf_ref, wt_ref, g_ref, gains_ref, cos_ref, sin_ref, first_ref, live_ref,
    x_res, h_one_res, q_res, k_res, v_res, att_res, lse_out, w_a_res, w_b_res, middle_res, h_two_res, g_res, e_res,
    ffn_res, x_out, h_one, q_out, k_out, v_out, att_out, w_a, middle, h_two, g_out, e_all,
    vf_all, away, back, w_b, ffn, sems, z_recv, v_recv, own_sems, res_sems,
):
    slots, rows, width = x_ref.shape
    part = wt_ref.shape[1]
    rows_a = w_a.shape[1]
    place = Place(n_seq, n_head, slots)
    ranks = place.ranks
    length = slots * ranks * rows
    per = LANES // head_cols
    pairs = slots // per
    mine = lanes(place.seq, part)
    sections = {"a": (w_a, pl.ds(0, rows_a)), "b": (w_b, pl.ds(rows_a, wt_ref.shape[0] - rows_a))}
    ids = {}
    elsewhere = place.device(seq=place.at_seq(1))

    def index(name):
        return ids.setdefault(name, len(ids))

    def remote(name, src, dst, device, recv=None):
        i = index(name)
        return pltpu.make_async_remote_copy(
            src_ref=src, dst_ref=dst, send_sem=sems.at[0, i],
            recv_sem=sems.at[1, i] if recv is None else recv,
            device_id=device, device_id_type=MESH,
        )

    def x_copy(k):
        to = place.at_slot(k)
        return remote(("x", k), x_ref.at[to], x_out.at[place.slot], place.device(slot=to))

    def g_copy(k):
        to = place.at_slot(k)
        return remote(("g", k), g_ref.at[to], g_out.at[place.slot], place.device(slot=to))

    def v_copy(k):
        to = place.source(k) if place.line else place.at_slot(k)
        return remote(("v", k), vf_ref.at[to], vf_all.at[place.slot], place.device(slot=to),
                      v_recv.at[place.slot])

    def v_wait(source):
        pltpu.make_async_remote_copy(
            src_ref=vf_ref.at[0], dst_ref=vf_all.at[source], send_sem=sems.at[0, 0],
            recv_sem=v_recv.at[source], device_id=elsewhere, device_id_type=MESH,
        ).wait_recv()

    def piece(sec, step):
        ref, at = sections[sec]
        return wt_ref.at[at] if step == 0 else ref.at[step, :, mine]

    def z_copy(name, sec, step, to, to_step):
        ref, _ = sections[sec]
        which = 0 if sec == "a" else 1
        return remote((name, sec, step), piece(sec, step), ref.at[to_step, :, mine],
                      place.device(slot=to), z_recv.at[which, to_step])

    def z_wait(sec, step):
        ref, _ = sections[sec]
        which = 0 if sec == "a" else 1
        pltpu.make_async_remote_copy(
            src_ref=piece(sec, 0), dst_ref=ref.at[step, :, mine], send_sem=sems.at[0, 0],
            recv_sem=z_recv.at[which, step], device_id=elsewhere, device_id_type=MESH,
        ).wait_recv()

    slot = place.slot
    upper = slot // 2
    inner = (slot + upper) % 2

    def z_start_own(sec):
        if not place.line:
            for k in range(1, slots):
                z_copy(("z", k), sec, 0, place.at_slot(k), k).start()
            return
        @pl.when(slot < 3)
        def _():
            to = slot + 1
            z_copy("up", sec, 0, to, 1 + (to == 2).astype(jnp.int32)).start()

        @pl.when(slot > 0)
        def _():
            to = slot - 1
            z_copy("down", sec, 0, to, 1 + (to == 1).astype(jnp.int32)).start()

    def z_own_sends(sec):
        if not place.line:
            for k in range(1, slots):
                z_copy(("z", k), sec, 0, place.at_slot(k), k).wait_send()
            return

        @pl.when(slot < 3)
        def _():
            z_copy("up", sec, 0, slot + 1, 1).wait_send()

        @pl.when(slot > 0)
        def _():
            z_copy("down", sec, 0, slot - 1, 1).wait_send()

    def z_relay(sec, step):
        if step == 1:
            return z_copy("on", sec, step, slot + 1 - 2 * upper, 3)
        return z_copy("on", sec, step, slot - 1 + 2 * upper, step)

    def near_copy(sec, step):
        ref, _ = sections[sec]
        dst = ref.at[step, :, mine]
        if not place.line:
            return [
                remote(("xy", d, sec, step), piece(sec, step), dst, place.device(seq=place.at_seq(d)))
                for d in range(1, n_seq)
            ]
        return [
            remote(("xy", 0, sec, step), piece(sec, step), dst, place.device(seq=place.beside)),
            remote(("xy", 1, sec, step), piece(sec, step), dst, place.device(seq=place.across)),
        ]

    def far_copy(sec, step, which):
        ref, at = sections[sec]
        half = at.size // 2
        cut = pl.ds(which * half, half)
        source = place.beside if which == 0 else place.across
        to = place.across if which == 0 else place.beside
        where = ref.at[step, cut, lanes(source, part)]
        return remote(("far", which, sec, step), where, where, place.device(seq=to))

    def z_event(sec, step):
        z_wait(sec, step)
        if place.line:
            @pl.when(inner == 1)
            def _():
                z_relay(sec, step).start()
        for copy in near_copy(sec, step):
            copy.start()

    def xy_event(sec, step):
        for which, copy in enumerate(near_copy(sec, step)):
            copy.wait_recv()
            if place.line:
                far_copy(sec, step, which).start()

    def done_event(sec, step):
        if place.line:
            for which in range(2):
                far_copy(sec, step, which).wait_recv()

    def position(p, rank):
        return pl.ds(pl.multiple_of((p * ranks + rank) * rows, rows), rows)

    def share(name, ref, p, j):
        where = ref.at[position(p, place.rank), :]
        return remote((name, p, j), where, where, place.device(rank=(place.rank + j) % ranks))

    results = {
        "x": (x_out, x_res), "h1": (h_one, h_one_res), "q": (q_out, q_res), "k": (k_out, k_res),
        "v": (v_out, v_res), "att": (att_out, att_res), "a": (w_a, w_a_res),
        "mid": (middle, middle_res), "h2": (h_two, h_two_res), "g": (g_out, g_res),
        "e": (e_all, e_res), "ffn": (ffn, ffn_res),
    }
    for step in range(slots):
        results["b", step] = (w_b.at[step], w_b_res.at[step])

    def result(name):
        src, dst = results[name]
        return pltpu.make_async_copy(src, dst, res_sems.at[list(results).index(name)])

    place.greet(True)
    own = [
        pltpu.make_async_copy(x_ref.at[slot], x_out.at[slot], own_sems.at[0]),
        pltpu.make_async_copy(wt_ref.at[sections["a"][1]], w_a.at[0, :, mine], own_sems.at[1]),
        pltpu.make_async_copy(wt_ref.at[sections["b"][1]], w_b.at[0, :, mine], own_sems.at[2]),
        pltpu.make_async_copy(vf_ref.at[slot], vf_all.at[slot], own_sems.at[3]),
        pltpu.make_async_copy(g_ref.at[slot], g_out.at[slot], own_sems.at[4]),
    ]
    def v_event(*steps):
        for k in steps:
            v_copy(k).start()

    def g_event():
        for k in range(1, slots):
            g_copy(k).start()

    def inside(kind, sec, step):
        @pl.when(inner == 1)
        def _():
            kind(sec, step)

    def outside(kind, sec, step):
        @pl.when(inner == 0)
        def _():
            kind(sec, step)

    z_start_own("a")
    if place.line:
        z_start_own("b")
    for k in (2, 3, 1):
        x_copy(k).start()
    v_event(1)
    for sec in ("a", "b"):
        for copy in near_copy(sec, 0):
            copy.start()
    for copy in own:
        copy.start()
    z_event("a", 1)
    if place.line:
        inside(z_event, "a", 2)
        z_event("b", 1)
        inside(z_event, "b", 2)
        v_event(2, 3)
    xy_event("a", 0)
    xy_event("b", 0)
    xy_event("a", 1)
    for k in range(1, slots):
        x_copy(k).wait_recv()
    own[0].wait()

    for p in range(slots):
        x = x_out[p].astype(F32)
        normed = x * lax.rsqrt(jnp.mean(x * x, axis=-1, keepdims=True) + EPSILON)
        h_one[position(p, place.rank), :] = (normed * gains_ref[0:1, :]).astype(BF16)
        for j in range(1, ranks):
            share("h1", h_one, p, j).start()
    own[1].wait()
    own[3].wait()
    done_event("a", 0)
    for p in range(slots):
        for j in range(1, ranks):
            share("h1", h_one, p, j).wait_recv()
    result("x").start()
    result("h1").start()

    if place.line:
        events = {
            (0, 1): [lambda: inside(z_event, "a", 3), lambda: outside(z_event, "a", 2)],
            (0, 3): [lambda: xy_event("b", 1)],
            (1, 0): [lambda: done_event("a", 1), lambda: v_wait(place.source(1))],
            (1, 2): [lambda: xy_event("a", 2)],
            (1, 3): [lambda: inside(z_event, "b", 3), lambda: outside(z_event, "b", 2)],
            (2, 0): [lambda: done_event("a", 2), lambda: v_wait(place.source(2))],
            (2, 1): [lambda: outside(z_event, "a", 3), lambda: inside(xy_event, "a", 3)],
            (2, 3): [lambda: xy_event("b", 2)],
            (3, 0): [lambda: outside(xy_event, "a", 3), lambda: done_event("a", 3), g_event,
                     lambda: v_wait(place.source(3))],
            (3, 3): [lambda: outside(z_event, "b", 3)],
        }
    else:
        events = {}
        z_start_own("b")
        v_event(2, 3)
        g_event()
        for step in range(2, slots):
            z_event("a", step)
            xy_event("a", step)
        for step in range(1, slots):
            z_event("b", step)
            xy_event("b", step)
            v_wait(place.source(step))

    def one_pair_of_heads(j, carry):
        def pump(point):
            for (step, at), todo in events.items():
                if at == point:
                    @pl.when(j == step)
                    def _(todo=todo):
                        for act in todo:
                            act()

        pump(0)
        if per == 1:
            w_in = w_a[j, : 3 * head_cols, :]
            first = vf_all[place.source(j)]
        else:
            w_in = jnp.concatenate(
                [
                    w_a[j * per + u, i * head_cols : (i + 1) * head_cols, :]
                    for i in range(3)
                    for u in range(per)
                ],
                axis=0,
            )
            first = jnp.concatenate([vf_all[place.source(j * per + u)] for u in range(per)], axis=1)
        half = length // 2
        for part_at in range(2):
            at = slice(part_at * half, (part_at + 1) * half)
            project = dot_nt(h_one[at, :], w_in)
            cosine, sine_part = cos_ref[at, :], sin_ref[at, :]
            q_raw, k_raw = project[:, :LANES], project[:, LANES : 2 * LANES]
            q_out[j, at, :] = ((q_raw * cosine + swap_halves(q_raw) * sine_part) * 0.125).astype(BF16)
            k_out[j, at, :] = (k_raw * cosine + swap_halves(k_raw) * sine_part).astype(BF16)
            v_out[j, at, :] = (0.5 * project[:, 2 * LANES :] + 0.5 * first[at].astype(F32)).astype(BF16)
        pump(1)
        v_turned = v_out[j].T
        for step in range(length // BLOCK):
            begin, keys = step * BLOCK, (step + 1) * BLOCK
            low = first_key(begin, length)
            queries = two_heads(q_out[j, begin:keys, :])
            scores = dot_nt(k_out[j, low:keys, :], queries)
            scores = jnp.where(seen(first_ref, begin, low, keys - low), scores, -1e30)
            top = jnp.max(scores, axis=0, keepdims=True)
            exps = jnp.exp(scores - top)
            total = jnp.sum(exps, axis=0, keepdims=True)
            chances = (exps * (1.0 / total)).astype(BF16)
            attended = dot_nn(v_turned[:, low:keys], chances)
            att_out[begin:keys, lanes(j, LANES)] = one_pair(attended, BLOCK).astype(BF16)
            log_total = top + jnp.log(total)
            lse_out[j, 0:1, begin:keys] = log_total[:, :BLOCK]
            lse_out[j, 1:2, begin:keys] = log_total[:, BLOCK:]
            if step == length // BLOCK // 2 - 1:
                pump(2)
        pump(3)
        return carry

    lax.fori_loop(0, pairs, one_pair_of_heads, 0)
    for name in ("q", "k", "v", "att", "a"):
        result(name).start()

    w_o = w_a[:, 3 * head_cols :, :].reshape(slots * head_cols, width)

    def away_copy(p, j):
        return remote(("away", p, j), away.at[j - 1, p], back.at[j - 1, p],
                      place.device(rank=(place.rank + j) % ranks))

    for p in range(slots):
        for j in range(1, ranks):
            at = position(p, (place.rank + j) % ranks)
            away[j - 1, p] = dot_nn(att_out[at, :], w_o).astype(BF16)
            away_copy(p, j).start()
    for p in range(slots):
        middle[p] = x_out[p].astype(F32) + dot_nn(att_out[position(p, place.rank), :], w_o)
    for p in range(slots):
        value = middle[p]
        for j in range(1, ranks):
            away_copy(p, j).wait_recv()
            value = value + back[j - 1, p].astype(F32)
        middle[p] = value
        normed = value * lax.rsqrt(jnp.mean(value * value, axis=-1, keepdims=True) + EPSILON)
        h_two[position(p, place.rank), :] = (normed * gains_ref[1:2, :]).astype(BF16)
        for j in range(1, ranks):
            share("h2", h_two, p, j).start()
    result("mid").start()
    for p in range(slots):
        for j in range(1, ranks):
            share("h2", h_two, p, j).wait_recv()
    result("h2").start()

    units = (w_b.shape[1]) // 3
    strip = length // 2

    def feed(k):
        def strips(n, carry):
            at = pl.ds(pl.multiple_of(n * strip, strip), strip)
            gate = dot_nt(h_two[at, :], w_b[k, :units, :])
            up = dot_nt(h_two[at, :], w_b[k, units : 2 * units, :])
            hid = (gate * (1.0 / (1.0 + jnp.exp(-gate))) * up).astype(BF16)
            out = dot_nn(hid, w_b[k, 2 * units :, :])
            if k == 0:
                ffn[at, :] = out
            else:
                ffn[at, :] += out
            return carry

        lax.fori_loop(0, length // strip, strips, 0)

    own[2].wait()
    for step in range(slots - 1):
        done_event("b", step)
        result(("b", step)).start()
        if early:
            feed(step)
        if step == 1 and place.line:
            xy_event("b", 3)
    if not early:
        ffn[0:8, :] = jnp.zeros((8, width), F32)
    result("ffn").start()
    own[4].wait()
    for k in range(1, slots):
        g_copy(k).wait_recv()
    result("g").start()
    for p in range(slots):
        e_all[position(p, place.rank), :] = (g_out[p].astype(F32) * live_ref[...]).astype(BF16)
        for j in range(1, ranks):
            share("e", e_all, p, j).start()
    for p in range(slots):
        for j in range(1, ranks):
            share("e", e_all, p, j).wait_recv()
            share("e", e_all, p, j).wait_send()
    result("e").start()
    done_event("b", slots - 1)
    result(("b", slots - 1)).start()
    for name in results:
        result(name).wait()
    for p in range(slots):
        for j in range(1, ranks):
            share("h1", h_one, p, j).wait_send()
            share("h2", h_two, p, j).wait_send()
            away_copy(p, j).wait_send()
    for k in range(1, slots):
        x_copy(k).wait_send()
        v_copy(k).wait_send()
        g_copy(k).wait_send()
    for sec in ("a", "b"):
        z_own_sends(sec)
        for step in range(slots):
            for copy in near_copy(sec, step):
                copy.wait_send()
            if place.line:
                for which in range(2):
                    far_copy(sec, step, which).wait_send()
                if step > 0:
                    @pl.when(inner == 1)
                    def _(sec=sec, step=step):
                        z_relay(sec, step).wait_send()


def forward_part(
    n_seq, n_head, head_cols, layer_input, values_first, weight_rows, out_grad, gains,
    cos_wide, sin_wide, first_pos, live, early,
):
    slots, rows, width = layer_input.shape
    all_rows, part = weight_rows.shape
    ranks = n_head // slots
    length = slots * ranks * rows
    rows_a = 4 * head_cols
    pairs = slots * head_cols // LANES
    count = 3 * (slots - 1) + 2 * (2 + 4 * slots + slots * n_seq) + 4 * slots * ranks
    any_space = pl.BlockSpec(memory_space=pl.ANY)
    vmem = pl.BlockSpec(memory_space=pltpu.VMEM)
    shape = jax.ShapeDtypeStruct
    heads = shape((pairs, length, LANES), BF16)
    return pl.pallas_call(
        functools.partial(forward_kernel, n_seq, n_head, head_cols, early),
        in_specs=[any_space] * 4 + [vmem] * 5,
        out_specs=[any_space] * 6 + [vmem] + [any_space] * 7,
        out_shape=[
            shape(layer_input.shape, BF16),
            shape((length, width), BF16),
            heads, heads, heads,
            shape((length, slots * head_cols), BF16),
            shape((pairs, 2, length), F32),
            shape((slots, rows_a, width), BF16),
            shape((slots, all_rows - rows_a, width), BF16),
            shape(layer_input.shape, F32),
            shape((length, width), BF16),
            shape(layer_input.shape, BF16),
            shape((length, width), BF16),
            shape((length if early else 8, width), F32),
        ],
        scratch_shapes=[
            pltpu.VMEM(layer_input.shape, BF16),
            pltpu.VMEM((length, width), BF16),
            pltpu.VMEM(heads.shape, BF16),
            pltpu.VMEM(heads.shape, BF16),
            pltpu.VMEM(heads.shape, BF16),
            pltpu.VMEM((length, slots * head_cols), BF16),
            pltpu.VMEM((slots, rows_a, width), BF16),
            pltpu.VMEM(layer_input.shape, F32),
            pltpu.VMEM((length, width), BF16),
            pltpu.VMEM(layer_input.shape, BF16),
            pltpu.VMEM((length, width), BF16),
            pltpu.VMEM(values_first.shape, BF16),
            pltpu.VMEM((ranks - 1, slots, rows, width), BF16),
            pltpu.VMEM((ranks - 1, slots, rows, width), BF16),
            pltpu.VMEM((slots, all_rows - rows_a, width), BF16),
            pltpu.VMEM((length if early else 8, width), F32),
            pltpu.SemaphoreType.DMA((2, count)),
            pltpu.SemaphoreType.DMA((2, slots)),
            pltpu.SemaphoreType.DMA((slots,)),
            pltpu.SemaphoreType.DMA((5,)),
            pltpu.SemaphoreType.DMA((12 + slots,)),
        ],
        compiler_params=pltpu.CompilerParams(
            collective_id=0, has_side_effects=True, vmem_limit_bytes=60 << 20
        ),
    )(
        layer_input, values_first, weight_rows, out_grad, gains, cos_wide, sin_wide,
        first_pos[None, :], live,
    )


def backward_kernel(
    n_seq, n_head, head_cols,
    wa_ref, wb_ref, h_one_ref, h_two_ref, x_ref, mid_ref, g_ref, q_ref, k_ref, v_ref, att_ref, e_ref,
    ffn_ref,
    lse_ref, gains_ref, cos_ref, sin_ref, first_ref, live_ref,
    block_out, input_out, first_out, gains_out, sum_a, sum_b, full_a, full_b,
    w_a, w_b, normed_all, e_all, x_own, middle, g_own, q_all, k_all, v_all, att_all,
    acc_one, acc_two, hidden, d_gate, d_project, away, back, delta_own,
    near_a, near_b, next_a, next_b, far_a, far_b,
    gain_sum, gain_seq, gain_slot, gain_rank,
    sems, near_sems, next_sems, far_sems, first_sems, load_sems, own_sems,
):
    slots, rows_b, width = w_b.shape
    rows_a = w_a.shape[1]
    ffn_cols = rows_b // 3
    ranks = n_head // slots
    rows = x_own.shape[1]
    length = slots * ranks * rows
    part = width // n_seq
    place = Place(n_seq, n_head, slots)
    slot = place.slot
    beside, across = place.beside, place.across
    corner = 3 - place.seq
    mine = lanes(place.seq, part)
    other = 1 - place.rank
    elsewhere = place.device(seq=beside)
    ids = {}
    sections = {
        "a": (0, w_a, near_a, next_a, far_a, sum_a, full_a, 128),
        "b": (1, w_b, near_b, next_b, far_b, sum_b, full_b, rows_b // 6),
    }

    def remote(name, src, dst, device, send=None, recv=None):
        if send is None:
            i = ids.setdefault(name, len(ids))
            send, recv = sems.at[0, i], sems.at[1, i]
        return pltpu.make_async_remote_copy(
            src_ref=src, dst_ref=dst, send_sem=send, recv_sem=recv,
            device_id=device, device_id_type=MESH,
        )

    def position(p, rank):
        return pl.ds(pl.multiple_of((p * ranks + rank) * rows, rows), rows)

    def halves(sec):
        half = sections[sec][1].shape[1] // 2
        return pl.ds(0, half), pl.ds(half, half)

    def near_copies(sec, k):
        i, grads, near = sections[sec][:3]
        upper, lower = halves(sec)
        plan = (
            (upper, beside, beside), (upper, corner, beside),
            (lower, across, across), (lower, corner, across),
        )
        return [
            remote(None, grads.at[k, cut, lanes(quarter, part)], near.at[k, n],
                   place.device(seq=to), near_sems.at[0, i, k, n], near_sems.at[1, i, k, n])
            for n, (cut, quarter, to) in enumerate(plan)
        ]

    def next_copies(sec, k):
        i, grads, _, then = sections[sec][:4]
        upper, lower = halves(sec)
        plan = ((upper, across), (lower, beside))
        return [
            remote(None, grads.at[k, cut, lanes(to, part)], then.at[k, n],
                   place.device(seq=to), next_sems.at[0, i, k, n], next_sems.at[1, i, k, n])
            for n, (cut, to) in enumerate(plan)
        ]

    upper = slot // 2
    inner = (slot + upper) % 2
    toward = 1 - 2 * upper

    def far_copy(sec, k):
        i, grads = sections[sec][:2]
        far = sections[sec][4]
        to = slot + toward * (1 - 2 * inner * (1 - k // 2))
        landing = inner * (4 - 3 * (k // 3)) + (1 - inner) * ((k // 2) * k)
        return remote(None, grads.at[k, :, mine], far.at[landing], place.device(slot=to),
                      far_sems.at[0, i, k], far_sems.at[1, i, landing])

    def far_wait(sec, landing):
        i, grads = sections[sec][:2]
        far = sections[sec][4]
        remote(None, grads.at[0, :, mine], far.at[landing], elsewhere,
               far_sems.at[0, i, 0], far_sems.at[1, i, landing]).wait_recv()

    def add_rows(sec, k, begin, where, addend):
        grads, strip = sections[sec][1], sections[sec][7]

        def one(i, carry):
            at = pl.ds(pl.multiple_of(begin + i * strip, 16), strip)
            value = grads[k, at, where].astype(F32)
            value = value + addend[pl.ds(pl.multiple_of(i * strip, 16), strip), :].astype(F32)
            grads[k, at, where] = value.astype(BF16)
            return carry

        lax.fori_loop(0, addend.shape[0] // strip, one, 0)

    def launch(sec, k):
        for copy in near_copies(sec, k):
            copy.start()

    def second(sec, k):
        near = sections[sec][2]
        half = near.shape[2]
        came = near_copies(sec, k)
        onward = next_copies(sec, k)
        came[1].wait_recv()
        add_rows(sec, k, 0, lanes(across, part), near.at[k, 1])
        onward[0].start()
        came[3].wait_recv()
        add_rows(sec, k, half, lanes(beside, part), near.at[k, 3])
        onward[1].start()
        came[0].wait_recv()
        add_rows(sec, k, 0, mine, near.at[k, 0])
        came[2].wait_recv()
        add_rows(sec, k, half, mine, near.at[k, 2])

    def third(sec, k, sends):
        then = sections[sec][3]
        half = then.shape[2]
        for n, copy in enumerate(next_copies(sec, k)):
            copy.wait_recv()
            add_rows(sec, k, n * half, mine, then.at[k, n])
        if sends:
            @pl.when(inner == 0)
            def _():
                far_copy(sec, k).start()

    def fourth(sec, k):
        @pl.when(inner == 1)
        def _():
            far_wait(sec, k)
            add_rows(sec, k, 0, mine, sections[sec][4].at[k])
            far_copy(sec, k).start()

    def gather_copies(sec):
        total, full = sections[sec][5:7]
        half = total.shape[0] // 2
        near = [
            remote(("full", sec, n), total, full.at[:, mine], place.device(seq=to))
            for n, to in enumerate((beside, across))
        ]
        far = []
        for n, (source, to) in enumerate(((beside, across), (across, beside))):
            where = full.at[pl.ds(n * half, half), lanes(source, part)]
            far.append(remote(("relay", sec, n), where, where, place.device(seq=to)))
        return near, far

    def own_copy(sec):
        i = sections[sec][0]
        return pltpu.make_async_copy(
            sections[sec][5], sections[sec][6].at[:, mine], own_sems.at[3 + i]
        )

    def finish(sec):
        grads = sections[sec][1]
        far, total, _, strip = sections[sec][4:]

        @pl.when(inner == 1)
        def _():
            far_wait(sec, 0)
            add_rows(sec, 0, 0, mine, far.at[0])

        far_wait(sec, 4)

        def one(r, carry):
            at = pl.ds(pl.multiple_of(r * strip, 16), strip)
            value = grads[0, at, mine].astype(F32) + far[4, at, :].astype(F32)
            total[at, :] = value.astype(BF16)
            return carry

        lax.fori_loop(0, total.shape[0] // strip, one, 0)
        own_copy(sec).start()
        for copy in gather_copies(sec)[0]:
            copy.start()

    def relay(sec):
        near, far = gather_copies(sec)
        for n in range(2):
            near[n].wait_recv()
            far[n].start()

    loads = {
        "h2": (h_two_ref, normed_all), "e": (e_ref, e_all), "h1": (h_one_ref, normed_all),
        "ffn": (ffn_ref, acc_one),
        "a": (wa_ref, w_a), "x": (x_ref, x_own), "mid": (mid_ref, middle),
        "g": (g_ref, g_own), "q": (q_ref, q_all), "k": (k_ref, k_all), "v": (v_ref, v_all),
        "att": (att_ref, att_all),
    }

    def load(name):
        src, dst = loads[name]
        return pltpu.make_async_copy(src, dst, load_sems.at[slots + list(loads).index(name)])

    def load_b(k):
        return pltpu.make_async_copy(wb_ref.at[k], w_b.at[k], load_sems.at[k])

    load_b(slots - 1).start()
    load("h2").start()
    load("e").start()
    load("ffn").start()
    load("x").start()
    load("mid").start()
    for k in reversed(range(slots - 1)):
        load_b(k).start()
    for name in loads:
        if name not in ("h1", "h2", "e", "ffn", "x", "mid"):
            load(name).start()
    place.greet(True)
    load("h2").wait()
    load("e").wait()
    load("ffn").wait()

    strip = length // 2
    key_sum, value_sum = acc_two.at[:, :LANES], acc_two.at[:, LANES : 2 * LANES]

    def away_copy(n, p):
        return remote(("away", n, p), away.at[n, p], back.at[n, p], place.device(rank=other))

    def swap(name, src, dst):
        return [
            remote((name, j), src.at[place.at_slot(j)], dst.at[slot],
                   place.device(slot=place.at_slot(j)))
            for j in (2, 3, 1)
        ]

    def keep(n, src, dst):
        return pltpu.make_async_copy(src, dst.at[slot], own_sems.at[n])

    def send_away(n, acc):
        for p in range(slots):
            away[n, p] = acc[position(p, other), :].astype(BF16)
            away_copy(n, p).start()

    live = live_ref[...]

    def block_delta():
        load("x").wait()
        load("mid").wait()
        for p in range(slots):
            away_copy(0, p).wait_recv()
            out = acc_one[position(p, place.rank), :] + back[0, p].astype(F32)
            delta_own[p] = ((middle[p] - x_own[p].astype(F32) + out) * live).astype(BF16)
        for copy in swap("block", delta_own, block_out):
            copy.start()
        keep(0, delta_own.at[slot], block_out).start()

    def units(i, carry):
        k = slots - 1 - i
        load_b(k).wait()

        def strips(n, carry):
            at = pl.ds(pl.multiple_of(n * strip, strip), strip)
            inner = normed_all[at, :]
            gate = dot_nt(inner, w_b[k, :ffn_cols, :])
            up = dot_nt(inner, w_b[k, ffn_cols : 2 * ffn_cols, :])
            sigmoid_gate = 1.0 / (1.0 + jnp.exp(-gate))
            activated = gate * sigmoid_gate
            hid = (activated * up).astype(BF16)
            hidden[at, :] = hid
            d_hidden = dot_nt(e_all[at, :], w_b[k, 2 * ffn_cols :, :])
            dg = (d_hidden * up * sigmoid_gate * (1.0 + gate * (1.0 - sigmoid_gate))).astype(BF16)
            du = (d_hidden * activated).astype(BF16)
            d_gate[at, :] = dg
            d_project[at, :ffn_cols] = du
            d_in = dot_nn(dg, w_b[k, :ffn_cols, :]) + dot_nn(du, w_b[k, ffn_cols : 2 * ffn_cols, :])

            @pl.when(i == 0)
            def _():
                acc_one[at, :] += dot_nn(hid, w_b[k, 2 * ffn_cols :, :])
                acc_two[at, :] = d_in

            @pl.when(i > 0)
            def _():
                acc_two[at, :] += d_in

            return carry

        lax.fori_loop(0, length // strip, strips, 0)
        w_b[k, 2 * ffn_cols :, :] = dot_tn(hidden[...], e_all[...]).astype(BF16)
        w_b[k, :ffn_cols, :] = dot_tn(d_gate[...], normed_all[...]).astype(BF16)
        w_b[k, ffn_cols : 2 * ffn_cols, :] = dot_tn(d_project[:, :ffn_cols], normed_all[...]).astype(BF16)
        launch("b", k)

        @pl.when(i == 0)
        def _():
            send_away(0, acc_one)

        @pl.when(i == 1)
        def _():
            block_delta()

        @pl.when(i > 0)
        def _():
            second("b", k + 1)

        @pl.when(i > 1)
        def _():
            third("b", k + 2, True)

        return carry

    lax.fori_loop(0, slots, units, 0)
    load("h1").start()

    def share(p):
        where = e_all.at[position(p, place.rank), :]
        return remote(("share", p), where, where, place.device(rank=other))

    send_away(1, acc_two)
    load("g").wait()
    gain_sum[...] = jnp.zeros_like(gain_sum)
    for p in range(slots):
        value = middle[p]
        inverse = lax.rsqrt(jnp.mean(value * value, axis=-1, keepdims=True) + EPSILON)
        normed = value * inverse
        away_copy(1, p).wait_recv()
        d_normed = acc_two[position(p, place.rank), :] + back[1, p].astype(F32)
        gain_sum[1:2, :] += jnp.sum(normed * d_normed, axis=0, keepdims=True)
        delta = norm_back(d_normed * gains_ref[1:2, :], normed, inverse)
        middle[p] = delta
        e_all[position(p, place.rank), :] = (g_own[p].astype(F32) * live + delta).astype(BF16)
        share(p).start()

    for name in ("a", "h1", "q", "k", "v", "att"):
        load(name).wait()
    for p in range(slots):
        share(p).wait_recv()

    def first_copy(k):
        return remote(None, v_all.at[k], first_out.at[slot],
                      place.device(slot=place.source(k)),
                      first_sems.at[0, k], first_sems.at[1, slot])

    def heads(i, carry):
        k = slots - 1 - i
        lane = lanes(k, LANES)
        d_att = dot_nt(e_all[...], w_a[k, 3 * head_cols :, :]).astype(BF16)
        product = (d_att.astype(F32) * att_all[:, lane].astype(F32)).T
        inner = [
            jnp.sum(product[:64], axis=0, keepdims=True),
            jnp.sum(product[64:], axis=0, keepdims=True),
        ]
        key_sum[...] = jnp.zeros_like(key_sum)
        value_sum[...] = jnp.zeros_like(value_sum)
        k_turned = k_all[k].T
        for step in range(length // BLOCK):
            begin, keys = step * BLOCK, (step + 1) * BLOCK
            low = first_key(begin, length)
            queries = two_heads(q_all[k, begin:keys, :])
            d_out = two_heads(d_att[begin:keys, :])
            scores = dot_nt(k_all[k, low:keys, :], queries)
            log_total = jnp.concatenate(
                [lse_ref[k, 0:1, begin:keys], lse_ref[k, 1:2, begin:keys]], axis=1
            )
            chances = jnp.where(seen(first_ref, begin, low, keys - low), jnp.exp(scores - log_total), 0.0)
            d_chances = dot_nt(v_all[k, low:keys, :], d_out)
            rest = jnp.concatenate([inner[0][:, begin:keys], inner[1][:, begin:keys]], axis=1)
            d_scores = (chances * (d_chances - rest)).astype(BF16)
            key_sum[low:keys, :] += dot_nn(d_scores, queries)
            value_sum[low:keys, :] += dot_nn(chances.astype(BF16), d_out)
            d_query = one_pair(dot_nn(k_turned[:, low:keys], d_scores), BLOCK) * 0.125
            d_project[begin:keys, :LANES] = (
                d_query * cos_ref[begin:keys, :] - swap_halves(d_query) * sin_ref[begin:keys, :]
            ).astype(BF16)
        d_key = key_sum[...]
        d_project[:, LANES : 2 * LANES] = (
            d_key * cos_ref[...] - swap_halves(d_key) * sin_ref[...]
        ).astype(BF16)
        d_value = (0.5 * value_sum[...]).astype(BF16)
        d_project[:, 2 * LANES :] = d_value
        v_all[k] = d_value

        @pl.when(k > 0)
        def _():
            first_copy(k).start()

        @pl.when(k == 0)
        def _():
            keep(2, v_all.at[0], first_out).start()

        for n in range(2):
            at = pl.ds(n * strip, strip)
            d_in = dot_nn(d_project[at, :], w_a[k, : 3 * head_cols, :])

            @pl.when(i == 0)
            def _():
                acc_one[at, :] = d_in

            @pl.when(i > 0)
            def _():
                acc_one[at, :] += d_in

        w_a[k, : 3 * head_cols, :] = dot_tn(d_project[...], normed_all[...]).astype(BF16)
        w_a[k, 3 * head_cols :, :] = dot_tn(att_all[:, lane], e_all[...]).astype(BF16)
        launch("a", k)

        @pl.when(i == 0)
        def _():
            second("b", 0)
            fourth("b", 3)
            third("b", 1, True)

        @pl.when(i == 1)
        def _():
            fourth("b", 2)
            third("b", 0, False)

        @pl.when(i == 2)
        def _():
            second("a", 3)
            fourth("b", 1)

        @pl.when(i == 3)
        def _():
            finish("b")

        return carry

    lax.fori_loop(0, slots, heads, 0)

    for copy in swap("block", delta_own, block_out):
        copy.wait_send()
    keep(0, delta_own.at[slot], block_out).wait()
    for p in range(slots):
        away_copy(0, p).wait_send()
        away[0, p] = acc_one[position(p, other), :].astype(BF16)
        remote(("again", p), away.at[0, p], back.at[0, p], place.device(rank=other)).start()
    for p in range(slots):
        value = x_own[p].astype(F32)
        inverse = lax.rsqrt(jnp.mean(value * value, axis=-1, keepdims=True) + EPSILON)
        normed = value * inverse
        remote(("again", p), away.at[0, p], back.at[0, p], place.device(rank=other)).wait_recv()
        d_normed = acc_one[position(p, place.rank), :] + back[0, p].astype(F32)
        gain_sum[0:1, :] += jnp.sum(normed * d_normed, axis=0, keepdims=True)
        delta = norm_back(d_normed * gains_ref[0:1, :], normed, inverse)
        delta_own[p] = ((middle[p] + delta) * live).astype(BF16)
    input_copies = swap("input", delta_own, input_out)
    input_copies[0].start()
    keep(1, delta_own.at[slot], input_out).start()

    def gain_copies(level):
        if level == 0:
            return [
                remote(("gain", 0, d), gain_seq.at[place.seq], gain_seq.at[place.seq],
                       place.device(seq=place.at_seq(d)))
                for d in range(1, n_seq)
            ]
        if level == 1:
            return [
                remote(("gain", 1, j), gain_slot.at[slot], gain_slot.at[slot],
                       place.device(slot=place.at_slot(j)))
                for j in range(1, slots)
            ]
        return [
            remote(("gain", 2, 0), gain_rank.at[place.rank], gain_rank.at[place.rank],
                   place.device(rank=other))
        ]

    def gain_step(level):
        value = gain_sum[...]
        if level > 0:
            for copy in gain_copies(level - 1):
                copy.wait_recv()
            held = (gain_seq, gain_slot, gain_rank)[level - 1]
            value = held[0]
            for j in range(1, held.shape[0]):
                value = value + held[j]
        if level == 3:
            gains_out[...] = value
            return
        target = (gain_seq, gain_slot, gain_rank)[level]
        target[(place.seq, slot, place.rank)[level]] = value
        for copy in gain_copies(level):
            copy.start()

    gain_step(0)
    second("a", 2)
    third("a", 3, True)
    input_copies[1].start()
    relay("b")
    second("a", 1)
    third("a", 2, True)
    fourth("a", 3)
    input_copies[2].start()
    gain_step(1)
    second("a", 0)
    third("a", 1, True)
    fourth("a", 2)
    gain_step(2)
    third("a", 0, False)
    fourth("a", 1)
    gain_step(3)
    finish("a")
    relay("a")
    for sec in ("b", "a"):
        near, far = gather_copies(sec)
        for copy in far:
            copy.wait_recv()
            copy.wait_send()
        for copy in near:
            copy.wait_send()
        own_copy(sec).wait()
        for k in range(slots):
            for copy in near_copies(sec, k) + next_copies(sec, k):
                copy.wait_send()
            if k > 0:
                far_copy(sec, k).wait_send()
    for copy in swap("block", delta_own, block_out):
        copy.wait_recv()
    for copy in swap("input", delta_own, input_out):
        copy.wait()
    for j in range(1, slots):
        source = place.at_slot(j)
        remote(None, v_all.at[0], first_out.at[source], elsewhere,
               first_sems.at[0, 0], first_sems.at[1, source]).wait_recv()
        first_copy(j).wait_send()
    for p in range(slots):
        away_copy(1, p).wait_send()
        remote(("again", p), away.at[0, p], back.at[0, p], place.device(rank=other)).wait_send()
        share(p).wait_send()
    for level in range(3):
        for copy in gain_copies(level):
            copy.wait_send()
    keep(1, delta_own.at[slot], input_out).wait()
    keep(2, v_all.at[0], first_out).wait()


def backward_part(n_seq, n_head, head_cols, saved, gains, tables, live):
    (
        x_own, h_one, q_rot, k_rot, v_mix, attended, log_total, weights_a, weights_b, middle, h_two,
        grad_own, e_all, ffn,
    ) = saved
    cos_wide, sin_wide, first_pos = tables
    slots, rows, width = x_own.shape
    length = h_one.shape[0]
    rows_a, rows_b = weights_a.shape[1], weights_b.shape[1]
    part = width // n_seq
    ranks = n_head // slots
    any_space = pl.BlockSpec(memory_space=pl.ANY)
    vmem = pl.BlockSpec(memory_space=pltpu.VMEM)
    shape = jax.ShapeDtypeStruct
    like = lambda value: pltpu.VMEM(value.shape, value.dtype)
    count = 2 * 4 + 2 * slots + slots + 2 * (slots - 1) + n_seq + slots + 4
    sem = pltpu.SemaphoreType.DMA
    return pl.pallas_call(
        functools.partial(backward_kernel, n_seq, n_head, head_cols),
        in_specs=[any_space] * 13 + [vmem] * 6,
        out_specs=[any_space] * 3 + [vmem] * 3 + [any_space] * 2,
        out_shape=[
            shape(x_own.shape, BF16),
            shape(x_own.shape, BF16),
            shape((slots, length, head_cols), BF16),
            shape((8, width), F32),
            shape((rows_a, part), BF16),
            shape((rows_b, part), BF16),
            shape((rows_a, width), BF16),
            shape((rows_b, width), BF16),
        ],
        scratch_shapes=[
            like(weights_a), like(weights_b), like(h_two), like(e_all), like(x_own), like(middle),
            like(grad_own),
            like(q_rot), like(k_rot), like(v_mix), like(attended),
            pltpu.VMEM((length, width), F32),
            pltpu.VMEM((length, width), F32),
            pltpu.VMEM((length, rows_b // 3), BF16),
            pltpu.VMEM((length, rows_b // 3), BF16),
            pltpu.VMEM((length, 3 * LANES), BF16),
            pltpu.VMEM((2, slots, rows, width), BF16),
            pltpu.VMEM((2, slots, rows, width), BF16),
            like(x_own),
            pltpu.VMEM((slots, 4, rows_a // 2, part), BF16),
            pltpu.VMEM((slots, 4, rows_b // 2, part), BF16),
            pltpu.VMEM((slots, 2, rows_a // 2, part), BF16),
            pltpu.VMEM((slots, 2, rows_b // 2, part), BF16),
            pltpu.VMEM((slots + 1, rows_a, part), BF16),
            pltpu.VMEM((slots + 1, rows_b, part), BF16),
            pltpu.VMEM((8, width), F32),
            pltpu.VMEM((n_seq, 8, width), F32),
            pltpu.VMEM((slots, 8, width), F32),
            pltpu.VMEM((ranks, 8, width), F32),
            sem((2, count)),
            sem((2, 2, slots, 4)),
            sem((2, 2, slots, 2)),
            sem((2, 2, slots + 1)),
            sem((2, slots)),
            sem((slots + 12,)),
            sem((5,)),
        ],
        compiler_params=pltpu.CompilerParams(
            collective_id=2, has_side_effects=True, vmem_limit_bytes=64 << 20
        ),
    )(
        weights_a, weights_b, h_one, h_two, x_own, middle, grad_own, q_rot, k_rot, v_mix, attended,
        e_all, ffn, log_total, gains, cos_wide, sin_wide, first_pos[None, :], live,
    )


def reduce_kernel(
    n_seq, n_head, chunks,
    block_ref, input_ref, first_ref, gains_ref, grads_a, grads_b,
    block_out, input_out, first_out, gains_out, sum_a, sum_b, full_a, full_b,
    near_a, near_b, turn_a, turn_b, far_a, far_b, gain_seq, gain_slot, gain_rank,
    send_sems, recv_sems, own_sems, far_recv, first_recv,
):
    slots = block_ref.shape[0]
    place = Place(n_seq, n_head, slots)
    place.greet(True)
    sender = Sender(send_sems, recv_sems)
    part = sum_a.shape[1]
    mine = lanes(place.seq, part)
    order = [2, 3, 1, 0]
    parts = ((grads_b, sum_b, full_b, near_b, turn_b, far_b, chunks[1]),
             (grads_a, sum_a, full_a, near_a, turn_a, far_a, chunks[0]))
    copies, received = [], []

    def arrive(copy):
        copy.wait_recv()
        received.append(copy)

    def swap(src, dst):
        return [
            sender.start(
                src.at[place.at_slot(k)], dst.at[place.slot], place.device(slot=place.at_slot(k))
            )
            for k in (2, 3, 1)
        ]

    gain_seq[place.seq] = gains_ref[...]
    small = [
        sender.start(gain_seq.at[place.seq], gain_seq.at[place.seq],
                     place.device(seq=place.at_seq(d)))
        for d in range(1, n_seq)
    ]
    copies += small

    def to_seqs(grads, near, k):
        return [
            sender.start(
                grads.at[k, :, lanes(place.at_seq(d), part)],
                near.at[k, d - 1],
                place.device(seq=place.at_seq(d)),
            )
            for d in range(1, n_seq)
        ]

    sent = {}
    units = [(which, k) for which in range(2) for k in order]

    def launch(unit):
        which, k = unit
        sent[unit] = to_seqs(parts[which][0], parts[which][3], k)
        copies.extend(sent[unit])

    own = [
        pltpu.make_async_copy(src, dst.at[place.slot], own_sems.at[i])
        for i, (src, dst) in enumerate(
            (
                (block_ref.at[place.slot], block_out),
                (input_ref.at[place.slot], input_out),
                (first_ref.at[0], first_out),
            )
        )
    ]
    for copy in own:
        copy.start()
    launch(units[0])
    launch(units[1])
    copies += swap(block_ref, block_out)
    for copy in small:
        arrive(copy)
    total = gain_seq[0]
    for i in range(1, n_seq):
        total = total + gain_seq[i]
    gain_slot[place.slot] = total
    small = [
        sender.start(gain_slot.at[place.slot], gain_slot.at[place.slot],
                     place.device(slot=place.at_slot(k)))
        for k in range(1, slots)
    ]
    copies += small
    elsewhere = place.device(seq=place.at_seq(1))
    for index, unit in enumerate(units):
        which, k = unit
        grads, _, _, near, turn, far, chunk = parts[which]
        if index + 2 < len(units):
            launch(units[index + 2])
        for copy in sent[unit]:
            arrive(copy)

        def add(i, carry, grads=grads, near=near, turn=turn, k=k, chunk=chunk):
            rows = pl.ds(pl.multiple_of(i * chunk, chunk), chunk)
            value = grads[k, rows, mine].astype(F32)
            for d in range(n_seq - 1):
                value = value + near[k, d, rows, :].astype(F32)
            turn[k, rows, :] = value.astype(BF16)
            return carry

        lax.fori_loop(0, grads.shape[1] // chunk, add, 0)
        if k != 0:
            copy = sender.start(
                turn.at[k], far.at[place.slot], place.device(slot=place.source(k)),
                far_recv.at[which, place.slot],
            )
            copies.append(copy)
            received.append(copy)
        if index == 1:
            for j in range(1, slots):
                copy = sender.start(
                    first_ref.at[j], first_out.at[place.slot],
                    place.device(slot=place.source(j)), first_recv.at[place.slot],
                )
                copies.append(copy)
                received.append(copy)
        if index == 4:
            copies += swap(input_ref, input_out)
            for copy in small:
                arrive(copy)
            total = gain_slot[0]
            for i in range(1, slots):
                total = total + gain_slot[i]
            gain_rank[place.rank] = total
            small = [
                sender.start(gain_rank.at[place.rank], gain_rank.at[place.rank],
                             place.device(rank=(place.rank + j) % place.ranks))
                for j in range(1, place.ranks)
            ]
            copies += small
        if k == 0:
            for j in range(1, slots):
                source = place.at_slot(j)
                pltpu.make_async_remote_copy(
                    src_ref=turn.at[0], dst_ref=far.at[source], send_sem=send_sems.at[0],
                    recv_sem=far_recv.at[which, source], device_id=elsewhere, device_id_type=MESH,
                ).wait_recv()
            _, total_ref, full, _, _, _, _ = parts[which]

            def finish(i, carry, turn=turn, far=far, total_ref=total_ref, full=full, chunk=chunk):
                rows = pl.ds(pl.multiple_of(i * chunk, chunk), chunk)
                value = turn[0, rows, :].astype(F32)
                for j in range(1, slots):
                    value = value + far[place.at_slot(j), rows, :].astype(F32)
                value = value.astype(BF16)
                total_ref[rows, :] = value
                full[rows, mine] = value
                return carry

            lax.fori_loop(0, grads.shape[1] // chunk, finish, 0)
            copies += [
                sender.start(total_ref, full.at[:, mine], place.device(seq=place.at_seq(d)))
                for d in range(1, n_seq)
            ]
    for copy in small:
        arrive(copy)
    total = gain_rank[0]
    for i in range(1, place.ranks):
        total = total + gain_rank[i]
    gains_out[...] = total
    for copy in copies:
        if all(copy is not other for other in received):
            copy.wait_recv()
    for j in range(1, slots):
        source = place.at_slot(j)
        pltpu.make_async_remote_copy(
            src_ref=first_ref.at[0], dst_ref=first_out.at[source], send_sem=send_sems.at[0],
            recv_sem=first_recv.at[source], device_id=elsewhere, device_id_type=MESH,
        ).wait_recv()
    for copy in copies:
        copy.wait_send()
    for copy in own:
        copy.wait()


def reduce_grads(n_seq, n_head, chunks, block_delta, input_delta, first_delta, gains, grads_a, grads_b):
    slots = block_delta.shape[0]
    part = grads_a.shape[2] // n_seq
    rows = (grads_a.shape[1], grads_b.shape[1])
    ranks = n_head // slots
    count = (
        3 * (slots - 1) + 2 * (slots * (n_seq - 1) + (slots - 1) + (n_seq - 1))
        + (n_seq - 1) + (slots - 1) + (ranks - 1)
    )
    any_space = pl.BlockSpec(memory_space=pl.ANY)
    vmem = pl.BlockSpec(memory_space=pltpu.VMEM)
    like = lambda value: jax.ShapeDtypeStruct(value.shape, value.dtype)
    return pl.pallas_call(
        functools.partial(reduce_kernel, n_seq, n_head, chunks),
        in_specs=[any_space] * 3 + [vmem] * 3,
        out_specs=[any_space] * 3 + [vmem] * 5,
        out_shape=[like(block_delta), like(input_delta), like(first_delta), like(gains)]
        + [jax.ShapeDtypeStruct((r, part), BF16) for r in rows]
        + [jax.ShapeDtypeStruct((r, part * n_seq), BF16) for r in rows],
        scratch_shapes=[pltpu.VMEM((slots, n_seq - 1, r, part), BF16) for r in rows]
        + [pltpu.VMEM((slots, r, part), BF16) for r in rows]
        + [pltpu.VMEM((slots, r, part), BF16) for r in rows]
        + [pltpu.VMEM((n,) + gains.shape, F32) for n in (n_seq, slots, ranks)]
        + [
            pltpu.SemaphoreType.DMA((count,)),
            pltpu.SemaphoreType.DMA((count,)),
            pltpu.SemaphoreType.DMA((3,)),
            pltpu.SemaphoreType.DMA((2, slots)),
            pltpu.SemaphoreType.DMA((slots,)),
        ],
        compiler_params=pltpu.CompilerParams(
            collective_id=1, has_side_effects=True, vmem_limit_bytes=56 << 20
        ),
    )(block_delta, input_delta, first_delta, gains, grads_a, grads_b)


def shampoo_kernel(
    stat_ref, root_ref, head_stat, head_root, unit_stat, unit_root, full_a, sum_a, full_b, sum_b,
    wide_ref, out_right_ref, new_head, new_unit, step_a, step_b,
):
    step = pl.program_id(0)
    blocks = stat_ref.shape[1]

    def one(member, width, small_stat, small_root, full, total, big_out, small_out, step_out):
        for b in range(blocks):
            rows = pl.ds(pl.multiple_of((member * blocks + b) * width, 16), width)
            grad, own = full[rows, :], total[rows, :]
            big_out[0, b] = STAT_DECAY * stat_ref[0, b] + (1.0 - STAT_DECAY) * dot_tn(own, grad)
            small_out[member, b] = STAT_DECAY * small_stat[member, b] + (
                1.0 - STAT_DECAY
            ) * dot_nt(grad, grad)
            turned = dot_nn(small_root[member, b].astype(BF16), grad).astype(BF16)
            turned = dot_nt(turned, root_ref[0, b].astype(BF16))
            scale = lax.rsqrt(jnp.mean(turned * turned, axis=0, keepdims=True) + EPSILON)
            step_out[rows, :] = turned * scale

    head_width, unit_width = head_stat.shape[2], unit_stat.shape[2]
    head_args = (head_width, head_stat, head_root, full_a, sum_a)
    unit_args = (unit_width, unit_stat, unit_root, full_b, sum_b)

    @pl.when(step < 3)
    def _():
        one(step, *head_args, wide_ref, new_head, step_a)

    @pl.when((step >= 3) & (step < 6))
    def _():
        one(step - 3, *unit_args, wide_ref, new_unit, step_b)

    @pl.when(step == 6)
    def _():
        one(3, *head_args, out_right_ref, new_head, step_a)


def shampoo(stats_wide, roots_wide, stats_head, roots_head, stats_unit, roots_unit, full_a, sum_a, full_b, sum_b):
    members, blocks, part, width = stats_wide.shape
    member = lambda i: (jnp.where(i == 5, 6, jnp.where(i == 6, 5, i)), 0, 0, 0)
    wide = pl.BlockSpec((1, blocks, part, width), member)
    vmem = pl.BlockSpec(memory_space=pltpu.VMEM)
    return pl.pallas_call(
        shampoo_kernel,
        grid=(members,),
        in_specs=[wide, wide] + [vmem] * 8,
        out_specs=[
            pl.BlockSpec((1, blocks, part, width), lambda i: (jnp.minimum(i, 5), 0, 0, 0)),
            pl.BlockSpec((1, blocks, part, width), lambda i: (0, 0, 0, 0)),
            vmem, vmem, vmem, vmem,
        ],
        out_shape=[
            jax.ShapeDtypeStruct((members - 1, blocks, part, width), F32),
            jax.ShapeDtypeStruct((1, blocks, part, width), F32),
            jax.ShapeDtypeStruct(stats_head.shape, F32),
            jax.ShapeDtypeStruct(stats_unit.shape, F32),
            jax.ShapeDtypeStruct(sum_a.shape, F32),
            jax.ShapeDtypeStruct(sum_b.shape, F32),
        ],
        compiler_params=pltpu.CompilerParams(vmem_limit_bytes=48 << 20),
    )(stats_wide, roots_wide, stats_head, roots_head, stats_unit, roots_unit, full_a, sum_a, full_b, sum_b)


class Links:
    def __init__(self, n_seq, n_head, slots):
        self.n_seq, self.n_head, self.slots = n_seq, n_head, slots
        self.ranks = n_head // slots
        self.slot = lax.axis_index("head") // self.ranks
        self.rank = lax.axis_index("head") % self.ranks

    def permute(self, value, partner):
        pairs = []
        for s in range(self.n_seq):
            for h in range(self.n_head):
                to_s, to_h = partner(s, h)
                pairs.append((s * self.n_head + h, to_s * self.n_head + to_h))
        return lax.ppermute(value, AXES, pairs)

    def swap_slots(self, value):
        got = [lax.dynamic_index_in_dim(value, self.slot, 0, keepdims=False)]
        for step in range(1, self.slots):
            piece = lax.dynamic_index_in_dim(value, self.slot ^ step, 0, keepdims=False)
            got.append(self.permute(piece, lambda s, h: (s, h ^ (step * self.ranks))))
        got = jnp.stack(got)
        return jnp.stack(
            [lax.dynamic_index_in_dim(got, self.slot ^ q, 0, keepdims=False) for q in range(self.slots)]
        )

    def gather_ranks(self, value):
        got = [value] + [
            self.permute(value, lambda s, h: (s, h ^ step)) for step in range(1, self.ranks)
        ]
        got = jnp.stack(got)
        return jnp.stack(
            [lax.dynamic_index_in_dim(got, self.rank ^ r, 0, keepdims=False) for r in range(self.ranks)]
        )

    def sum_ranks(self, value):
        total = lax.dynamic_index_in_dim(value, self.rank, 0, keepdims=False)
        for step in range(1, self.ranks):
            piece = lax.dynamic_index_in_dim(value, self.rank ^ step, 0, keepdims=False)
            got = self.permute(piece.astype(BF16), lambda s, h: (s, h ^ step))
            total = total + got.astype(F32)
        return total

    def whole_sequence(self, own):
        both = self.gather_ranks(own)
        return jnp.swapaxes(both, 0, 1).reshape(-1, own.shape[-1])

    def own_sum(self, full):
        rows = full.shape[0] // (self.slots * self.ranks)
        parts = full.reshape(self.slots, self.ranks, rows, full.shape[-1])
        return self.sum_ranks(jnp.swapaxes(parts, 0, 1)).reshape(-1, full.shape[-1])


def backward_plain(n_seq, n_head, head_cols, ffn_cols, links, saved, gains, tables, is_live):
    (
        x_bf16, h_one, q_rot, k_rot, v_mix, attended, log_total, weights_a, weights_b, middle,
        h_two, grad_own, d_ffn, _,
    ) = saved
    cos_wide, sin_wide, first_pos = tables
    slots, rows, width = x_bf16.shape
    length = h_one.shape[0]
    rows_a, rows_b = weights_a.shape[1], weights_b.shape[1]
    pairs = slots * head_cols // LANES
    per = LANES // head_cols

    def pair_major(value):
        n = value.shape[2]
        value = value.reshape(pairs, per, length, n, head_cols)
        return value.transpose(0, 2, 3, 1, 4).reshape(pairs, length, n, LANES)

    def slot_major(value):
        n = value.shape[2]
        value = value.reshape(pairs, length, n, per, head_cols)
        return value.transpose(0, 3, 1, 2, 4).reshape(slots, length, n, head_cols)

    w_in, w_o = weights_a[:, : 3 * head_cols], weights_a[:, 3 * head_cols :]
    w_gu, w_d = weights_b[:, : 2 * ffn_cols], weights_b[:, 2 * ffn_cols :]
    x_own = x_bf16.reshape(slots * rows, width).astype(F32)
    middle = middle.reshape(slots * rows, width)
    ein = functools.partial(jnp.einsum, preferred_element_type=F32)
    inverse_one = lax.rsqrt(jnp.mean(x_own * x_own, axis=-1, keepdims=True) + EPSILON)
    normed_one = x_own * inverse_one
    inverse_two = lax.rsqrt(jnp.mean(middle * middle, axis=-1, keepdims=True) + EPSILON)
    normed_two = middle * inverse_two
    saved = (q_rot, k_rot, v_mix, attended, log_total)
    attended = jnp.swapaxes(attended.reshape(length, slots, head_cols), 0, 1)
    gate_up = ein("ld,qfd->qlf", h_two, w_gu)
    gate, up = gate_up[..., :ffn_cols], gate_up[..., ffn_cols:]
    sigmoid_gate = jax.nn.sigmoid(gate)
    activated = gate * sigmoid_gate
    hidden = (activated * up).astype(BF16)
    ffn_out = links.own_sum(ein("qlf,qfd->ld", hidden, w_d))
    block_delta = jnp.where(is_live, middle - x_own + ffn_out, 0.0).astype(BF16)

    d_own = jnp.where(is_live, grad_own, jnp.zeros_like(grad_own))
    d_out = d_own.reshape(slots * rows, width).astype(F32)
    g_down = ein("qlf,ld->qfd", hidden, d_ffn)
    d_hidden = ein("ld,qfd->qlf", d_ffn, w_d)
    d_gate = (
        d_hidden * up * sigmoid_gate * (1.0 + gate * (1.0 - sigmoid_gate))
    ).astype(BF16)
    d_up = (d_hidden * activated).astype(BF16)
    d_gate_up = jnp.concatenate([d_gate, d_up], axis=2)
    d_normed_two = links.own_sum(ein("qlf,qfd->ld", d_gate_up, w_gu))
    g_gate_up = ein("qlf,ld->qfd", d_gate_up, h_two)
    grads_b = jnp.concatenate([g_gate_up.astype(BF16), g_down.astype(BF16)], axis=1)
    gain_two = jnp.sum(normed_two * d_normed_two, axis=0)
    middle_delta = norm_back(d_normed_two * gains[1], normed_two, inverse_two)
    d_middle = d_out + middle_delta
    d_attn = links.whole_sequence(d_middle.astype(BF16).reshape(slots, rows, width))
    d_attended = ein("ld,qcd->qlc", d_attn, w_o).astype(BF16)
    if per > 1:
        d_attended = pair_major(d_attended[:, :, None])[:, :, 0]
    d_project = jnp.concatenate(
        attend_back(saved, d_attended, cos_wide, sin_wide, first_pos), axis=2
    )
    if per > 1:
        d_project = slot_major(d_project.reshape(pairs, length, 3, LANES)).reshape(
            slots, length, 3 * head_cols
        )
    d_value = d_project[:, :, 2 * head_cols :]
    g_out = ein("qlc,ld->qcd", attended, d_attn)
    g_qkv = ein("qlc,ld->qcd", d_project, h_one)
    grads_a = jnp.concatenate([g_qkv.astype(BF16), g_out.astype(BF16)], axis=1)
    d_normed_one = links.own_sum(ein("qlc,qcd->ld", d_project, w_in))
    gain_one = jnp.sum(normed_one * d_normed_one, axis=0)
    input_delta = middle_delta + norm_back(d_normed_one * gains[0], normed_one, inverse_one)
    input_delta = jnp.where(is_live, input_delta, 0.0).astype(BF16)
    gain_rows = jnp.concatenate([gain_one.reshape(8, -1), gain_two.reshape(8, -1)], axis=0)

    return reduce_grads(
        n_seq,
        n_head,
        (LANES, unit_chunk(rows_b)),
        block_delta.reshape(slots, rows, width),
        input_delta.reshape(slots, rows, width),
        d_value,
        gain_rows,
        grads_a,
        grads_b,
    )


def shards(
    n_seq,
    n_head,
    layer_input,
    values_first,
    w_qkv,
    w_gate_up,
    w_out,
    w_down,
    norm_gains,
    out_grad,
    segments,
    counts,
    stats_wide,
    roots_wide,
    stats_head,
    roots_head,
    stats_unit,
    roots_unit,
):
    slots, rows, width = layer_input.shape
    length = segments.shape[1]
    row_part, head_cols, ffn_cols = w_qkv.shape[1], w_qkv.shape[2], w_gate_up.shape[2]
    head_dim = stats_head.shape[2]
    links = Links(n_seq, n_head, slots)
    is_live = links.slot < counts[0]
    pairs = slots * head_cols // LANES
    per = LANES // head_cols
    rows_a, rows_b = 4 * head_cols, 3 * ffn_cols

    weight_rows = jnp.concatenate(
        [
            jnp.swapaxes(w_qkv.astype(BF16), 1, 2).reshape(3 * head_cols, row_part),
            w_out.astype(BF16),
            jnp.swapaxes(w_gate_up.astype(BF16), 1, 2).reshape(2 * ffn_cols, row_part),
            w_down.astype(BF16),
        ],
        axis=0,
    )
    segment_ids = lax.dynamic_index_in_dim(segments, links.slot, 0, keepdims=False)
    first_pos, cos_wide, sin_wide = position_tables(segment_ids, head_dim)
    live = jnp.full((1, width), is_live, F32)
    fused = n_seq == 4 and slots == 4 and links.ranks == 2 and per == 1
    saved = forward_part(
        n_seq, n_head, head_cols, layer_input, values_first, weight_rows, out_grad, norm_gains,
        cos_wide, sin_wide, first_pos, live, fused,
    )
    tables = (cos_wide, sin_wide, first_pos)
    if fused:
        block_got, input_got, first_got, gains, sum_a, sum_b, full_a, full_b = backward_part(
            n_seq, n_head, head_cols, saved, norm_gains, tables, live
        )
        gains = gains[:2]
    else:
        block_got, input_got, first_got, gains, sum_a, sum_b, full_a, full_b = backward_plain(
            n_seq, n_head, head_cols, ffn_cols, links, saved, norm_gains, tables, is_live
        )
        gains = gains.reshape(2, width)
    block_out = layer_input.astype(F32) + block_got.astype(F32)
    input_grad = out_grad.astype(F32) + input_got.astype(F32)
    first_grad = first_got.astype(F32)
    grad_gains = gains
    new_gains = norm_gains - GAIN_RATE * grad_gains * lax.rsqrt(
        jnp.mean(grad_gains * grad_gains, axis=-1, keepdims=True) + EPSILON
    )

    wide, out_right, new_head, new_unit, step_a, step_b = shampoo(
        stats_wide, roots_wide, stats_head, roots_head, stats_unit, roots_unit,
        full_a, sum_a, full_b, sum_b,
    )
    cut = 3 * head_cols
    turned = lambda value, n: jnp.swapaxes(value.reshape(n, -1, row_part), 1, 2)
    return (
        block_out,
        input_grad,
        first_grad,
        turned(sum_a[:cut], 3).astype(F32),
        turned(sum_b[: 2 * ffn_cols], 2).astype(F32),
        sum_a[cut:].astype(F32),
        sum_b[2 * ffn_cols :].astype(F32),
        grad_gains,
        w_qkv - STEP_RATE * turned(step_a[:cut], 3),
        w_gate_up - STEP_RATE * turned(step_b[: 2 * ffn_cols], 2),
        w_out - OUT_RATE * step_a[cut:],
        w_down - STEP_RATE * step_b[2 * ffn_cols :],
        new_gains,
        wide,
        out_right[0],
        new_head,
        new_unit,
    )


def unit_chunk(rows):
    return max(c for c in range(16, 177, 16) if rows % c == 0)


def solution(mesh):
    return jax.shard_map(
        functools.partial(shards, mesh.shape["seq"], mesh.shape["head"]),
        mesh=mesh,
        in_specs=(
            P("seq", "head", None),
            P("seq", None, "head"),
            P(None, "seq", "head"),
            P(None, "seq", "head"),
            P("head", "seq"),
            P("head", "seq"),
            P(),
            P("seq", "head", None),
            P("seq", None),
            P("seq"),
            P(None, "head", "seq", None),
            P(None, "head", "seq", None),
            P(None, "head", None, None),
            P(None, "head", None, None),
            P(None, "head", None, None),
            P(None, "head", None, None),
        ),
        out_specs=(
            P("seq", "head", None),
            P("seq", "head", None),
            P("seq", None, "head"),
            P(None, "seq", "head"),
            P(None, "seq", "head"),
            P("head", "seq"),
            P("head", "seq"),
            P(),
            P(None, "seq", "head"),
            P(None, "seq", "head"),
            P("head", "seq"),
            P("head", "seq"),
            P(),
            P(None, "head", "seq", None),
            P("head", "seq", None),
            P(None, "head", None, None),
            P(None, "head", None, None),
        ),
        check_vma=False,
    )
```

```python
import functools

import jax
import jax.numpy as jnp
from jax import lax
from jax.experimental import pallas as pl
from jax.experimental.pallas import tpu as pltpu
from jax.sharding import PartitionSpec as P

EPSILON = 1e-06
STAT_DECAY = 0.5
STEP_RATE = 0.02
OUT_RATE = 0.1
GAIN_RATE = 0.25
AXES = ("seq", "head")
MESH = pl.DeviceIdType.MESH
LANES = 128
BLOCK = 128
BF16 = jnp.bfloat16
F32 = jnp.float32


def dot_nt(matrix_a, matrix_b):
    return lax.dot_general(
        matrix_a, matrix_b, (((1,), (1,)), ((), ())), preferred_element_type=F32
    )


def dot_tn(matrix_a, matrix_b):
    return lax.dot_general(
        matrix_a, matrix_b, (((0,), (0,)), ((), ())), preferred_element_type=F32
    )


def dot_nn(matrix_a, matrix_b):
    return jnp.dot(matrix_a, matrix_b, preferred_element_type=F32)


def norm_back(d_normed, normed, inverse):
    return inverse * (d_normed - normed * jnp.mean(d_normed * normed, axis=-1, keepdims=True))


def swap_halves(values):
    lane = lax.broadcasted_iota(jnp.int32, values.shape, 1)
    return jnp.where((lane & 32) == 0, pltpu.roll(values, 96, 1), pltpu.roll(values, 32, 1))


def two_heads(block):
    lane = lax.broadcasted_iota(jnp.int32, block.shape, 1)
    zero = jnp.zeros_like(block)
    return jnp.concatenate(
        [jnp.where(lane < 64, block, zero), jnp.where(lane >= 64, block, zero)], axis=0
    )


def one_pair(transposed, width):
    kept = jnp.concatenate([transposed[:64, :width], transposed[64:, width:]], axis=0)
    return kept.T


def first_key(begin, length):
    return max(0, (begin - length // 2 + 1) // BLOCK * BLOCK)


def seen(first_ref, begin, low, key_count):
    first = first_ref[0:1, begin : begin + BLOCK]
    query = begin + lax.broadcasted_iota(jnp.int32, (1, BLOCK), 1)
    first = jnp.concatenate([first, first], axis=1)
    query = jnp.concatenate([query, query], axis=1)
    key = low + lax.broadcasted_iota(jnp.int32, (key_count, 2 * BLOCK), 0)
    return (key >= first) & (key <= query)


def attend_back_kernel(
    qr_ref, kr_ref, vm_ref, att_ref, d_ref, lse_ref, cos_ref, sin_ref, first_ref,
    dq_ref, dk_ref, dv_ref, key_sum, value_sum,
):
    length = qr_ref.shape[1]
    key_sum[...] = jnp.zeros_like(key_sum)
    value_sum[...] = jnp.zeros_like(value_sum)
    k_turned = kr_ref[0].T
    cosine, sine_part = cos_ref[...], sin_ref[...]
    product = (d_ref[0].astype(F32) * att_ref[...].astype(F32)).T
    inner = [
        jnp.sum(product[:64], axis=0, keepdims=True),
        jnp.sum(product[64:], axis=0, keepdims=True),
    ]
    for step in range(length // BLOCK):
        begin, keys = step * BLOCK, (step + 1) * BLOCK
        low = first_key(begin, length)
        queries = two_heads(qr_ref[0, begin:keys, :])
        d_out = two_heads(d_ref[0, begin:keys, :])
        scores = dot_nt(kr_ref[0, low:keys, :], queries)
        log_total = jnp.concatenate(
            [lse_ref[0, 0:1, begin:keys], lse_ref[0, 1:2, begin:keys]], axis=1
        )
        chances = jnp.where(seen(first_ref, begin, low, keys - low), jnp.exp(scores - log_total), 0.0)
        d_chances = dot_nt(vm_ref[0, low:keys, :], d_out)
        part = jnp.concatenate([inner[0][:, begin:keys], inner[1][:, begin:keys]], axis=1)
        d_scores = (chances * (d_chances - part)).astype(BF16)
        key_sum[low:keys, :] += dot_nn(d_scores, queries)
        value_sum[low:keys, :] += dot_nn(chances.astype(BF16), d_out)
        d_query = one_pair(dot_nn(k_turned[:, low:keys], d_scores), BLOCK) * 0.125
        dq_ref[0, begin:keys, :] = (
            d_query * cosine[begin:keys] - swap_halves(d_query) * sine_part[begin:keys]
        ).astype(BF16)
    d_key = key_sum[...]
    dk_ref[0] = (d_key * cosine - swap_halves(d_key) * sine_part).astype(BF16)
    dv_ref[0] = (0.5 * value_sum[...]).astype(BF16)


def attend_back(saved, d_attended, cos_wide, sin_wide, first_pos):
    q_rot, k_rot, v_mix, attended, log_total = saved
    pairs, length, _ = q_rot.shape
    part = pl.BlockSpec((1, length, LANES), lambda p: (p, 0, 0))
    table = pl.BlockSpec((length, LANES), lambda p: (0, 0))
    out = jax.ShapeDtypeStruct((pairs, length, LANES), BF16)
    return pl.pallas_call(
        attend_back_kernel,
        grid=(pairs,),
        in_specs=[part] * 3 + [pl.BlockSpec((length, LANES), lambda p: (0, p)), part,
                               pl.BlockSpec((1, 2, length), lambda p: (p, 0, 0)), table, table,
                               pl.BlockSpec((1, length), lambda p: (0, 0))],
        out_specs=[part] * 3,
        out_shape=[out] * 3,
        scratch_shapes=[pltpu.VMEM((length, LANES), F32)] * 2,
        compiler_params=pltpu.CompilerParams(vmem_limit_bytes=48 << 20),
        cost_estimate=pl.CostEstimate(
            flops=pairs * length * length * 128 * 20, bytes_accessed=pairs * length * 128 * 24,
            transcendentals=pairs * length * length),
    )(q_rot, k_rot, v_mix, attended, d_attended, log_total, cos_wide, sin_wide, first_pos[None, :])


class Place:
    def __init__(self, n_seq, n_head, slots):
        self.n_seq, self.slots, self.ranks = n_seq, slots, n_head // slots
        self.seq = lax.axis_index("seq")
        head = lax.axis_index("head")
        self.slot, self.rank = head // self.ranks, head % self.ranks

    def at_slot(self, step):
        return (self.slot + step + self.slots) % self.slots

    def at_seq(self, step):
        return (self.seq + step + self.n_seq) % self.n_seq

    @property
    def line(self):
        return self.slots == 4 and self.n_seq == 4

    def source(self, step):
        if not self.line:
            return self.at_slot(-step)
        upper = self.slot // 2
        inner = (self.slot + upper) % 2
        near = step + inner * (1 - 2 * step) * (1 - step // 2)
        return near + upper * (3 - 2 * near)

    @property
    def beside(self):
        return self.seq + 1 - 2 * (self.seq % 2)

    @property
    def across(self):
        return self.seq + 2 - 4 * (self.seq // 2)

    def device(self, seq=None, slot=None, rank=None):
        seq = self.seq if seq is None else seq
        slot = self.slot if slot is None else slot
        rank = self.rank if rank is None else rank
        return (seq, slot * self.ranks + rank)

    def greet(self, with_ranks):
        others = [self.device(slot=self.at_slot(k)) for k in range(1, self.slots)]
        others += [self.device(seq=self.at_seq(d)) for d in range(1, self.n_seq)]
        if with_ranks:
            others += [
                self.device(rank=(self.rank + j) % self.ranks) for j in range(1, self.ranks)
            ]
        barrier = pltpu.get_barrier_semaphore()
        for other in others:
            pl.semaphore_signal(barrier, inc=1, device_id=other, device_id_type=MESH)
        pl.semaphore_wait(barrier, len(others))


class Sender:
    def __init__(self, send_sems, recv_sems):
        self.send_sems, self.recv_sems, self.used = send_sems, recv_sems, 0

    def start(self, src, dst, device, recv=None):
        copy = pltpu.make_async_remote_copy(
            src_ref=src,
            dst_ref=dst,
            send_sem=self.send_sems.at[self.used],
            recv_sem=self.recv_sems.at[self.used] if recv is None else recv,
            device_id=device,
            device_id_type=MESH,
        )
        self.used += 1
        copy.start()
        return copy


def lanes(index, width):
    return pl.ds(pl.multiple_of(index * width, width), width)


def forward_kernel(
    n_seq, n_head, head_cols, head_dim, early,
    x_ref, vf_ref, g_ref, w_qkv, w_gate_up, w_out, w_down, gains_ref, seg_ref, count_ref,
    cos_ref, sin_ref, first_ref, live_ref, x_res, h_one_res, q_res, k_res, v_res, att_res, lse_out, w_a_res, w_b_res, middle_res, h_two_res, g_res, e_res,
    ffn_res, x_out, h_one, q_out, k_out, v_out, att_out, w_a, middle, h_two, g_out, e_all,
    vf_all, away, back, w_b, ffn, wt_ref, sems, z_recv, v_recv, own_sems, res_sems,
):
    slots, rows, width = x_ref.shape
    part = wt_ref.shape[1]
    rows_a = w_a.shape[1]
    place = Place(n_seq, n_head, slots)
    ranks = place.ranks
    length = slots * ranks * rows
    per = LANES // head_cols
    pairs = slots // per
    mine = lanes(place.seq, part)
    sections = {"a": (w_a, pl.ds(0, rows_a)), "b": (w_b, pl.ds(rows_a, wt_ref.shape[0] - rows_a))}
    ids = {}
    elsewhere = place.device(seq=place.at_seq(1))

    def index(name):
        return ids.setdefault(name, len(ids))

    def remote(name, src, dst, device, recv=None):
        i = index(name)
        return pltpu.make_async_remote_copy(
            src_ref=src, dst_ref=dst, send_sem=sems.at[0, i],
            recv_sem=sems.at[1, i] if recv is None else recv,
            device_id=device, device_id_type=MESH,
        )

    def x_copy(k):
        to = place.at_slot(k)
        return remote(("x", k), x_ref.at[to], x_out.at[place.slot], place.device(slot=to))

    def g_copy(k):
        to = place.at_slot(k)
        return remote(("g", k), g_ref.at[to], g_out.at[place.slot], place.device(slot=to))

    def v_copy(k):
        to = place.source(k) if place.line else place.at_slot(k)
        return remote(("v", k), vf_ref.at[to], vf_all.at[place.slot], place.device(slot=to),
                      v_recv.at[place.slot])

    def v_wait(source):
        pltpu.make_async_remote_copy(
            src_ref=vf_ref.at[0], dst_ref=vf_all.at[source], send_sem=sems.at[0, 0],
            recv_sem=v_recv.at[source], device_id=elsewhere, device_id_type=MESH,
        ).wait_recv()

    def piece(sec, step):
        ref, at = sections[sec]
        return wt_ref.at[at] if step == 0 else ref.at[step, :, mine]

    def z_copy(name, sec, step, to, to_step):
        ref, _ = sections[sec]
        which = 0 if sec == "a" else 1
        return remote((name, sec, step), piece(sec, step), ref.at[to_step, :, mine],
                      place.device(slot=to), z_recv.at[which, to_step])

    def z_wait(sec, step):
        ref, _ = sections[sec]
        which = 0 if sec == "a" else 1
        pltpu.make_async_remote_copy(
            src_ref=piece(sec, 0), dst_ref=ref.at[step, :, mine], send_sem=sems.at[0, 0],
            recv_sem=z_recv.at[which, step], device_id=elsewhere, device_id_type=MESH,
        ).wait_recv()

    slot = place.slot
    upper = slot // 2
    inner = (slot + upper) % 2

    def z_start_own(sec):
        if not place.line:
            for k in range(1, slots):
                z_copy(("z", k), sec, 0, place.at_slot(k), k).start()
            return
        @pl.when(slot < 3)
        def _():
            to = slot + 1
            z_copy("up", sec, 0, to, 1 + (to == 2).astype(jnp.int32)).start()

        @pl.when(slot > 0)
        def _():
            to = slot - 1
            z_copy("down", sec, 0, to, 1 + (to == 1).astype(jnp.int32)).start()

    def z_own_sends(sec):
        if not place.line:
            for k in range(1, slots):
                z_copy(("z", k), sec, 0, place.at_slot(k), k).wait_send()
            return

        @pl.when(slot < 3)
        def _():
            z_copy("up", sec, 0, slot + 1, 1).wait_send()

        @pl.when(slot > 0)
        def _():
            z_copy("down", sec, 0, slot - 1, 1).wait_send()

    def z_relay(sec, step):
        if step == 1:
            return z_copy("on", sec, step, slot + 1 - 2 * upper, 3)
        return z_copy("on", sec, step, slot - 1 + 2 * upper, step)

    def near_copy(sec, step):
        ref, _ = sections[sec]
        dst = ref.at[step, :, mine]
        if not place.line:
            return [
                remote(("xy", d, sec, step), piece(sec, step), dst, place.device(seq=place.at_seq(d)))
                for d in range(1, n_seq)
            ]
        return [
            remote(("xy", 0, sec, step), piece(sec, step), dst, place.device(seq=place.beside)),
            remote(("xy", 1, sec, step), piece(sec, step), dst, place.device(seq=place.across)),
        ]

    def far_copy(sec, step, which):
        ref, at = sections[sec]
        half = at.size // 2
        cut = pl.ds(which * half, half)
        source = place.beside if which == 0 else place.across
        to = place.across if which == 0 else place.beside
        where = ref.at[step, cut, lanes(source, part)]
        return remote(("far", which, sec, step), where, where, place.device(seq=to))

    def z_event(sec, step):
        z_wait(sec, step)
        if place.line:
            @pl.when(inner == 1)
            def _():
                z_relay(sec, step).start()
        for copy in near_copy(sec, step):
            copy.start()

    def xy_event(sec, step):
        for which, copy in enumerate(near_copy(sec, step)):
            copy.wait_recv()
            if place.line:
                far_copy(sec, step, which).start()

    def done_event(sec, step):
        if place.line:
            for which in range(2):
                far_copy(sec, step, which).wait_recv()

    def position(p, rank):
        return pl.ds(pl.multiple_of((p * ranks + rank) * rows, rows), rows)

    def share(name, ref, p, j):
        where = ref.at[position(p, place.rank), :]
        return remote((name, p, j), where, where, place.device(rank=(place.rank + j) % ranks))

    results = {
        "x": (x_out, x_res), "h1": (h_one, h_one_res), "q": (q_out, q_res), "k": (k_out, k_res),
        "v": (v_out, v_res), "att": (att_out, att_res), "a": (w_a, w_a_res),
        "mid": (middle, middle_res), "h2": (h_two, h_two_res), "g": (g_out, g_res),
        "e": (e_all, e_res), "ffn": (ffn, ffn_res),
    }
    for step in range(slots):
        results["b", step] = (w_b.at[step], w_b_res.at[step])

    def result(name):
        src, dst = results[name]
        return pltpu.make_async_copy(src, dst, res_sems.at[list(results).index(name)])

    high, tall = w_qkv.shape[2], w_gate_up.shape[1]
    for i in range(3):
        wt_ref[i * high : (i + 1) * high, :] = w_qkv[i].T.astype(BF16)
    wt_ref[3 * high : 4 * high, :] = w_out[...].astype(BF16)
    for i in range(2):
        wt_ref[rows_a + i * tall : rows_a + (i + 1) * tall, :] = w_gate_up[i].astype(BF16)
    wt_ref[rows_a + 2 * tall :, :] = w_down[...].astype(BF16)
    place.greet(True)
    own = [
        pltpu.make_async_copy(x_ref.at[slot], x_out.at[slot], own_sems.at[0]),
        pltpu.make_async_copy(wt_ref.at[sections["a"][1]], w_a.at[0, :, mine], own_sems.at[1]),
        pltpu.make_async_copy(wt_ref.at[sections["b"][1]], w_b.at[0, :, mine], own_sems.at[2]),
        pltpu.make_async_copy(vf_ref.at[slot], vf_all.at[slot], own_sems.at[3]),
        pltpu.make_async_copy(g_ref.at[slot], g_out.at[slot], own_sems.at[4]),
    ]
    def v_event(*steps):
        for k in steps:
            v_copy(k).start()

    def g_event():
        for k in range(1, slots):
            g_copy(k).start()

    def inside(kind, sec, step):
        @pl.when(inner == 1)
        def _():
            kind(sec, step)

    def outside(kind, sec, step):
        @pl.when(inner == 0)
        def _():
            kind(sec, step)

    z_start_own("a")
    if place.line:
        z_start_own("b")
    for k in (2, 3, 1):
        x_copy(k).start()
    v_event(1)
    for sec in ("a", "b"):
        for copy in near_copy(sec, 0):
            copy.start()
    for copy in own:
        copy.start()
    segment = seg_ref[pl.ds(slot, 1), :]
    first_pos = jnp.zeros_like(segment)
    for document in range(1, 4):
        before = jnp.sum((segment < document).astype(jnp.int32), axis=1, keepdims=True)
        first_pos = jnp.where(segment == document, before, first_pos)
    first_ref[...] = first_pos
    offset = lax.broadcasted_iota(jnp.int32, segment.shape, 1) - first_pos
    offset = jnp.broadcast_to(offset.astype(F32), (LANES, length)).T
    lane = lax.broadcasted_iota(jnp.int32, (1, LANES), 1)
    half_width = head_dim // 2
    place_in_half = (lane % half_width).astype(F32)
    frequency = jnp.exp(-jnp.log(10000.0) * place_in_half / half_width)
    cos_ref[...] = jnp.cos(offset * frequency)
    sin_ref[...] = jnp.sin(offset * frequency) * jnp.where(lane % head_dim < half_width, -1.0, 1.0)
    live = (slot < count_ref[...]).astype(F32)
    live_ref[...] = jnp.broadcast_to(live, live_ref.shape)

    z_event("a", 1)
    if place.line:
        inside(z_event, "a", 2)
        z_event("b", 1)
        inside(z_event, "b", 2)
        v_event(2, 3)
    xy_event("a", 0)
    xy_event("b", 0)
    xy_event("a", 1)
    for k in range(1, slots):
        x_copy(k).wait_recv()
    own[0].wait()

    for p in range(slots):
        x = x_out[p].astype(F32)
        normed = x * lax.rsqrt(jnp.mean(x * x, axis=-1, keepdims=True) + EPSILON)
        h_one[position(p, place.rank), :] = (normed * gains_ref[0:1, :]).astype(BF16)
        for j in range(1, ranks):
            share("h1", h_one, p, j).start()
    own[1].wait()
    own[3].wait()
    done_event("a", 0)
    for p in range(slots):
        for j in range(1, ranks):
            share("h1", h_one, p, j).wait_recv()
    result("x").start()
    result("h1").start()

    if place.line:
        events = {
            (0, 1): [lambda: inside(z_event, "a", 3), lambda: outside(z_event, "a", 2)],
            (0, 3): [lambda: xy_event("b", 1)],
            (1, 0): [lambda: done_event("a", 1), lambda: v_wait(place.source(1))],
            (1, 2): [lambda: xy_event("a", 2)],
            (1, 3): [lambda: inside(z_event, "b", 3), lambda: outside(z_event, "b", 2)],
            (2, 0): [lambda: done_event("a", 2), lambda: v_wait(place.source(2))],
            (2, 1): [lambda: outside(z_event, "a", 3), lambda: inside(xy_event, "a", 3)],
            (2, 3): [lambda: xy_event("b", 2)],
            (3, 0): [lambda: outside(xy_event, "a", 3), lambda: done_event("a", 3), g_event,
                     lambda: v_wait(place.source(3))],
            (3, 3): [lambda: outside(z_event, "b", 3)],
        }
    else:
        events = {}
        z_start_own("b")
        v_event(2, 3)
        g_event()
        for step in range(2, slots):
            z_event("a", step)
            xy_event("a", step)
        for step in range(1, slots):
            z_event("b", step)
            xy_event("b", step)
            v_wait(place.source(step))

    def one_pair_of_heads(j, carry):
        def pump(point):
            for (step, at), todo in events.items():
                if at == point:
                    @pl.when(j == step)
                    def _(todo=todo):
                        for act in todo:
                            act()

        pump(0)
        if per == 1:
            w_in = w_a[j, : 3 * head_cols, :]
            first = vf_all[place.source(j)]
        else:
            w_in = jnp.concatenate(
                [
                    w_a[j * per + u, i * head_cols : (i + 1) * head_cols, :]
                    for i in range(3)
                    for u in range(per)
                ],
                axis=0,
            )
            first = jnp.concatenate([vf_all[place.source(j * per + u)] for u in range(per)], axis=1)
        half = length // 2
        for part_at in range(2):
            at = slice(part_at * half, (part_at + 1) * half)
            project = dot_nt(h_one[at, :], w_in)
            cosine, sine_part = cos_ref[at, :], sin_ref[at, :]
            q_raw, k_raw = project[:, :LANES], project[:, LANES : 2 * LANES]
            q_out[j, at, :] = ((q_raw * cosine + swap_halves(q_raw) * sine_part) * 0.125).astype(BF16)
            k_out[j, at, :] = (k_raw * cosine + swap_halves(k_raw) * sine_part).astype(BF16)
            v_out[j, at, :] = (0.5 * project[:, 2 * LANES :] + 0.5 * first[at].astype(F32)).astype(BF16)
        pump(1)
        v_turned = v_out[j].T
        for step in range(length // BLOCK):
            begin, keys = step * BLOCK, (step + 1) * BLOCK
            low = first_key(begin, length)
            queries = two_heads(q_out[j, begin:keys, :])
            scores = dot_nt(k_out[j, low:keys, :], queries)
            scores = jnp.where(seen(first_ref, begin, low, keys - low), scores, -1e30)
            top = jnp.max(scores, axis=0, keepdims=True)
            exps = jnp.exp(scores - top)
            total = jnp.sum(exps, axis=0, keepdims=True)
            chances = (exps * (1.0 / total)).astype(BF16)
            attended = dot_nn(v_turned[:, low:keys], chances)
            att_out[begin:keys, lanes(j, LANES)] = one_pair(attended, BLOCK).astype(BF16)
            log_total = top + jnp.log(total)
            lse_out[j, 0:1, begin:keys] = log_total[:, :BLOCK]
            lse_out[j, 1:2, begin:keys] = log_total[:, BLOCK:]
            if step == length // BLOCK // 2 - 1:
                pump(2)
        pump(3)
        return carry

    lax.fori_loop(0, pairs, one_pair_of_heads, 0)
    for name in ("q", "k", "v", "att", "a"):
        result(name).start()

    w_o = w_a[:, 3 * head_cols :, :].reshape(slots * head_cols, width)

    def away_copy(p, j):
        return remote(("away", p, j), away.at[j - 1, p], back.at[j - 1, p],
                      place.device(rank=(place.rank + j) % ranks))

    for p in range(slots):
        for j in range(1, ranks):
            at = position(p, (place.rank + j) % ranks)
            away[j - 1, p] = dot_nn(att_out[at, :], w_o).astype(BF16)
            away_copy(p, j).start()
    for p in range(slots):
        middle[p] = x_out[p].astype(F32) + dot_nn(att_out[position(p, place.rank), :], w_o)
    for p in range(slots):
        value = middle[p]
        for j in range(1, ranks):
            away_copy(p, j).wait_recv()
            value = value + back[j - 1, p].astype(F32)
        middle[p] = value
        normed = value * lax.rsqrt(jnp.mean(value * value, axis=-1, keepdims=True) + EPSILON)
        h_two[position(p, place.rank), :] = (normed * gains_ref[1:2, :]).astype(BF16)
        for j in range(1, ranks):
            share("h2", h_two, p, j).start()
    result("mid").start()
    for p in range(slots):
        for j in range(1, ranks):
            share("h2", h_two, p, j).wait_recv()
    result("h2").start()

    units = (w_b.shape[1]) // 3
    strip = length // 2

    def feed(k):
        def strips(n, carry):
            at = pl.ds(pl.multiple_of(n * strip, strip), strip)
            gate = dot_nt(h_two[at, :], w_b[k, :units, :])
            up = dot_nt(h_two[at, :], w_b[k, units : 2 * units, :])
            hid = (gate * (1.0 / (1.0 + jnp.exp(-gate))) * up).astype(BF16)
            out = dot_nn(hid, w_b[k, 2 * units :, :])
            if k == 0:
                ffn[at, :] = out
            else:
                ffn[at, :] += out
            return carry

        lax.fori_loop(0, length // strip, strips, 0)

    own[2].wait()
    for step in range(slots - 1):
        done_event("b", step)
        result(("b", step)).start()
        if early:
            feed(step)
        if step == 1 and place.line:
            xy_event("b", 3)
    if not early:
        ffn[0:8, :] = jnp.zeros((8, width), F32)
    result("ffn").start()
    own[4].wait()
    for k in range(1, slots):
        g_copy(k).wait_recv()
    result("g").start()
    for p in range(slots):
        e_all[position(p, place.rank), :] = (g_out[p].astype(F32) * live_ref[...]).astype(BF16)
        for j in range(1, ranks):
            share("e", e_all, p, j).start()
    for p in range(slots):
        for j in range(1, ranks):
            share("e", e_all, p, j).wait_recv()
            share("e", e_all, p, j).wait_send()
    result("e").start()
    done_event("b", slots - 1)
    result(("b", slots - 1)).start()
    for name in results:
        result(name).wait()
    for p in range(slots):
        for j in range(1, ranks):
            share("h1", h_one, p, j).wait_send()
            share("h2", h_two, p, j).wait_send()
            away_copy(p, j).wait_send()
    for k in range(1, slots):
        x_copy(k).wait_send()
        v_copy(k).wait_send()
        g_copy(k).wait_send()
    for sec in ("a", "b"):
        z_own_sends(sec)
        for step in range(slots):
            for copy in near_copy(sec, step):
                copy.wait_send()
            if place.line:
                for which in range(2):
                    far_copy(sec, step, which).wait_send()
                if step > 0:
                    @pl.when(inner == 1)
                    def _(sec=sec, step=step):
                        z_relay(sec, step).wait_send()


def forward_part(
    n_seq, n_head, head_cols, head_dim, layer_input, values_first, out_grad, weights, gains,
    segments, counts, early,
):
    slots, rows, width = layer_input.shape
    part = weights[0].shape[1]
    all_rows = 4 * head_cols + 3 * weights[1].shape[1]
    ranks = n_head // slots
    length = slots * ranks * rows
    rows_a = 4 * head_cols
    pairs = slots * head_cols // LANES
    count = 3 * (slots - 1) + 2 * (2 + 4 * slots + slots * n_seq) + 4 * slots * ranks
    any_space = pl.BlockSpec(memory_space=pl.ANY)
    vmem = pl.BlockSpec(memory_space=pltpu.VMEM)
    shape = jax.ShapeDtypeStruct
    heads = shape((pairs, length, LANES), BF16)
    return pl.pallas_call(
        functools.partial(forward_kernel, n_seq, n_head, head_cols, head_dim, early),
        in_specs=[any_space] * 3 + [vmem] * 7,
        out_specs=[vmem] * 4 + [any_space] * 6 + [vmem] + [any_space] * 7,
        out_shape=[
            shape((length, LANES), F32),
            shape((length, LANES), F32),
            shape((1, length), jnp.int32),
            shape((1, width), F32),
            shape(layer_input.shape, BF16),
            shape((length, width), BF16),
            heads, heads, heads,
            shape((length, slots * head_cols), BF16),
            shape((pairs, 2, length), F32),
            shape((slots, rows_a, width), BF16),
            shape((slots, all_rows - rows_a, width), BF16),
            shape(layer_input.shape, F32),
            shape((length, width), BF16),
            shape(layer_input.shape, BF16),
            shape((length, width), BF16),
            shape((length if early else 8, width), F32),
        ],
        scratch_shapes=[
            pltpu.VMEM(layer_input.shape, BF16),
            pltpu.VMEM((length, width), BF16),
            pltpu.VMEM(heads.shape, BF16),
            pltpu.VMEM(heads.shape, BF16),
            pltpu.VMEM(heads.shape, BF16),
            pltpu.VMEM((length, slots * head_cols), BF16),
            pltpu.VMEM((slots, rows_a, width), BF16),
            pltpu.VMEM(layer_input.shape, F32),
            pltpu.VMEM((length, width), BF16),
            pltpu.VMEM(layer_input.shape, BF16),
            pltpu.VMEM((length, width), BF16),
            pltpu.VMEM(values_first.shape, BF16),
            pltpu.VMEM((ranks - 1, slots, rows, width), BF16),
            pltpu.VMEM((ranks - 1, slots, rows, width), BF16),
            pltpu.VMEM((slots, all_rows - rows_a, width), BF16),
            pltpu.VMEM((length if early else 8, width), F32),
            pltpu.VMEM((all_rows, part), BF16),
            pltpu.SemaphoreType.DMA((2, count)),
            pltpu.SemaphoreType.DMA((2, slots)),
            pltpu.SemaphoreType.DMA((slots,)),
            pltpu.SemaphoreType.DMA((5,)),
            pltpu.SemaphoreType.DMA((12 + slots,)),
        ],
        compiler_params=pltpu.CompilerParams(
            collective_id=0, has_side_effects=True, vmem_limit_bytes=60 << 20
        ),
    )(
        layer_input, values_first, out_grad, *weights, gains, segments, counts.reshape(1, 1)
    )


def backward_kernel(
    n_seq, n_head, head_cols,
    wa_ref, wb_ref, h_one_ref, h_two_ref, x_ref, mid_ref, g_ref, q_ref, k_ref, v_ref, att_ref, e_ref,
    ffn_ref, root_ref, head_root, unit_root,
    lse_ref, gains_ref, cos_ref, sin_ref, first_ref, live_ref,
    block_out, input_out, first_out, gains_out, sum_a, sum_b, full_a_out, full_b_out, step_a, step_b,
    w_a, w_b, normed_all, e_all, x_own, middle, g_own, q_all, k_all, v_all, att_all,
    acc_one, acc_two, hidden, d_gate, d_project, away, back, delta_own,
    full_a, full_b, head_buf, unit_buf, near_a, near_b, next_a, next_b, far_a, far_b,
    gain_sum, gain_seq, gain_slot, gain_rank,
    sems, near_sems, next_sems, far_sems, first_sems, load_sems, own_sems, step_sems, credit,
):
    slots, rows_b, width = w_b.shape
    rows_a = w_a.shape[1]
    ffn_cols = rows_b // 3
    ranks = n_head // slots
    rows = x_own.shape[1]
    length = slots * ranks * rows
    part = width // n_seq
    place = Place(n_seq, n_head, slots)
    slot = place.slot
    beside, across = place.beside, place.across
    corner = 3 - place.seq
    mine = lanes(place.seq, part)
    other = 1 - place.rank
    elsewhere = place.device(seq=beside)
    ids = {}
    sections = {
        "a": (0, w_a, near_a, next_a, far_a, sum_a, full_a, 128),
        "b": (1, w_b, near_b, next_b, far_b, sum_b, full_b, rows_b // 6),
    }

    def remote(name, src, dst, device, send=None, recv=None):
        if send is None:
            i = ids.setdefault(name, len(ids))
            send, recv = sems.at[0, i], sems.at[1, i]
        return pltpu.make_async_remote_copy(
            src_ref=src, dst_ref=dst, send_sem=send, recv_sem=recv,
            device_id=device, device_id_type=MESH,
        )

    def position(p, rank):
        return pl.ds(pl.multiple_of((p * ranks + rank) * rows, rows), rows)

    def halves(sec):
        half = sections[sec][1].shape[1] // 2
        return pl.ds(0, half), pl.ds(half, half)

    def near_copies(sec, k):
        i, grads, near = sections[sec][:3]
        upper, lower = halves(sec)
        plan = (
            (upper, beside, beside), (upper, corner, beside),
            (lower, across, across), (lower, corner, across),
        )
        return [
            remote(None, grads.at[k, cut, lanes(quarter, part)], near.at[k, n],
                   place.device(seq=to), near_sems.at[0, i, k, n], near_sems.at[1, i, k, n])
            for n, (cut, quarter, to) in enumerate(plan)
        ]

    def next_copies(sec, k):
        i, grads, _, then = sections[sec][:4]
        upper, lower = halves(sec)
        plan = ((upper, across), (lower, beside))
        return [
            remote(None, grads.at[k, cut, lanes(to, part)], then.at[k, n],
                   place.device(seq=to), next_sems.at[0, i, k, n], next_sems.at[1, i, k, n])
            for n, (cut, to) in enumerate(plan)
        ]

    upper = slot // 2
    inner = (slot + upper) % 2
    toward = 1 - 2 * upper

    def far_copy(sec, k):
        i, grads = sections[sec][:2]
        far = sections[sec][4]
        to = slot + toward * (1 - 2 * inner * (1 - k // 2))
        landing = inner * (4 - 3 * (k // 3)) + (1 - inner) * ((k // 2) * k)
        return remote(None, grads.at[k, :, mine], far.at[landing], place.device(slot=to),
                      far_sems.at[0, i, k], far_sems.at[1, i, landing])

    def far_wait(sec, landing):
        i, grads = sections[sec][:2]
        far = sections[sec][4]
        remote(None, grads.at[0, :, mine], far.at[landing], elsewhere,
               far_sems.at[0, i, 0], far_sems.at[1, i, landing]).wait_recv()

    def add_rows(sec, k, begin, where, addend):
        grads, strip = sections[sec][1], sections[sec][7]

        def one(i, carry):
            at = pl.ds(pl.multiple_of(begin + i * strip, 16), strip)
            value = grads[k, at, where].astype(F32)
            value = value + addend[pl.ds(pl.multiple_of(i * strip, 16), strip), :].astype(F32)
            grads[k, at, where] = value.astype(BF16)
            return carry

        lax.fori_loop(0, addend.shape[0] // strip, one, 0)

    def launch(sec, k):
        for copy in near_copies(sec, k):
            copy.start()

    def second(sec, k):
        near = sections[sec][2]
        half = near.shape[2]
        came = near_copies(sec, k)
        onward = next_copies(sec, k)
        came[1].wait_recv()
        add_rows(sec, k, 0, lanes(across, part), near.at[k, 1])
        onward[0].start()
        came[3].wait_recv()
        add_rows(sec, k, half, lanes(beside, part), near.at[k, 3])
        onward[1].start()
        came[0].wait_recv()
        add_rows(sec, k, 0, mine, near.at[k, 0])
        came[2].wait_recv()
        add_rows(sec, k, half, mine, near.at[k, 2])

    def third(sec, k, sends):
        then = sections[sec][3]
        half = then.shape[2]
        for n, copy in enumerate(next_copies(sec, k)):
            copy.wait_recv()
            add_rows(sec, k, n * half, mine, then.at[k, n])
        if sends:
            @pl.when(inner == 0)
            def _():
                far_copy(sec, k).start()

    def fourth(sec, k):
        @pl.when(inner == 1)
        def _():
            far_wait(sec, k)
            add_rows(sec, k, 0, mine, sections[sec][4].at[k])
            far_copy(sec, k).start()

    def gather_copies(sec):
        total, full = sections[sec][5:7]
        half = total.shape[0] // 2
        near = [
            remote(("full", sec, n), total, full.at[:, mine], place.device(seq=to))
            for n, to in enumerate((beside, across))
        ]
        far = []
        for n, (source, to) in enumerate(((beside, across), (across, beside))):
            where = full.at[pl.ds(n * half, half), lanes(source, part)]
            far.append(remote(("relay", sec, n), where, where, place.device(seq=to)))
        return near, far

    def own_copy(sec):
        i = sections[sec][0]
        return pltpu.make_async_copy(
            sections[sec][5], sections[sec][6].at[:, mine], own_sems.at[3 + i]
        )

    def finish(sec):
        grads = sections[sec][1]
        far, total, _, strip = sections[sec][4:]

        @pl.when(inner == 1)
        def _():
            far_wait(sec, 0)
            add_rows(sec, 0, 0, mine, far.at[0])

        far_wait(sec, 4)

        def one(r, carry):
            at = pl.ds(pl.multiple_of(r * strip, 16), strip)
            value = grads[0, at, mine].astype(F32) + far[4, at, :].astype(F32)
            total[at, :] = value.astype(BF16)
            return carry

        lax.fori_loop(0, total.shape[0] // strip, one, 0)
        own_copy(sec).start()
        for copy in gather_copies(sec)[0]:
            copy.start()

    def relay(sec):
        near, far = gather_copies(sec)
        for n in range(2):
            near[n].wait_recv()
            far[n].start()

    loads = {
        "h2": (h_two_ref, normed_all), "e": (e_ref, e_all), "h1": (h_one_ref, normed_all),
        "ffn": (ffn_ref, acc_one),
        "a": (wa_ref, w_a), "x": (x_ref, x_own), "mid": (mid_ref, middle),
        "g": (g_ref, g_own), "q": (q_ref, q_all), "k": (k_ref, k_all), "v": (v_ref, v_all),
        "att": (att_ref, att_all),
    }

    def load(name):
        src, dst = loads[name]
        return pltpu.make_async_copy(src, dst, load_sems.at[slots + list(loads).index(name)])

    def load_b(k):
        return pltpu.make_async_copy(wb_ref.at[k], w_b.at[k], load_sems.at[k])

    load_b(slots - 1).start()
    load("h2").start()
    load("e").start()
    load("ffn").start()
    load("x").start()
    load("mid").start()
    for k in reversed(range(slots - 1)):
        load_b(k).start()
    for name in loads:
        if name not in ("h1", "h2", "e", "ffn", "x", "mid"):
            load(name).start()
    place.greet(True)
    load("h2").wait()
    load("e").wait()
    load("ffn").wait()

    strip = length // 2
    key_sum, value_sum = acc_two.at[:, :LANES], acc_two.at[:, LANES : 2 * LANES]

    def away_copy(n, p):
        return remote(("away", n, p), away.at[p], back.at[p], place.device(rank=other))

    def swap(name, src, dst):
        return [
            remote((name, j), src.at[place.at_slot(j)], dst.at[slot],
                   place.device(slot=place.at_slot(j)))
            for j in (2, 3, 1)
        ]

    def keep(n, src, dst):
        return pltpu.make_async_copy(src, dst.at[slot], own_sems.at[n])

    def send_away(n, acc):
        if n > 0:
            pl.semaphore_wait(credit, 1)
        for p in range(slots):
            if n > 0:
                away_copy(n - 1, p).wait_send()
            away[p] = acc[position(p, other), :].astype(BF16)
            away_copy(n, p).start()

    def taken():
        pl.semaphore_signal(credit, inc=1, device_id=place.device(rank=other), device_id_type=MESH)

    live = live_ref[...]

    def block_delta():
        load("x").wait()
        load("mid").wait()
        for p in range(slots):
            away_copy(0, p).wait_recv()
            out = acc_one[position(p, place.rank), :] + back[p].astype(F32)
            delta_own[p] = ((middle[p] - x_own[p].astype(F32) + out) * live).astype(BF16)
        taken()
        for copy in swap("block", delta_own, block_out):
            copy.start()
        keep(0, delta_own.at[slot], block_out).start()

    def units(i, carry):
        k = slots - 1 - i
        load_b(k).wait()

        def strips(n, carry):
            at = pl.ds(pl.multiple_of(n * strip, strip), strip)
            inner = normed_all[at, :]
            gate = dot_nt(inner, w_b[k, :ffn_cols, :])
            up = dot_nt(inner, w_b[k, ffn_cols : 2 * ffn_cols, :])
            sigmoid_gate = 1.0 / (1.0 + jnp.exp(-gate))
            activated = gate * sigmoid_gate
            hid = (activated * up).astype(BF16)
            hidden[at, :] = hid
            d_hidden = dot_nt(e_all[at, :], w_b[k, 2 * ffn_cols :, :])
            dg = (d_hidden * up * sigmoid_gate * (1.0 + gate * (1.0 - sigmoid_gate))).astype(BF16)
            du = (d_hidden * activated).astype(BF16)
            d_gate[at, :] = dg
            d_project[at, :ffn_cols] = du
            d_in = dot_nn(dg, w_b[k, :ffn_cols, :]) + dot_nn(du, w_b[k, ffn_cols : 2 * ffn_cols, :])

            @pl.when(i == 0)
            def _():
                acc_one[at, :] += dot_nn(hid, w_b[k, 2 * ffn_cols :, :])
                acc_two[at, :] = d_in

            @pl.when(i > 0)
            def _():
                acc_two[at, :] += d_in

            return carry

        lax.fori_loop(0, length // strip, strips, 0)
        w_b[k, 2 * ffn_cols :, :] = dot_tn(hidden[...], e_all[...]).astype(BF16)
        w_b[k, :ffn_cols, :] = dot_tn(d_gate[...], normed_all[...]).astype(BF16)
        w_b[k, ffn_cols : 2 * ffn_cols, :] = dot_tn(d_project[:, :ffn_cols], normed_all[...]).astype(BF16)
        launch("b", k)

        @pl.when(i == 0)
        def _():
            send_away(0, acc_one)

        @pl.when(i == 1)
        def _():
            block_delta()

        @pl.when(i > 0)
        def _():
            second("b", k + 1)

        @pl.when(i > 1)
        def _():
            third("b", k + 2, True)

        return carry

    lax.fori_loop(0, slots, units, 0)
    load("h1").start()

    def share(p):
        where = e_all.at[position(p, place.rank), :]
        return remote(("share", p), where, where, place.device(rank=other))

    send_away(1, acc_two)
    load("g").wait()
    gain_sum[...] = jnp.zeros_like(gain_sum)
    for p in range(slots):
        value = middle[p]
        inverse = lax.rsqrt(jnp.mean(value * value, axis=-1, keepdims=True) + EPSILON)
        normed = value * inverse
        away_copy(1, p).wait_recv()
        d_normed = acc_two[position(p, place.rank), :] + back[p].astype(F32)
        gain_sum[1:2, :] += jnp.sum(normed * d_normed, axis=0, keepdims=True)
        delta = norm_back(d_normed * gains_ref[1:2, :], normed, inverse)
        middle[p] = delta
        e_all[position(p, place.rank), :] = (g_own[p].astype(F32) * live + delta).astype(BF16)
        share(p).start()
    taken()

    for name in ("a", "h1", "q", "k", "v", "att"):
        load(name).wait()
    for p in range(slots):
        share(p).wait_recv()

    def first_copy(k):
        return remote(None, v_all.at[k], first_out.at[slot],
                      place.device(slot=place.source(k)),
                      first_sems.at[0, k], first_sems.at[1, slot])

    def heads(i, carry):
        k = slots - 1 - i
        lane = lanes(k, LANES)
        d_att = dot_nt(e_all[...], w_a[k, 3 * head_cols :, :]).astype(BF16)
        product = (d_att.astype(F32) * att_all[:, lane].astype(F32)).T
        inner = [
            jnp.sum(product[:64], axis=0, keepdims=True),
            jnp.sum(product[64:], axis=0, keepdims=True),
        ]
        key_sum[...] = jnp.zeros_like(key_sum)
        value_sum[...] = jnp.zeros_like(value_sum)
        k_turned = k_all[k].T
        for step in range(length // BLOCK):
            begin, keys = step * BLOCK, (step + 1) * BLOCK
            low = first_key(begin, length)
            queries = two_heads(q_all[k, begin:keys, :])
            d_out = two_heads(d_att[begin:keys, :])
            scores = dot_nt(k_all[k, low:keys, :], queries)
            log_total = jnp.concatenate(
                [lse_ref[k, 0:1, begin:keys], lse_ref[k, 1:2, begin:keys]], axis=1
            )
            chances = jnp.where(seen(first_ref, begin, low, keys - low), jnp.exp(scores - log_total), 0.0)
            d_chances = dot_nt(v_all[k, low:keys, :], d_out)
            rest = jnp.concatenate([inner[0][:, begin:keys], inner[1][:, begin:keys]], axis=1)
            d_scores = (chances * (d_chances - rest)).astype(BF16)
            key_sum[low:keys, :] += dot_nn(d_scores, queries)
            value_sum[low:keys, :] += dot_nn(chances.astype(BF16), d_out)
            d_query = one_pair(dot_nn(k_turned[:, low:keys], d_scores), BLOCK) * 0.125
            d_project[begin:keys, :LANES] = (
                d_query * cos_ref[begin:keys, :] - swap_halves(d_query) * sin_ref[begin:keys, :]
            ).astype(BF16)
        d_key = key_sum[...]
        d_project[:, LANES : 2 * LANES] = (
            d_key * cos_ref[...] - swap_halves(d_key) * sin_ref[...]
        ).astype(BF16)
        d_value = (0.5 * value_sum[...]).astype(BF16)
        d_project[:, 2 * LANES :] = d_value
        v_all[k] = d_value

        @pl.when(k > 0)
        def _():
            first_copy(k).start()

        @pl.when(k == 0)
        def _():
            keep(2, v_all.at[0], first_out).start()

        for n in range(2):
            at = pl.ds(n * strip, strip)
            d_in = dot_nn(d_project[at, :], w_a[k, : 3 * head_cols, :])

            @pl.when(i == 0)
            def _():
                acc_one[at, :] = d_in

            @pl.when(i > 0)
            def _():
                acc_one[at, :] += d_in

        w_a[k, : 3 * head_cols, :] = dot_tn(d_project[...], normed_all[...]).astype(BF16)
        w_a[k, 3 * head_cols :, :] = dot_tn(att_all[:, lane], e_all[...]).astype(BF16)
        launch("a", k)

        @pl.when(i == 0)
        def _():
            second("b", 0)
            fourth("b", 3)
            third("b", 1, True)

        @pl.when(i == 1)
        def _():
            fourth("b", 2)
            third("b", 0, False)

        @pl.when(i == 2)
        def _():
            second("a", 3)
            fourth("b", 1)

        @pl.when(i == 3)
        def _():
            finish("b")

        return carry

    lax.fori_loop(0, slots, heads, 0)

    for copy in swap("block", delta_own, block_out):
        copy.wait_send()
    keep(0, delta_own.at[slot], block_out).wait()
    send_away(2, acc_one)
    for p in range(slots):
        value = x_own[p].astype(F32)
        inverse = lax.rsqrt(jnp.mean(value * value, axis=-1, keepdims=True) + EPSILON)
        normed = value * inverse
        away_copy(2, p).wait_recv()
        d_normed = acc_one[position(p, place.rank), :] + back[p].astype(F32)
        gain_sum[0:1, :] += jnp.sum(normed * d_normed, axis=0, keepdims=True)
        delta = norm_back(d_normed * gains_ref[0:1, :], normed, inverse)
        delta_own[p] = ((middle[p] + delta) * live).astype(BF16)
    input_copies = swap("input", delta_own, input_out)
    input_copies[0].start()
    keep(1, delta_own.at[slot], input_out).start()

    def gain_copies(level):
        if level == 0:
            return [
                remote(("gain", 0, d), gain_seq.at[place.seq], gain_seq.at[place.seq],
                       place.device(seq=place.at_seq(d)))
                for d in range(1, n_seq)
            ]
        if level == 1:
            return [
                remote(("gain", 1, j), gain_slot.at[slot], gain_slot.at[slot],
                       place.device(slot=place.at_slot(j)))
                for j in range(1, slots)
            ]
        return [
            remote(("gain", 2, 0), gain_rank.at[place.rank], gain_rank.at[place.rank],
                   place.device(rank=other))
        ]

    def gain_step(level):
        value = gain_sum[...]
        if level > 0:
            for copy in gain_copies(level - 1):
                copy.wait_recv()
            held = (gain_seq, gain_slot, gain_rank)[level - 1]
            value = held[0]
            for j in range(1, held.shape[0]):
                value = value + held[j]
        if level == 3:
            gains_out[...] = value
            return
        target = (gain_seq, gain_slot, gain_rank)[level]
        target[(place.seq, slot, place.rank)[level]] = value
        for copy in gain_copies(level):
            copy.start()

    blocks = root_ref.shape[1]
    jobs = [("b", m, b) for m in range(3) for b in range(blocks)]
    jobs += [("a", m, b) for m in range(4) for b in range(blocks)]
    members = {"a": (0, 1, 2, 5), "b": (3, 4, 6)}
    small = {"a": (head_root, head_buf, step_a), "b": (unit_root, unit_buf, step_b)}
    depth = 8

    def job_root(n):
        acc = (acc_two, acc_one)[n % depth // 4]
        return acc.at[pl.ds(n % 4 * part, part)]

    def job_loads(n):
        sec, m, b = jobs[n]
        root_in, held, _ = small[sec]
        pairs = ((root_ref.at[members[sec][m], b], job_root(n)), (root_in.at[m, b], held.at[n % depth]))
        return [
            pltpu.make_async_copy(src, dst, step_sems.at[0, n % depth, i])
            for i, (src, dst) in enumerate(pairs)
        ]

    def job_store(n):
        sec, m, b = jobs[n]
        _, held, step = small[sec]
        high = held.shape[1]
        return pltpu.make_async_copy(
            job_root(n).at[pl.ds(0, high), pl.ds(0, part)],
            step.at[pl.ds((m * blocks + b) * high, high)], step_sems.at[1, n % depth, 0],
        )

    def run_jobs(first, last):
        for n in range(first, last):
            sec, m, b = jobs[n]
            root = job_root(n)
            held = small[sec][1]
            high = held.shape[1]
            for copy in job_loads(n):
                copy.wait()
            grad = sections[sec][6][pl.ds((m * blocks + b) * high, high), :]
            turned = dot_nn(held[n % depth].astype(BF16), grad).astype(BF16)
            turned = dot_nt(turned, root[...].astype(BF16))
            scale = lax.rsqrt(jnp.mean(turned * turned, axis=0, keepdims=True) + EPSILON)
            root[pl.ds(0, high), pl.ds(0, part)] = turned * scale
            job_store(n).start()
            if n > 0 and n - 1 + depth < len(jobs):
                job_store(n - 1).wait()
                for copy in job_loads(n - 1 + depth):
                    copy.start()

    def full_copy(sec):
        i = sections[sec][0]
        return pltpu.make_async_copy(
            sections[sec][6], (full_a_out, full_b_out)[i], step_sems.at[1, i, 1]
        )

    for n in range(depth):
        for copy in job_loads(n):
            copy.start()
    gain_step(0)
    second("a", 2)
    third("a", 3, True)
    input_copies[1].start()
    relay("b")
    second("a", 1)
    third("a", 2, True)
    fourth("a", 3)
    input_copies[2].start()
    gain_step(1)
    second("a", 0)
    third("a", 1, True)
    fourth("a", 2)
    for copy in gather_copies("b")[1]:
        copy.wait_recv()
    own_copy("b").wait()
    full_copy("b").start()
    run_jobs(0, 2)
    gain_step(2)
    third("a", 0, False)
    fourth("a", 1)
    run_jobs(2, 4)
    gain_step(3)
    finish("a")
    run_jobs(4, 6)
    relay("a")
    for copy in gather_copies("a")[1]:
        copy.wait_recv()
    own_copy("a").wait()
    full_copy("a").start()
    run_jobs(6, len(jobs))
    for n in range(len(jobs) - depth, len(jobs)):
        job_store(n).wait()
    full_copy("a").wait()
    full_copy("b").wait()
    for sec in ("b", "a"):
        near, far = gather_copies(sec)
        for copy in far:
            copy.wait_send()
        for copy in near:
            copy.wait_send()
        for k in range(slots):
            for copy in near_copies(sec, k) + next_copies(sec, k):
                copy.wait_send()
            if k > 0:
                far_copy(sec, k).wait_send()
    for copy in swap("block", delta_own, block_out):
        copy.wait_recv()
    for copy in swap("input", delta_own, input_out):
        copy.wait()
    for j in range(1, slots):
        source = place.at_slot(j)
        remote(None, v_all.at[0], first_out.at[source], elsewhere,
               first_sems.at[0, 0], first_sems.at[1, source]).wait_recv()
        first_copy(j).wait_send()
    for p in range(slots):
        away_copy(2, p).wait_send()
        share(p).wait_send()
    for level in range(3):
        for copy in gain_copies(level):
            copy.wait_send()
    keep(1, delta_own.at[slot], input_out).wait()
    keep(2, v_all.at[0], first_out).wait()


def backward_part(n_seq, n_head, head_cols, saved, gains, tables, live, roots):
    (
        x_own, h_one, q_rot, k_rot, v_mix, attended, log_total, weights_a, weights_b, middle, h_two,
        grad_own, e_all, ffn,
    ) = saved
    cos_wide, sin_wide, first_pos = tables
    _, roots_head, roots_unit = roots
    slots, rows, width = x_own.shape
    length = h_one.shape[0]
    rows_a, rows_b = weights_a.shape[1], weights_b.shape[1]
    part = width // n_seq
    ranks = n_head // slots
    any_space = pl.BlockSpec(memory_space=pl.ANY)
    vmem = pl.BlockSpec(memory_space=pltpu.VMEM)
    shape = jax.ShapeDtypeStruct
    like = lambda value: pltpu.VMEM(value.shape, value.dtype)
    count = 2 * 4 + 3 * slots + slots + 2 * (slots - 1) + n_seq + slots + 4
    sem = pltpu.SemaphoreType.DMA
    return pl.pallas_call(
        functools.partial(backward_kernel, n_seq, n_head, head_cols),
        in_specs=[any_space] * 16 + [vmem] * 6,
        out_specs=[any_space] * 3 + [vmem] * 3 + [any_space] * 4,
        out_shape=[
            shape(x_own.shape, BF16),
            shape(x_own.shape, BF16),
            shape((slots, length, head_cols), BF16),
            shape((8, width), F32),
            shape((rows_a, part), BF16),
            shape((rows_b, part), BF16),
            shape((rows_a, width), BF16),
            shape((rows_b, width), BF16),
            shape((rows_a, part), F32),
            shape((rows_b, part), F32),
        ],
        scratch_shapes=[
            like(weights_a), like(weights_b), like(h_two), like(e_all), like(x_own), like(middle),
            like(grad_own),
            like(q_rot), like(k_rot), like(v_mix), like(attended),
            pltpu.VMEM((length, width), F32),
            pltpu.VMEM((length, width), F32),
            pltpu.VMEM((length, rows_b // 3), BF16),
            pltpu.VMEM((length, rows_b // 3), BF16),
            pltpu.VMEM((length, 3 * LANES), BF16),
            like(x_own), like(x_own), like(x_own),
            pltpu.VMEM((rows_a, width), BF16),
            pltpu.VMEM((rows_b, width), BF16),
            pltpu.VMEM((8,) + roots_head.shape[2:], F32),
            pltpu.VMEM((8,) + roots_unit.shape[2:], F32),
            pltpu.VMEM((slots, 4, rows_a // 2, part), BF16),
            pltpu.VMEM((slots, 4, rows_b // 2, part), BF16),
            pltpu.VMEM((slots, 2, rows_a // 2, part), BF16),
            pltpu.VMEM((slots, 2, rows_b // 2, part), BF16),
            pltpu.VMEM((slots + 1, rows_a, part), BF16),
            pltpu.VMEM((slots + 1, rows_b, part), BF16),
            pltpu.VMEM((8, width), F32),
            pltpu.VMEM((n_seq, 8, width), F32),
            pltpu.VMEM((slots, 8, width), F32),
            pltpu.VMEM((ranks, 8, width), F32),
            sem((2, count)),
            sem((2, 2, slots, 4)),
            sem((2, 2, slots, 2)),
            sem((2, 2, slots + 1)),
            sem((2, slots)),
            sem((slots + 12,)),
            sem((5,)),
            sem((2, 8, 2)),
            pltpu.SemaphoreType.REGULAR,
        ],
        compiler_params=pltpu.CompilerParams(
            collective_id=2, has_side_effects=True, vmem_limit_bytes=64 << 20
        ),
    )(
        weights_a, weights_b, h_one, h_two, x_own, middle, grad_own, q_rot, k_rot, v_mix, attended,
        e_all, ffn, *roots, log_total, gains, cos_wide, sin_wide, first_pos[None, :], live,
    )


def reduce_kernel(
    n_seq, n_head, chunks,
    block_ref, input_ref, first_ref, gains_ref, grads_a, grads_b,
    block_out, input_out, first_out, gains_out, sum_a, sum_b, full_a, full_b,
    near_a, near_b, turn_a, turn_b, far_a, far_b, gain_seq, gain_slot, gain_rank,
    send_sems, recv_sems, own_sems, far_recv, first_recv,
):
    slots = block_ref.shape[0]
    place = Place(n_seq, n_head, slots)
    place.greet(True)
    sender = Sender(send_sems, recv_sems)
    part = sum_a.shape[1]
    mine = lanes(place.seq, part)
    order = [2, 3, 1, 0]
    parts = ((grads_b, sum_b, full_b, near_b, turn_b, far_b, chunks[1]),
             (grads_a, sum_a, full_a, near_a, turn_a, far_a, chunks[0]))
    copies, received = [], []

    def arrive(copy):
        copy.wait_recv()
        received.append(copy)

    def swap(src, dst):
        return [
            sender.start(
                src.at[place.at_slot(k)], dst.at[place.slot], place.device(slot=place.at_slot(k))
            )
            for k in (2, 3, 1)
        ]

    gain_seq[place.seq] = gains_ref[...]
    small = [
        sender.start(gain_seq.at[place.seq], gain_seq.at[place.seq],
                     place.device(seq=place.at_seq(d)))
        for d in range(1, n_seq)
    ]
    copies += small

    def to_seqs(grads, near, k):
        return [
            sender.start(
                grads.at[k, :, lanes(place.at_seq(d), part)],
                near.at[k, d - 1],
                place.device(seq=place.at_seq(d)),
            )
            for d in range(1, n_seq)
        ]

    sent = {}
    units = [(which, k) for which in range(2) for k in order]

    def launch(unit):
        which, k = unit
        sent[unit] = to_seqs(parts[which][0], parts[which][3], k)
        copies.extend(sent[unit])

    own = [
        pltpu.make_async_copy(src, dst.at[place.slot], own_sems.at[i])
        for i, (src, dst) in enumerate(
            (
                (block_ref.at[place.slot], block_out),
                (input_ref.at[place.slot], input_out),
                (first_ref.at[0], first_out),
            )
        )
    ]
    for copy in own:
        copy.start()
    launch(units[0])
    launch(units[1])
    copies += swap(block_ref, block_out)
    for copy in small:
        arrive(copy)
    total = gain_seq[0]
    for i in range(1, n_seq):
        total = total + gain_seq[i]
    gain_slot[place.slot] = total
    small = [
        sender.start(gain_slot.at[place.slot], gain_slot.at[place.slot],
                     place.device(slot=place.at_slot(k)))
        for k in range(1, slots)
    ]
    copies += small
    elsewhere = place.device(seq=place.at_seq(1))
    for index, unit in enumerate(units):
        which, k = unit
        grads, _, _, near, turn, far, chunk = parts[which]
        if index + 2 < len(units):
            launch(units[index + 2])
        for copy in sent[unit]:
            arrive(copy)

        def add(i, carry, grads=grads, near=near, turn=turn, k=k, chunk=chunk):
            rows = pl.ds(pl.multiple_of(i * chunk, chunk), chunk)
            value = grads[k, rows, mine].astype(F32)
            for d in range(n_seq - 1):
                value = value + near[k, d, rows, :].astype(F32)
            turn[k, rows, :] = value.astype(BF16)
            return carry

        lax.fori_loop(0, grads.shape[1] // chunk, add, 0)
        if k != 0:
            copy = sender.start(
                turn.at[k], far.at[place.slot], place.device(slot=place.source(k)),
                far_recv.at[which, place.slot],
            )
            copies.append(copy)
            received.append(copy)
        if index == 1:
            for j in range(1, slots):
                copy = sender.start(
                    first_ref.at[j], first_out.at[place.slot],
                    place.device(slot=place.source(j)), first_recv.at[place.slot],
                )
                copies.append(copy)
                received.append(copy)
        if index == 4:
            copies += swap(input_ref, input_out)
            for copy in small:
                arrive(copy)
            total = gain_slot[0]
            for i in range(1, slots):
                total = total + gain_slot[i]
            gain_rank[place.rank] = total
            small = [
                sender.start(gain_rank.at[place.rank], gain_rank.at[place.rank],
                             place.device(rank=(place.rank + j) % place.ranks))
                for j in range(1, place.ranks)
            ]
            copies += small
        if k == 0:
            for j in range(1, slots):
                source = place.at_slot(j)
                pltpu.make_async_remote_copy(
                    src_ref=turn.at[0], dst_ref=far.at[source], send_sem=send_sems.at[0],
                    recv_sem=far_recv.at[which, source], device_id=elsewhere, device_id_type=MESH,
                ).wait_recv()
            _, total_ref, full, _, _, _, _ = parts[which]

            def finish(i, carry, turn=turn, far=far, total_ref=total_ref, full=full, chunk=chunk):
                rows = pl.ds(pl.multiple_of(i * chunk, chunk), chunk)
                value = turn[0, rows, :].astype(F32)
                for j in range(1, slots):
                    value = value + far[place.at_slot(j), rows, :].astype(F32)
                value = value.astype(BF16)
                total_ref[rows, :] = value
                full[rows, mine] = value
                return carry

            lax.fori_loop(0, grads.shape[1] // chunk, finish, 0)
            copies += [
                sender.start(total_ref, full.at[:, mine], place.device(seq=place.at_seq(d)))
                for d in range(1, n_seq)
            ]
    for copy in small:
        arrive(copy)
    total = gain_rank[0]
    for i in range(1, place.ranks):
        total = total + gain_rank[i]
    gains_out[...] = total
    for copy in copies:
        if all(copy is not other for other in received):
            copy.wait_recv()
    for j in range(1, slots):
        source = place.at_slot(j)
        pltpu.make_async_remote_copy(
            src_ref=first_ref.at[0], dst_ref=first_out.at[source], send_sem=send_sems.at[0],
            recv_sem=first_recv.at[source], device_id=elsewhere, device_id_type=MESH,
        ).wait_recv()
    for copy in copies:
        copy.wait_send()
    for copy in own:
        copy.wait()


def reduce_grads(n_seq, n_head, chunks, block_delta, input_delta, first_delta, gains, grads_a, grads_b):
    slots = block_delta.shape[0]
    part = grads_a.shape[2] // n_seq
    rows = (grads_a.shape[1], grads_b.shape[1])
    ranks = n_head // slots
    count = (
        3 * (slots - 1) + 2 * (slots * (n_seq - 1) + (slots - 1) + (n_seq - 1))
        + (n_seq - 1) + (slots - 1) + (ranks - 1)
    )
    any_space = pl.BlockSpec(memory_space=pl.ANY)
    vmem = pl.BlockSpec(memory_space=pltpu.VMEM)
    like = lambda value: jax.ShapeDtypeStruct(value.shape, value.dtype)
    return pl.pallas_call(
        functools.partial(reduce_kernel, n_seq, n_head, chunks),
        in_specs=[any_space] * 3 + [vmem] * 3,
        out_specs=[any_space] * 3 + [vmem] * 5,
        out_shape=[like(block_delta), like(input_delta), like(first_delta), like(gains)]
        + [jax.ShapeDtypeStruct((r, part), BF16) for r in rows]
        + [jax.ShapeDtypeStruct((r, part * n_seq), BF16) for r in rows],
        scratch_shapes=[pltpu.VMEM((slots, n_seq - 1, r, part), BF16) for r in rows]
        + [pltpu.VMEM((slots, r, part), BF16) for r in rows]
        + [pltpu.VMEM((slots, r, part), BF16) for r in rows]
        + [pltpu.VMEM((n,) + gains.shape, F32) for n in (n_seq, slots, ranks)]
        + [
            pltpu.SemaphoreType.DMA((count,)),
            pltpu.SemaphoreType.DMA((count,)),
            pltpu.SemaphoreType.DMA((3,)),
            pltpu.SemaphoreType.DMA((2, slots)),
            pltpu.SemaphoreType.DMA((slots,)),
        ],
        compiler_params=pltpu.CompilerParams(
            collective_id=1, has_side_effects=True, vmem_limit_bytes=56 << 20
        ),
    )(block_delta, input_delta, first_delta, gains, grads_a, grads_b)


def shampoo_kernel(
    stat_ref, root_ref, head_stat, head_root, unit_stat, unit_root, full_a, sum_a, full_b, sum_b,
    wide_ref, out_right_ref, new_head, new_unit, step_a, step_b,
):
    step = pl.program_id(0)
    blocks = stat_ref.shape[1]

    def one(member, width, small_stat, small_root, full, total, big_out, small_out, step_out):
        for b in range(blocks):
            rows = pl.ds(pl.multiple_of((member * blocks + b) * width, 16), width)
            grad, own = full[rows, :], total[rows, :]
            big_out[0, b] = STAT_DECAY * stat_ref[0, b] + (1.0 - STAT_DECAY) * dot_tn(own, grad)
            small_out[member, b] = STAT_DECAY * small_stat[member, b] + (
                1.0 - STAT_DECAY
            ) * dot_nt(grad, grad)
            turned = dot_nn(small_root[member, b].astype(BF16), grad).astype(BF16)
            turned = dot_nt(turned, root_ref[0, b].astype(BF16))
            scale = lax.rsqrt(jnp.mean(turned * turned, axis=0, keepdims=True) + EPSILON)
            step_out[rows, :] = turned * scale

    head_width, unit_width = head_stat.shape[2], unit_stat.shape[2]
    head_args = (head_width, head_stat, head_root, full_a, sum_a)
    unit_args = (unit_width, unit_stat, unit_root, full_b, sum_b)

    @pl.when(step < 3)
    def _():
        one(step, *head_args, wide_ref, new_head, step_a)

    @pl.when((step >= 3) & (step < 6))
    def _():
        one(step - 3, *unit_args, wide_ref, new_unit, step_b)

    @pl.when(step == 6)
    def _():
        one(3, *head_args, out_right_ref, new_head, step_a)


def shampoo(stats_wide, roots_wide, stats_head, roots_head, stats_unit, roots_unit, full_a, sum_a, full_b, sum_b):
    members, blocks, part, width = stats_wide.shape
    member = lambda i: (jnp.where(i == 5, 6, jnp.where(i == 6, 5, i)), 0, 0, 0)
    wide = pl.BlockSpec((1, blocks, part, width), member)
    vmem = pl.BlockSpec(memory_space=pltpu.VMEM)
    return pl.pallas_call(
        shampoo_kernel,
        grid=(members,),
        in_specs=[wide, wide] + [vmem] * 8,
        out_specs=[
            pl.BlockSpec((1, blocks, part, width), lambda i: (jnp.minimum(i, 5), 0, 0, 0)),
            pl.BlockSpec((1, blocks, part, width), lambda i: (0, 0, 0, 0)),
            vmem, vmem, vmem, vmem,
        ],
        out_shape=[
            jax.ShapeDtypeStruct((members - 1, blocks, part, width), F32),
            jax.ShapeDtypeStruct((1, blocks, part, width), F32),
            jax.ShapeDtypeStruct(stats_head.shape, F32),
            jax.ShapeDtypeStruct(stats_unit.shape, F32),
            jax.ShapeDtypeStruct(sum_a.shape, F32),
            jax.ShapeDtypeStruct(sum_b.shape, F32),
        ],
        compiler_params=pltpu.CompilerParams(vmem_limit_bytes=48 << 20),
    )(stats_wide, roots_wide, stats_head, roots_head, stats_unit, roots_unit, full_a, sum_a, full_b, sum_b)


def finish_kernel(
    blocks, stat_ref, head_stat, unit_stat, full_a, sum_a, full_b, sum_b, step_a, step_b,
    w_qkv, w_gate_up, w_out, w_down, gains_ref, norm_ref,
    block_got, x_ref, input_got, g_ref, first_got,
    wide_ref, right_ref, new_head, new_unit, grad_qkv, grad_gate_up, grad_out, grad_down,
    new_qkv, new_gate_up, new_out, new_down, grad_gains, new_gains, block_out, input_out, first_out,
):
    step = pl.program_id(0)
    member, b = step // blocks, step % blocks

    def one(m, small_stat, full, total, big_out, small_out):
        width = small_stat.shape[2]
        rows = pl.ds(pl.multiple_of((m * blocks + b) * width, 16), width)
        grad, own = full[rows, :], total[rows, :]
        big_out[0, 0] = STAT_DECAY * stat_ref[0, 0] + (1.0 - STAT_DECAY) * dot_tn(own, grad)
        small_out[m, b] = STAT_DECAY * small_stat[m, b] + (1.0 - STAT_DECAY) * dot_nt(grad, grad)

    head_args, unit_args = (head_stat, full_a, sum_a), (unit_stat, full_b, sum_b)

    @pl.when(member < 3)
    def _():
        one(member, *head_args, wide_ref, new_head)

    @pl.when((member >= 3) & (member < 6))
    def _():
        one(member - 3, *unit_args, wide_ref, new_unit)

    @pl.when(member == 6)
    def _():
        one(3, *head_args, right_ref, new_head)

    @pl.when(step % 4 == 0)
    def _():
        block_out[...] = x_ref[...].astype(F32) + block_got[...].astype(F32)

    @pl.when(step % 4 == 1)
    def _():
        input_out[...] = g_ref[...].astype(F32) + input_got[...].astype(F32)

    @pl.when(step % 4 == 2)
    def _():
        first_out[...] = first_got[...].astype(F32)

    def stepped(i, at, total, steps, old, grad_ref, new_ref, turn):
        grad, change = total[at, :].astype(F32), STEP_RATE * steps[at, :]
        grad_ref[i] = grad.T if turn else grad
        new_ref[i] = old[i] - (change.T if turn else change)

    high = w_qkv.shape[2]
    for i in range(3):
        @pl.when(step == i)
        def _(i=i):
            stepped(i, pl.ds(i * high, high), sum_a, step_a, w_qkv, grad_qkv, new_qkv, True)

    tall = w_gate_up.shape[1]
    for i in range(2):
        @pl.when(step == 3 + i)
        def _(i=i):
            stepped(
                i, pl.ds(i * tall, tall), sum_b, step_b, w_gate_up, grad_gate_up, new_gate_up, False
            )

    @pl.when(step == 5)
    def _():
        at = pl.ds(3 * high, high)
        grad_out[...] = sum_a[at, :].astype(F32)
        new_out[...] = w_out[...] - OUT_RATE * step_a[at, :]

    @pl.when(step == 6)
    def _():
        at = pl.ds(2 * tall, tall)
        grad_down[...] = sum_b[at, :].astype(F32)
        new_down[...] = w_down[...] - STEP_RATE * step_b[at, :]

    @pl.when(step == 7)
    def _():
        gains = gains_ref[0:2, :]
        grad_gains[...] = gains
        scale = lax.rsqrt(jnp.mean(gains * gains, axis=-1, keepdims=True) + EPSILON)
        new_gains[...] = norm_ref[...] - GAIN_RATE * gains * scale


def finish(
    stats_wide, stats_head, stats_unit, full_a, sum_a, full_b, sum_b, step_a, step_b,
    w_qkv, w_gate_up, w_out, w_down, gains, norm_gains,
    block_got, layer_input, input_got, out_grad, first_got,
):
    members, blocks, part, width = stats_wide.shape
    slots, rows, _ = layer_input.shape
    length, head_cols = first_got.shape[1:]
    steps = 4 * slots

    def source(i):
        m = jnp.minimum(i // blocks, members - 1)
        return jnp.where(m == 5, 6, jnp.where(m == 6, 5, m)), i % blocks, 0, 0

    last = (members - 1) * blocks
    block = (1, 1, part, width)

    def right(i):
        return 0, jnp.clip(i - last, 0, blocks - 1), 0, 0

    def wide(i):
        at = jnp.minimum(i, last - 1)
        return at // blocks, at % blocks, 0, 0

    vmem = pl.BlockSpec(memory_space=pltpu.VMEM)
    tokens = pl.BlockSpec((1, rows, width), lambda i: (i // 4, 0, 0))
    firsts = pl.BlockSpec((1, length, head_cols), lambda i: (i // 4, 0, 0))
    like = lambda *values: [jax.ShapeDtypeStruct(v.shape, F32) for v in values]
    weights = (w_qkv, w_gate_up, w_out, w_down)
    return pl.pallas_call(
        functools.partial(finish_kernel, blocks),
        grid=(steps,),
        in_specs=[pl.BlockSpec(block, source)] + [vmem] * 14 + [tokens] * 4 + [firsts],
        out_specs=[pl.BlockSpec(block, wide), pl.BlockSpec(block, right)] + [vmem] * 12
        + [tokens, tokens, firsts],
        out_shape=[
            jax.ShapeDtypeStruct((members - 1, blocks, part, width), F32),
            jax.ShapeDtypeStruct((1, blocks, part, width), F32),
        ]
        + like(stats_head, stats_unit, *weights, *weights, norm_gains, norm_gains, layer_input, out_grad, first_got),
        compiler_params=pltpu.CompilerParams(vmem_limit_bytes=60 << 20),
    )(
        stats_wide, stats_head, stats_unit, full_a, sum_a, full_b, sum_b, step_a, step_b,
        w_qkv, w_gate_up, w_out, w_down, gains, norm_gains,
        block_got, layer_input, input_got, out_grad, first_got,
    )


class Links:
    def __init__(self, n_seq, n_head, slots):
        self.n_seq, self.n_head, self.slots = n_seq, n_head, slots
        self.ranks = n_head // slots
        self.slot = lax.axis_index("head") // self.ranks
        self.rank = lax.axis_index("head") % self.ranks

    def permute(self, value, partner):
        pairs = []
        for s in range(self.n_seq):
            for h in range(self.n_head):
                to_s, to_h = partner(s, h)
                pairs.append((s * self.n_head + h, to_s * self.n_head + to_h))
        return lax.ppermute(value, AXES, pairs)

    def swap_slots(self, value):
        got = [lax.dynamic_index_in_dim(value, self.slot, 0, keepdims=False)]
        for step in range(1, self.slots):
            piece = lax.dynamic_index_in_dim(value, self.slot ^ step, 0, keepdims=False)
            got.append(self.permute(piece, lambda s, h: (s, h ^ (step * self.ranks))))
        got = jnp.stack(got)
        return jnp.stack(
            [lax.dynamic_index_in_dim(got, self.slot ^ q, 0, keepdims=False) for q in range(self.slots)]
        )

    def gather_ranks(self, value):
        got = [value] + [
            self.permute(value, lambda s, h: (s, h ^ step)) for step in range(1, self.ranks)
        ]
        got = jnp.stack(got)
        return jnp.stack(
            [lax.dynamic_index_in_dim(got, self.rank ^ r, 0, keepdims=False) for r in range(self.ranks)]
        )

    def sum_ranks(self, value):
        total = lax.dynamic_index_in_dim(value, self.rank, 0, keepdims=False)
        for step in range(1, self.ranks):
            piece = lax.dynamic_index_in_dim(value, self.rank ^ step, 0, keepdims=False)
            got = self.permute(piece.astype(BF16), lambda s, h: (s, h ^ step))
            total = total + got.astype(F32)
        return total

    def whole_sequence(self, own):
        both = self.gather_ranks(own)
        return jnp.swapaxes(both, 0, 1).reshape(-1, own.shape[-1])

    def own_sum(self, full):
        rows = full.shape[0] // (self.slots * self.ranks)
        parts = full.reshape(self.slots, self.ranks, rows, full.shape[-1])
        return self.sum_ranks(jnp.swapaxes(parts, 0, 1)).reshape(-1, full.shape[-1])


def backward_plain(n_seq, n_head, head_cols, ffn_cols, links, saved, gains, tables, is_live):
    (
        x_bf16, h_one, q_rot, k_rot, v_mix, attended, log_total, weights_a, weights_b, middle,
        h_two, grad_own, d_ffn, _,
    ) = saved
    cos_wide, sin_wide, first_pos = tables
    slots, rows, width = x_bf16.shape
    length = h_one.shape[0]
    rows_a, rows_b = weights_a.shape[1], weights_b.shape[1]
    pairs = slots * head_cols // LANES
    per = LANES // head_cols

    def pair_major(value):
        n = value.shape[2]
        value = value.reshape(pairs, per, length, n, head_cols)
        return value.transpose(0, 2, 3, 1, 4).reshape(pairs, length, n, LANES)

    def slot_major(value):
        n = value.shape[2]
        value = value.reshape(pairs, length, n, per, head_cols)
        return value.transpose(0, 3, 1, 2, 4).reshape(slots, length, n, head_cols)

    w_in, w_o = weights_a[:, : 3 * head_cols], weights_a[:, 3 * head_cols :]
    w_gu, w_d = weights_b[:, : 2 * ffn_cols], weights_b[:, 2 * ffn_cols :]
    x_own = x_bf16.reshape(slots * rows, width).astype(F32)
    middle = middle.reshape(slots * rows, width)
    ein = functools.partial(jnp.einsum, preferred_element_type=F32)
    inverse_one = lax.rsqrt(jnp.mean(x_own * x_own, axis=-1, keepdims=True) + EPSILON)
    normed_one = x_own * inverse_one
    inverse_two = lax.rsqrt(jnp.mean(middle * middle, axis=-1, keepdims=True) + EPSILON)
    normed_two = middle * inverse_two
    saved = (q_rot, k_rot, v_mix, attended, log_total)
    attended = jnp.swapaxes(attended.reshape(length, slots, head_cols), 0, 1)
    gate_up = ein("ld,qfd->qlf", h_two, w_gu)
    gate, up = gate_up[..., :ffn_cols], gate_up[..., ffn_cols:]
    sigmoid_gate = jax.nn.sigmoid(gate)
    activated = gate * sigmoid_gate
    hidden = (activated * up).astype(BF16)
    ffn_out = links.own_sum(ein("qlf,qfd->ld", hidden, w_d))
    block_delta = jnp.where(is_live, middle - x_own + ffn_out, 0.0).astype(BF16)

    d_own = jnp.where(is_live, grad_own, jnp.zeros_like(grad_own))
    d_out = d_own.reshape(slots * rows, width).astype(F32)
    g_down = ein("qlf,ld->qfd", hidden, d_ffn)
    d_hidden = ein("ld,qfd->qlf", d_ffn, w_d)
    d_gate = (
        d_hidden * up * sigmoid_gate * (1.0 + gate * (1.0 - sigmoid_gate))
    ).astype(BF16)
    d_up = (d_hidden * activated).astype(BF16)
    d_gate_up = jnp.concatenate([d_gate, d_up], axis=2)
    d_normed_two = links.own_sum(ein("qlf,qfd->ld", d_gate_up, w_gu))
    g_gate_up = ein("qlf,ld->qfd", d_gate_up, h_two)
    grads_b = jnp.concatenate([g_gate_up.astype(BF16), g_down.astype(BF16)], axis=1)
    gain_two = jnp.sum(normed_two * d_normed_two, axis=0)
    middle_delta = norm_back(d_normed_two * gains[1], normed_two, inverse_two)
    d_middle = d_out + middle_delta
    d_attn = links.whole_sequence(d_middle.astype(BF16).reshape(slots, rows, width))
    d_attended = ein("ld,qcd->qlc", d_attn, w_o).astype(BF16)
    if per > 1:
        d_attended = pair_major(d_attended[:, :, None])[:, :, 0]
    d_project = jnp.concatenate(
        attend_back(saved, d_attended, cos_wide, sin_wide, first_pos), axis=2
    )
    if per > 1:
        d_project = slot_major(d_project.reshape(pairs, length, 3, LANES)).reshape(
            slots, length, 3 * head_cols
        )
    d_value = d_project[:, :, 2 * head_cols :]
    g_out = ein("qlc,ld->qcd", attended, d_attn)
    g_qkv = ein("qlc,ld->qcd", d_project, h_one)
    grads_a = jnp.concatenate([g_qkv.astype(BF16), g_out.astype(BF16)], axis=1)
    d_normed_one = links.own_sum(ein("qlc,qcd->ld", d_project, w_in))
    gain_one = jnp.sum(normed_one * d_normed_one, axis=0)
    input_delta = middle_delta + norm_back(d_normed_one * gains[0], normed_one, inverse_one)
    input_delta = jnp.where(is_live, input_delta, 0.0).astype(BF16)
    gain_rows = jnp.concatenate([gain_one.reshape(8, -1), gain_two.reshape(8, -1)], axis=0)

    return reduce_grads(
        n_seq,
        n_head,
        (LANES, unit_chunk(rows_b)),
        block_delta.reshape(slots, rows, width),
        input_delta.reshape(slots, rows, width),
        d_value,
        gain_rows,
        grads_a,
        grads_b,
    )


def shards(
    n_seq,
    n_head,
    layer_input,
    values_first,
    w_qkv,
    w_gate_up,
    w_out,
    w_down,
    norm_gains,
    out_grad,
    segments,
    counts,
    stats_wide,
    roots_wide,
    stats_head,
    roots_head,
    stats_unit,
    roots_unit,
):
    slots, rows, width = layer_input.shape
    length = segments.shape[1]
    row_part, head_cols, ffn_cols = w_qkv.shape[1], w_qkv.shape[2], w_gate_up.shape[2]
    head_dim = stats_head.shape[2]
    links = Links(n_seq, n_head, slots)
    is_live = links.slot < counts[0]
    pairs = slots * head_cols // LANES
    per = LANES // head_cols
    rows_a, rows_b = 4 * head_cols, 3 * ffn_cols

    fused = n_seq == 4 and slots == 4 and links.ranks == 2 and head_cols == LANES
    cos_wide, sin_wide, first_pos, live, *saved = forward_part(
        n_seq, n_head, head_cols, head_dim, layer_input, values_first, out_grad,
        (w_qkv, jnp.swapaxes(w_gate_up, 1, 2), w_out, w_down), norm_gains, segments, counts, fused,
    )
    first_pos = first_pos[0]
    tables = (cos_wide, sin_wide, first_pos)
    if fused:
        (
            block_got, input_got, first_got, gains, sum_a, sum_b, full_a, full_b, step_a, step_b
        ) = backward_part(
            n_seq, n_head, head_cols, saved, norm_gains, tables, live,
            (roots_wide, roots_head, roots_unit),
        )
        (
            wide, out_right, new_head, new_unit, grad_qkv, grad_gate_up, grad_out, grad_down,
            new_qkv, new_gate_up, new_out, new_down, grad_gains, new_gains,
            block_out, input_grad, first_grad,
        ) = finish(
            stats_wide, stats_head, stats_unit, full_a, sum_a, full_b, sum_b, step_a, step_b,
            w_qkv, jnp.swapaxes(w_gate_up, 1, 2), w_out, w_down, gains, norm_gains,
            block_got, layer_input, input_got, out_grad, first_got,
        )
        return (
            block_out, input_grad, first_grad, grad_qkv, jnp.swapaxes(grad_gate_up, 1, 2),
            grad_out, grad_down, grad_gains, new_qkv, jnp.swapaxes(new_gate_up, 1, 2), new_out, new_down, new_gains,
            wide, out_right[0], new_head, new_unit,
        )
    else:
        block_got, input_got, first_got, gains, sum_a, sum_b, full_a, full_b = backward_plain(
            n_seq, n_head, head_cols, ffn_cols, links, saved, norm_gains, tables, is_live
        )
        gains = gains.reshape(2, width)
        wide, out_right, new_head, new_unit, step_a, step_b = shampoo(
            stats_wide, roots_wide, stats_head, roots_head, stats_unit, roots_unit,
            full_a, sum_a, full_b, sum_b,
        )
        out_right = out_right[0]
    block_out = layer_input.astype(F32) + block_got.astype(F32)
    input_grad = out_grad.astype(F32) + input_got.astype(F32)
    first_grad = first_got.astype(F32)
    grad_gains = gains
    new_gains = norm_gains - GAIN_RATE * grad_gains * lax.rsqrt(
        jnp.mean(grad_gains * grad_gains, axis=-1, keepdims=True) + EPSILON
    )

    cut = 3 * head_cols
    turned = lambda value, n: jnp.swapaxes(value.reshape(n, -1, row_part), 1, 2)
    return (
        block_out,
        input_grad,
        first_grad,
        turned(sum_a[:cut], 3).astype(F32),
        turned(sum_b[: 2 * ffn_cols], 2).astype(F32),
        sum_a[cut:].astype(F32),
        sum_b[2 * ffn_cols :].astype(F32),
        grad_gains,
        w_qkv - STEP_RATE * turned(step_a[:cut], 3),
        w_gate_up - STEP_RATE * turned(step_b[: 2 * ffn_cols], 2),
        w_out - OUT_RATE * step_a[cut:],
        w_down - STEP_RATE * step_b[2 * ffn_cols :],
        new_gains,
        wide,
        out_right,
        new_head,
        new_unit,
    )


def unit_chunk(rows):
    return max(c for c in range(16, 177, 16) if rows % c == 0)


def solution(mesh):
    return jax.shard_map(
        functools.partial(shards, mesh.shape["seq"], mesh.shape["head"]),
        mesh=mesh,
        in_specs=(
            P("seq", "head", None),
            P("seq", None, "head"),
            P(None, "seq", "head"),
            P(None, "seq", "head"),
            P("head", "seq"),
            P("head", "seq"),
            P(),
            P("seq", "head", None),
            P("seq", None),
            P("seq"),
            P(None, "head", "seq", None),
            P(None, "head", "seq", None),
            P(None, "head", None, None),
            P(None, "head", None, None),
            P(None, "head", None, None),
            P(None, "head", None, None),
        ),
        out_specs=(
            P("seq", "head", None),
            P("seq", "head", None),
            P("seq", None, "head"),
            P(None, "seq", "head"),
            P(None, "seq", "head"),
            P("head", "seq"),
            P("head", "seq"),
            P(),
            P(None, "seq", "head"),
            P(None, "seq", "head"),
            P("head", "seq"),
            P("head", "seq"),
            P(),
            P(None, "head", "seq", None),
            P("head", "seq", None),
            P(None, "head", None, None),
            P(None, "head", None, None),
        ),
        check_vma=False,
    )
```

```python
import functools

import jax
import jax.numpy as jnp
from jax import lax
from jax.experimental import pallas as pl
from jax.experimental.pallas import tpu as pltpu
from jax.sharding import PartitionSpec as P

EPSILON = 1e-06
STAT_DECAY = 0.5
STEP_RATE = 0.02
OUT_RATE = 0.1
GAIN_RATE = 0.25
AXES = ("seq", "head")
MESH = pl.DeviceIdType.MESH
LANES = 128
BLOCK = 128
BF16 = jnp.bfloat16
F32 = jnp.float32


def dot_nt(matrix_a, matrix_b):
    return lax.dot_general(
        matrix_a, matrix_b, (((1,), (1,)), ((), ())), preferred_element_type=F32
    )


def dot_tn(matrix_a, matrix_b):
    return lax.dot_general(
        matrix_a, matrix_b, (((0,), (0,)), ((), ())), preferred_element_type=F32
    )


def dot_nn(matrix_a, matrix_b):
    return jnp.dot(matrix_a, matrix_b, preferred_element_type=F32)


def norm_back(d_normed, normed, inverse):
    return inverse * (d_normed - normed * jnp.mean(d_normed * normed, axis=-1, keepdims=True))


def swap_halves(values):
    lane = lax.broadcasted_iota(jnp.int32, values.shape, 1)
    return jnp.where((lane & 32) == 0, pltpu.roll(values, 96, 1), pltpu.roll(values, 32, 1))


def two_heads(block):
    lane = lax.broadcasted_iota(jnp.int32, block.shape, 1)
    zero = jnp.zeros_like(block)
    return jnp.concatenate(
        [jnp.where(lane < 64, block, zero), jnp.where(lane >= 64, block, zero)], axis=0
    )


def one_pair(transposed, width):
    kept = jnp.concatenate([transposed[:64, :width], transposed[64:, width:]], axis=0)
    return kept.T


def first_key(begin, length):
    return max(0, (begin - length // 2 + 1) // BLOCK * BLOCK)


def seen(first_ref, begin, low, key_count):
    first = first_ref[0:1, begin : begin + BLOCK]
    query = begin + lax.broadcasted_iota(jnp.int32, (1, BLOCK), 1)
    first = jnp.concatenate([first, first], axis=1)
    query = jnp.concatenate([query, query], axis=1)
    key = low + lax.broadcasted_iota(jnp.int32, (key_count, 2 * BLOCK), 0)
    return (key >= first) & (key <= query)


def attend_back_kernel(
    qr_ref, kr_ref, vm_ref, att_ref, d_ref, lse_ref, cos_ref, sin_ref, first_ref,
    dq_ref, dk_ref, dv_ref, key_sum, value_sum,
):
    length = qr_ref.shape[1]
    key_sum[...] = jnp.zeros_like(key_sum)
    value_sum[...] = jnp.zeros_like(value_sum)
    k_turned = kr_ref[0].T
    cosine, sine_part = cos_ref[...], sin_ref[...]
    product = (d_ref[0].astype(F32) * att_ref[...].astype(F32)).T
    inner = [
        jnp.sum(product[:64], axis=0, keepdims=True),
        jnp.sum(product[64:], axis=0, keepdims=True),
    ]
    for step in range(length // BLOCK):
        begin, keys = step * BLOCK, (step + 1) * BLOCK
        low = first_key(begin, length)
        queries = two_heads(qr_ref[0, begin:keys, :])
        d_out = two_heads(d_ref[0, begin:keys, :])
        scores = dot_nt(kr_ref[0, low:keys, :], queries)
        log_total = jnp.concatenate(
            [lse_ref[0, 0:1, begin:keys], lse_ref[0, 1:2, begin:keys]], axis=1
        )
        chances = jnp.where(seen(first_ref, begin, low, keys - low), jnp.exp(scores - log_total), 0.0)
        d_chances = dot_nt(vm_ref[0, low:keys, :], d_out)
        part = jnp.concatenate([inner[0][:, begin:keys], inner[1][:, begin:keys]], axis=1)
        d_scores = (chances * (d_chances - part)).astype(BF16)
        key_sum[low:keys, :] += dot_nn(d_scores, queries)
        value_sum[low:keys, :] += dot_nn(chances.astype(BF16), d_out)
        d_query = one_pair(dot_nn(k_turned[:, low:keys], d_scores), BLOCK) * 0.125
        dq_ref[0, begin:keys, :] = (
            d_query * cosine[begin:keys] - swap_halves(d_query) * sine_part[begin:keys]
        ).astype(BF16)
    d_key = key_sum[...]
    dk_ref[0] = (d_key * cosine - swap_halves(d_key) * sine_part).astype(BF16)
    dv_ref[0] = (0.5 * value_sum[...]).astype(BF16)


def attend_back(saved, d_attended, cos_wide, sin_wide, first_pos):
    q_rot, k_rot, v_mix, attended, log_total = saved
    pairs, length, _ = q_rot.shape
    part = pl.BlockSpec((1, length, LANES), lambda p: (p, 0, 0))
    table = pl.BlockSpec((length, LANES), lambda p: (0, 0))
    out = jax.ShapeDtypeStruct((pairs, length, LANES), BF16)
    return pl.pallas_call(
        attend_back_kernel,
        grid=(pairs,),
        in_specs=[part] * 3 + [pl.BlockSpec((length, LANES), lambda p: (0, p)), part,
                               pl.BlockSpec((1, 2, length), lambda p: (p, 0, 0)), table, table,
                               pl.BlockSpec((1, length), lambda p: (0, 0))],
        out_specs=[part] * 3,
        out_shape=[out] * 3,
        scratch_shapes=[pltpu.VMEM((length, LANES), F32)] * 2,
        compiler_params=pltpu.CompilerParams(vmem_limit_bytes=48 << 20),
        cost_estimate=pl.CostEstimate(
            flops=pairs * length * length * 128 * 20, bytes_accessed=pairs * length * 128 * 24,
            transcendentals=pairs * length * length),
    )(q_rot, k_rot, v_mix, attended, d_attended, log_total, cos_wide, sin_wide, first_pos[None, :])


class Place:
    def __init__(self, n_seq, n_head, slots):
        self.n_seq, self.slots, self.ranks = n_seq, slots, n_head // slots
        self.seq = lax.axis_index("seq")
        head = lax.axis_index("head")
        self.slot, self.rank = head // self.ranks, head % self.ranks

    def at_slot(self, step):
        return (self.slot + step + self.slots) % self.slots

    def at_seq(self, step):
        return (self.seq + step + self.n_seq) % self.n_seq

    @property
    def line(self):
        return self.slots == 4 and self.n_seq == 4

    def source(self, step):
        if not self.line:
            return self.at_slot(-step)
        upper = self.slot // 2
        inner = (self.slot + upper) % 2
        near = step + inner * (1 - 2 * step) * (1 - step // 2)
        return near + upper * (3 - 2 * near)

    @property
    def beside(self):
        return self.seq + 1 - 2 * (self.seq % 2)

    @property
    def across(self):
        return self.seq + 2 - 4 * (self.seq // 2)

    def device(self, seq=None, slot=None, rank=None):
        seq = self.seq if seq is None else seq
        slot = self.slot if slot is None else slot
        rank = self.rank if rank is None else rank
        return (seq, slot * self.ranks + rank)

    def greet(self, with_ranks):
        others = [self.device(slot=self.at_slot(k)) for k in range(1, self.slots)]
        others += [self.device(seq=self.at_seq(d)) for d in range(1, self.n_seq)]
        if with_ranks:
            others += [
                self.device(rank=(self.rank + j) % self.ranks) for j in range(1, self.ranks)
            ]
        barrier = pltpu.get_barrier_semaphore()
        for other in others:
            pl.semaphore_signal(barrier, inc=1, device_id=other, device_id_type=MESH)
        pl.semaphore_wait(barrier, len(others))


class Sender:
    def __init__(self, send_sems, recv_sems):
        self.send_sems, self.recv_sems, self.used = send_sems, recv_sems, 0

    def start(self, src, dst, device, recv=None):
        copy = pltpu.make_async_remote_copy(
            src_ref=src,
            dst_ref=dst,
            send_sem=self.send_sems.at[self.used],
            recv_sem=self.recv_sems.at[self.used] if recv is None else recv,
            device_id=device,
            device_id_type=MESH,
        )
        self.used += 1
        copy.start()
        return copy


def lanes(index, width):
    return pl.ds(pl.multiple_of(index * width, width), width)


def forward_kernel(
    n_seq, n_head, head_cols, head_dim, early,
    x_ref, vf_ref, g_ref, w_qkv, w_gate_up, w_out, w_down, gains_ref, seg_ref, count_ref,
    cos_ref, sin_ref, first_ref, live_ref, x_res, h_one_res, q_res, k_res, v_res, att_res, lse_out, w_a_res, w_b_res, middle_res, h_two_res, g_res, e_res,
    ffn_res, x_out, h_one, q_out, k_out, v_out, att_out, w_a, middle, h_two, g_out, e_all,
    vf_all, away, back, w_b, ffn, wt_ref, sems, z_recv, v_recv, own_sems, res_sems,
):
    slots, rows, width = x_ref.shape
    part = wt_ref.shape[1]
    rows_a = w_a.shape[1]
    place = Place(n_seq, n_head, slots)
    ranks = place.ranks
    length = slots * ranks * rows
    per = LANES // head_cols
    pairs = slots // per
    mine = lanes(place.seq, part)
    sections = {"a": (w_a, pl.ds(0, rows_a)), "b": (w_b, pl.ds(rows_a, wt_ref.shape[0] - rows_a))}
    ids = {}
    elsewhere = place.device(seq=place.at_seq(1))

    def index(name):
        return ids.setdefault(name, len(ids))

    def remote(name, src, dst, device, recv=None):
        i = index(name)
        return pltpu.make_async_remote_copy(
            src_ref=src, dst_ref=dst, send_sem=sems.at[0, i],
            recv_sem=sems.at[1, i] if recv is None else recv,
            device_id=device, device_id_type=MESH,
        )

    def x_copy(k):
        to = place.at_slot(k)
        return remote(("x", k), x_ref.at[to], x_out.at[place.slot], place.device(slot=to))

    def g_copy(k):
        to = place.at_slot(k)
        return remote(("g", k), g_ref.at[to], g_out.at[place.slot], place.device(slot=to))

    def v_copy(k):
        to = place.source(k) if place.line else place.at_slot(k)
        return remote(("v", k), vf_ref.at[to], vf_all.at[place.slot], place.device(slot=to),
                      v_recv.at[place.slot])

    def v_wait(source):
        pltpu.make_async_remote_copy(
            src_ref=vf_ref.at[0], dst_ref=vf_all.at[source], send_sem=sems.at[0, 0],
            recv_sem=v_recv.at[source], device_id=elsewhere, device_id_type=MESH,
        ).wait_recv()

    def piece(sec, step):
        ref, at = sections[sec]
        return wt_ref.at[at] if step == 0 else ref.at[step, :, mine]

    def z_copy(name, sec, step, to, to_step):
        ref, _ = sections[sec]
        which = 0 if sec == "a" else 1
        return remote((name, sec, step), piece(sec, step), ref.at[to_step, :, mine],
                      place.device(slot=to), z_recv.at[which, to_step])

    def z_wait(sec, step):
        ref, _ = sections[sec]
        which = 0 if sec == "a" else 1
        pltpu.make_async_remote_copy(
            src_ref=piece(sec, 0), dst_ref=ref.at[step, :, mine], send_sem=sems.at[0, 0],
            recv_sem=z_recv.at[which, step], device_id=elsewhere, device_id_type=MESH,
        ).wait_recv()

    slot = place.slot
    upper = slot // 2
    inner = (slot + upper) % 2

    def z_start_own(sec):
        if not place.line:
            for k in range(1, slots):
                z_copy(("z", k), sec, 0, place.at_slot(k), k).start()
            return
        @pl.when(slot < 3)
        def _():
            to = slot + 1
            z_copy("up", sec, 0, to, 1 + (to == 2).astype(jnp.int32)).start()

        @pl.when(slot > 0)
        def _():
            to = slot - 1
            z_copy("down", sec, 0, to, 1 + (to == 1).astype(jnp.int32)).start()

    def z_own_sends(sec):
        if not place.line:
            for k in range(1, slots):
                z_copy(("z", k), sec, 0, place.at_slot(k), k).wait_send()
            return

        @pl.when(slot < 3)
        def _():
            z_copy("up", sec, 0, slot + 1, 1).wait_send()

        @pl.when(slot > 0)
        def _():
            z_copy("down", sec, 0, slot - 1, 1).wait_send()

    def z_relay(sec, step):
        if step == 1:
            return z_copy("on", sec, step, slot + 1 - 2 * upper, 3)
        return z_copy("on", sec, step, slot - 1 + 2 * upper, step)

    def near_copy(sec, step):
        ref, _ = sections[sec]
        dst = ref.at[step, :, mine]
        if not place.line:
            return [
                remote(("xy", d, sec, step), piece(sec, step), dst, place.device(seq=place.at_seq(d)))
                for d in range(1, n_seq)
            ]
        return [
            remote(("xy", 0, sec, step), piece(sec, step), dst, place.device(seq=place.beside)),
            remote(("xy", 1, sec, step), piece(sec, step), dst, place.device(seq=place.across)),
        ]

    def far_copy(sec, step, which):
        ref, at = sections[sec]
        half = at.size // 2
        cut = pl.ds(which * half, half)
        source = place.beside if which == 0 else place.across
        to = place.across if which == 0 else place.beside
        where = ref.at[step, cut, lanes(source, part)]
        return remote(("far", which, sec, step), where, where, place.device(seq=to))

    def z_event(sec, step):
        z_wait(sec, step)
        if place.line:
            @pl.when(inner == 1)
            def _():
                z_relay(sec, step).start()
        for copy in near_copy(sec, step):
            copy.start()

    def xy_event(sec, step):
        for which, copy in enumerate(near_copy(sec, step)):
            copy.wait_recv()
            if place.line:
                far_copy(sec, step, which).start()

    def done_event(sec, step):
        if place.line:
            for which in range(2):
                far_copy(sec, step, which).wait_recv()

    def position(p, rank):
        return pl.ds(pl.multiple_of((p * ranks + rank) * rows, rows), rows)

    def share(name, ref, p, j):
        where = ref.at[position(p, place.rank), :]
        return remote((name, p, j), where, where, place.device(rank=(place.rank + j) % ranks))

    results = {
        "x": (x_out, x_res), "h1": (h_one, h_one_res), "q": (q_out, q_res), "k": (k_out, k_res),
        "v": (v_out, v_res), "att": (att_out, att_res), "a": (w_a, w_a_res),
        "mid": (middle, middle_res), "h2": (h_two, h_two_res), "g": (g_out, g_res),
        "e": (e_all, e_res), "ffn": (ffn, ffn_res),
    }
    for step in range(slots):
        results["b", step] = (w_b.at[step], w_b_res.at[step])

    def result(name):
        src, dst = results[name]
        return pltpu.make_async_copy(src, dst, res_sems.at[list(results).index(name)])

    high, tall = w_qkv.shape[2], w_gate_up.shape[1]
    for i in range(3):
        wt_ref[i * high : (i + 1) * high, :] = w_qkv[i].T.astype(BF16)
    wt_ref[3 * high : 4 * high, :] = w_out[...].astype(BF16)
    for i in range(2):
        wt_ref[rows_a + i * tall : rows_a + (i + 1) * tall, :] = w_gate_up[i].astype(BF16)
    wt_ref[rows_a + 2 * tall :, :] = w_down[...].astype(BF16)
    place.greet(True)
    own = [
        pltpu.make_async_copy(x_ref.at[slot], x_out.at[slot], own_sems.at[0]),
        pltpu.make_async_copy(wt_ref.at[sections["a"][1]], w_a.at[0, :, mine], own_sems.at[1]),
        pltpu.make_async_copy(wt_ref.at[sections["b"][1]], w_b.at[0, :, mine], own_sems.at[2]),
        pltpu.make_async_copy(vf_ref.at[slot], vf_all.at[slot], own_sems.at[3]),
        pltpu.make_async_copy(g_ref.at[slot], g_out.at[slot], own_sems.at[4]),
    ]
    def v_event(*steps):
        for k in steps:
            v_copy(k).start()

    def g_event():
        for k in range(1, slots):
            g_copy(k).start()

    def inside(kind, sec, step):
        @pl.when(inner == 1)
        def _():
            kind(sec, step)

    def outside(kind, sec, step):
        @pl.when(inner == 0)
        def _():
            kind(sec, step)

    z_start_own("a")
    if place.line:
        z_start_own("b")
    for k in (2, 3, 1):
        x_copy(k).start()
    v_event(1)
    for sec in ("a", "b"):
        for copy in near_copy(sec, 0):
            copy.start()
    for copy in own:
        copy.start()
    segment = seg_ref[pl.ds(slot, 1), :]
    first_pos = jnp.zeros_like(segment)
    for document in range(1, 4):
        before = jnp.sum((segment < document).astype(jnp.int32), axis=1, keepdims=True)
        first_pos = jnp.where(segment == document, before, first_pos)
    first_ref[...] = first_pos
    offset = lax.broadcasted_iota(jnp.int32, segment.shape, 1) - first_pos
    offset = jnp.broadcast_to(offset.astype(F32), (LANES, length)).T
    lane = lax.broadcasted_iota(jnp.int32, (1, LANES), 1)
    half_width = head_dim // 2
    place_in_half = (lane % half_width).astype(F32)
    frequency = jnp.exp(-jnp.log(10000.0) * place_in_half / half_width)
    cos_ref[...] = jnp.cos(offset * frequency)
    sin_ref[...] = jnp.sin(offset * frequency) * jnp.where(lane % head_dim < half_width, -1.0, 1.0)
    live = (slot < count_ref[...]).astype(F32)
    live_ref[...] = jnp.broadcast_to(live, live_ref.shape)

    z_event("a", 1)
    if place.line:
        inside(z_event, "a", 2)
        z_event("b", 1)
        inside(z_event, "b", 2)
        v_event(2, 3)
    xy_event("a", 0)
    xy_event("b", 0)
    xy_event("a", 1)
    for k in range(1, slots):
        x_copy(k).wait_recv()
    own[0].wait()

    for p in range(slots):
        x = x_out[p].astype(F32)
        normed = x * lax.rsqrt(jnp.mean(x * x, axis=-1, keepdims=True) + EPSILON)
        h_one[position(p, place.rank), :] = (normed * gains_ref[0:1, :]).astype(BF16)
        for j in range(1, ranks):
            share("h1", h_one, p, j).start()
    own[1].wait()
    own[3].wait()
    done_event("a", 0)
    for p in range(slots):
        for j in range(1, ranks):
            share("h1", h_one, p, j).wait_recv()
    result("x").start()
    result("h1").start()

    if place.line:
        events = {
            (0, 1): [lambda: inside(z_event, "a", 3), lambda: outside(z_event, "a", 2)],
            (0, 3): [lambda: xy_event("b", 1)],
            (1, 0): [lambda: done_event("a", 1), lambda: v_wait(place.source(1))],
            (1, 2): [lambda: xy_event("a", 2)],
            (1, 3): [lambda: inside(z_event, "b", 3), lambda: outside(z_event, "b", 2)],
            (2, 0): [lambda: done_event("a", 2), lambda: v_wait(place.source(2))],
            (2, 1): [lambda: outside(z_event, "a", 3), lambda: inside(xy_event, "a", 3)],
            (2, 3): [lambda: xy_event("b", 2)],
            (3, 0): [lambda: outside(xy_event, "a", 3), lambda: done_event("a", 3), g_event,
                     lambda: v_wait(place.source(3))],
            (3, 3): [lambda: outside(z_event, "b", 3)],
        }
    else:
        events = {}
        z_start_own("b")
        v_event(2, 3)
        g_event()
        for step in range(2, slots):
            z_event("a", step)
            xy_event("a", step)
        for step in range(1, slots):
            z_event("b", step)
            xy_event("b", step)
            v_wait(place.source(step))

    def one_pair_of_heads(j, carry):
        def pump(point):
            for (step, at), todo in events.items():
                if at == point:
                    @pl.when(j == step)
                    def _(todo=todo):
                        for act in todo:
                            act()

        pump(0)
        if per == 1:
            w_in = w_a[j, : 3 * head_cols, :]
            first = vf_all[place.source(j)]
        else:
            w_in = jnp.concatenate(
                [
                    w_a[j * per + u, i * head_cols : (i + 1) * head_cols, :]
                    for i in range(3)
                    for u in range(per)
                ],
                axis=0,
            )
            first = jnp.concatenate([vf_all[place.source(j * per + u)] for u in range(per)], axis=1)
        half = length // 2
        for part_at in range(2):
            at = slice(part_at * half, (part_at + 1) * half)
            project = dot_nt(h_one[at, :], w_in)
            cosine, sine_part = cos_ref[at, :], sin_ref[at, :]
            q_raw, k_raw = project[:, :LANES], project[:, LANES : 2 * LANES]
            q_out[j, at, :] = ((q_raw * cosine + swap_halves(q_raw) * sine_part) * 0.125).astype(BF16)
            k_out[j, at, :] = (k_raw * cosine + swap_halves(k_raw) * sine_part).astype(BF16)
            v_out[j, at, :] = (0.5 * project[:, 2 * LANES :] + 0.5 * first[at].astype(F32)).astype(BF16)
        pump(1)
        v_turned = v_out[j].T
        for step in range(length // BLOCK):
            begin, keys = step * BLOCK, (step + 1) * BLOCK
            low = first_key(begin, length)
            queries = two_heads(q_out[j, begin:keys, :])
            scores = dot_nt(k_out[j, low:keys, :], queries)
            scores = jnp.where(seen(first_ref, begin, low, keys - low), scores, -1e30)
            top = jnp.max(scores, axis=0, keepdims=True)
            exps = jnp.exp(scores - top)
            total = jnp.sum(exps, axis=0, keepdims=True)
            chances = (exps * (1.0 / total)).astype(BF16)
            attended = dot_nn(v_turned[:, low:keys], chances)
            att_out[begin:keys, lanes(j, LANES)] = one_pair(attended, BLOCK).astype(BF16)
            log_total = top + jnp.log(total)
            lse_out[j, 0:1, begin:keys] = log_total[:, :BLOCK]
            lse_out[j, 1:2, begin:keys] = log_total[:, BLOCK:]
            if step == length // BLOCK // 2 - 1:
                pump(2)
        pump(3)
        return carry

    lax.fori_loop(0, pairs, one_pair_of_heads, 0)
    for name in ("q", "k", "v", "att", "a"):
        result(name).start()

    w_o = w_a[:, 3 * head_cols :, :].reshape(slots * head_cols, width)

    def away_copy(p, j):
        return remote(("away", p, j), away.at[j - 1, p], back.at[j - 1, p],
                      place.device(rank=(place.rank + j) % ranks))

    for p in range(slots):
        for j in range(1, ranks):
            at = position(p, (place.rank + j) % ranks)
            away[j - 1, p] = dot_nn(att_out[at, :], w_o).astype(BF16)
            away_copy(p, j).start()
    for p in range(slots):
        middle[p] = x_out[p].astype(F32) + dot_nn(att_out[position(p, place.rank), :], w_o)
    for p in range(slots):
        value = middle[p]
        for j in range(1, ranks):
            away_copy(p, j).wait_recv()
            value = value + back[j - 1, p].astype(F32)
        middle[p] = value
        normed = value * lax.rsqrt(jnp.mean(value * value, axis=-1, keepdims=True) + EPSILON)
        h_two[position(p, place.rank), :] = (normed * gains_ref[1:2, :]).astype(BF16)
        for j in range(1, ranks):
            share("h2", h_two, p, j).start()
    result("mid").start()
    for p in range(slots):
        for j in range(1, ranks):
            share("h2", h_two, p, j).wait_recv()
    result("h2").start()

    units = (w_b.shape[1]) // 3
    strip = length // 2

    def feed(k):
        def strips(n, carry):
            at = pl.ds(pl.multiple_of(n * strip, strip), strip)
            gate = dot_nt(h_two[at, :], w_b[k, :units, :])
            up = dot_nt(h_two[at, :], w_b[k, units : 2 * units, :])
            hid = (gate * (1.0 / (1.0 + jnp.exp(-gate))) * up).astype(BF16)
            out = dot_nn(hid, w_b[k, 2 * units :, :])
            if k == 0:
                ffn[at, :] = out
            else:
                ffn[at, :] += out
            return carry

        lax.fori_loop(0, length // strip, strips, 0)

    own[2].wait()
    for step in range(slots - 1):
        done_event("b", step)
        result(("b", step)).start()
        if early:
            feed(step)
        if step == 1 and place.line:
            xy_event("b", 3)
    if not early:
        ffn[0:8, :] = jnp.zeros((8, width), F32)
    result("ffn").start()
    own[4].wait()
    for k in range(1, slots):
        g_copy(k).wait_recv()
    result("g").start()
    for p in range(slots):
        e_all[position(p, place.rank), :] = (g_out[p].astype(F32) * live_ref[...]).astype(BF16)
        for j in range(1, ranks):
            share("e", e_all, p, j).start()
    for p in range(slots):
        for j in range(1, ranks):
            share("e", e_all, p, j).wait_recv()
            share("e", e_all, p, j).wait_send()
    result("e").start()
    done_event("b", slots - 1)
    result(("b", slots - 1)).start()
    for name in results:
        result(name).wait()
    for p in range(slots):
        for j in range(1, ranks):
            share("h1", h_one, p, j).wait_send()
            share("h2", h_two, p, j).wait_send()
            away_copy(p, j).wait_send()
    for k in range(1, slots):
        x_copy(k).wait_send()
        v_copy(k).wait_send()
        g_copy(k).wait_send()
    for sec in ("a", "b"):
        z_own_sends(sec)
        for step in range(slots):
            for copy in near_copy(sec, step):
                copy.wait_send()
            if place.line:
                for which in range(2):
                    far_copy(sec, step, which).wait_send()
                if step > 0:
                    @pl.when(inner == 1)
                    def _(sec=sec, step=step):
                        z_relay(sec, step).wait_send()


def forward_part(
    n_seq, n_head, head_cols, head_dim, layer_input, values_first, out_grad, weights, gains,
    segments, counts, early,
):
    slots, rows, width = layer_input.shape
    part = weights[0].shape[1]
    all_rows = 4 * head_cols + 3 * weights[1].shape[1]
    ranks = n_head // slots
    length = slots * ranks * rows
    rows_a = 4 * head_cols
    pairs = slots * head_cols // LANES
    count = 3 * (slots - 1) + 2 * (2 + 4 * slots + slots * n_seq) + 4 * slots * ranks
    any_space = pl.BlockSpec(memory_space=pl.ANY)
    vmem = pl.BlockSpec(memory_space=pltpu.VMEM)
    shape = jax.ShapeDtypeStruct
    heads = shape((pairs, length, LANES), BF16)
    return pl.pallas_call(
        functools.partial(forward_kernel, n_seq, n_head, head_cols, head_dim, early),
        in_specs=[any_space] * 3 + [vmem] * 7,
        out_specs=[vmem] * 4 + [any_space] * 6 + [vmem] + [any_space] * 7,
        out_shape=[
            shape((length, LANES), F32),
            shape((length, LANES), F32),
            shape((1, length), jnp.int32),
            shape((1, width), F32),
            shape(layer_input.shape, BF16),
            shape((length, width), BF16),
            heads, heads, heads,
            shape((length, slots * head_cols), BF16),
            shape((pairs, 2, length), F32),
            shape((slots, rows_a, width), BF16),
            shape((slots, all_rows - rows_a, width), BF16),
            shape(layer_input.shape, F32),
            shape((length, width), BF16),
            shape(layer_input.shape, BF16),
            shape((length, width), BF16),
            shape((length if early else 8, width), F32),
        ],
        scratch_shapes=[
            pltpu.VMEM(layer_input.shape, BF16),
            pltpu.VMEM((length, width), BF16),
            pltpu.VMEM(heads.shape, BF16),
            pltpu.VMEM(heads.shape, BF16),
            pltpu.VMEM(heads.shape, BF16),
            pltpu.VMEM((length, slots * head_cols), BF16),
            pltpu.VMEM((slots, rows_a, width), BF16),
            pltpu.VMEM(layer_input.shape, F32),
            pltpu.VMEM((length, width), BF16),
            pltpu.VMEM(layer_input.shape, BF16),
            pltpu.VMEM((length, width), BF16),
            pltpu.VMEM(values_first.shape, BF16),
            pltpu.VMEM((ranks - 1, slots, rows, width), BF16),
            pltpu.VMEM((ranks - 1, slots, rows, width), BF16),
            pltpu.VMEM((slots, all_rows - rows_a, width), BF16),
            pltpu.VMEM((length if early else 8, width), F32),
            pltpu.VMEM((all_rows, part), BF16),
            pltpu.SemaphoreType.DMA((2, count)),
            pltpu.SemaphoreType.DMA((2, slots)),
            pltpu.SemaphoreType.DMA((slots,)),
            pltpu.SemaphoreType.DMA((5,)),
            pltpu.SemaphoreType.DMA((12 + slots,)),
        ],
        compiler_params=pltpu.CompilerParams(
            collective_id=0, has_side_effects=True, vmem_limit_bytes=60 << 20
        ),
    )(
        layer_input, values_first, out_grad, *weights, gains, segments, counts.reshape(1, 1)
    )


def backward_kernel(
    n_seq, n_head, head_cols,
    wa_ref, wb_ref, h_one_ref, h_two_ref, x_ref, mid_ref, g_ref, q_ref, k_ref, v_ref, att_ref, e_ref,
    ffn_ref, root_ref, head_root, unit_root,
    lse_ref, gains_ref, cos_ref, sin_ref, first_ref, live_ref,
    block_out, input_out, first_out, gains_out, sum_a, sum_b, full_a_out, full_b_out, step_a, step_b,
    w_a, w_b, normed_all, e_all, x_own, middle, g_own, q_all, k_all, v_all, att_all,
    acc_one, acc_two, hidden, d_gate, d_project, away, back, delta_own,
    full_a, full_b, head_buf, unit_buf, near_a, near_b, next_a, next_b, far_a, far_b,
    gain_sum, gain_seq, gain_slot, gain_rank,
    sems, near_sems, next_sems, far_sems, first_sems, load_sems, own_sems, step_sems, credit,
):
    slots, rows_b, width = w_b.shape
    rows_a = w_a.shape[1]
    ffn_cols = rows_b // 3
    ranks = n_head // slots
    rows = x_own.shape[1]
    length = slots * ranks * rows
    part = width // n_seq
    place = Place(n_seq, n_head, slots)
    slot = place.slot
    beside, across = place.beside, place.across
    corner = 3 - place.seq
    mine = lanes(place.seq, part)
    other = 1 - place.rank
    elsewhere = place.device(seq=beside)
    ids = {}
    sections = {
        "a": (0, w_a, near_a, next_a, far_a, sum_a, full_a, 128),
        "b": (1, w_b, near_b, next_b, far_b, sum_b, full_b, rows_b // 6),
    }

    def remote(name, src, dst, device, send=None, recv=None):
        if send is None:
            i = ids.setdefault(name, len(ids))
            send, recv = sems.at[0, i], sems.at[1, i]
        return pltpu.make_async_remote_copy(
            src_ref=src, dst_ref=dst, send_sem=send, recv_sem=recv,
            device_id=device, device_id_type=MESH,
        )

    def position(p, rank):
        return pl.ds(pl.multiple_of((p * ranks + rank) * rows, rows), rows)

    def halves(sec):
        half = sections[sec][1].shape[1] // 2
        return pl.ds(0, half), pl.ds(half, half)

    def near_copies(sec, k):
        i, grads, near = sections[sec][:3]
        upper, lower = halves(sec)
        plan = (
            (upper, beside, beside), (upper, corner, beside),
            (lower, across, across), (lower, corner, across),
        )
        return [
            remote(None, grads.at[k, cut, lanes(quarter, part)], near.at[k, n],
                   place.device(seq=to), near_sems.at[0, i, k, n], near_sems.at[1, i, k, n])
            for n, (cut, quarter, to) in enumerate(plan)
        ]

    def next_copies(sec, k):
        i, grads, _, then = sections[sec][:4]
        upper, lower = halves(sec)
        plan = ((upper, across), (lower, beside))
        return [
            remote(None, grads.at[k, cut, lanes(to, part)], then.at[k, n],
                   place.device(seq=to), next_sems.at[0, i, k, n], next_sems.at[1, i, k, n])
            for n, (cut, to) in enumerate(plan)
        ]

    upper = slot // 2
    inner = (slot + upper) % 2
    toward = 1 - 2 * upper

    def far_copy(sec, k):
        i, grads = sections[sec][:2]
        far = sections[sec][4]
        to = slot + toward * (1 - 2 * inner * (1 - k // 2))
        landing = inner * (4 - 3 * (k // 3)) + (1 - inner) * ((k // 2) * k)
        return remote(None, grads.at[k, :, mine], far.at[landing], place.device(slot=to),
                      far_sems.at[0, i, k], far_sems.at[1, i, landing])

    def far_wait(sec, landing):
        i, grads = sections[sec][:2]
        far = sections[sec][4]
        remote(None, grads.at[0, :, mine], far.at[landing], elsewhere,
               far_sems.at[0, i, 0], far_sems.at[1, i, landing]).wait_recv()

    def add_rows(sec, k, begin, where, addend):
        grads, strip = sections[sec][1], sections[sec][7]

        def one(i, carry):
            at = pl.ds(pl.multiple_of(begin + i * strip, 16), strip)
            value = grads[k, at, where].astype(F32)
            value = value + addend[pl.ds(pl.multiple_of(i * strip, 16), strip), :].astype(F32)
            grads[k, at, where] = value.astype(BF16)
            return carry

        lax.fori_loop(0, addend.shape[0] // strip, one, 0)

    def launch(sec, k):
        for copy in near_copies(sec, k):
            copy.start()

    def second(sec, k):
        near = sections[sec][2]
        half = near.shape[2]
        came = near_copies(sec, k)
        onward = next_copies(sec, k)
        came[1].wait_recv()
        add_rows(sec, k, 0, lanes(across, part), near.at[k, 1])
        onward[0].start()
        came[3].wait_recv()
        add_rows(sec, k, half, lanes(beside, part), near.at[k, 3])
        onward[1].start()
        came[0].wait_recv()
        add_rows(sec, k, 0, mine, near.at[k, 0])
        came[2].wait_recv()
        add_rows(sec, k, half, mine, near.at[k, 2])

    def third(sec, k, sends):
        then = sections[sec][3]
        half = then.shape[2]
        for n, copy in enumerate(next_copies(sec, k)):
            copy.wait_recv()
            add_rows(sec, k, n * half, mine, then.at[k, n])
        if sends:
            @pl.when(inner == 0)
            def _():
                far_copy(sec, k).start()

    def fourth(sec, k):
        @pl.when(inner == 1)
        def _():
            far_wait(sec, k)
            add_rows(sec, k, 0, mine, sections[sec][4].at[k])
            far_copy(sec, k).start()

    def gather_copies(sec):
        total, full = sections[sec][5:7]
        half = total.shape[0] // 2
        near = [
            remote(("full", sec, n), total, full.at[:, mine], place.device(seq=to))
            for n, to in enumerate((beside, across))
        ]
        far = []
        for n, (source, to) in enumerate(((beside, across), (across, beside))):
            where = full.at[pl.ds(n * half, half), lanes(source, part)]
            far.append(remote(("relay", sec, n), where, where, place.device(seq=to)))
        return near, far

    def own_copy(sec):
        i = sections[sec][0]
        return pltpu.make_async_copy(
            sections[sec][5], sections[sec][6].at[:, mine], own_sems.at[3 + i]
        )

    def finish(sec):
        grads = sections[sec][1]
        far, total, _, strip = sections[sec][4:]

        @pl.when(inner == 1)
        def _():
            far_wait(sec, 0)
            add_rows(sec, 0, 0, mine, far.at[0])

        far_wait(sec, 4)

        def one(r, carry):
            at = pl.ds(pl.multiple_of(r * strip, 16), strip)
            value = grads[0, at, mine].astype(F32) + far[4, at, :].astype(F32)
            total[at, :] = value.astype(BF16)
            return carry

        lax.fori_loop(0, total.shape[0] // strip, one, 0)
        own_copy(sec).start()
        for copy in gather_copies(sec)[0]:
            copy.start()

    def relay(sec):
        near, far = gather_copies(sec)
        for n in range(2):
            near[n].wait_recv()
            far[n].start()

    loads = {
        "h2": (h_two_ref, normed_all), "e": (e_ref, e_all), "h1": (h_one_ref, normed_all),
        "ffn": (ffn_ref, acc_one),
        "a": (wa_ref, w_a), "x": (x_ref, x_own), "mid": (mid_ref, middle),
        "g": (g_ref, g_own), "q": (q_ref, q_all), "k": (k_ref, k_all), "v": (v_ref, v_all),
        "att": (att_ref, att_all),
    }

    def load(name):
        src, dst = loads[name]
        return pltpu.make_async_copy(src, dst, load_sems.at[slots + list(loads).index(name)])

    def load_b(k):
        return pltpu.make_async_copy(wb_ref.at[k], w_b.at[k], load_sems.at[k])

    load_b(slots - 1).start()
    load("h2").start()
    load("e").start()
    load("ffn").start()
    load("x").start()
    load("mid").start()
    for k in reversed(range(slots - 1)):
        load_b(k).start()
    for name in loads:
        if name not in ("h1", "h2", "e", "ffn", "x", "mid"):
            load(name).start()
    place.greet(True)
    load("h2").wait()
    load("e").wait()
    load("ffn").wait()

    strip = length // 2
    key_sum, value_sum = acc_two.at[:, :LANES], acc_two.at[:, LANES : 2 * LANES]

    def away_copy(n, p):
        return remote(("away", n, p), away.at[p], back.at[p], place.device(rank=other))

    def swap(name, src, dst):
        return [
            remote((name, j), src.at[place.at_slot(j)], dst.at[slot],
                   place.device(slot=place.at_slot(j)))
            for j in (2, 3, 1)
        ]

    def keep(n, src, dst):
        return pltpu.make_async_copy(src, dst.at[slot], own_sems.at[n])

    def send_away(n, acc):
        if n > 0:
            pl.semaphore_wait(credit, 1)
        for p in range(slots):
            if n > 0:
                away_copy(n - 1, p).wait_send()
            away[p] = acc[position(p, other), :].astype(BF16)
            away_copy(n, p).start()

    def taken():
        pl.semaphore_signal(credit, inc=1, device_id=place.device(rank=other), device_id_type=MESH)

    live = live_ref[...]

    def block_delta():
        load("x").wait()
        load("mid").wait()
        for p in range(slots):
            away_copy(0, p).wait_recv()
            out = acc_one[position(p, place.rank), :] + back[p].astype(F32)
            delta_own[p] = ((middle[p] - x_own[p].astype(F32) + out) * live).astype(BF16)
        taken()
        for copy in swap("block", delta_own, block_out):
            copy.start()
        keep(0, delta_own.at[slot], block_out).start()

    def pump(schedule, i, point):
        for (turn, at), acts in schedule.items():
            if at == point:
                @pl.when(i == turn)
                def _(acts=acts):
                    for act in acts:
                        act()

    unit_events = {
        (2, 0): [lambda: second("b", 3)],
        (3, 0): [lambda: second("b", 2)],
    }
    head_events = {
        (0, 0): [lambda: third("b", 3, True)],
        (0, 2): [lambda: second("b", 1)],
        (1, 1): [lambda: third("b", 2, True)],
        (2, 1): [lambda: fourth("b", 3)],
        (2, 2): [lambda: second("b", 0)],
    }

    def units(i, carry):
        k = slots - 1 - i
        load_b(k).wait()

        def strips(n, carry):
            at = pl.ds(pl.multiple_of(n * strip, strip), strip)
            inner = normed_all[at, :]
            gate = dot_nt(inner, w_b[k, :ffn_cols, :])
            up = dot_nt(inner, w_b[k, ffn_cols : 2 * ffn_cols, :])
            sigmoid_gate = 1.0 / (1.0 + jnp.exp(-gate))
            activated = gate * sigmoid_gate
            hid = (activated * up).astype(BF16)
            hidden[at, :] = hid
            d_hidden = dot_nt(e_all[at, :], w_b[k, 2 * ffn_cols :, :])
            dg = (d_hidden * up * sigmoid_gate * (1.0 + gate * (1.0 - sigmoid_gate))).astype(BF16)
            du = (d_hidden * activated).astype(BF16)
            d_gate[at, :] = dg
            d_project[at, :ffn_cols] = du
            d_in = dot_nn(dg, w_b[k, :ffn_cols, :]) + dot_nn(du, w_b[k, ffn_cols : 2 * ffn_cols, :])

            @pl.when(i == 0)
            def _():
                acc_one[at, :] += dot_nn(hid, w_b[k, 2 * ffn_cols :, :])
                acc_two[at, :] = d_in

            @pl.when(i > 0)
            def _():
                acc_two[at, :] += d_in

            return carry

        lax.fori_loop(0, length // strip, strips, 0)
        pump(unit_events, i, 0)
        w_b[k, 2 * ffn_cols :, :] = dot_tn(hidden[...], e_all[...]).astype(BF16)
        w_b[k, :ffn_cols, :] = dot_tn(d_gate[...], normed_all[...]).astype(BF16)
        w_b[k, ffn_cols : 2 * ffn_cols, :] = dot_tn(d_project[:, :ffn_cols], normed_all[...]).astype(BF16)
        launch("b", k)

        @pl.when(i == 0)
        def _():
            send_away(0, acc_one)

        @pl.when(i == 1)
        def _():
            block_delta()

        return carry

    lax.fori_loop(0, slots, units, 0)
    load("h1").start()

    def share(p):
        where = e_all.at[position(p, place.rank), :]
        return remote(("share", p), where, where, place.device(rank=other))

    send_away(1, acc_two)
    load("g").wait()
    gain_sum[...] = jnp.zeros_like(gain_sum)
    for p in range(slots):
        value = middle[p]
        inverse = lax.rsqrt(jnp.mean(value * value, axis=-1, keepdims=True) + EPSILON)
        normed = value * inverse
        away_copy(1, p).wait_recv()
        d_normed = acc_two[position(p, place.rank), :] + back[p].astype(F32)
        gain_sum[1:2, :] += jnp.sum(normed * d_normed, axis=0, keepdims=True)
        delta = norm_back(d_normed * gains_ref[1:2, :], normed, inverse)
        middle[p] = delta
        e_all[position(p, place.rank), :] = (g_own[p].astype(F32) * live + delta).astype(BF16)
        share(p).start()
    taken()

    for name in ("a", "h1", "q", "k", "v", "att"):
        load(name).wait()
    for p in range(slots):
        share(p).wait_recv()

    def first_copy(k):
        return remote(None, v_all.at[k], first_out.at[slot],
                      place.device(slot=place.source(k)),
                      first_sems.at[0, k], first_sems.at[1, slot])

    def heads(i, carry):
        k = slots - 1 - i
        lane = lanes(k, LANES)
        pump(head_events, i, 0)
        d_att = dot_nt(e_all[...], w_a[k, 3 * head_cols :, :]).astype(BF16)
        product = (d_att.astype(F32) * att_all[:, lane].astype(F32)).T
        inner = [
            jnp.sum(product[:64], axis=0, keepdims=True),
            jnp.sum(product[64:], axis=0, keepdims=True),
        ]
        key_sum[...] = jnp.zeros_like(key_sum)
        value_sum[...] = jnp.zeros_like(value_sum)
        k_turned = k_all[k].T
        for step in range(length // BLOCK):
            begin, keys = step * BLOCK, (step + 1) * BLOCK
            low = first_key(begin, length)
            queries = two_heads(q_all[k, begin:keys, :])
            d_out = two_heads(d_att[begin:keys, :])
            scores = dot_nt(k_all[k, low:keys, :], queries)
            log_total = jnp.concatenate(
                [lse_ref[k, 0:1, begin:keys], lse_ref[k, 1:2, begin:keys]], axis=1
            )
            chances = jnp.where(seen(first_ref, begin, low, keys - low), jnp.exp(scores - log_total), 0.0)
            d_chances = dot_nt(v_all[k, low:keys, :], d_out)
            rest = jnp.concatenate([inner[0][:, begin:keys], inner[1][:, begin:keys]], axis=1)
            d_scores = (chances * (d_chances - rest)).astype(BF16)
            key_sum[low:keys, :] += dot_nn(d_scores, queries)
            value_sum[low:keys, :] += dot_nn(chances.astype(BF16), d_out)
            d_query = one_pair(dot_nn(k_turned[:, low:keys], d_scores), BLOCK) * 0.125
            d_project[begin:keys, :LANES] = (
                d_query * cos_ref[begin:keys, :] - swap_halves(d_query) * sin_ref[begin:keys, :]
            ).astype(BF16)
        pump(head_events, i, 1)
        d_key = key_sum[...]
        d_project[:, LANES : 2 * LANES] = (
            d_key * cos_ref[...] - swap_halves(d_key) * sin_ref[...]
        ).astype(BF16)
        d_value = (0.5 * value_sum[...]).astype(BF16)
        d_project[:, 2 * LANES :] = d_value
        v_all[k] = d_value

        @pl.when(k > 0)
        def _():
            first_copy(k).start()

        @pl.when(k == 0)
        def _():
            keep(2, v_all.at[0], first_out).start()

        for n in range(2):
            at = pl.ds(n * strip, strip)
            d_in = dot_nn(d_project[at, :], w_a[k, : 3 * head_cols, :])

            @pl.when(i == 0)
            def _():
                acc_one[at, :] = d_in

            @pl.when(i > 0)
            def _():
                acc_one[at, :] += d_in

        w_a[k, : 3 * head_cols, :] = dot_tn(d_project[...], normed_all[...]).astype(BF16)
        w_a[k, 3 * head_cols :, :] = dot_tn(att_all[:, lane], e_all[...]).astype(BF16)
        launch("a", k)

        pump(head_events, i, 2)
        return carry

    lax.fori_loop(0, slots, heads, 0)

    for copy in swap("block", delta_own, block_out):
        copy.wait_send()
    keep(0, delta_own.at[slot], block_out).wait()
    send_away(2, acc_one)
    for p in range(slots):
        value = x_own[p].astype(F32)
        inverse = lax.rsqrt(jnp.mean(value * value, axis=-1, keepdims=True) + EPSILON)
        normed = value * inverse
        away_copy(2, p).wait_recv()
        d_normed = acc_one[position(p, place.rank), :] + back[p].astype(F32)
        gain_sum[0:1, :] += jnp.sum(normed * d_normed, axis=0, keepdims=True)
        delta = norm_back(d_normed * gains_ref[0:1, :], normed, inverse)
        delta_own[p] = ((middle[p] + delta) * live).astype(BF16)
    input_copies = swap("input", delta_own, input_out)
    input_copies[0].start()
    keep(1, delta_own.at[slot], input_out).start()

    def gain_copies(level):
        if level == 0:
            return [
                remote(("gain", 0, d), gain_seq.at[place.seq], gain_seq.at[place.seq],
                       place.device(seq=place.at_seq(d)))
                for d in range(1, n_seq)
            ]
        if level == 1:
            return [
                remote(("gain", 1, j), gain_slot.at[slot], gain_slot.at[slot],
                       place.device(slot=place.at_slot(j)))
                for j in range(1, slots)
            ]
        return [
            remote(("gain", 2, 0), gain_rank.at[place.rank], gain_rank.at[place.rank],
                   place.device(rank=other))
        ]

    def gain_step(level):
        value = gain_sum[...]
        if level > 0:
            for copy in gain_copies(level - 1):
                copy.wait_recv()
            held = (gain_seq, gain_slot, gain_rank)[level - 1]
            value = held[0]
            for j in range(1, held.shape[0]):
                value = value + held[j]
        if level == 3:
            gains_out[...] = value
            return
        target = (gain_seq, gain_slot, gain_rank)[level]
        target[(place.seq, slot, place.rank)[level]] = value
        for copy in gain_copies(level):
            copy.start()

    blocks = root_ref.shape[1]
    jobs = [("b", m, b) for m in range(3) for b in range(blocks)]
    jobs += [("a", m, b) for m in range(4) for b in range(blocks)]
    members = {"a": (0, 1, 2, 5), "b": (3, 4, 6)}
    small = {"a": (head_root, head_buf, step_a), "b": (unit_root, unit_buf, step_b)}
    depth = 8

    def job_root(n):
        acc = (acc_two, acc_one)[n % depth // 4]
        return acc.at[pl.ds(n % 4 * part, part)]

    def job_loads(n):
        sec, m, b = jobs[n]
        root_in, held, _ = small[sec]
        pairs = ((root_ref.at[members[sec][m], b], job_root(n)), (root_in.at[m, b], held.at[n % depth]))
        return [
            pltpu.make_async_copy(src, dst, step_sems.at[0, n % depth, i])
            for i, (src, dst) in enumerate(pairs)
        ]

    def job_store(n):
        sec, m, b = jobs[n]
        _, held, step = small[sec]
        high = held.shape[1]
        return pltpu.make_async_copy(
            job_root(n).at[pl.ds(0, high), pl.ds(0, part)],
            step.at[pl.ds((m * blocks + b) * high, high)], step_sems.at[1, n % depth, 0],
        )

    def run_jobs(first, last):
        for n in range(first, last):
            sec, m, b = jobs[n]
            root = job_root(n)
            held = small[sec][1]
            high = held.shape[1]
            for copy in job_loads(n):
                copy.wait()
            grad = sections[sec][6][pl.ds((m * blocks + b) * high, high), :]
            turned = dot_nn(held[n % depth].astype(BF16), grad).astype(BF16)
            turned = dot_nt(turned, root[...].astype(BF16))
            scale = lax.rsqrt(jnp.mean(turned * turned, axis=0, keepdims=True) + EPSILON)
            root[pl.ds(0, high), pl.ds(0, part)] = turned * scale
            job_store(n).start()
            if n > 0 and n - 1 + depth < len(jobs):
                job_store(n - 1).wait()
                for copy in job_loads(n - 1 + depth):
                    copy.start()

    def full_copy(sec):
        i = sections[sec][0]
        return pltpu.make_async_copy(
            sections[sec][6], (full_a_out, full_b_out)[i], step_sems.at[1, i, 1]
        )

    for n in range(depth):
        for copy in job_loads(n):
            copy.start()
    gain_step(0)
    second("a", 3)
    third("b", 1, True)
    fourth("b", 2)
    input_copies[1].start()
    second("a", 2)
    fourth("b", 1)
    input_copies[2].start()
    second("a", 1)
    gain_step(1)
    third("b", 0, False)
    second("a", 0)
    finish("b")
    third("a", 3, True)
    third("a", 2, True)
    fourth("a", 3)
    third("a", 1, True)
    fourth("a", 2)
    relay("b")
    gain_step(2)
    third("a", 0, False)
    fourth("a", 1)
    gain_step(3)
    finish("a")
    for copy in gather_copies("b")[1]:
        copy.wait_recv()
    own_copy("b").wait()
    full_copy("b").start()
    run_jobs(0, 6)
    relay("a")
    for copy in gather_copies("a")[1]:
        copy.wait_recv()
    own_copy("a").wait()
    full_copy("a").start()
    run_jobs(6, len(jobs))
    for n in range(len(jobs) - depth, len(jobs)):
        job_store(n).wait()
    full_copy("a").wait()
    full_copy("b").wait()
    for sec in ("b", "a"):
        near, far = gather_copies(sec)
        for copy in far:
            copy.wait_send()
        for copy in near:
            copy.wait_send()
        for k in range(slots):
            for copy in near_copies(sec, k) + next_copies(sec, k):
                copy.wait_send()
            if k > 0:
                far_copy(sec, k).wait_send()
    for copy in swap("block", delta_own, block_out):
        copy.wait_recv()
    for copy in swap("input", delta_own, input_out):
        copy.wait()
    for j in range(1, slots):
        source = place.at_slot(j)
        remote(None, v_all.at[0], first_out.at[source], elsewhere,
               first_sems.at[0, 0], first_sems.at[1, source]).wait_recv()
        first_copy(j).wait_send()
    for p in range(slots):
        away_copy(2, p).wait_send()
        share(p).wait_send()
    for level in range(3):
        for copy in gain_copies(level):
            copy.wait_send()
    keep(1, delta_own.at[slot], input_out).wait()
    keep(2, v_all.at[0], first_out).wait()


def backward_part(n_seq, n_head, head_cols, saved, gains, tables, live, roots):
    (
        x_own, h_one, q_rot, k_rot, v_mix, attended, log_total, weights_a, weights_b, middle, h_two,
        grad_own, e_all, ffn,
    ) = saved
    cos_wide, sin_wide, first_pos = tables
    _, roots_head, roots_unit = roots
    slots, rows, width = x_own.shape
    length = h_one.shape[0]
    rows_a, rows_b = weights_a.shape[1], weights_b.shape[1]
    part = width // n_seq
    ranks = n_head // slots
    any_space = pl.BlockSpec(memory_space=pl.ANY)
    vmem = pl.BlockSpec(memory_space=pltpu.VMEM)
    shape = jax.ShapeDtypeStruct
    like = lambda value: pltpu.VMEM(value.shape, value.dtype)
    count = 2 * 4 + 3 * slots + slots + 2 * (slots - 1) + n_seq + slots + 4
    sem = pltpu.SemaphoreType.DMA
    return pl.pallas_call(
        functools.partial(backward_kernel, n_seq, n_head, head_cols),
        in_specs=[any_space] * 16 + [vmem] * 6,
        out_specs=[any_space] * 3 + [vmem] * 3 + [any_space] * 4,
        out_shape=[
            shape(x_own.shape, BF16),
            shape(x_own.shape, BF16),
            shape((slots, length, head_cols), BF16),
            shape((8, width), F32),
            shape((rows_a, part), BF16),
            shape((rows_b, part), BF16),
            shape((rows_a, width), BF16),
            shape((rows_b, width), BF16),
            shape((rows_a, part), F32),
            shape((rows_b, part), F32),
        ],
        scratch_shapes=[
            like(weights_a), like(weights_b), like(h_two), like(e_all), like(x_own), like(middle),
            like(grad_own),
            like(q_rot), like(k_rot), like(v_mix), like(attended),
            pltpu.VMEM((length, width), F32),
            pltpu.VMEM((length, width), F32),
            pltpu.VMEM((length, rows_b // 3), BF16),
            pltpu.VMEM((length, rows_b // 3), BF16),
            pltpu.VMEM((length, 3 * LANES), BF16),
            like(x_own), like(x_own), like(x_own),
            pltpu.VMEM((rows_a, width), BF16),
            pltpu.VMEM((rows_b, width), BF16),
            pltpu.VMEM((8,) + roots_head.shape[2:], F32),
            pltpu.VMEM((8,) + roots_unit.shape[2:], F32),
            pltpu.VMEM((slots, 4, rows_a // 2, part), BF16),
            pltpu.VMEM((slots, 4, rows_b // 2, part), BF16),
            pltpu.VMEM((slots, 2, rows_a // 2, part), BF16),
            pltpu.VMEM((slots, 2, rows_b // 2, part), BF16),
            pltpu.VMEM((slots + 1, rows_a, part), BF16),
            pltpu.VMEM((slots + 1, rows_b, part), BF16),
            pltpu.VMEM((8, width), F32),
            pltpu.VMEM((n_seq, 8, width), F32),
            pltpu.VMEM((slots, 8, width), F32),
            pltpu.VMEM((ranks, 8, width), F32),
            sem((2, count)),
            sem((2, 2, slots, 4)),
            sem((2, 2, slots, 2)),
            sem((2, 2, slots + 1)),
            sem((2, slots)),
            sem((slots + 12,)),
            sem((5,)),
            sem((2, 8, 2)),
            pltpu.SemaphoreType.REGULAR,
        ],
        compiler_params=pltpu.CompilerParams(
            collective_id=2, has_side_effects=True, vmem_limit_bytes=64 << 20
        ),
    )(
        weights_a, weights_b, h_one, h_two, x_own, middle, grad_own, q_rot, k_rot, v_mix, attended,
        e_all, ffn, *roots, log_total, gains, cos_wide, sin_wide, first_pos[None, :], live,
    )


def reduce_kernel(
    n_seq, n_head, chunks,
    block_ref, input_ref, first_ref, gains_ref, grads_a, grads_b,
    block_out, input_out, first_out, gains_out, sum_a, sum_b, full_a, full_b,
    near_a, near_b, turn_a, turn_b, far_a, far_b, gain_seq, gain_slot, gain_rank,
    send_sems, recv_sems, own_sems, far_recv, first_recv,
):
    slots = block_ref.shape[0]
    place = Place(n_seq, n_head, slots)
    place.greet(True)
    sender = Sender(send_sems, recv_sems)
    part = sum_a.shape[1]
    mine = lanes(place.seq, part)
    order = [2, 3, 1, 0]
    parts = ((grads_b, sum_b, full_b, near_b, turn_b, far_b, chunks[1]),
             (grads_a, sum_a, full_a, near_a, turn_a, far_a, chunks[0]))
    copies, received = [], []

    def arrive(copy):
        copy.wait_recv()
        received.append(copy)

    def swap(src, dst):
        return [
            sender.start(
                src.at[place.at_slot(k)], dst.at[place.slot], place.device(slot=place.at_slot(k))
            )
            for k in (2, 3, 1)
        ]

    gain_seq[place.seq] = gains_ref[...]
    small = [
        sender.start(gain_seq.at[place.seq], gain_seq.at[place.seq],
                     place.device(seq=place.at_seq(d)))
        for d in range(1, n_seq)
    ]
    copies += small

    def to_seqs(grads, near, k):
        return [
            sender.start(
                grads.at[k, :, lanes(place.at_seq(d), part)],
                near.at[k, d - 1],
                place.device(seq=place.at_seq(d)),
            )
            for d in range(1, n_seq)
        ]

    sent = {}
    units = [(which, k) for which in range(2) for k in order]

    def launch(unit):
        which, k = unit
        sent[unit] = to_seqs(parts[which][0], parts[which][3], k)
        copies.extend(sent[unit])

    own = [
        pltpu.make_async_copy(src, dst.at[place.slot], own_sems.at[i])
        for i, (src, dst) in enumerate(
            (
                (block_ref.at[place.slot], block_out),
                (input_ref.at[place.slot], input_out),
                (first_ref.at[0], first_out),
            )
        )
    ]
    for copy in own:
        copy.start()
    launch(units[0])
    launch(units[1])
    copies += swap(block_ref, block_out)
    for copy in small:
        arrive(copy)
    total = gain_seq[0]
    for i in range(1, n_seq):
        total = total + gain_seq[i]
    gain_slot[place.slot] = total
    small = [
        sender.start(gain_slot.at[place.slot], gain_slot.at[place.slot],
                     place.device(slot=place.at_slot(k)))
        for k in range(1, slots)
    ]
    copies += small
    elsewhere = place.device(seq=place.at_seq(1))
    for index, unit in enumerate(units):
        which, k = unit
        grads, _, _, near, turn, far, chunk = parts[which]
        if index + 2 < len(units):
            launch(units[index + 2])
        for copy in sent[unit]:
            arrive(copy)

        def add(i, carry, grads=grads, near=near, turn=turn, k=k, chunk=chunk):
            rows = pl.ds(pl.multiple_of(i * chunk, chunk), chunk)
            value = grads[k, rows, mine].astype(F32)
            for d in range(n_seq - 1):
                value = value + near[k, d, rows, :].astype(F32)
            turn[k, rows, :] = value.astype(BF16)
            return carry

        lax.fori_loop(0, grads.shape[1] // chunk, add, 0)
        if k != 0:
            copy = sender.start(
                turn.at[k], far.at[place.slot], place.device(slot=place.source(k)),
                far_recv.at[which, place.slot],
            )
            copies.append(copy)
            received.append(copy)
        if index == 1:
            for j in range(1, slots):
                copy = sender.start(
                    first_ref.at[j], first_out.at[place.slot],
                    place.device(slot=place.source(j)), first_recv.at[place.slot],
                )
                copies.append(copy)
                received.append(copy)
        if index == 4:
            copies += swap(input_ref, input_out)
            for copy in small:
                arrive(copy)
            total = gain_slot[0]
            for i in range(1, slots):
                total = total + gain_slot[i]
            gain_rank[place.rank] = total
            small = [
                sender.start(gain_rank.at[place.rank], gain_rank.at[place.rank],
                             place.device(rank=(place.rank + j) % place.ranks))
                for j in range(1, place.ranks)
            ]
            copies += small
        if k == 0:
            for j in range(1, slots):
                source = place.at_slot(j)
                pltpu.make_async_remote_copy(
                    src_ref=turn.at[0], dst_ref=far.at[source], send_sem=send_sems.at[0],
                    recv_sem=far_recv.at[which, source], device_id=elsewhere, device_id_type=MESH,
                ).wait_recv()
            _, total_ref, full, _, _, _, _ = parts[which]

            def finish(i, carry, turn=turn, far=far, total_ref=total_ref, full=full, chunk=chunk):
                rows = pl.ds(pl.multiple_of(i * chunk, chunk), chunk)
                value = turn[0, rows, :].astype(F32)
                for j in range(1, slots):
                    value = value + far[place.at_slot(j), rows, :].astype(F32)
                value = value.astype(BF16)
                total_ref[rows, :] = value
                full[rows, mine] = value
                return carry

            lax.fori_loop(0, grads.shape[1] // chunk, finish, 0)
            copies += [
                sender.start(total_ref, full.at[:, mine], place.device(seq=place.at_seq(d)))
                for d in range(1, n_seq)
            ]
    for copy in small:
        arrive(copy)
    total = gain_rank[0]
    for i in range(1, place.ranks):
        total = total + gain_rank[i]
    gains_out[...] = total
    for copy in copies:
        if all(copy is not other for other in received):
            copy.wait_recv()
    for j in range(1, slots):
        source = place.at_slot(j)
        pltpu.make_async_remote_copy(
            src_ref=first_ref.at[0], dst_ref=first_out.at[source], send_sem=send_sems.at[0],
            recv_sem=first_recv.at[source], device_id=elsewhere, device_id_type=MESH,
        ).wait_recv()
    for copy in copies:
        copy.wait_send()
    for copy in own:
        copy.wait()


def reduce_grads(n_seq, n_head, chunks, block_delta, input_delta, first_delta, gains, grads_a, grads_b):
    slots = block_delta.shape[0]
    part = grads_a.shape[2] // n_seq
    rows = (grads_a.shape[1], grads_b.shape[1])
    ranks = n_head // slots
    count = (
        3 * (slots - 1) + 2 * (slots * (n_seq - 1) + (slots - 1) + (n_seq - 1))
        + (n_seq - 1) + (slots - 1) + (ranks - 1)
    )
    any_space = pl.BlockSpec(memory_space=pl.ANY)
    vmem = pl.BlockSpec(memory_space=pltpu.VMEM)
    like = lambda value: jax.ShapeDtypeStruct(value.shape, value.dtype)
    return pl.pallas_call(
        functools.partial(reduce_kernel, n_seq, n_head, chunks),
        in_specs=[any_space] * 3 + [vmem] * 3,
        out_specs=[any_space] * 3 + [vmem] * 5,
        out_shape=[like(block_delta), like(input_delta), like(first_delta), like(gains)]
        + [jax.ShapeDtypeStruct((r, part), BF16) for r in rows]
        + [jax.ShapeDtypeStruct((r, part * n_seq), BF16) for r in rows],
        scratch_shapes=[pltpu.VMEM((slots, n_seq - 1, r, part), BF16) for r in rows]
        + [pltpu.VMEM((slots, r, part), BF16) for r in rows]
        + [pltpu.VMEM((slots, r, part), BF16) for r in rows]
        + [pltpu.VMEM((n,) + gains.shape, F32) for n in (n_seq, slots, ranks)]
        + [
            pltpu.SemaphoreType.DMA((count,)),
            pltpu.SemaphoreType.DMA((count,)),
            pltpu.SemaphoreType.DMA((3,)),
            pltpu.SemaphoreType.DMA((2, slots)),
            pltpu.SemaphoreType.DMA((slots,)),
        ],
        compiler_params=pltpu.CompilerParams(
            collective_id=1, has_side_effects=True, vmem_limit_bytes=56 << 20
        ),
    )(block_delta, input_delta, first_delta, gains, grads_a, grads_b)


def shampoo_kernel(
    stat_ref, root_ref, head_stat, head_root, unit_stat, unit_root, full_a, sum_a, full_b, sum_b,
    wide_ref, out_right_ref, new_head, new_unit, step_a, step_b,
):
    step = pl.program_id(0)
    blocks = stat_ref.shape[1]

    def one(member, width, small_stat, small_root, full, total, big_out, small_out, step_out):
        for b in range(blocks):
            rows = pl.ds(pl.multiple_of((member * blocks + b) * width, 16), width)
            grad, own = full[rows, :], total[rows, :]
            big_out[0, b] = STAT_DECAY * stat_ref[0, b] + (1.0 - STAT_DECAY) * dot_tn(own, grad)
            small_out[member, b] = STAT_DECAY * small_stat[member, b] + (
                1.0 - STAT_DECAY
            ) * dot_nt(grad, grad)
            turned = dot_nn(small_root[member, b].astype(BF16), grad).astype(BF16)
            turned = dot_nt(turned, root_ref[0, b].astype(BF16))
            scale = lax.rsqrt(jnp.mean(turned * turned, axis=0, keepdims=True) + EPSILON)
            step_out[rows, :] = turned * scale

    head_width, unit_width = head_stat.shape[2], unit_stat.shape[2]
    head_args = (head_width, head_stat, head_root, full_a, sum_a)
    unit_args = (unit_width, unit_stat, unit_root, full_b, sum_b)

    @pl.when(step < 3)
    def _():
        one(step, *head_args, wide_ref, new_head, step_a)

    @pl.when((step >= 3) & (step < 6))
    def _():
        one(step - 3, *unit_args, wide_ref, new_unit, step_b)

    @pl.when(step == 6)
    def _():
        one(3, *head_args, out_right_ref, new_head, step_a)


def shampoo(stats_wide, roots_wide, stats_head, roots_head, stats_unit, roots_unit, full_a, sum_a, full_b, sum_b):
    members, blocks, part, width = stats_wide.shape
    member = lambda i: (jnp.where(i == 5, 6, jnp.where(i == 6, 5, i)), 0, 0, 0)
    wide = pl.BlockSpec((1, blocks, part, width), member)
    vmem = pl.BlockSpec(memory_space=pltpu.VMEM)
    return pl.pallas_call(
        shampoo_kernel,
        grid=(members,),
        in_specs=[wide, wide] + [vmem] * 8,
        out_specs=[
            pl.BlockSpec((1, blocks, part, width), lambda i: (jnp.minimum(i, 5), 0, 0, 0)),
            pl.BlockSpec((1, blocks, part, width), lambda i: (0, 0, 0, 0)),
            vmem, vmem, vmem, vmem,
        ],
        out_shape=[
            jax.ShapeDtypeStruct((members - 1, blocks, part, width), F32),
            jax.ShapeDtypeStruct((1, blocks, part, width), F32),
            jax.ShapeDtypeStruct(stats_head.shape, F32),
            jax.ShapeDtypeStruct(stats_unit.shape, F32),
            jax.ShapeDtypeStruct(sum_a.shape, F32),
            jax.ShapeDtypeStruct(sum_b.shape, F32),
        ],
        compiler_params=pltpu.CompilerParams(vmem_limit_bytes=48 << 20),
    )(stats_wide, roots_wide, stats_head, roots_head, stats_unit, roots_unit, full_a, sum_a, full_b, sum_b)


def finish_kernel(
    blocks, stat_ref, head_stat, unit_stat, full_a, sum_a, full_b, sum_b, step_a, step_b,
    w_qkv, w_gate_up, w_out, w_down, gains_ref, norm_ref,
    block_got, x_ref, input_got, g_ref, first_got,
    wide_ref, right_ref, new_head, new_unit, grad_qkv, grad_gate_up, grad_out, grad_down,
    new_qkv, new_gate_up, new_out, new_down, grad_gains, new_gains, block_out, input_out, first_out,
):
    step = pl.program_id(0)
    member, b = step // blocks, step % blocks

    def one(m, small_stat, full, total, big_out, small_out):
        width = small_stat.shape[2]
        rows = pl.ds(pl.multiple_of((m * blocks + b) * width, 16), width)
        grad, own = full[rows, :], total[rows, :]
        big_out[0, 0] = STAT_DECAY * stat_ref[0, 0] + (1.0 - STAT_DECAY) * dot_tn(own, grad)
        small_out[m, b] = STAT_DECAY * small_stat[m, b] + (1.0 - STAT_DECAY) * dot_nt(grad, grad)

    head_args, unit_args = (head_stat, full_a, sum_a), (unit_stat, full_b, sum_b)

    @pl.when(member < 3)
    def _():
        one(member, *head_args, wide_ref, new_head)

    @pl.when((member >= 3) & (member < 6))
    def _():
        one(member - 3, *unit_args, wide_ref, new_unit)

    @pl.when(member == 6)
    def _():
        one(3, *head_args, right_ref, new_head)

    @pl.when(step % 4 == 0)
    def _():
        block_out[...] = x_ref[...].astype(F32) + block_got[...].astype(F32)

    @pl.when(step % 4 == 1)
    def _():
        input_out[...] = g_ref[...].astype(F32) + input_got[...].astype(F32)

    @pl.when(step % 4 == 2)
    def _():
        first_out[...] = first_got[...].astype(F32)

    def stepped(i, at, total, steps, old, grad_ref, new_ref, turn):
        grad, change = total[at, :].astype(F32), STEP_RATE * steps[at, :]
        grad_ref[i] = grad.T if turn else grad
        new_ref[i] = old[i] - (change.T if turn else change)

    high = w_qkv.shape[2]
    for i in range(3):
        @pl.when(step == i)
        def _(i=i):
            stepped(i, pl.ds(i * high, high), sum_a, step_a, w_qkv, grad_qkv, new_qkv, True)

    tall = w_gate_up.shape[1]
    for i in range(2):
        @pl.when(step == 3 + i)
        def _(i=i):
            stepped(
                i, pl.ds(i * tall, tall), sum_b, step_b, w_gate_up, grad_gate_up, new_gate_up, False
            )

    @pl.when(step == 5)
    def _():
        at = pl.ds(3 * high, high)
        grad_out[...] = sum_a[at, :].astype(F32)
        new_out[...] = w_out[...] - OUT_RATE * step_a[at, :]

    @pl.when(step == 6)
    def _():
        at = pl.ds(2 * tall, tall)
        grad_down[...] = sum_b[at, :].astype(F32)
        new_down[...] = w_down[...] - STEP_RATE * step_b[at, :]

    @pl.when(step == 7)
    def _():
        gains = gains_ref[0:2, :]
        grad_gains[...] = gains
        scale = lax.rsqrt(jnp.mean(gains * gains, axis=-1, keepdims=True) + EPSILON)
        new_gains[...] = norm_ref[...] - GAIN_RATE * gains * scale


def finish(
    stats_wide, stats_head, stats_unit, full_a, sum_a, full_b, sum_b, step_a, step_b,
    w_qkv, w_gate_up, w_out, w_down, gains, norm_gains,
    block_got, layer_input, input_got, out_grad, first_got,
):
    members, blocks, part, width = stats_wide.shape
    slots, rows, _ = layer_input.shape
    length, head_cols = first_got.shape[1:]
    steps = 4 * slots

    def source(i):
        m = jnp.minimum(i // blocks, members - 1)
        return jnp.where(m == 5, 6, jnp.where(m == 6, 5, m)), i % blocks, 0, 0

    last = (members - 1) * blocks
    block = (1, 1, part, width)

    def right(i):
        return 0, jnp.clip(i - last, 0, blocks - 1), 0, 0

    def wide(i):
        at = jnp.minimum(i, last - 1)
        return at // blocks, at % blocks, 0, 0

    vmem = pl.BlockSpec(memory_space=pltpu.VMEM)
    tokens = pl.BlockSpec((1, rows, width), lambda i: (i // 4, 0, 0))
    firsts = pl.BlockSpec((1, length, head_cols), lambda i: (i // 4, 0, 0))
    like = lambda *values: [jax.ShapeDtypeStruct(v.shape, F32) for v in values]
    weights = (w_qkv, w_gate_up, w_out, w_down)
    return pl.pallas_call(
        functools.partial(finish_kernel, blocks),
        grid=(steps,),
        in_specs=[pl.BlockSpec(block, source)] + [vmem] * 14 + [tokens] * 4 + [firsts],
        out_specs=[pl.BlockSpec(block, wide), pl.BlockSpec(block, right)] + [vmem] * 12
        + [tokens, tokens, firsts],
        out_shape=[
            jax.ShapeDtypeStruct((members - 1, blocks, part, width), F32),
            jax.ShapeDtypeStruct((1, blocks, part, width), F32),
        ]
        + like(stats_head, stats_unit, *weights, *weights, norm_gains, norm_gains, layer_input, out_grad, first_got),
        compiler_params=pltpu.CompilerParams(vmem_limit_bytes=60 << 20),
    )(
        stats_wide, stats_head, stats_unit, full_a, sum_a, full_b, sum_b, step_a, step_b,
        w_qkv, w_gate_up, w_out, w_down, gains, norm_gains,
        block_got, layer_input, input_got, out_grad, first_got,
    )


class Links:
    def __init__(self, n_seq, n_head, slots):
        self.n_seq, self.n_head, self.slots = n_seq, n_head, slots
        self.ranks = n_head // slots
        self.slot = lax.axis_index("head") // self.ranks
        self.rank = lax.axis_index("head") % self.ranks

    def permute(self, value, partner):
        pairs = []
        for s in range(self.n_seq):
            for h in range(self.n_head):
                to_s, to_h = partner(s, h)
                pairs.append((s * self.n_head + h, to_s * self.n_head + to_h))
        return lax.ppermute(value, AXES, pairs)

    def swap_slots(self, value):
        got = [lax.dynamic_index_in_dim(value, self.slot, 0, keepdims=False)]
        for step in range(1, self.slots):
            piece = lax.dynamic_index_in_dim(value, self.slot ^ step, 0, keepdims=False)
            got.append(self.permute(piece, lambda s, h: (s, h ^ (step * self.ranks))))
        got = jnp.stack(got)
        return jnp.stack(
            [lax.dynamic_index_in_dim(got, self.slot ^ q, 0, keepdims=False) for q in range(self.slots)]
        )

    def gather_ranks(self, value):
        got = [value] + [
            self.permute(value, lambda s, h: (s, h ^ step)) for step in range(1, self.ranks)
        ]
        got = jnp.stack(got)
        return jnp.stack(
            [lax.dynamic_index_in_dim(got, self.rank ^ r, 0, keepdims=False) for r in range(self.ranks)]
        )

    def sum_ranks(self, value):
        total = lax.dynamic_index_in_dim(value, self.rank, 0, keepdims=False)
        for step in range(1, self.ranks):
            piece = lax.dynamic_index_in_dim(value, self.rank ^ step, 0, keepdims=False)
            got = self.permute(piece.astype(BF16), lambda s, h: (s, h ^ step))
            total = total + got.astype(F32)
        return total

    def whole_sequence(self, own):
        both = self.gather_ranks(own)
        return jnp.swapaxes(both, 0, 1).reshape(-1, own.shape[-1])

    def own_sum(self, full):
        rows = full.shape[0] // (self.slots * self.ranks)
        parts = full.reshape(self.slots, self.ranks, rows, full.shape[-1])
        return self.sum_ranks(jnp.swapaxes(parts, 0, 1)).reshape(-1, full.shape[-1])


def backward_plain(n_seq, n_head, head_cols, ffn_cols, links, saved, gains, tables, is_live):
    (
        x_bf16, h_one, q_rot, k_rot, v_mix, attended, log_total, weights_a, weights_b, middle,
        h_two, grad_own, d_ffn, _,
    ) = saved
    cos_wide, sin_wide, first_pos = tables
    slots, rows, width = x_bf16.shape
    length = h_one.shape[0]
    rows_a, rows_b = weights_a.shape[1], weights_b.shape[1]
    pairs = slots * head_cols // LANES
    per = LANES // head_cols

    def pair_major(value):
        n = value.shape[2]
        value = value.reshape(pairs, per, length, n, head_cols)
        return value.transpose(0, 2, 3, 1, 4).reshape(pairs, length, n, LANES)

    def slot_major(value):
        n = value.shape[2]
        value = value.reshape(pairs, length, n, per, head_cols)
        return value.transpose(0, 3, 1, 2, 4).reshape(slots, length, n, head_cols)

    w_in, w_o = weights_a[:, : 3 * head_cols], weights_a[:, 3 * head_cols :]
    w_gu, w_d = weights_b[:, : 2 * ffn_cols], weights_b[:, 2 * ffn_cols :]
    x_own = x_bf16.reshape(slots * rows, width).astype(F32)
    middle = middle.reshape(slots * rows, width)
    ein = functools.partial(jnp.einsum, preferred_element_type=F32)
    inverse_one = lax.rsqrt(jnp.mean(x_own * x_own, axis=-1, keepdims=True) + EPSILON)
    normed_one = x_own * inverse_one
    inverse_two = lax.rsqrt(jnp.mean(middle * middle, axis=-1, keepdims=True) + EPSILON)
    normed_two = middle * inverse_two
    saved = (q_rot, k_rot, v_mix, attended, log_total)
    attended = jnp.swapaxes(attended.reshape(length, slots, head_cols), 0, 1)
    gate_up = ein("ld,qfd->qlf", h_two, w_gu)
    gate, up = gate_up[..., :ffn_cols], gate_up[..., ffn_cols:]
    sigmoid_gate = jax.nn.sigmoid(gate)
    activated = gate * sigmoid_gate
    hidden = (activated * up).astype(BF16)
    ffn_out = links.own_sum(ein("qlf,qfd->ld", hidden, w_d))
    block_delta = jnp.where(is_live, middle - x_own + ffn_out, 0.0).astype(BF16)

    d_own = jnp.where(is_live, grad_own, jnp.zeros_like(grad_own))
    d_out = d_own.reshape(slots * rows, width).astype(F32)
    g_down = ein("qlf,ld->qfd", hidden, d_ffn)
    d_hidden = ein("ld,qfd->qlf", d_ffn, w_d)
    d_gate = (
        d_hidden * up * sigmoid_gate * (1.0 + gate * (1.0 - sigmoid_gate))
    ).astype(BF16)
    d_up = (d_hidden * activated).astype(BF16)
    d_gate_up = jnp.concatenate([d_gate, d_up], axis=2)
    d_normed_two = links.own_sum(ein("qlf,qfd->ld", d_gate_up, w_gu))
    g_gate_up = ein("qlf,ld->qfd", d_gate_up, h_two)
    grads_b = jnp.concatenate([g_gate_up.astype(BF16), g_down.astype(BF16)], axis=1)
    gain_two = jnp.sum(normed_two * d_normed_two, axis=0)
    middle_delta = norm_back(d_normed_two * gains[1], normed_two, inverse_two)
    d_middle = d_out + middle_delta
    d_attn = links.whole_sequence(d_middle.astype(BF16).reshape(slots, rows, width))
    d_attended = ein("ld,qcd->qlc", d_attn, w_o).astype(BF16)
    if per > 1:
        d_attended = pair_major(d_attended[:, :, None])[:, :, 0]
    d_project = jnp.concatenate(
        attend_back(saved, d_attended, cos_wide, sin_wide, first_pos), axis=2
    )
    if per > 1:
        d_project = slot_major(d_project.reshape(pairs, length, 3, LANES)).reshape(
            slots, length, 3 * head_cols
        )
    d_value = d_project[:, :, 2 * head_cols :]
    g_out = ein("qlc,ld->qcd", attended, d_attn)
    g_qkv = ein("qlc,ld->qcd", d_project, h_one)
    grads_a = jnp.concatenate([g_qkv.astype(BF16), g_out.astype(BF16)], axis=1)
    d_normed_one = links.own_sum(ein("qlc,qcd->ld", d_project, w_in))
    gain_one = jnp.sum(normed_one * d_normed_one, axis=0)
    input_delta = middle_delta + norm_back(d_normed_one * gains[0], normed_one, inverse_one)
    input_delta = jnp.where(is_live, input_delta, 0.0).astype(BF16)
    gain_rows = jnp.concatenate([gain_one.reshape(8, -1), gain_two.reshape(8, -1)], axis=0)

    return reduce_grads(
        n_seq,
        n_head,
        (LANES, unit_chunk(rows_b)),
        block_delta.reshape(slots, rows, width),
        input_delta.reshape(slots, rows, width),
        d_value,
        gain_rows,
        grads_a,
        grads_b,
    )


def shards(
    n_seq,
    n_head,
    layer_input,
    values_first,
    w_qkv,
    w_gate_up,
    w_out,
    w_down,
    norm_gains,
    out_grad,
    segments,
    counts,
    stats_wide,
    roots_wide,
    stats_head,
    roots_head,
    stats_unit,
    roots_unit,
):
    slots, rows, width = layer_input.shape
    length = segments.shape[1]
    row_part, head_cols, ffn_cols = w_qkv.shape[1], w_qkv.shape[2], w_gate_up.shape[2]
    head_dim = stats_head.shape[2]
    links = Links(n_seq, n_head, slots)
    is_live = links.slot < counts[0]
    pairs = slots * head_cols // LANES
    per = LANES // head_cols
    rows_a, rows_b = 4 * head_cols, 3 * ffn_cols

    fused = n_seq == 4 and slots == 4 and links.ranks == 2 and head_cols == LANES
    cos_wide, sin_wide, first_pos, live, *saved = forward_part(
        n_seq, n_head, head_cols, head_dim, layer_input, values_first, out_grad,
        (w_qkv, jnp.swapaxes(w_gate_up, 1, 2), w_out, w_down), norm_gains, segments, counts, fused,
    )
    first_pos = first_pos[0]
    tables = (cos_wide, sin_wide, first_pos)
    if fused:
        (
            block_got, input_got, first_got, gains, sum_a, sum_b, full_a, full_b, step_a, step_b
        ) = backward_part(
            n_seq, n_head, head_cols, saved, norm_gains, tables, live,
            (roots_wide, roots_head, roots_unit),
        )
        (
            wide, out_right, new_head, new_unit, grad_qkv, grad_gate_up, grad_out, grad_down,
            new_qkv, new_gate_up, new_out, new_down, grad_gains, new_gains,
            block_out, input_grad, first_grad,
        ) = finish(
            stats_wide, stats_head, stats_unit, full_a, sum_a, full_b, sum_b, step_a, step_b,
            w_qkv, jnp.swapaxes(w_gate_up, 1, 2), w_out, w_down, gains, norm_gains,
            block_got, layer_input, input_got, out_grad, first_got,
        )
        return (
            block_out, input_grad, first_grad, grad_qkv, jnp.swapaxes(grad_gate_up, 1, 2),
            grad_out, grad_down, grad_gains, new_qkv, jnp.swapaxes(new_gate_up, 1, 2), new_out, new_down, new_gains,
            wide, out_right[0], new_head, new_unit,
        )
    else:
        block_got, input_got, first_got, gains, sum_a, sum_b, full_a, full_b = backward_plain(
            n_seq, n_head, head_cols, ffn_cols, links, saved, norm_gains, tables, is_live
        )
        gains = gains.reshape(2, width)
        wide, out_right, new_head, new_unit, step_a, step_b = shampoo(
            stats_wide, roots_wide, stats_head, roots_head, stats_unit, roots_unit,
            full_a, sum_a, full_b, sum_b,
        )
        out_right = out_right[0]
    block_out = layer_input.astype(F32) + block_got.astype(F32)
    input_grad = out_grad.astype(F32) + input_got.astype(F32)
    first_grad = first_got.astype(F32)
    grad_gains = gains
    new_gains = norm_gains - GAIN_RATE * grad_gains * lax.rsqrt(
        jnp.mean(grad_gains * grad_gains, axis=-1, keepdims=True) + EPSILON
    )

    cut = 3 * head_cols
    turned = lambda value, n: jnp.swapaxes(value.reshape(n, -1, row_part), 1, 2)
    return (
        block_out,
        input_grad,
        first_grad,
        turned(sum_a[:cut], 3).astype(F32),
        turned(sum_b[: 2 * ffn_cols], 2).astype(F32),
        sum_a[cut:].astype(F32),
        sum_b[2 * ffn_cols :].astype(F32),
        grad_gains,
        w_qkv - STEP_RATE * turned(step_a[:cut], 3),
        w_gate_up - STEP_RATE * turned(step_b[: 2 * ffn_cols], 2),
        w_out - OUT_RATE * step_a[cut:],
        w_down - STEP_RATE * step_b[2 * ffn_cols :],
        new_gains,
        wide,
        out_right,
        new_head,
        new_unit,
    )


def unit_chunk(rows):
    return max(c for c in range(16, 177, 16) if rows % c == 0)


def solution(mesh):
    return jax.shard_map(
        functools.partial(shards, mesh.shape["seq"], mesh.shape["head"]),
        mesh=mesh,
        in_specs=(
            P("seq", "head", None),
            P("seq", None, "head"),
            P(None, "seq", "head"),
            P(None, "seq", "head"),
            P("head", "seq"),
            P("head", "seq"),
            P(),
            P("seq", "head", None),
            P("seq", None),
            P("seq"),
            P(None, "head", "seq", None),
            P(None, "head", "seq", None),
            P(None, "head", None, None),
            P(None, "head", None, None),
            P(None, "head", None, None),
            P(None, "head", None, None),
        ),
        out_specs=(
            P("seq", "head", None),
            P("seq", "head", None),
            P("seq", None, "head"),
            P(None, "seq", "head"),
            P(None, "seq", "head"),
            P("head", "seq"),
            P("head", "seq"),
            P(),
            P(None, "seq", "head"),
            P(None, "seq", "head"),
            P("head", "seq"),
            P("head", "seq"),
            P(),
            P(None, "head", "seq", None),
            P("head", "seq", None),
            P(None, "head", None, None),
            P(None, "head", None, None),
        ),
        check_vma=False,
    )
```

```python
import functools

import jax
import jax.numpy as jnp
from jax import lax
from jax.experimental import pallas as pl
from jax.experimental.pallas import tpu as pltpu
from jax.sharding import PartitionSpec as P

EPSILON = 1e-06
STAT_DECAY = 0.5
STEP_RATE = 0.02
OUT_RATE = 0.1
GAIN_RATE = 0.25
AXES = ("seq", "head")
MESH = pl.DeviceIdType.MESH
LANES = 128
BLOCK = 128
BF16 = jnp.bfloat16
F32 = jnp.float32


def dot_nt(matrix_a, matrix_b):
    return lax.dot_general(
        matrix_a, matrix_b, (((1,), (1,)), ((), ())), preferred_element_type=F32
    )


def dot_tn(matrix_a, matrix_b):
    return lax.dot_general(
        matrix_a, matrix_b, (((0,), (0,)), ((), ())), preferred_element_type=F32
    )


def dot_nn(matrix_a, matrix_b):
    return jnp.dot(matrix_a, matrix_b, preferred_element_type=F32)


def norm_back(d_normed, normed, inverse):
    return inverse * (d_normed - normed * jnp.mean(d_normed * normed, axis=-1, keepdims=True))


def swap_halves(values):
    lane = lax.broadcasted_iota(jnp.int32, values.shape, 1)
    return jnp.where((lane & 32) == 0, pltpu.roll(values, 96, 1), pltpu.roll(values, 32, 1))


def two_heads(block):
    lane = lax.broadcasted_iota(jnp.int32, block.shape, 1)
    zero = jnp.zeros_like(block)
    return jnp.concatenate(
        [jnp.where(lane < 64, block, zero), jnp.where(lane >= 64, block, zero)], axis=0
    )


def one_pair(transposed, width):
    kept = jnp.concatenate([transposed[:64, :width], transposed[64:, width:]], axis=0)
    return kept.T


def first_key(begin, length):
    return max(0, (begin - length // 2 + 1) // BLOCK * BLOCK)


def seen(first_ref, begin, low, key_count):
    first = first_ref[0:1, begin : begin + BLOCK]
    query = begin + lax.broadcasted_iota(jnp.int32, (1, BLOCK), 1)
    first = jnp.concatenate([first, first], axis=1)
    query = jnp.concatenate([query, query], axis=1)
    key = low + lax.broadcasted_iota(jnp.int32, (key_count, 2 * BLOCK), 0)
    return (key >= first) & (key <= query)


def attend_back_kernel(
    qr_ref, kr_ref, vm_ref, att_ref, d_ref, lse_ref, cos_ref, sin_ref, first_ref,
    dq_ref, dk_ref, dv_ref, key_sum, value_sum,
):
    length = qr_ref.shape[1]
    key_sum[...] = jnp.zeros_like(key_sum)
    value_sum[...] = jnp.zeros_like(value_sum)
    k_turned = kr_ref[0].T
    cosine, sine_part = cos_ref[...], sin_ref[...]
    product = (d_ref[0].astype(F32) * att_ref[...].astype(F32)).T
    inner = [
        jnp.sum(product[:64], axis=0, keepdims=True),
        jnp.sum(product[64:], axis=0, keepdims=True),
    ]
    for step in range(length // BLOCK):
        begin, keys = step * BLOCK, (step + 1) * BLOCK
        low = first_key(begin, length)
        queries = two_heads(qr_ref[0, begin:keys, :])
        d_out = two_heads(d_ref[0, begin:keys, :])
        scores = dot_nt(kr_ref[0, low:keys, :], queries)
        log_total = jnp.concatenate(
            [lse_ref[0, 0:1, begin:keys], lse_ref[0, 1:2, begin:keys]], axis=1
        )
        chances = jnp.where(seen(first_ref, begin, low, keys - low), jnp.exp(scores - log_total), 0.0)
        d_chances = dot_nt(vm_ref[0, low:keys, :], d_out)
        part = jnp.concatenate([inner[0][:, begin:keys], inner[1][:, begin:keys]], axis=1)
        d_scores = (chances * (d_chances - part)).astype(BF16)
        key_sum[low:keys, :] += dot_nn(d_scores, queries)
        value_sum[low:keys, :] += dot_nn(chances.astype(BF16), d_out)
        d_query = one_pair(dot_nn(k_turned[:, low:keys], d_scores), BLOCK) * 0.125
        dq_ref[0, begin:keys, :] = (
            d_query * cosine[begin:keys] - swap_halves(d_query) * sine_part[begin:keys]
        ).astype(BF16)
    d_key = key_sum[...]
    dk_ref[0] = (d_key * cosine - swap_halves(d_key) * sine_part).astype(BF16)
    dv_ref[0] = (0.5 * value_sum[...]).astype(BF16)


def attend_back(saved, d_attended, cos_wide, sin_wide, first_pos):
    q_rot, k_rot, v_mix, attended, log_total = saved
    pairs, length, _ = q_rot.shape
    part = pl.BlockSpec((1, length, LANES), lambda p: (p, 0, 0))
    table = pl.BlockSpec((length, LANES), lambda p: (0, 0))
    out = jax.ShapeDtypeStruct((pairs, length, LANES), BF16)
    return pl.pallas_call(
        attend_back_kernel,
        grid=(pairs,),
        in_specs=[part] * 3 + [pl.BlockSpec((length, LANES), lambda p: (0, p)), part,
                               pl.BlockSpec((1, 2, length), lambda p: (p, 0, 0)), table, table,
                               pl.BlockSpec((1, length), lambda p: (0, 0))],
        out_specs=[part] * 3,
        out_shape=[out] * 3,
        scratch_shapes=[pltpu.VMEM((length, LANES), F32)] * 2,
        compiler_params=pltpu.CompilerParams(vmem_limit_bytes=48 << 20),
        cost_estimate=pl.CostEstimate(
            flops=pairs * length * length * 128 * 20, bytes_accessed=pairs * length * 128 * 24,
            transcendentals=pairs * length * length),
    )(q_rot, k_rot, v_mix, attended, d_attended, log_total, cos_wide, sin_wide, first_pos[None, :])


class Place:
    def __init__(self, n_seq, n_head, slots):
        self.n_seq, self.slots, self.ranks = n_seq, slots, n_head // slots
        self.seq = lax.axis_index("seq")
        head = lax.axis_index("head")
        self.slot, self.rank = head // self.ranks, head % self.ranks

    def at_slot(self, step):
        return (self.slot + step + self.slots) % self.slots

    def at_seq(self, step):
        return (self.seq + step + self.n_seq) % self.n_seq

    @property
    def line(self):
        return self.slots == 4 and self.n_seq == 4

    def source(self, step):
        if not self.line:
            return self.at_slot(-step)
        upper = self.slot // 2
        inner = (self.slot + upper) % 2
        near = step + inner * (1 - 2 * step) * (1 - step // 2)
        return near + upper * (3 - 2 * near)

    @property
    def beside(self):
        return self.seq + 1 - 2 * (self.seq % 2)

    @property
    def across(self):
        return self.seq + 2 - 4 * (self.seq // 2)

    def device(self, seq=None, slot=None, rank=None):
        seq = self.seq if seq is None else seq
        slot = self.slot if slot is None else slot
        rank = self.rank if rank is None else rank
        return (seq, slot * self.ranks + rank)

    def greet(self, with_ranks):
        others = [self.device(slot=self.at_slot(k)) for k in range(1, self.slots)]
        others += [self.device(seq=self.at_seq(d)) for d in range(1, self.n_seq)]
        if with_ranks:
            others += [
                self.device(rank=(self.rank + j) % self.ranks) for j in range(1, self.ranks)
            ]
        barrier = pltpu.get_barrier_semaphore()
        for other in others:
            pl.semaphore_signal(barrier, inc=1, device_id=other, device_id_type=MESH)
        pl.semaphore_wait(barrier, len(others))


class Sender:
    def __init__(self, send_sems, recv_sems):
        self.send_sems, self.recv_sems, self.used = send_sems, recv_sems, 0

    def start(self, src, dst, device, recv=None):
        copy = pltpu.make_async_remote_copy(
            src_ref=src,
            dst_ref=dst,
            send_sem=self.send_sems.at[self.used],
            recv_sem=self.recv_sems.at[self.used] if recv is None else recv,
            device_id=device,
            device_id_type=MESH,
        )
        self.used += 1
        copy.start()
        return copy


def lanes(index, width):
    return pl.ds(pl.multiple_of(index * width, width), width)


def forward_kernel(
    n_seq, n_head, head_cols, head_dim, early,
    x_ref, vf_ref, g_ref, w_qkv, w_gate_up, w_out, w_down, gains_ref, seg_ref, count_ref,
    cos_ref, sin_ref, first_ref, live_ref, x_res, h_one_res, q_res, k_res, v_res, att_res, lse_out, w_a_res, w_b_res, middle_res, h_two_res, g_res, e_res,
    ffn_res, x_out, h_one, q_out, k_out, v_out, att_out, w_a, middle, h_two, g_out, e_all,
    vf_all, away, back, w_b, ffn, wt_ref, sems, z_recv, v_recv, own_sems, res_sems,
):
    slots, rows, width = x_ref.shape
    part = wt_ref.shape[1]
    rows_a = w_a.shape[1]
    place = Place(n_seq, n_head, slots)
    ranks = place.ranks
    length = slots * ranks * rows
    per = LANES // head_cols
    pairs = slots // per
    mine = lanes(place.seq, part)
    sections = {"a": (w_a, pl.ds(0, rows_a)), "b": (w_b, pl.ds(rows_a, wt_ref.shape[0] - rows_a))}
    ids = {}
    elsewhere = place.device(seq=place.at_seq(1))

    def index(name):
        return ids.setdefault(name, len(ids))

    def remote(name, src, dst, device, recv=None):
        i = index(name)
        return pltpu.make_async_remote_copy(
            src_ref=src, dst_ref=dst, send_sem=sems.at[0, i],
            recv_sem=sems.at[1, i] if recv is None else recv,
            device_id=device, device_id_type=MESH,
        )

    def x_copy(k):
        to = place.at_slot(k)
        return remote(("x", k), x_ref.at[to], x_out.at[place.slot], place.device(slot=to))

    def g_copy(k):
        to = place.at_slot(k)
        return remote(("g", k), g_ref.at[to], g_out.at[place.slot], place.device(slot=to))

    def v_copy(k):
        to = place.source(k) if place.line else place.at_slot(k)
        return remote(("v", k), vf_ref.at[to], vf_all.at[place.slot], place.device(slot=to),
                      v_recv.at[place.slot])

    def v_wait(source):
        pltpu.make_async_remote_copy(
            src_ref=vf_ref.at[0], dst_ref=vf_all.at[source], send_sem=sems.at[0, 0],
            recv_sem=v_recv.at[source], device_id=elsewhere, device_id_type=MESH,
        ).wait_recv()

    def piece(sec, step):
        ref, at = sections[sec]
        return wt_ref.at[at] if step == 0 else ref.at[step, :, mine]

    def z_copy(name, sec, step, to, to_step):
        ref, _ = sections[sec]
        which = 0 if sec == "a" else 1
        return remote((name, sec, step), piece(sec, step), ref.at[to_step, :, mine],
                      place.device(slot=to), z_recv.at[which, to_step])

    def z_wait(sec, step):
        ref, _ = sections[sec]
        which = 0 if sec == "a" else 1
        pltpu.make_async_remote_copy(
            src_ref=piece(sec, 0), dst_ref=ref.at[step, :, mine], send_sem=sems.at[0, 0],
            recv_sem=z_recv.at[which, step], device_id=elsewhere, device_id_type=MESH,
        ).wait_recv()

    slot = place.slot
    upper = slot // 2
    inner = (slot + upper) % 2

    def z_start_own(sec):
        if not place.line:
            for k in range(1, slots):
                z_copy(("z", k), sec, 0, place.at_slot(k), k).start()
            return
        @pl.when(slot < 3)
        def _():
            to = slot + 1
            z_copy("up", sec, 0, to, 1 + (to == 2).astype(jnp.int32)).start()

        @pl.when(slot > 0)
        def _():
            to = slot - 1
            z_copy("down", sec, 0, to, 1 + (to == 1).astype(jnp.int32)).start()

    def z_own_sends(sec):
        if not place.line:
            for k in range(1, slots):
                z_copy(("z", k), sec, 0, place.at_slot(k), k).wait_send()
            return

        @pl.when(slot < 3)
        def _():
            z_copy("up", sec, 0, slot + 1, 1).wait_send()

        @pl.when(slot > 0)
        def _():
            z_copy("down", sec, 0, slot - 1, 1).wait_send()

    def z_relay(sec, step):
        if step == 1:
            return z_copy("on", sec, step, slot + 1 - 2 * upper, 3)
        return z_copy("on", sec, step, slot - 1 + 2 * upper, step)

    def near_copy(sec, step):
        ref, _ = sections[sec]
        dst = ref.at[step, :, mine]
        if not place.line:
            return [
                remote(("xy", d, sec, step), piece(sec, step), dst, place.device(seq=place.at_seq(d)))
                for d in range(1, n_seq)
            ]
        return [
            remote(("xy", 0, sec, step), piece(sec, step), dst, place.device(seq=place.beside)),
            remote(("xy", 1, sec, step), piece(sec, step), dst, place.device(seq=place.across)),
        ]

    def far_copy(sec, step, which):
        ref, at = sections[sec]
        half = at.size // 2
        cut = pl.ds(which * half, half)
        source = place.beside if which == 0 else place.across
        to = place.across if which == 0 else place.beside
        where = ref.at[step, cut, lanes(source, part)]
        return remote(("far", which, sec, step), where, where, place.device(seq=to))

    def z_event(sec, step):
        z_wait(sec, step)
        if place.line:
            @pl.when(inner == 1)
            def _():
                z_relay(sec, step).start()
        for copy in near_copy(sec, step):
            copy.start()

    def xy_event(sec, step):
        for which, copy in enumerate(near_copy(sec, step)):
            copy.wait_recv()
            if place.line:
                far_copy(sec, step, which).start()

    def done_event(sec, step):
        if place.line:
            for which in range(2):
                far_copy(sec, step, which).wait_recv()

    def position(p, rank):
        return pl.ds(pl.multiple_of((p * ranks + rank) * rows, rows), rows)

    def share(name, ref, p, j):
        where = ref.at[position(p, place.rank), :]
        return remote((name, p, j), where, where, place.device(rank=(place.rank + j) % ranks))

    results = {
        "x": (x_out, x_res), "h1": (h_one, h_one_res), "q": (q_out, q_res), "k": (k_out, k_res),
        "v": (v_out, v_res), "att": (att_out, att_res), "a": (w_a, w_a_res),
        "mid": (middle, middle_res), "h2": (h_two, h_two_res), "g": (g_out, g_res),
        "e": (e_all, e_res), "ffn": (ffn, ffn_res),
    }
    for step in range(slots):
        results["b", step] = (w_b.at[step], w_b_res.at[step])

    def result(name):
        src, dst = results[name]
        return pltpu.make_async_copy(src, dst, res_sems.at[list(results).index(name)])

    high, tall = w_qkv.shape[2], w_gate_up.shape[1]
    for i in range(3):
        wt_ref[i * high : (i + 1) * high, :] = w_qkv[i].T.astype(BF16)
    wt_ref[3 * high : 4 * high, :] = w_out[...].astype(BF16)
    for i in range(2):
        wt_ref[rows_a + i * tall : rows_a + (i + 1) * tall, :] = w_gate_up[i].astype(BF16)
    wt_ref[rows_a + 2 * tall :, :] = w_down[...].astype(BF16)
    place.greet(True)
    own = [
        pltpu.make_async_copy(x_ref.at[slot], x_out.at[slot], own_sems.at[0]),
        pltpu.make_async_copy(wt_ref.at[sections["a"][1]], w_a.at[0, :, mine], own_sems.at[1]),
        pltpu.make_async_copy(wt_ref.at[sections["b"][1]], w_b.at[0, :, mine], own_sems.at[2]),
        pltpu.make_async_copy(vf_ref.at[slot], vf_all.at[slot], own_sems.at[3]),
        pltpu.make_async_copy(g_ref.at[slot], g_out.at[slot], own_sems.at[4]),
    ]
    def v_event(*steps):
        for k in steps:
            v_copy(k).start()

    def g_event():
        for k in range(1, slots):
            g_copy(k).start()

    def inside(kind, sec, step):
        @pl.when(inner == 1)
        def _():
            kind(sec, step)

    def outside(kind, sec, step):
        @pl.when(inner == 0)
        def _():
            kind(sec, step)

    z_start_own("a")
    if place.line:
        z_start_own("b")
    for k in (2, 3, 1):
        x_copy(k).start()
    v_event(1)
    for sec in ("a", "b"):
        for copy in near_copy(sec, 0):
            copy.start()
    for copy in own:
        copy.start()
    segment = seg_ref[pl.ds(slot, 1), :]
    first_pos = jnp.zeros_like(segment)
    for document in range(1, 4):
        before = jnp.sum((segment < document).astype(jnp.int32), axis=1, keepdims=True)
        first_pos = jnp.where(segment == document, before, first_pos)
    first_ref[...] = first_pos
    offset = lax.broadcasted_iota(jnp.int32, segment.shape, 1) - first_pos
    offset = jnp.broadcast_to(offset.astype(F32), (LANES, length)).T
    lane = lax.broadcasted_iota(jnp.int32, (1, LANES), 1)
    half_width = head_dim // 2
    place_in_half = (lane % half_width).astype(F32)
    frequency = jnp.exp(-jnp.log(10000.0) * place_in_half / half_width)
    cos_ref[...] = jnp.cos(offset * frequency)
    sin_ref[...] = jnp.sin(offset * frequency) * jnp.where(lane % head_dim < half_width, -1.0, 1.0)
    live = (slot < count_ref[...]).astype(F32)
    live_ref[...] = jnp.broadcast_to(live, live_ref.shape)

    z_event("a", 1)
    if place.line:
        inside(z_event, "a", 2)
        z_event("b", 1)
        inside(z_event, "b", 2)
        v_event(2, 3)
    xy_event("a", 0)
    xy_event("b", 0)
    xy_event("a", 1)
    for k in range(1, slots):
        x_copy(k).wait_recv()
    own[0].wait()

    for p in range(slots):
        x = x_out[p].astype(F32)
        normed = x * lax.rsqrt(jnp.mean(x * x, axis=-1, keepdims=True) + EPSILON)
        h_one[position(p, place.rank), :] = (normed * gains_ref[0:1, :]).astype(BF16)
        for j in range(1, ranks):
            share("h1", h_one, p, j).start()
    own[1].wait()
    own[3].wait()
    done_event("a", 0)
    for p in range(slots):
        for j in range(1, ranks):
            share("h1", h_one, p, j).wait_recv()
    result("x").start()
    result("h1").start()

    if place.line:
        events = {
            (0, 1): [lambda: inside(z_event, "a", 3), lambda: outside(z_event, "a", 2)],
            (0, 6): [lambda: xy_event("b", 1)],
            (1, 0): [lambda: done_event("a", 1), lambda: v_wait(place.source(1))],
            (1, 2): [lambda: xy_event("a", 2)],
            (1, 6): [lambda: inside(z_event, "b", 3), lambda: outside(z_event, "b", 2)],
            (2, 0): [lambda: done_event("a", 2), lambda: v_wait(place.source(2))],
            (2, 1): [lambda: outside(z_event, "a", 3), lambda: inside(xy_event, "a", 3)],
            (2, 6): [lambda: xy_event("b", 2)],
            (2, 3): [lambda: outside(xy_event, "a", 3)],
            (3, 0): [lambda: done_event("a", 3), g_event,
                     lambda: v_wait(place.source(3))],
            (3, 6): [lambda: outside(z_event, "b", 3)],
        }
    else:
        events = {}
        z_start_own("b")
        v_event(2, 3)
        g_event()
        for step in range(2, slots):
            z_event("a", step)
            xy_event("a", step)
        for step in range(1, slots):
            z_event("b", step)
            xy_event("b", step)
            v_wait(place.source(step))

    def one_pair_of_heads(j, carry):
        def pump(point):
            for (step, at), todo in events.items():
                if at == point:
                    @pl.when(j == step)
                    def _(todo=todo):
                        for act in todo:
                            act()

        pump(0)
        if per == 1:
            w_in = w_a[j, : 3 * head_cols, :]
            first = vf_all[place.source(j)]
        else:
            w_in = jnp.concatenate(
                [
                    w_a[j * per + u, i * head_cols : (i + 1) * head_cols, :]
                    for i in range(3)
                    for u in range(per)
                ],
                axis=0,
            )
            first = jnp.concatenate([vf_all[place.source(j * per + u)] for u in range(per)], axis=1)
        half = length // 2
        for part_at in range(2):
            at = slice(part_at * half, (part_at + 1) * half)
            project = dot_nt(h_one[at, :], w_in)
            cosine, sine_part = cos_ref[at, :], sin_ref[at, :]
            q_raw, k_raw = project[:, :LANES], project[:, LANES : 2 * LANES]
            q_out[j, at, :] = ((q_raw * cosine + swap_halves(q_raw) * sine_part) * 0.125).astype(BF16)
            k_out[j, at, :] = (k_raw * cosine + swap_halves(k_raw) * sine_part).astype(BF16)
            v_out[j, at, :] = (0.5 * project[:, 2 * LANES :] + 0.5 * first[at].astype(F32)).astype(BF16)
        pump(1)
        v_turned = v_out[j].T
        for step in range(length // BLOCK):
            begin, keys = step * BLOCK, (step + 1) * BLOCK
            low = first_key(begin, length)
            queries = two_heads(q_out[j, begin:keys, :])
            scores = dot_nt(k_out[j, low:keys, :], queries)
            scores = jnp.where(seen(first_ref, begin, low, keys - low), scores, -1e30)
            top = jnp.max(scores, axis=0, keepdims=True)
            exps = jnp.exp(scores - top)
            total = jnp.sum(exps, axis=0, keepdims=True)
            chances = (exps * (1.0 / total)).astype(BF16)
            attended = dot_nn(v_turned[:, low:keys], chances)
            att_out[begin:keys, lanes(j, LANES)] = one_pair(attended, BLOCK).astype(BF16)
            log_total = top + jnp.log(total)
            lse_out[j, 0:1, begin:keys] = log_total[:, :BLOCK]
            lse_out[j, 1:2, begin:keys] = log_total[:, BLOCK:]
            if step % (length // BLOCK // 4) == 0:
                pump(2 + step // (length // BLOCK // 4))
        pump(6)
        return carry

    lax.fori_loop(0, pairs, one_pair_of_heads, 0)
    for name in ("q", "k", "v", "att", "a"):
        result(name).start()

    w_o = w_a[:, 3 * head_cols :, :].reshape(slots * head_cols, width)

    def away_copy(p, j):
        return remote(("away", p, j), away.at[j - 1, p], back.at[j - 1, p],
                      place.device(rank=(place.rank + j) % ranks))

    for p in range(slots):
        for j in range(1, ranks):
            at = position(p, (place.rank + j) % ranks)
            away[j - 1, p] = dot_nn(att_out[at, :], w_o).astype(BF16)
            away_copy(p, j).start()
    for p in range(slots):
        middle[p] = x_out[p].astype(F32) + dot_nn(att_out[position(p, place.rank), :], w_o)
    for p in range(slots):
        value = middle[p]
        for j in range(1, ranks):
            away_copy(p, j).wait_recv()
            value = value + back[j - 1, p].astype(F32)
        middle[p] = value
        normed = value * lax.rsqrt(jnp.mean(value * value, axis=-1, keepdims=True) + EPSILON)
        h_two[position(p, place.rank), :] = (normed * gains_ref[1:2, :]).astype(BF16)
        for j in range(1, ranks):
            share("h2", h_two, p, j).start()
    result("mid").start()
    for p in range(slots):
        for j in range(1, ranks):
            share("h2", h_two, p, j).wait_recv()
    result("h2").start()

    units = (w_b.shape[1]) // 3
    strip = length // 2

    def feed(k):
        def strips(n, carry):
            at = pl.ds(pl.multiple_of(n * strip, strip), strip)
            gate = dot_nt(h_two[at, :], w_b[k, :units, :])
            up = dot_nt(h_two[at, :], w_b[k, units : 2 * units, :])
            hid = (gate * (1.0 / (1.0 + jnp.exp(-gate))) * up).astype(BF16)
            out = dot_nn(hid, w_b[k, 2 * units :, :])
            if k == 0:
                ffn[at, :] = out
            else:
                ffn[at, :] += out
            return carry

        lax.fori_loop(0, length // strip, strips, 0)

    own[2].wait()
    for step in range(slots - 1):
        done_event("b", step)
        result(("b", step)).start()
        if early:
            feed(step)
        if step == 1 and place.line:
            xy_event("b", 3)
    if not early:
        ffn[0:8, :] = jnp.zeros((8, width), F32)
    result("ffn").start()
    own[4].wait()
    for k in range(1, slots):
        g_copy(k).wait_recv()
    result("g").start()
    for p in range(slots):
        e_all[position(p, place.rank), :] = (g_out[p].astype(F32) * live_ref[...]).astype(BF16)
        for j in range(1, ranks):
            share("e", e_all, p, j).start()
    for p in range(slots):
        for j in range(1, ranks):
            share("e", e_all, p, j).wait_recv()
            share("e", e_all, p, j).wait_send()
    result("e").start()
    done_event("b", slots - 1)
    result(("b", slots - 1)).start()
    for name in results:
        result(name).wait()
    for p in range(slots):
        for j in range(1, ranks):
            share("h1", h_one, p, j).wait_send()
            share("h2", h_two, p, j).wait_send()
            away_copy(p, j).wait_send()
    for k in range(1, slots):
        x_copy(k).wait_send()
        v_copy(k).wait_send()
        g_copy(k).wait_send()
    for sec in ("a", "b"):
        z_own_sends(sec)
        for step in range(slots):
            for copy in near_copy(sec, step):
                copy.wait_send()
            if place.line:
                for which in range(2):
                    far_copy(sec, step, which).wait_send()
                if step > 0:
                    @pl.when(inner == 1)
                    def _(sec=sec, step=step):
                        z_relay(sec, step).wait_send()


def forward_part(
    n_seq, n_head, head_cols, head_dim, layer_input, values_first, out_grad, weights, gains,
    segments, counts, early,
):
    slots, rows, width = layer_input.shape
    part = weights[0].shape[1]
    all_rows = 4 * head_cols + 3 * weights[1].shape[1]
    ranks = n_head // slots
    length = slots * ranks * rows
    rows_a = 4 * head_cols
    pairs = slots * head_cols // LANES
    count = 3 * (slots - 1) + 2 * (2 + 4 * slots + slots * n_seq) + 4 * slots * ranks
    any_space = pl.BlockSpec(memory_space=pl.ANY)
    vmem = pl.BlockSpec(memory_space=pltpu.VMEM)
    shape = jax.ShapeDtypeStruct
    heads = shape((pairs, length, LANES), BF16)
    return pl.pallas_call(
        functools.partial(forward_kernel, n_seq, n_head, head_cols, head_dim, early),
        in_specs=[any_space] * 3 + [vmem] * 7,
        out_specs=[vmem] * 4 + [any_space] * 6 + [vmem] + [any_space] * 7,
        out_shape=[
            shape((length, LANES), F32),
            shape((length, LANES), F32),
            shape((1, length), jnp.int32),
            shape((1, width), F32),
            shape(layer_input.shape, BF16),
            shape((length, width), BF16),
            heads, heads, heads,
            shape((length, slots * head_cols), BF16),
            shape((pairs, 2, length), F32),
            shape((slots, rows_a, width), BF16),
            shape((slots, all_rows - rows_a, width), BF16),
            shape(layer_input.shape, F32),
            shape((length, width), BF16),
            shape(layer_input.shape, BF16),
            shape((length, width), BF16),
            shape((length if early else 8, width), F32),
        ],
        scratch_shapes=[
            pltpu.VMEM(layer_input.shape, BF16),
            pltpu.VMEM((length, width), BF16),
            pltpu.VMEM(heads.shape, BF16),
            pltpu.VMEM(heads.shape, BF16),
            pltpu.VMEM(heads.shape, BF16),
            pltpu.VMEM((length, slots * head_cols), BF16),
            pltpu.VMEM((slots, rows_a, width), BF16),
            pltpu.VMEM(layer_input.shape, F32),
            pltpu.VMEM((length, width), BF16),
            pltpu.VMEM(layer_input.shape, BF16),
            pltpu.VMEM((length, width), BF16),
            pltpu.VMEM(values_first.shape, BF16),
            pltpu.VMEM((ranks - 1, slots, rows, width), BF16),
            pltpu.VMEM((ranks - 1, slots, rows, width), BF16),
            pltpu.VMEM((slots, all_rows - rows_a, width), BF16),
            pltpu.VMEM((length if early else 8, width), F32),
            pltpu.VMEM((all_rows, part), BF16),
            pltpu.SemaphoreType.DMA((2, count)),
            pltpu.SemaphoreType.DMA((2, slots)),
            pltpu.SemaphoreType.DMA((slots,)),
            pltpu.SemaphoreType.DMA((5,)),
            pltpu.SemaphoreType.DMA((12 + slots,)),
        ],
        compiler_params=pltpu.CompilerParams(
            collective_id=0, has_side_effects=True, vmem_limit_bytes=60 << 20
        ),
    )(
        layer_input, values_first, out_grad, *weights, gains, segments, counts.reshape(1, 1)
    )


def backward_kernel(
    n_seq, n_head, head_cols,
    wa_ref, wb_ref, h_one_ref, h_two_ref, x_ref, mid_ref, g_ref, q_ref, k_ref, v_ref, att_ref, e_ref,
    ffn_ref, root_ref, head_root, unit_root,
    lse_ref, gains_ref, cos_ref, sin_ref, first_ref, live_ref,
    block_out, input_out, first_out, gains_out, sum_a, sum_b, full_a_out, full_b_out, step_a, step_b,
    w_a, w_b, normed_all, e_all, x_own, middle, g_own, q_all, k_all, v_all, att_all,
    acc_one, acc_two, hidden, d_gate, d_project, away, back, delta_own,
    full_a, full_b, head_buf, unit_buf, near_a, near_b, next_a, next_b, far_a, far_b,
    gain_sum, gain_seq, gain_slot, gain_rank,
    sems, near_sems, next_sems, far_sems, first_sems, load_sems, own_sems, step_sems, credit,
):
    slots, rows_b, width = w_b.shape
    rows_a = w_a.shape[1]
    ffn_cols = rows_b // 3
    ranks = n_head // slots
    rows = x_own.shape[1]
    length = slots * ranks * rows
    part = width // n_seq
    place = Place(n_seq, n_head, slots)
    slot = place.slot
    beside, across = place.beside, place.across
    corner = 3 - place.seq
    mine = lanes(place.seq, part)
    other = 1 - place.rank
    elsewhere = place.device(seq=beside)
    ids = {}
    sections = {
        "a": (0, w_a, near_a, next_a, far_a, sum_a, full_a, 128),
        "b": (1, w_b, near_b, next_b, far_b, sum_b, full_b, rows_b // 6),
    }

    def remote(name, src, dst, device, send=None, recv=None):
        if send is None:
            i = ids.setdefault(name, len(ids))
            send, recv = sems.at[0, i], sems.at[1, i]
        return pltpu.make_async_remote_copy(
            src_ref=src, dst_ref=dst, send_sem=send, recv_sem=recv,
            device_id=device, device_id_type=MESH,
        )

    def position(p, rank):
        return pl.ds(pl.multiple_of((p * ranks + rank) * rows, rows), rows)

    def halves(sec):
        half = sections[sec][1].shape[1] // 2
        return pl.ds(0, half), pl.ds(half, half)

    def near_copies(sec, k):
        i, grads, near = sections[sec][:3]
        upper, lower = halves(sec)
        plan = (
            (upper, beside, beside), (upper, corner, beside),
            (lower, across, across), (lower, corner, across),
        )
        return [
            remote(None, grads.at[k, cut, lanes(quarter, part)], near.at[k, n],
                   place.device(seq=to), near_sems.at[0, i, k, n], near_sems.at[1, i, k, n])
            for n, (cut, quarter, to) in enumerate(plan)
        ]

    def next_copies(sec, k):
        i, grads, _, then = sections[sec][:4]
        upper, lower = halves(sec)
        plan = ((upper, across), (lower, beside))
        return [
            remote(None, grads.at[k, cut, lanes(to, part)], then.at[k, n],
                   place.device(seq=to), next_sems.at[0, i, k, n], next_sems.at[1, i, k, n])
            for n, (cut, to) in enumerate(plan)
        ]

    upper = slot // 2
    inner = (slot + upper) % 2
    toward = 1 - 2 * upper

    def far_copy(sec, k):
        i, grads = sections[sec][:2]
        far = sections[sec][4]
        to = slot + toward * (1 - 2 * inner * (1 - k // 2))
        landing = inner * (4 - 3 * (k // 3)) + (1 - inner) * ((k // 2) * k)
        return remote(None, grads.at[k, :, mine], far.at[landing], place.device(slot=to),
                      far_sems.at[0, i, k], far_sems.at[1, i, landing])

    def far_wait(sec, landing):
        i, grads = sections[sec][:2]
        far = sections[sec][4]
        remote(None, grads.at[0, :, mine], far.at[landing], elsewhere,
               far_sems.at[0, i, 0], far_sems.at[1, i, landing]).wait_recv()

    def add_rows(sec, k, begin, where, addend):
        grads, strip = sections[sec][1], sections[sec][7]

        def one(i, carry):
            at = pl.ds(pl.multiple_of(begin + i * strip, 16), strip)
            value = grads[k, at, where].astype(F32)
            value = value + addend[pl.ds(pl.multiple_of(i * strip, 16), strip), :].astype(F32)
            grads[k, at, where] = value.astype(BF16)
            return carry

        lax.fori_loop(0, addend.shape[0] // strip, one, 0)

    def launch(sec, k):
        for copy in near_copies(sec, k):
            copy.start()

    def second(sec, k):
        near = sections[sec][2]
        half = near.shape[2]
        came = near_copies(sec, k)
        onward = next_copies(sec, k)
        came[1].wait_recv()
        add_rows(sec, k, 0, lanes(across, part), near.at[k, 1])
        onward[0].start()
        came[3].wait_recv()
        add_rows(sec, k, half, lanes(beside, part), near.at[k, 3])
        onward[1].start()
        came[0].wait_recv()
        add_rows(sec, k, 0, mine, near.at[k, 0])
        came[2].wait_recv()
        add_rows(sec, k, half, mine, near.at[k, 2])

    def third(sec, k, sends):
        then = sections[sec][3]
        half = then.shape[2]
        for n, copy in enumerate(next_copies(sec, k)):
            copy.wait_recv()
            add_rows(sec, k, n * half, mine, then.at[k, n])
        if sends:
            @pl.when(inner == 0)
            def _():
                far_copy(sec, k).start()

    def fourth(sec, k):
        @pl.when(inner == 1)
        def _():
            far_wait(sec, k)
            add_rows(sec, k, 0, mine, sections[sec][4].at[k])
            far_copy(sec, k).start()

    def gather_copies(sec):
        total, full = sections[sec][5:7]
        half = total.shape[0] // 2
        near = [
            remote(("full", sec, n), total, full.at[:, mine], place.device(seq=to))
            for n, to in enumerate((beside, across))
        ]
        far = []
        for n, (source, to) in enumerate(((beside, across), (across, beside))):
            where = full.at[pl.ds(n * half, half), lanes(source, part)]
            far.append(remote(("relay", sec, n), where, where, place.device(seq=to)))
        return near, far

    def own_copy(sec):
        i = sections[sec][0]
        return pltpu.make_async_copy(
            sections[sec][5], sections[sec][6].at[:, mine], own_sems.at[3 + i]
        )

    def finish(sec):
        grads = sections[sec][1]
        far, total, _, strip = sections[sec][4:]

        @pl.when(inner == 1)
        def _():
            far_wait(sec, 0)
            add_rows(sec, 0, 0, mine, far.at[0])

        far_wait(sec, 4)

        def one(r, carry):
            at = pl.ds(pl.multiple_of(r * strip, 16), strip)
            value = grads[0, at, mine].astype(F32) + far[4, at, :].astype(F32)
            total[at, :] = value.astype(BF16)
            return carry

        lax.fori_loop(0, total.shape[0] // strip, one, 0)
        own_copy(sec).start()
        for copy in gather_copies(sec)[0]:
            copy.start()

    def relay(sec):
        near, far = gather_copies(sec)
        for n in range(2):
            near[n].wait_recv()
            far[n].start()

    loads = {
        "h2": (h_two_ref, normed_all), "e": (e_ref, e_all), "h1": (h_one_ref, normed_all),
        "ffn": (ffn_ref, acc_one),
        "a": (wa_ref, w_a), "x": (x_ref, x_own), "mid": (mid_ref, middle),
        "g": (g_ref, g_own), "q": (q_ref, q_all), "k": (k_ref, k_all), "v": (v_ref, v_all),
        "att": (att_ref, att_all),
    }

    def load(name):
        src, dst = loads[name]
        return pltpu.make_async_copy(src, dst, load_sems.at[slots + list(loads).index(name)])

    def load_b(k):
        return pltpu.make_async_copy(wb_ref.at[k], w_b.at[k], load_sems.at[k])

    load_b(slots - 1).start()
    load("h2").start()
    load("e").start()
    load("ffn").start()
    load("x").start()
    load("mid").start()
    for k in reversed(range(slots - 1)):
        load_b(k).start()
    for name in loads:
        if name not in ("h1", "h2", "e", "ffn", "x", "mid"):
            load(name).start()
    place.greet(True)
    load("h2").wait()
    load("e").wait()
    load("ffn").wait()

    strip = length // 2
    key_sum, value_sum = acc_two.at[:, :LANES], acc_two.at[:, LANES : 2 * LANES]

    def away_copy(n, p):
        return remote(("away", n, p), away.at[p], back.at[p], place.device(rank=other))

    def swap(name, src, dst):
        return [
            remote((name, j), src.at[place.at_slot(j)], dst.at[slot],
                   place.device(slot=place.at_slot(j)))
            for j in (2, 3, 1)
        ]

    def keep(n, src, dst):
        return pltpu.make_async_copy(src, dst.at[slot], own_sems.at[n])

    def send_away(n, acc):
        if n > 0:
            pl.semaphore_wait(credit, 1)
        for p in range(slots):
            if n > 0:
                away_copy(n - 1, p).wait_send()
            away[p] = acc[position(p, other), :].astype(BF16)
            away_copy(n, p).start()

    def taken():
        pl.semaphore_signal(credit, inc=1, device_id=place.device(rank=other), device_id_type=MESH)

    live = live_ref[...]

    def block_delta():
        load("x").wait()
        load("mid").wait()
        for p in range(slots):
            away_copy(0, p).wait_recv()
            out = acc_one[position(p, place.rank), :] + back[p].astype(F32)
            delta_own[p] = ((middle[p] - x_own[p].astype(F32) + out) * live).astype(BF16)
        taken()
        for copy in swap("block", delta_own, block_out):
            copy.start()
        keep(0, delta_own.at[slot], block_out).start()

    def pump(schedule, i, point):
        for (turn, at), acts in schedule.items():
            if at == point:
                @pl.when(i == turn)
                def _(acts=acts):
                    for act in acts:
                        act()

    unit_events = {
        (2, 0): [lambda: second("b", 3)],
        (3, 0): [lambda: second("b", 2)],
    }
    head_events = {
        (0, 0): [lambda: third("b", 3, True)],
        (0, 2): [lambda: second("b", 1)],
        (1, 1): [lambda: third("b", 2, True)],
        (2, 1): [lambda: fourth("b", 3)],
        (2, 2): [lambda: second("b", 0)],
    }

    def units(i, carry):
        k = slots - 1 - i
        load_b(k).wait()

        def strips(n, carry):
            at = pl.ds(pl.multiple_of(n * strip, strip), strip)
            inner = normed_all[at, :]
            gate = dot_nt(inner, w_b[k, :ffn_cols, :])
            up = dot_nt(inner, w_b[k, ffn_cols : 2 * ffn_cols, :])
            sigmoid_gate = 1.0 / (1.0 + jnp.exp(-gate))
            activated = gate * sigmoid_gate
            hid = (activated * up).astype(BF16)
            hidden[at, :] = hid
            d_hidden = dot_nt(e_all[at, :], w_b[k, 2 * ffn_cols :, :])
            dg = (d_hidden * up * sigmoid_gate * (1.0 + gate * (1.0 - sigmoid_gate))).astype(BF16)
            du = (d_hidden * activated).astype(BF16)
            d_gate[at, :] = dg
            d_project[at, :ffn_cols] = du
            d_in = dot_nn(dg, w_b[k, :ffn_cols, :]) + dot_nn(du, w_b[k, ffn_cols : 2 * ffn_cols, :])

            @pl.when(i == 0)
            def _():
                acc_one[at, :] += dot_nn(hid, w_b[k, 2 * ffn_cols :, :])
                acc_two[at, :] = d_in

            @pl.when(i > 0)
            def _():
                acc_two[at, :] += d_in

            return carry

        lax.fori_loop(0, length // strip, strips, 0)
        pump(unit_events, i, 0)
        w_b[k, 2 * ffn_cols :, :] = dot_tn(hidden[...], e_all[...]).astype(BF16)
        w_b[k, :ffn_cols, :] = dot_tn(d_gate[...], normed_all[...]).astype(BF16)
        w_b[k, ffn_cols : 2 * ffn_cols, :] = dot_tn(d_project[:, :ffn_cols], normed_all[...]).astype(BF16)
        launch("b", k)

        @pl.when(i == 0)
        def _():
            send_away(0, acc_one)

        @pl.when(i == 1)
        def _():
            block_delta()

        return carry

    lax.fori_loop(0, slots, units, 0)
    load("h1").start()

    def share(p):
        where = e_all.at[position(p, place.rank), :]
        return remote(("share", p), where, where, place.device(rank=other))

    send_away(1, acc_two)
    load("g").wait()
    gain_sum[...] = jnp.zeros_like(gain_sum)
    for p in range(slots):
        value = middle[p]
        inverse = lax.rsqrt(jnp.mean(value * value, axis=-1, keepdims=True) + EPSILON)
        normed = value * inverse
        away_copy(1, p).wait_recv()
        d_normed = acc_two[position(p, place.rank), :] + back[p].astype(F32)
        gain_sum[1:2, :] += jnp.sum(normed * d_normed, axis=0, keepdims=True)
        delta = norm_back(d_normed * gains_ref[1:2, :], normed, inverse)
        middle[p] = delta
        e_all[position(p, place.rank), :] = (g_own[p].astype(F32) * live + delta).astype(BF16)
        share(p).start()
    taken()

    for name in ("a", "h1", "q", "k", "v", "att"):
        load(name).wait()
    for p in range(slots):
        share(p).wait_recv()

    def first_copy(k):
        return remote(None, v_all.at[k], first_out.at[slot],
                      place.device(slot=place.source(k)),
                      first_sems.at[0, k], first_sems.at[1, slot])

    def heads(i, carry):
        k = slots - 1 - i
        lane = lanes(k, LANES)
        pump(head_events, i, 0)
        d_att = dot_nt(e_all[...], w_a[k, 3 * head_cols :, :]).astype(BF16)
        product = (d_att.astype(F32) * att_all[:, lane].astype(F32)).T
        inner = [
            jnp.sum(product[:64], axis=0, keepdims=True),
            jnp.sum(product[64:], axis=0, keepdims=True),
        ]
        key_sum[...] = jnp.zeros_like(key_sum)
        value_sum[...] = jnp.zeros_like(value_sum)
        k_turned = k_all[k].T
        for step in range(length // BLOCK):
            begin, keys = step * BLOCK, (step + 1) * BLOCK
            low = first_key(begin, length)
            queries = two_heads(q_all[k, begin:keys, :])
            d_out = two_heads(d_att[begin:keys, :])
            scores = dot_nt(k_all[k, low:keys, :], queries)
            log_total = jnp.concatenate(
                [lse_ref[k, 0:1, begin:keys], lse_ref[k, 1:2, begin:keys]], axis=1
            )
            chances = jnp.where(seen(first_ref, begin, low, keys - low), jnp.exp(scores - log_total), 0.0)
            d_chances = dot_nt(v_all[k, low:keys, :], d_out)
            rest = jnp.concatenate([inner[0][:, begin:keys], inner[1][:, begin:keys]], axis=1)
            d_scores = (chances * (d_chances - rest)).astype(BF16)
            key_sum[low:keys, :] += dot_nn(d_scores, queries)
            value_sum[low:keys, :] += dot_nn(chances.astype(BF16), d_out)
            d_query = one_pair(dot_nn(k_turned[:, low:keys], d_scores), BLOCK) * 0.125
            d_project[begin:keys, :LANES] = (
                d_query * cos_ref[begin:keys, :] - swap_halves(d_query) * sin_ref[begin:keys, :]
            ).astype(BF16)
        pump(head_events, i, 1)
        d_key = key_sum[...]
        d_project[:, LANES : 2 * LANES] = (
            d_key * cos_ref[...] - swap_halves(d_key) * sin_ref[...]
        ).astype(BF16)
        d_value = (0.5 * value_sum[...]).astype(BF16)
        d_project[:, 2 * LANES :] = d_value
        v_all[k] = d_value

        @pl.when(k > 0)
        def _():
            first_copy(k).start()

        @pl.when(k == 0)
        def _():
            keep(2, v_all.at[0], first_out).start()

        for n in range(2):
            at = pl.ds(n * strip, strip)
            d_in = dot_nn(d_project[at, :], w_a[k, : 3 * head_cols, :])

            @pl.when(i == 0)
            def _():
                acc_one[at, :] = d_in

            @pl.when(i > 0)
            def _():
                acc_one[at, :] += d_in

        w_a[k, : 3 * head_cols, :] = dot_tn(d_project[...], normed_all[...]).astype(BF16)
        w_a[k, 3 * head_cols :, :] = dot_tn(att_all[:, lane], e_all[...]).astype(BF16)
        launch("a", k)

        pump(head_events, i, 2)
        return carry

    lax.fori_loop(0, slots, heads, 0)

    for copy in swap("block", delta_own, block_out):
        copy.wait_send()
    keep(0, delta_own.at[slot], block_out).wait()
    send_away(2, acc_one)
    for p in range(slots):
        value = x_own[p].astype(F32)
        inverse = lax.rsqrt(jnp.mean(value * value, axis=-1, keepdims=True) + EPSILON)
        normed = value * inverse
        away_copy(2, p).wait_recv()
        d_normed = acc_one[position(p, place.rank), :] + back[p].astype(F32)
        gain_sum[0:1, :] += jnp.sum(normed * d_normed, axis=0, keepdims=True)
        delta = norm_back(d_normed * gains_ref[0:1, :], normed, inverse)
        delta_own[p] = ((middle[p] + delta) * live).astype(BF16)
    input_copies = swap("input", delta_own, input_out)
    input_copies[0].start()
    keep(1, delta_own.at[slot], input_out).start()

    def gain_copies(level):
        if level == 0:
            return [
                remote(("gain", 0, d), gain_seq.at[place.seq], gain_seq.at[place.seq],
                       place.device(seq=place.at_seq(d)))
                for d in range(1, n_seq)
            ]
        if level == 1:
            return [
                remote(("gain", 1, j), gain_slot.at[slot], gain_slot.at[slot],
                       place.device(slot=place.at_slot(j)))
                for j in range(1, slots)
            ]
        return [
            remote(("gain", 2, 0), gain_rank.at[place.rank], gain_rank.at[place.rank],
                   place.device(rank=other))
        ]

    def gain_step(level):
        value = gain_sum[...]
        if level > 0:
            for copy in gain_copies(level - 1):
                copy.wait_recv()
            held = (gain_seq, gain_slot, gain_rank)[level - 1]
            value = held[0]
            for j in range(1, held.shape[0]):
                value = value + held[j]
        if level == 3:
            gains_out[...] = value
            return
        target = (gain_seq, gain_slot, gain_rank)[level]
        target[(place.seq, slot, place.rank)[level]] = value
        for copy in gain_copies(level):
            copy.start()

    blocks = root_ref.shape[1]
    jobs = [("b", m, b) for m in range(3) for b in range(blocks)]
    jobs += [("a", m, b) for m in range(4) for b in range(blocks)]
    members = {"a": (0, 1, 2, 5), "b": (3, 4, 6)}
    small = {"a": (head_root, head_buf, step_a), "b": (unit_root, unit_buf, step_b)}
    depth = 8

    def job_root(n):
        acc = (acc_two, acc_one)[n % depth // 4]
        return acc.at[pl.ds(n % 4 * part, part)]

    def job_loads(n):
        sec, m, b = jobs[n]
        root_in, held, _ = small[sec]
        pairs = ((root_ref.at[members[sec][m], b], job_root(n)), (root_in.at[m, b], held.at[n % depth]))
        return [
            pltpu.make_async_copy(src, dst, step_sems.at[0, n % depth, i])
            for i, (src, dst) in enumerate(pairs)
        ]

    def job_store(n):
        sec, m, b = jobs[n]
        _, held, step = small[sec]
        high = held.shape[1]
        return pltpu.make_async_copy(
            job_root(n).at[pl.ds(0, high), pl.ds(0, part)],
            step.at[pl.ds((m * blocks + b) * high, high)], step_sems.at[1, n % depth, 0],
        )

    def run_jobs(first, last):
        for n in range(first, last):
            sec, m, b = jobs[n]
            root = job_root(n)
            held = small[sec][1]
            high = held.shape[1]
            for copy in job_loads(n):
                copy.wait()
            grad = sections[sec][6][pl.ds((m * blocks + b) * high, high), :]
            turned = dot_nn(held[n % depth].astype(BF16), grad).astype(BF16)
            turned = dot_nt(turned, root[...].astype(BF16))
            scale = lax.rsqrt(jnp.mean(turned * turned, axis=0, keepdims=True) + EPSILON)
            root[pl.ds(0, high), pl.ds(0, part)] = turned * scale
            job_store(n).start()
            if n > 0 and n - 1 + depth < len(jobs):
                job_store(n - 1).wait()
                for copy in job_loads(n - 1 + depth):
                    copy.start()

    def full_copy(sec):
        i = sections[sec][0]
        return pltpu.make_async_copy(
            sections[sec][6], (full_a_out, full_b_out)[i], step_sems.at[1, i, 1]
        )

    for n in range(depth):
        for copy in job_loads(n):
            copy.start()
    gain_step(0)
    second("a", 3)
    third("b", 1, True)
    fourth("b", 2)
    input_copies[1].start()
    second("a", 2)
    fourth("b", 1)
    input_copies[2].start()
    second("a", 1)
    gain_step(1)
    third("b", 0, False)
    second("a", 0)
    finish("b")
    third("a", 3, True)
    third("a", 2, True)
    fourth("a", 3)
    third("a", 1, True)
    fourth("a", 2)
    relay("b")
    gain_step(2)
    third("a", 0, False)
    fourth("a", 1)
    gain_step(3)
    finish("a")
    for copy in gather_copies("b")[1]:
        copy.wait_recv()
    own_copy("b").wait()
    full_copy("b").start()
    run_jobs(0, 6)
    relay("a")
    for copy in gather_copies("a")[1]:
        copy.wait_recv()
    own_copy("a").wait()
    full_copy("a").start()
    run_jobs(6, len(jobs))
    for n in range(len(jobs) - depth, len(jobs)):
        job_store(n).wait()
    full_copy("a").wait()
    full_copy("b").wait()
    for sec in ("b", "a"):
        near, far = gather_copies(sec)
        for copy in far:
            copy.wait_send()
        for copy in near:
            copy.wait_send()
        for k in range(slots):
            for copy in near_copies(sec, k) + next_copies(sec, k):
                copy.wait_send()
            if k > 0:
                far_copy(sec, k).wait_send()
    for copy in swap("block", delta_own, block_out):
        copy.wait_recv()
    for copy in swap("input", delta_own, input_out):
        copy.wait()
    for j in range(1, slots):
        source = place.at_slot(j)
        remote(None, v_all.at[0], first_out.at[source], elsewhere,
               first_sems.at[0, 0], first_sems.at[1, source]).wait_recv()
        first_copy(j).wait_send()
    for p in range(slots):
        away_copy(2, p).wait_send()
        share(p).wait_send()
    for level in range(3):
        for copy in gain_copies(level):
            copy.wait_send()
    keep(1, delta_own.at[slot], input_out).wait()
    keep(2, v_all.at[0], first_out).wait()


def backward_part(n_seq, n_head, head_cols, saved, gains, tables, live, roots):
    (
        x_own, h_one, q_rot, k_rot, v_mix, attended, log_total, weights_a, weights_b, middle, h_two,
        grad_own, e_all, ffn,
    ) = saved
    cos_wide, sin_wide, first_pos = tables
    _, roots_head, roots_unit = roots
    slots, rows, width = x_own.shape
    length = h_one.shape[0]
    rows_a, rows_b = weights_a.shape[1], weights_b.shape[1]
    part = width // n_seq
    ranks = n_head // slots
    any_space = pl.BlockSpec(memory_space=pl.ANY)
    vmem = pl.BlockSpec(memory_space=pltpu.VMEM)
    shape = jax.ShapeDtypeStruct
    like = lambda value: pltpu.VMEM(value.shape, value.dtype)
    count = 2 * 4 + 3 * slots + slots + 2 * (slots - 1) + n_seq + slots + 4
    sem = pltpu.SemaphoreType.DMA
    return pl.pallas_call(
        functools.partial(backward_kernel, n_seq, n_head, head_cols),
        in_specs=[any_space] * 16 + [vmem] * 6,
        out_specs=[any_space] * 3 + [vmem] * 3 + [any_space] * 4,
        out_shape=[
            shape(x_own.shape, BF16),
            shape(x_own.shape, BF16),
            shape((slots, length, head_cols), BF16),
            shape((8, width), F32),
            shape((rows_a, part), BF16),
            shape((rows_b, part), BF16),
            shape((rows_a, width), BF16),
            shape((rows_b, width), BF16),
            shape((rows_a, part), F32),
            shape((rows_b, part), F32),
        ],
        scratch_shapes=[
            like(weights_a), like(weights_b), like(h_two), like(e_all), like(x_own), like(middle),
            like(grad_own),
            like(q_rot), like(k_rot), like(v_mix), like(attended),
            pltpu.VMEM((length, width), F32),
            pltpu.VMEM((length, width), F32),
            pltpu.VMEM((length, rows_b // 3), BF16),
            pltpu.VMEM((length, rows_b // 3), BF16),
            pltpu.VMEM((length, 3 * LANES), BF16),
            like(x_own), like(x_own), like(x_own),
            pltpu.VMEM((rows_a, width), BF16),
            pltpu.VMEM((rows_b, width), BF16),
            pltpu.VMEM((8,) + roots_head.shape[2:], F32),
            pltpu.VMEM((8,) + roots_unit.shape[2:], F32),
            pltpu.VMEM((slots, 4, rows_a // 2, part), BF16),
            pltpu.VMEM((slots, 4, rows_b // 2, part), BF16),
            pltpu.VMEM((slots, 2, rows_a // 2, part), BF16),
            pltpu.VMEM((slots, 2, rows_b // 2, part), BF16),
            pltpu.VMEM((slots + 1, rows_a, part), BF16),
            pltpu.VMEM((slots + 1, rows_b, part), BF16),
            pltpu.VMEM((8, width), F32),
            pltpu.VMEM((n_seq, 8, width), F32),
            pltpu.VMEM((slots, 8, width), F32),
            pltpu.VMEM((ranks, 8, width), F32),
            sem((2, count)),
            sem((2, 2, slots, 4)),
            sem((2, 2, slots, 2)),
            sem((2, 2, slots + 1)),
            sem((2, slots)),
            sem((slots + 12,)),
            sem((5,)),
            sem((2, 8, 2)),
            pltpu.SemaphoreType.REGULAR,
        ],
        compiler_params=pltpu.CompilerParams(
            collective_id=2, has_side_effects=True, vmem_limit_bytes=64 << 20
        ),
    )(
        weights_a, weights_b, h_one, h_two, x_own, middle, grad_own, q_rot, k_rot, v_mix, attended,
        e_all, ffn, *roots, log_total, gains, cos_wide, sin_wide, first_pos[None, :], live,
    )


def reduce_kernel(
    n_seq, n_head, chunks,
    block_ref, input_ref, first_ref, gains_ref, grads_a, grads_b,
    block_out, input_out, first_out, gains_out, sum_a, sum_b, full_a, full_b,
    near_a, near_b, turn_a, turn_b, far_a, far_b, gain_seq, gain_slot, gain_rank,
    send_sems, recv_sems, own_sems, far_recv, first_recv,
):
    slots = block_ref.shape[0]
    place = Place(n_seq, n_head, slots)
    place.greet(True)
    sender = Sender(send_sems, recv_sems)
    part = sum_a.shape[1]
    mine = lanes(place.seq, part)
    order = [2, 3, 1, 0]
    parts = ((grads_b, sum_b, full_b, near_b, turn_b, far_b, chunks[1]),
             (grads_a, sum_a, full_a, near_a, turn_a, far_a, chunks[0]))
    copies, received = [], []

    def arrive(copy):
        copy.wait_recv()
        received.append(copy)

    def swap(src, dst):
        return [
            sender.start(
                src.at[place.at_slot(k)], dst.at[place.slot], place.device(slot=place.at_slot(k))
            )
            for k in (2, 3, 1)
        ]

    gain_seq[place.seq] = gains_ref[...]
    small = [
        sender.start(gain_seq.at[place.seq], gain_seq.at[place.seq],
                     place.device(seq=place.at_seq(d)))
        for d in range(1, n_seq)
    ]
    copies += small

    def to_seqs(grads, near, k):
        return [
            sender.start(
                grads.at[k, :, lanes(place.at_seq(d), part)],
                near.at[k, d - 1],
                place.device(seq=place.at_seq(d)),
            )
            for d in range(1, n_seq)
        ]

    sent = {}
    units = [(which, k) for which in range(2) for k in order]

    def launch(unit):
        which, k = unit
        sent[unit] = to_seqs(parts[which][0], parts[which][3], k)
        copies.extend(sent[unit])

    own = [
        pltpu.make_async_copy(src, dst.at[place.slot], own_sems.at[i])
        for i, (src, dst) in enumerate(
            (
                (block_ref.at[place.slot], block_out),
                (input_ref.at[place.slot], input_out),
                (first_ref.at[0], first_out),
            )
        )
    ]
    for copy in own:
        copy.start()
    launch(units[0])
    launch(units[1])
    copies += swap(block_ref, block_out)
    for copy in small:
        arrive(copy)
    total = gain_seq[0]
    for i in range(1, n_seq):
        total = total + gain_seq[i]
    gain_slot[place.slot] = total
    small = [
        sender.start(gain_slot.at[place.slot], gain_slot.at[place.slot],
                     place.device(slot=place.at_slot(k)))
        for k in range(1, slots)
    ]
    copies += small
    elsewhere = place.device(seq=place.at_seq(1))
    for index, unit in enumerate(units):
        which, k = unit
        grads, _, _, near, turn, far, chunk = parts[which]
        if index + 2 < len(units):
            launch(units[index + 2])
        for copy in sent[unit]:
            arrive(copy)

        def add(i, carry, grads=grads, near=near, turn=turn, k=k, chunk=chunk):
            rows = pl.ds(pl.multiple_of(i * chunk, chunk), chunk)
            value = grads[k, rows, mine].astype(F32)
            for d in range(n_seq - 1):
                value = value + near[k, d, rows, :].astype(F32)
            turn[k, rows, :] = value.astype(BF16)
            return carry

        lax.fori_loop(0, grads.shape[1] // chunk, add, 0)
        if k != 0:
            copy = sender.start(
                turn.at[k], far.at[place.slot], place.device(slot=place.source(k)),
                far_recv.at[which, place.slot],
            )
            copies.append(copy)
            received.append(copy)
        if index == 1:
            for j in range(1, slots):
                copy = sender.start(
                    first_ref.at[j], first_out.at[place.slot],
                    place.device(slot=place.source(j)), first_recv.at[place.slot],
                )
                copies.append(copy)
                received.append(copy)
        if index == 4:
            copies += swap(input_ref, input_out)
            for copy in small:
                arrive(copy)
            total = gain_slot[0]
            for i in range(1, slots):
                total = total + gain_slot[i]
            gain_rank[place.rank] = total
            small = [
                sender.start(gain_rank.at[place.rank], gain_rank.at[place.rank],
                             place.device(rank=(place.rank + j) % place.ranks))
                for j in range(1, place.ranks)
            ]
            copies += small
        if k == 0:
            for j in range(1, slots):
                source = place.at_slot(j)
                pltpu.make_async_remote_copy(
                    src_ref=turn.at[0], dst_ref=far.at[source], send_sem=send_sems.at[0],
                    recv_sem=far_recv.at[which, source], device_id=elsewhere, device_id_type=MESH,
                ).wait_recv()
            _, total_ref, full, _, _, _, _ = parts[which]

            def finish(i, carry, turn=turn, far=far, total_ref=total_ref, full=full, chunk=chunk):
                rows = pl.ds(pl.multiple_of(i * chunk, chunk), chunk)
                value = turn[0, rows, :].astype(F32)
                for j in range(1, slots):
                    value = value + far[place.at_slot(j), rows, :].astype(F32)
                value = value.astype(BF16)
                total_ref[rows, :] = value
                full[rows, mine] = value
                return carry

            lax.fori_loop(0, grads.shape[1] // chunk, finish, 0)
            copies += [
                sender.start(total_ref, full.at[:, mine], place.device(seq=place.at_seq(d)))
                for d in range(1, n_seq)
            ]
    for copy in small:
        arrive(copy)
    total = gain_rank[0]
    for i in range(1, place.ranks):
        total = total + gain_rank[i]
    gains_out[...] = total
    for copy in copies:
        if all(copy is not other for other in received):
            copy.wait_recv()
    for j in range(1, slots):
        source = place.at_slot(j)
        pltpu.make_async_remote_copy(
            src_ref=first_ref.at[0], dst_ref=first_out.at[source], send_sem=send_sems.at[0],
            recv_sem=first_recv.at[source], device_id=elsewhere, device_id_type=MESH,
        ).wait_recv()
    for copy in copies:
        copy.wait_send()
    for copy in own:
        copy.wait()


def reduce_grads(n_seq, n_head, chunks, block_delta, input_delta, first_delta, gains, grads_a, grads_b):
    slots = block_delta.shape[0]
    part = grads_a.shape[2] // n_seq
    rows = (grads_a.shape[1], grads_b.shape[1])
    ranks = n_head // slots
    count = (
        3 * (slots - 1) + 2 * (slots * (n_seq - 1) + (slots - 1) + (n_seq - 1))
        + (n_seq - 1) + (slots - 1) + (ranks - 1)
    )
    any_space = pl.BlockSpec(memory_space=pl.ANY)
    vmem = pl.BlockSpec(memory_space=pltpu.VMEM)
    like = lambda value: jax.ShapeDtypeStruct(value.shape, value.dtype)
    return pl.pallas_call(
        functools.partial(reduce_kernel, n_seq, n_head, chunks),
        in_specs=[any_space] * 3 + [vmem] * 3,
        out_specs=[any_space] * 3 + [vmem] * 5,
        out_shape=[like(block_delta), like(input_delta), like(first_delta), like(gains)]
        + [jax.ShapeDtypeStruct((r, part), BF16) for r in rows]
        + [jax.ShapeDtypeStruct((r, part * n_seq), BF16) for r in rows],
        scratch_shapes=[pltpu.VMEM((slots, n_seq - 1, r, part), BF16) for r in rows]
        + [pltpu.VMEM((slots, r, part), BF16) for r in rows]
        + [pltpu.VMEM((slots, r, part), BF16) for r in rows]
        + [pltpu.VMEM((n,) + gains.shape, F32) for n in (n_seq, slots, ranks)]
        + [
            pltpu.SemaphoreType.DMA((count,)),
            pltpu.SemaphoreType.DMA((count,)),
            pltpu.SemaphoreType.DMA((3,)),
            pltpu.SemaphoreType.DMA((2, slots)),
            pltpu.SemaphoreType.DMA((slots,)),
        ],
        compiler_params=pltpu.CompilerParams(
            collective_id=1, has_side_effects=True, vmem_limit_bytes=56 << 20
        ),
    )(block_delta, input_delta, first_delta, gains, grads_a, grads_b)


def shampoo_kernel(
    stat_ref, root_ref, head_stat, head_root, unit_stat, unit_root, full_a, sum_a, full_b, sum_b,
    wide_ref, out_right_ref, new_head, new_unit, step_a, step_b,
):
    step = pl.program_id(0)
    blocks = stat_ref.shape[1]

    def one(member, width, small_stat, small_root, full, total, big_out, small_out, step_out):
        for b in range(blocks):
            rows = pl.ds(pl.multiple_of((member * blocks + b) * width, 16), width)
            grad, own = full[rows, :], total[rows, :]
            big_out[0, b] = STAT_DECAY * stat_ref[0, b] + (1.0 - STAT_DECAY) * dot_tn(own, grad)
            small_out[member, b] = STAT_DECAY * small_stat[member, b] + (
                1.0 - STAT_DECAY
            ) * dot_nt(grad, grad)
            turned = dot_nn(small_root[member, b].astype(BF16), grad).astype(BF16)
            turned = dot_nt(turned, root_ref[0, b].astype(BF16))
            scale = lax.rsqrt(jnp.mean(turned * turned, axis=0, keepdims=True) + EPSILON)
            step_out[rows, :] = turned * scale

    head_width, unit_width = head_stat.shape[2], unit_stat.shape[2]
    head_args = (head_width, head_stat, head_root, full_a, sum_a)
    unit_args = (unit_width, unit_stat, unit_root, full_b, sum_b)

    @pl.when(step < 3)
    def _():
        one(step, *head_args, wide_ref, new_head, step_a)

    @pl.when((step >= 3) & (step < 6))
    def _():
        one(step - 3, *unit_args, wide_ref, new_unit, step_b)

    @pl.when(step == 6)
    def _():
        one(3, *head_args, out_right_ref, new_head, step_a)


def shampoo(stats_wide, roots_wide, stats_head, roots_head, stats_unit, roots_unit, full_a, sum_a, full_b, sum_b):
    members, blocks, part, width = stats_wide.shape
    member = lambda i: (jnp.where(i == 5, 6, jnp.where(i == 6, 5, i)), 0, 0, 0)
    wide = pl.BlockSpec((1, blocks, part, width), member)
    vmem = pl.BlockSpec(memory_space=pltpu.VMEM)
    return pl.pallas_call(
        shampoo_kernel,
        grid=(members,),
        in_specs=[wide, wide] + [vmem] * 8,
        out_specs=[
            pl.BlockSpec((1, blocks, part, width), lambda i: (jnp.minimum(i, 5), 0, 0, 0)),
            pl.BlockSpec((1, blocks, part, width), lambda i: (0, 0, 0, 0)),
            vmem, vmem, vmem, vmem,
        ],
        out_shape=[
            jax.ShapeDtypeStruct((members - 1, blocks, part, width), F32),
            jax.ShapeDtypeStruct((1, blocks, part, width), F32),
            jax.ShapeDtypeStruct(stats_head.shape, F32),
            jax.ShapeDtypeStruct(stats_unit.shape, F32),
            jax.ShapeDtypeStruct(sum_a.shape, F32),
            jax.ShapeDtypeStruct(sum_b.shape, F32),
        ],
        compiler_params=pltpu.CompilerParams(vmem_limit_bytes=48 << 20),
    )(stats_wide, roots_wide, stats_head, roots_head, stats_unit, roots_unit, full_a, sum_a, full_b, sum_b)


def finish_kernel(
    blocks, stat_ref, head_stat, unit_stat, full_a, sum_a, full_b, sum_b, step_a, step_b,
    w_qkv, w_gate_up, w_out, w_down, gains_ref, norm_ref,
    block_got, x_ref, input_got, g_ref, first_got,
    wide_ref, right_ref, new_head, new_unit, grad_qkv, grad_gate_up, grad_out, grad_down,
    new_qkv, new_gate_up, new_out, new_down, grad_gains, new_gains, block_out, input_out, first_out,
):
    step = pl.program_id(0)
    member, b = step // blocks, step % blocks

    def one(m, small_stat, full, total, big_out, small_out):
        width = small_stat.shape[2]
        rows = pl.ds(pl.multiple_of((m * blocks + b) * width, 16), width)
        grad, own = full[rows, :], total[rows, :]
        big_out[0, 0] = STAT_DECAY * stat_ref[0, 0] + (1.0 - STAT_DECAY) * dot_tn(own, grad)
        small_out[m, b] = STAT_DECAY * small_stat[m, b] + (1.0 - STAT_DECAY) * dot_nt(grad, grad)

    head_args, unit_args = (head_stat, full_a, sum_a), (unit_stat, full_b, sum_b)

    @pl.when(member < 3)
    def _():
        one(member, *head_args, wide_ref, new_head)

    @pl.when((member >= 3) & (member < 6))
    def _():
        one(member - 3, *unit_args, wide_ref, new_unit)

    @pl.when(member == 6)
    def _():
        one(3, *head_args, right_ref, new_head)

    @pl.when(step % 4 == 0)
    def _():
        block_out[...] = x_ref[...].astype(F32) + block_got[...].astype(F32)

    @pl.when(step % 4 == 1)
    def _():
        input_out[...] = g_ref[...].astype(F32) + input_got[...].astype(F32)

    @pl.when(step % 4 == 2)
    def _():
        first_out[...] = first_got[...].astype(F32)

    def stepped(i, at, total, steps, old, grad_ref, new_ref, turn):
        grad, change = total[at, :].astype(F32), STEP_RATE * steps[at, :]
        grad_ref[i] = grad.T if turn else grad
        new_ref[i] = old[i] - (change.T if turn else change)

    high = w_qkv.shape[2]
    for i in range(3):
        @pl.when(step == i)
        def _(i=i):
            stepped(i, pl.ds(i * high, high), sum_a, step_a, w_qkv, grad_qkv, new_qkv, True)

    tall = w_gate_up.shape[1]
    for i in range(2):
        @pl.when(step == 3 + i)
        def _(i=i):
            stepped(
                i, pl.ds(i * tall, tall), sum_b, step_b, w_gate_up, grad_gate_up, new_gate_up, False
            )

    @pl.when(step == 5)
    def _():
        at = pl.ds(3 * high, high)
        grad_out[...] = sum_a[at, :].astype(F32)
        new_out[...] = w_out[...] - OUT_RATE * step_a[at, :]

    @pl.when(step == 6)
    def _():
        at = pl.ds(2 * tall, tall)
        grad_down[...] = sum_b[at, :].astype(F32)
        new_down[...] = w_down[...] - STEP_RATE * step_b[at, :]

    @pl.when(step == 7)
    def _():
        gains = gains_ref[0:2, :]
        grad_gains[...] = gains
        scale = lax.rsqrt(jnp.mean(gains * gains, axis=-1, keepdims=True) + EPSILON)
        new_gains[...] = norm_ref[...] - GAIN_RATE * gains * scale


def finish(
    stats_wide, stats_head, stats_unit, full_a, sum_a, full_b, sum_b, step_a, step_b,
    w_qkv, w_gate_up, w_out, w_down, gains, norm_gains,
    block_got, layer_input, input_got, out_grad, first_got,
):
    members, blocks, part, width = stats_wide.shape
    slots, rows, _ = layer_input.shape
    length, head_cols = first_got.shape[1:]
    steps = 4 * slots

    def source(i):
        m = jnp.minimum(i // blocks, members - 1)
        return jnp.where(m == 5, 6, jnp.where(m == 6, 5, m)), i % blocks, 0, 0

    last = (members - 1) * blocks
    block = (1, 1, part, width)

    def right(i):
        return 0, jnp.clip(i - last, 0, blocks - 1), 0, 0

    def wide(i):
        at = jnp.minimum(i, last - 1)
        return at // blocks, at % blocks, 0, 0

    vmem = pl.BlockSpec(memory_space=pltpu.VMEM)
    tokens = pl.BlockSpec((1, rows, width), lambda i: (i // 4, 0, 0))
    firsts = pl.BlockSpec((1, length, head_cols), lambda i: (i // 4, 0, 0))
    like = lambda *values: [jax.ShapeDtypeStruct(v.shape, F32) for v in values]
    weights = (w_qkv, w_gate_up, w_out, w_down)
    return pl.pallas_call(
        functools.partial(finish_kernel, blocks),
        grid=(steps,),
        in_specs=[pl.BlockSpec(block, source)] + [vmem] * 14 + [tokens] * 4 + [firsts],
        out_specs=[pl.BlockSpec(block, wide), pl.BlockSpec(block, right)] + [vmem] * 12
        + [tokens, tokens, firsts],
        out_shape=[
            jax.ShapeDtypeStruct((members - 1, blocks, part, width), F32),
            jax.ShapeDtypeStruct((1, blocks, part, width), F32),
        ]
        + like(stats_head, stats_unit, *weights, *weights, norm_gains, norm_gains, layer_input, out_grad, first_got),
        compiler_params=pltpu.CompilerParams(vmem_limit_bytes=60 << 20),
    )(
        stats_wide, stats_head, stats_unit, full_a, sum_a, full_b, sum_b, step_a, step_b,
        w_qkv, w_gate_up, w_out, w_down, gains, norm_gains,
        block_got, layer_input, input_got, out_grad, first_got,
    )


class Links:
    def __init__(self, n_seq, n_head, slots):
        self.n_seq, self.n_head, self.slots = n_seq, n_head, slots
        self.ranks = n_head // slots
        self.slot = lax.axis_index("head") // self.ranks
        self.rank = lax.axis_index("head") % self.ranks

    def permute(self, value, partner):
        pairs = []
        for s in range(self.n_seq):
            for h in range(self.n_head):
                to_s, to_h = partner(s, h)
                pairs.append((s * self.n_head + h, to_s * self.n_head + to_h))
        return lax.ppermute(value, AXES, pairs)

    def swap_slots(self, value):
        got = [lax.dynamic_index_in_dim(value, self.slot, 0, keepdims=False)]
        for step in range(1, self.slots):
            piece = lax.dynamic_index_in_dim(value, self.slot ^ step, 0, keepdims=False)
            got.append(self.permute(piece, lambda s, h: (s, h ^ (step * self.ranks))))
        got = jnp.stack(got)
        return jnp.stack(
            [lax.dynamic_index_in_dim(got, self.slot ^ q, 0, keepdims=False) for q in range(self.slots)]
        )

    def gather_ranks(self, value):
        got = [value] + [
            self.permute(value, lambda s, h: (s, h ^ step)) for step in range(1, self.ranks)
        ]
        got = jnp.stack(got)
        return jnp.stack(
            [lax.dynamic_index_in_dim(got, self.rank ^ r, 0, keepdims=False) for r in range(self.ranks)]
        )

    def sum_ranks(self, value):
        total = lax.dynamic_index_in_dim(value, self.rank, 0, keepdims=False)
        for step in range(1, self.ranks):
            piece = lax.dynamic_index_in_dim(value, self.rank ^ step, 0, keepdims=False)
            got = self.permute(piece.astype(BF16), lambda s, h: (s, h ^ step))
            total = total + got.astype(F32)
        return total

    def whole_sequence(self, own):
        both = self.gather_ranks(own)
        return jnp.swapaxes(both, 0, 1).reshape(-1, own.shape[-1])

    def own_sum(self, full):
        rows = full.shape[0] // (self.slots * self.ranks)
        parts = full.reshape(self.slots, self.ranks, rows, full.shape[-1])
        return self.sum_ranks(jnp.swapaxes(parts, 0, 1)).reshape(-1, full.shape[-1])


def backward_plain(n_seq, n_head, head_cols, ffn_cols, links, saved, gains, tables, is_live):
    (
        x_bf16, h_one, q_rot, k_rot, v_mix, attended, log_total, weights_a, weights_b, middle,
        h_two, grad_own, d_ffn, _,
    ) = saved
    cos_wide, sin_wide, first_pos = tables
    slots, rows, width = x_bf16.shape
    length = h_one.shape[0]
    rows_a, rows_b = weights_a.shape[1], weights_b.shape[1]
    pairs = slots * head_cols // LANES
    per = LANES // head_cols

    def pair_major(value):
        n = value.shape[2]
        value = value.reshape(pairs, per, length, n, head_cols)
        return value.transpose(0, 2, 3, 1, 4).reshape(pairs, length, n, LANES)

    def slot_major(value):
        n = value.shape[2]
        value = value.reshape(pairs, length, n, per, head_cols)
        return value.transpose(0, 3, 1, 2, 4).reshape(slots, length, n, head_cols)

    w_in, w_o = weights_a[:, : 3 * head_cols], weights_a[:, 3 * head_cols :]
    w_gu, w_d = weights_b[:, : 2 * ffn_cols], weights_b[:, 2 * ffn_cols :]
    x_own = x_bf16.reshape(slots * rows, width).astype(F32)
    middle = middle.reshape(slots * rows, width)
    ein = functools.partial(jnp.einsum, preferred_element_type=F32)
    inverse_one = lax.rsqrt(jnp.mean(x_own * x_own, axis=-1, keepdims=True) + EPSILON)
    normed_one = x_own * inverse_one
    inverse_two = lax.rsqrt(jnp.mean(middle * middle, axis=-1, keepdims=True) + EPSILON)
    normed_two = middle * inverse_two
    saved = (q_rot, k_rot, v_mix, attended, log_total)
    attended = jnp.swapaxes(attended.reshape(length, slots, head_cols), 0, 1)
    gate_up = ein("ld,qfd->qlf", h_two, w_gu)
    gate, up = gate_up[..., :ffn_cols], gate_up[..., ffn_cols:]
    sigmoid_gate = jax.nn.sigmoid(gate)
    activated = gate * sigmoid_gate
    hidden = (activated * up).astype(BF16)
    ffn_out = links.own_sum(ein("qlf,qfd->ld", hidden, w_d))
    block_delta = jnp.where(is_live, middle - x_own + ffn_out, 0.0).astype(BF16)

    d_own = jnp.where(is_live, grad_own, jnp.zeros_like(grad_own))
    d_out = d_own.reshape(slots * rows, width).astype(F32)
    g_down = ein("qlf,ld->qfd", hidden, d_ffn)
    d_hidden = ein("ld,qfd->qlf", d_ffn, w_d)
    d_gate = (
        d_hidden * up * sigmoid_gate * (1.0 + gate * (1.0 - sigmoid_gate))
    ).astype(BF16)
    d_up = (d_hidden * activated).astype(BF16)
    d_gate_up = jnp.concatenate([d_gate, d_up], axis=2)
    d_normed_two = links.own_sum(ein("qlf,qfd->ld", d_gate_up, w_gu))
    g_gate_up = ein("qlf,ld->qfd", d_gate_up, h_two)
    grads_b = jnp.concatenate([g_gate_up.astype(BF16), g_down.astype(BF16)], axis=1)
    gain_two = jnp.sum(normed_two * d_normed_two, axis=0)
    middle_delta = norm_back(d_normed_two * gains[1], normed_two, inverse_two)
    d_middle = d_out + middle_delta
    d_attn = links.whole_sequence(d_middle.astype(BF16).reshape(slots, rows, width))
    d_attended = ein("ld,qcd->qlc", d_attn, w_o).astype(BF16)
    if per > 1:
        d_attended = pair_major(d_attended[:, :, None])[:, :, 0]
    d_project = jnp.concatenate(
        attend_back(saved, d_attended, cos_wide, sin_wide, first_pos), axis=2
    )
    if per > 1:
        d_project = slot_major(d_project.reshape(pairs, length, 3, LANES)).reshape(
            slots, length, 3 * head_cols
        )
    d_value = d_project[:, :, 2 * head_cols :]
    g_out = ein("qlc,ld->qcd", attended, d_attn)
    g_qkv = ein("qlc,ld->qcd", d_project, h_one)
    grads_a = jnp.concatenate([g_qkv.astype(BF16), g_out.astype(BF16)], axis=1)
    d_normed_one = links.own_sum(ein("qlc,qcd->ld", d_project, w_in))
    gain_one = jnp.sum(normed_one * d_normed_one, axis=0)
    input_delta = middle_delta + norm_back(d_normed_one * gains[0], normed_one, inverse_one)
    input_delta = jnp.where(is_live, input_delta, 0.0).astype(BF16)
    gain_rows = jnp.concatenate([gain_one.reshape(8, -1), gain_two.reshape(8, -1)], axis=0)

    return reduce_grads(
        n_seq,
        n_head,
        (LANES, unit_chunk(rows_b)),
        block_delta.reshape(slots, rows, width),
        input_delta.reshape(slots, rows, width),
        d_value,
        gain_rows,
        grads_a,
        grads_b,
    )


def shards(
    n_seq,
    n_head,
    layer_input,
    values_first,
    w_qkv,
    w_gate_up,
    w_out,
    w_down,
    norm_gains,
    out_grad,
    segments,
    counts,
    stats_wide,
    roots_wide,
    stats_head,
    roots_head,
    stats_unit,
    roots_unit,
):
    slots, rows, width = layer_input.shape
    length = segments.shape[1]
    row_part, head_cols, ffn_cols = w_qkv.shape[1], w_qkv.shape[2], w_gate_up.shape[2]
    head_dim = stats_head.shape[2]
    links = Links(n_seq, n_head, slots)
    is_live = links.slot < counts[0]
    pairs = slots * head_cols // LANES
    per = LANES // head_cols
    rows_a, rows_b = 4 * head_cols, 3 * ffn_cols

    fused = n_seq == 4 and slots == 4 and links.ranks == 2 and head_cols == LANES
    cos_wide, sin_wide, first_pos, live, *saved = forward_part(
        n_seq, n_head, head_cols, head_dim, layer_input, values_first, out_grad,
        (w_qkv, jnp.swapaxes(w_gate_up, 1, 2), w_out, w_down), norm_gains, segments, counts, fused,
    )
    first_pos = first_pos[0]
    tables = (cos_wide, sin_wide, first_pos)
    if fused:
        (
            block_got, input_got, first_got, gains, sum_a, sum_b, full_a, full_b, step_a, step_b
        ) = backward_part(
            n_seq, n_head, head_cols, saved, norm_gains, tables, live,
            (roots_wide, roots_head, roots_unit),
        )
        (
            wide, out_right, new_head, new_unit, grad_qkv, grad_gate_up, grad_out, grad_down,
            new_qkv, new_gate_up, new_out, new_down, grad_gains, new_gains,
            block_out, input_grad, first_grad,
        ) = finish(
            stats_wide, stats_head, stats_unit, full_a, sum_a, full_b, sum_b, step_a, step_b,
            w_qkv, jnp.swapaxes(w_gate_up, 1, 2), w_out, w_down, gains, norm_gains,
            block_got, layer_input, input_got, out_grad, first_got,
        )
        return (
            block_out, input_grad, first_grad, grad_qkv, jnp.swapaxes(grad_gate_up, 1, 2),
            grad_out, grad_down, grad_gains, new_qkv, jnp.swapaxes(new_gate_up, 1, 2), new_out, new_down, new_gains,
            wide, out_right[0], new_head, new_unit,
        )
    else:
        block_got, input_got, first_got, gains, sum_a, sum_b, full_a, full_b = backward_plain(
            n_seq, n_head, head_cols, ffn_cols, links, saved, norm_gains, tables, is_live
        )
        gains = gains.reshape(2, width)
        wide, out_right, new_head, new_unit, step_a, step_b = shampoo(
            stats_wide, roots_wide, stats_head, roots_head, stats_unit, roots_unit,
            full_a, sum_a, full_b, sum_b,
        )
        out_right = out_right[0]
    block_out = layer_input.astype(F32) + block_got.astype(F32)
    input_grad = out_grad.astype(F32) + input_got.astype(F32)
    first_grad = first_got.astype(F32)
    grad_gains = gains
    new_gains = norm_gains - GAIN_RATE * grad_gains * lax.rsqrt(
        jnp.mean(grad_gains * grad_gains, axis=-1, keepdims=True) + EPSILON
    )

    cut = 3 * head_cols
    turned = lambda value, n: jnp.swapaxes(value.reshape(n, -1, row_part), 1, 2)
    return (
        block_out,
        input_grad,
        first_grad,
        turned(sum_a[:cut], 3).astype(F32),
        turned(sum_b[: 2 * ffn_cols], 2).astype(F32),
        sum_a[cut:].astype(F32),
        sum_b[2 * ffn_cols :].astype(F32),
        grad_gains,
        w_qkv - STEP_RATE * turned(step_a[:cut], 3),
        w_gate_up - STEP_RATE * turned(step_b[: 2 * ffn_cols], 2),
        w_out - OUT_RATE * step_a[cut:],
        w_down - STEP_RATE * step_b[2 * ffn_cols :],
        new_gains,
        wide,
        out_right,
        new_head,
        new_unit,
    )


def unit_chunk(rows):
    return max(c for c in range(16, 177, 16) if rows % c == 0)


def solution(mesh):
    return jax.shard_map(
        functools.partial(shards, mesh.shape["seq"], mesh.shape["head"]),
        mesh=mesh,
        in_specs=(
            P("seq", "head", None),
            P("seq", None, "head"),
            P(None, "seq", "head"),
            P(None, "seq", "head"),
            P("head", "seq"),
            P("head", "seq"),
            P(),
            P("seq", "head", None),
            P("seq", None),
            P("seq"),
            P(None, "head", "seq", None),
            P(None, "head", "seq", None),
            P(None, "head", None, None),
            P(None, "head", None, None),
            P(None, "head", None, None),
            P(None, "head", None, None),
        ),
        out_specs=(
            P("seq", "head", None),
            P("seq", "head", None),
            P("seq", None, "head"),
            P(None, "seq", "head"),
            P(None, "seq", "head"),
            P("head", "seq"),
            P("head", "seq"),
            P(),
            P(None, "seq", "head"),
            P(None, "seq", "head"),
            P("head", "seq"),
            P("head", "seq"),
            P(),
            P(None, "head", "seq", None),
            P("head", "seq", None),
            P(None, "head", None, None),
            P(None, "head", None, None),
        ),
        check_vma=False,
    )
```

```python
import functools

import jax
import jax.numpy as jnp
from jax import lax
from jax.experimental import pallas as pl
from jax.experimental.pallas import tpu as pltpu
from jax.sharding import PartitionSpec as P

EPSILON = 1e-06
STAT_DECAY = 0.5
STEP_RATE = 0.02
OUT_RATE = 0.1
GAIN_RATE = 0.25
AXES = ("seq", "head")
MESH = pl.DeviceIdType.MESH
LANES = 128
BLOCK = 128
BF16 = jnp.bfloat16
F32 = jnp.float32


def dot_nt(matrix_a, matrix_b):
    return lax.dot_general(
        matrix_a, matrix_b, (((1,), (1,)), ((), ())), preferred_element_type=F32
    )


def dot_tn(matrix_a, matrix_b):
    return lax.dot_general(
        matrix_a, matrix_b, (((0,), (0,)), ((), ())), preferred_element_type=F32
    )


def dot_nn(matrix_a, matrix_b):
    return jnp.dot(matrix_a, matrix_b, preferred_element_type=F32)


def norm_back(d_normed, normed, inverse):
    return inverse * (d_normed - normed * jnp.mean(d_normed * normed, axis=-1, keepdims=True))


def swap_halves(values):
    lane = lax.broadcasted_iota(jnp.int32, values.shape, 1)
    return jnp.where((lane & 32) == 0, pltpu.roll(values, 96, 1), pltpu.roll(values, 32, 1))


def two_heads(block):
    lane = lax.broadcasted_iota(jnp.int32, block.shape, 1)
    zero = jnp.zeros_like(block)
    return jnp.concatenate(
        [jnp.where(lane < 64, block, zero), jnp.where(lane >= 64, block, zero)], axis=0
    )


def one_pair(transposed, width):
    kept = jnp.concatenate([transposed[:64, :width], transposed[64:, width:]], axis=0)
    return kept.T


def first_key(begin, length):
    return max(0, (begin - length // 2 + 1) // BLOCK * BLOCK)


def seen(first_ref, begin, low, key_count):
    first = first_ref[0:1, begin : begin + BLOCK]
    query = begin + lax.broadcasted_iota(jnp.int32, (1, BLOCK), 1)
    first = jnp.concatenate([first, first], axis=1)
    query = jnp.concatenate([query, query], axis=1)
    key = low + lax.broadcasted_iota(jnp.int32, (key_count, 2 * BLOCK), 0)
    return (key >= first) & (key <= query)


def attend_back_kernel(
    qr_ref, kr_ref, vm_ref, att_ref, d_ref, lse_ref, cos_ref, sin_ref, first_ref,
    dq_ref, dk_ref, dv_ref, key_sum, value_sum,
):
    length = qr_ref.shape[1]
    key_sum[...] = jnp.zeros_like(key_sum)
    value_sum[...] = jnp.zeros_like(value_sum)
    k_turned = kr_ref[0].T
    cosine, sine_part = cos_ref[...], sin_ref[...]
    product = (d_ref[0].astype(F32) * att_ref[...].astype(F32)).T
    inner = [
        jnp.sum(product[:64], axis=0, keepdims=True),
        jnp.sum(product[64:], axis=0, keepdims=True),
    ]
    for step in range(length // BLOCK):
        begin, keys = step * BLOCK, (step + 1) * BLOCK
        low = first_key(begin, length)
        queries = two_heads(qr_ref[0, begin:keys, :])
        d_out = two_heads(d_ref[0, begin:keys, :])
        scores = dot_nt(kr_ref[0, low:keys, :], queries)
        log_total = jnp.concatenate(
            [lse_ref[0, 0:1, begin:keys], lse_ref[0, 1:2, begin:keys]], axis=1
        )
        chances = jnp.where(seen(first_ref, begin, low, keys - low), jnp.exp(scores - log_total), 0.0)
        d_chances = dot_nt(vm_ref[0, low:keys, :], d_out)
        part = jnp.concatenate([inner[0][:, begin:keys], inner[1][:, begin:keys]], axis=1)
        d_scores = (chances * (d_chances - part)).astype(BF16)
        key_sum[low:keys, :] += dot_nn(d_scores, queries)
        value_sum[low:keys, :] += dot_nn(chances.astype(BF16), d_out)
        d_query = one_pair(dot_nn(k_turned[:, low:keys], d_scores), BLOCK) * 0.125
        dq_ref[0, begin:keys, :] = (
            d_query * cosine[begin:keys] - swap_halves(d_query) * sine_part[begin:keys]
        ).astype(BF16)
    d_key = key_sum[...]
    dk_ref[0] = (d_key * cosine - swap_halves(d_key) * sine_part).astype(BF16)
    dv_ref[0] = (0.5 * value_sum[...]).astype(BF16)


def attend_back(saved, d_attended, cos_wide, sin_wide, first_pos):
    q_rot, k_rot, v_mix, attended, log_total = saved
    pairs, length, _ = q_rot.shape
    part = pl.BlockSpec((1, length, LANES), lambda p: (p, 0, 0))
    table = pl.BlockSpec((length, LANES), lambda p: (0, 0))
    out = jax.ShapeDtypeStruct((pairs, length, LANES), BF16)
    return pl.pallas_call(
        attend_back_kernel,
        grid=(pairs,),
        in_specs=[part] * 3 + [pl.BlockSpec((length, LANES), lambda p: (0, p)), part,
                               pl.BlockSpec((1, 2, length), lambda p: (p, 0, 0)), table, table,
                               pl.BlockSpec((1, length), lambda p: (0, 0))],
        out_specs=[part] * 3,
        out_shape=[out] * 3,
        scratch_shapes=[pltpu.VMEM((length, LANES), F32)] * 2,
        compiler_params=pltpu.CompilerParams(vmem_limit_bytes=48 << 20),
        cost_estimate=pl.CostEstimate(
            flops=pairs * length * length * 128 * 20, bytes_accessed=pairs * length * 128 * 24,
            transcendentals=pairs * length * length),
    )(q_rot, k_rot, v_mix, attended, d_attended, log_total, cos_wide, sin_wide, first_pos[None, :])


class Place:
    def __init__(self, n_seq, n_head, slots):
        self.n_seq, self.slots, self.ranks = n_seq, slots, n_head // slots
        self.seq = lax.axis_index("seq")
        head = lax.axis_index("head")
        self.slot, self.rank = head // self.ranks, head % self.ranks

    def at_slot(self, step):
        return (self.slot + step + self.slots) % self.slots

    def at_seq(self, step):
        return (self.seq + step + self.n_seq) % self.n_seq

    @property
    def line(self):
        return self.slots == 4 and self.n_seq == 4

    def source(self, step):
        if not self.line:
            return self.at_slot(-step)
        upper = self.slot // 2
        inner = (self.slot + upper) % 2
        near = step + inner * (1 - 2 * step) * (1 - step // 2)
        return near + upper * (3 - 2 * near)

    @property
    def beside(self):
        return self.seq + 1 - 2 * (self.seq % 2)

    @property
    def across(self):
        return self.seq + 2 - 4 * (self.seq // 2)

    def device(self, seq=None, slot=None, rank=None):
        seq = self.seq if seq is None else seq
        slot = self.slot if slot is None else slot
        rank = self.rank if rank is None else rank
        return (seq, slot * self.ranks + rank)

    def greet(self, with_ranks):
        others = [self.device(slot=self.at_slot(k)) for k in range(1, self.slots)]
        others += [self.device(seq=self.at_seq(d)) for d in range(1, self.n_seq)]
        if with_ranks:
            others += [
                self.device(rank=(self.rank + j) % self.ranks) for j in range(1, self.ranks)
            ]
        barrier = pltpu.get_barrier_semaphore()
        for other in others:
            pl.semaphore_signal(barrier, inc=1, device_id=other, device_id_type=MESH)
        pl.semaphore_wait(barrier, len(others))


class Sender:
    def __init__(self, send_sems, recv_sems):
        self.send_sems, self.recv_sems, self.used = send_sems, recv_sems, 0

    def start(self, src, dst, device, recv=None):
        copy = pltpu.make_async_remote_copy(
            src_ref=src,
            dst_ref=dst,
            send_sem=self.send_sems.at[self.used],
            recv_sem=self.recv_sems.at[self.used] if recv is None else recv,
            device_id=device,
            device_id_type=MESH,
        )
        self.used += 1
        copy.start()
        return copy


def lanes(index, width):
    return pl.ds(pl.multiple_of(index * width, width), width)


def forward_kernel(
    n_seq, n_head, head_cols, head_dim, early,
    x_ref, vf_ref, g_ref, w_qkv, w_gate_up, w_out, w_down, gains_ref, seg_ref, count_ref,
    cos_ref, sin_ref, first_ref, live_ref, x_res, h_one_res, q_res, k_res, v_res, att_res, lse_out, w_a_res, w_b_res, middle_res, h_two_res, g_res, e_res,
    ffn_res, x_out, h_one, q_out, k_out, v_out, att_out, w_a, middle, h_two, g_out, e_all,
    vf_all, away, back, w_b, ffn, wt_ref, sems, z_recv, v_recv, own_sems, res_sems,
):
    slots, rows, width = x_ref.shape
    part = wt_ref.shape[1]
    rows_a = w_a.shape[1]
    place = Place(n_seq, n_head, slots)
    ranks = place.ranks
    length = slots * ranks * rows
    per = LANES // head_cols
    pairs = slots // per
    mine = lanes(place.seq, part)
    sections = {"a": (w_a, pl.ds(0, rows_a)), "b": (w_b, pl.ds(rows_a, wt_ref.shape[0] - rows_a))}
    ids = {}
    elsewhere = place.device(seq=place.at_seq(1))

    def index(name):
        return ids.setdefault(name, len(ids))

    def remote(name, src, dst, device, recv=None):
        i = index(name)
        return pltpu.make_async_remote_copy(
            src_ref=src, dst_ref=dst, send_sem=sems.at[0, i],
            recv_sem=sems.at[1, i] if recv is None else recv,
            device_id=device, device_id_type=MESH,
        )

    def x_copy(k):
        to = place.at_slot(k)
        return remote(("x", k), x_ref.at[to], x_out.at[place.slot], place.device(slot=to))

    def g_copy(k):
        to = place.at_slot(k)
        return remote(("g", k), g_ref.at[to], g_out.at[place.slot], place.device(slot=to))

    def v_copy(k):
        to = place.source(k) if place.line else place.at_slot(k)
        return remote(("v", k), vf_ref.at[to], vf_all.at[place.slot], place.device(slot=to),
                      v_recv.at[place.slot])

    def v_wait(source):
        pltpu.make_async_remote_copy(
            src_ref=vf_ref.at[0], dst_ref=vf_all.at[source], send_sem=sems.at[0, 0],
            recv_sem=v_recv.at[source], device_id=elsewhere, device_id_type=MESH,
        ).wait_recv()

    def piece(sec, step):
        ref, at = sections[sec]
        return wt_ref.at[at] if step == 0 else ref.at[step, :, mine]

    def z_copy(name, sec, step, to, to_step):
        ref, _ = sections[sec]
        which = 0 if sec == "a" else 1
        return remote((name, sec, step), piece(sec, step), ref.at[to_step, :, mine],
                      place.device(slot=to), z_recv.at[which, to_step])

    def z_wait(sec, step):
        ref, _ = sections[sec]
        which = 0 if sec == "a" else 1
        pltpu.make_async_remote_copy(
            src_ref=piece(sec, 0), dst_ref=ref.at[step, :, mine], send_sem=sems.at[0, 0],
            recv_sem=z_recv.at[which, step], device_id=elsewhere, device_id_type=MESH,
        ).wait_recv()

    slot = place.slot
    upper = slot // 2
    inner = (slot + upper) % 2

    def z_start_own(sec):
        if not place.line:
            for k in range(1, slots):
                z_copy(("z", k), sec, 0, place.at_slot(k), k).start()
            return
        @pl.when(slot < 3)
        def _():
            to = slot + 1
            z_copy("up", sec, 0, to, 1 + (to == 2).astype(jnp.int32)).start()

        @pl.when(slot > 0)
        def _():
            to = slot - 1
            z_copy("down", sec, 0, to, 1 + (to == 1).astype(jnp.int32)).start()

    def z_own_sends(sec):
        if not place.line:
            for k in range(1, slots):
                z_copy(("z", k), sec, 0, place.at_slot(k), k).wait_send()
            return

        @pl.when(slot < 3)
        def _():
            z_copy("up", sec, 0, slot + 1, 1).wait_send()

        @pl.when(slot > 0)
        def _():
            z_copy("down", sec, 0, slot - 1, 1).wait_send()

    def z_relay(sec, step):
        if step == 1:
            return z_copy("on", sec, step, slot + 1 - 2 * upper, 3)
        return z_copy("on", sec, step, slot - 1 + 2 * upper, step)

    def near_copy(sec, step):
        ref, _ = sections[sec]
        dst = ref.at[step, :, mine]
        if not place.line:
            return [
                remote(("xy", d, sec, step), piece(sec, step), dst, place.device(seq=place.at_seq(d)))
                for d in range(1, n_seq)
            ]
        return [
            remote(("xy", 0, sec, step), piece(sec, step), dst, place.device(seq=place.beside)),
            remote(("xy", 1, sec, step), piece(sec, step), dst, place.device(seq=place.across)),
        ]

    def far_copy(sec, step, which):
        ref, at = sections[sec]
        half = at.size // 2
        cut = pl.ds(which * half, half)
        source = place.beside if which == 0 else place.across
        to = place.across if which == 0 else place.beside
        where = ref.at[step, cut, lanes(source, part)]
        return remote(("far", which, sec, step), where, where, place.device(seq=to))

    def z_event(sec, step):
        z_wait(sec, step)
        if place.line:
            @pl.when(inner == 1)
            def _():
                z_relay(sec, step).start()
        for copy in near_copy(sec, step):
            copy.start()

    def xy_event(sec, step):
        for which, copy in enumerate(near_copy(sec, step)):
            copy.wait_recv()
            if place.line:
                far_copy(sec, step, which).start()

    def done_event(sec, step):
        if place.line:
            for which in range(2):
                far_copy(sec, step, which).wait_recv()

    def position(p, rank):
        return pl.ds(pl.multiple_of((p * ranks + rank) * rows, rows), rows)

    def share(name, ref, p, j):
        where = ref.at[position(p, place.rank), :]
        return remote((name, p, j), where, where, place.device(rank=(place.rank + j) % ranks))

    results = {
        "x": (x_out, x_res), "h1": (h_one, h_one_res), "q": (q_out, q_res), "k": (k_out, k_res),
        "v": (v_out, v_res), "att": (att_out, att_res), "a": (w_a, w_a_res),
        "mid": (middle, middle_res), "h2": (h_two, h_two_res), "g": (g_out, g_res),
        "e": (e_all, e_res), "ffn": (ffn, ffn_res),
    }
    for step in range(slots):
        results["b", step] = (w_b.at[step], w_b_res.at[step])

    def result(name):
        src, dst = results[name]
        return pltpu.make_async_copy(src, dst, res_sems.at[list(results).index(name)])

    high, tall = w_qkv.shape[2], w_gate_up.shape[1]
    for i in range(3):
        wt_ref[i * high : (i + 1) * high, :] = w_qkv[i].T.astype(BF16)
    wt_ref[3 * high : 4 * high, :] = w_out[...].astype(BF16)
    for i in range(2):
        wt_ref[rows_a + i * tall : rows_a + (i + 1) * tall, :] = w_gate_up[i].astype(BF16)
    wt_ref[rows_a + 2 * tall :, :] = w_down[...].astype(BF16)
    place.greet(True)
    own = [
        pltpu.make_async_copy(x_ref.at[slot], x_out.at[slot], own_sems.at[0]),
        pltpu.make_async_copy(wt_ref.at[sections["a"][1]], w_a.at[0, :, mine], own_sems.at[1]),
        pltpu.make_async_copy(wt_ref.at[sections["b"][1]], w_b.at[0, :, mine], own_sems.at[2]),
        pltpu.make_async_copy(vf_ref.at[slot], vf_all.at[slot], own_sems.at[3]),
        pltpu.make_async_copy(g_ref.at[slot], g_out.at[slot], own_sems.at[4]),
    ]
    def v_event(*steps):
        for k in steps:
            v_copy(k).start()

    def g_event():
        for k in range(1, slots):
            g_copy(k).start()

    def inside(kind, sec, step):
        @pl.when(inner == 1)
        def _():
            kind(sec, step)

    def outside(kind, sec, step):
        @pl.when(inner == 0)
        def _():
            kind(sec, step)

    z_start_own("a")
    if place.line:
        z_start_own("b")
    for k in (2, 3, 1):
        x_copy(k).start()
    v_event(1)
    for sec in ("a", "b"):
        for copy in near_copy(sec, 0):
            copy.start()
    for copy in own:
        copy.start()
    segment = seg_ref[pl.ds(slot, 1), :]
    first_pos = jnp.zeros_like(segment)
    for document in range(1, 4):
        before = jnp.sum((segment < document).astype(jnp.int32), axis=1, keepdims=True)
        first_pos = jnp.where(segment == document, before, first_pos)
    first_ref[...] = first_pos
    offset = lax.broadcasted_iota(jnp.int32, segment.shape, 1) - first_pos
    offset = jnp.broadcast_to(offset.astype(F32), (LANES, length)).T
    lane = lax.broadcasted_iota(jnp.int32, (1, LANES), 1)
    half_width = head_dim // 2
    place_in_half = (lane % half_width).astype(F32)
    frequency = jnp.exp(-jnp.log(10000.0) * place_in_half / half_width)
    cos_ref[...] = jnp.cos(offset * frequency)
    sin_ref[...] = jnp.sin(offset * frequency) * jnp.where(lane % head_dim < half_width, -1.0, 1.0)
    live = (slot < count_ref[...]).astype(F32)
    live_ref[...] = jnp.broadcast_to(live, live_ref.shape)

    z_event("a", 1)
    if place.line:
        inside(z_event, "a", 2)
        z_event("b", 1)
        inside(z_event, "b", 2)
        v_event(2, 3)
    xy_event("a", 0)
    xy_event("b", 0)
    xy_event("a", 1)
    for k in range(1, slots):
        x_copy(k).wait_recv()
    own[0].wait()

    for p in range(slots):
        x = x_out[p].astype(F32)
        normed = x * lax.rsqrt(jnp.mean(x * x, axis=-1, keepdims=True) + EPSILON)
        h_one[position(p, place.rank), :] = (normed * gains_ref[0:1, :]).astype(BF16)
        for j in range(1, ranks):
            share("h1", h_one, p, j).start()
    own[1].wait()
    own[3].wait()
    done_event("a", 0)
    for p in range(slots):
        for j in range(1, ranks):
            share("h1", h_one, p, j).wait_recv()
    result("x").start()
    result("h1").start()

    if place.line:
        events = {
            (0, 1): [lambda: inside(z_event, "a", 3), lambda: outside(z_event, "a", 2)],
            (0, 4): [lambda: xy_event("b", 1)],
            (1, 0): [lambda: done_event("a", 1), lambda: v_wait(place.source(1))],
            (1, 2): [lambda: xy_event("a", 2)],
            (1, 6): [lambda: inside(z_event, "b", 3), lambda: outside(z_event, "b", 2)],
            (2, 0): [lambda: done_event("a", 2), lambda: v_wait(place.source(2))],
            (2, 1): [lambda: outside(z_event, "a", 3), lambda: inside(xy_event, "a", 3)],
            (2, 6): [lambda: xy_event("b", 2)],
            (2, 3): [lambda: outside(xy_event, "a", 3)],
            (3, 0): [lambda: done_event("a", 3), g_event,
                     lambda: v_wait(place.source(3))],
            (3, 6): [lambda: outside(z_event, "b", 3)],
        }
    else:
        events = {}
        z_start_own("b")
        v_event(2, 3)
        g_event()
        for step in range(2, slots):
            z_event("a", step)
            xy_event("a", step)
        for step in range(1, slots):
            z_event("b", step)
            xy_event("b", step)
            v_wait(place.source(step))

    def one_pair_of_heads(j, carry):
        def pump(point):
            for (step, at), todo in events.items():
                if at == point:
                    @pl.when(j == step)
                    def _(todo=todo):
                        for act in todo:
                            act()

        pump(0)
        if per == 1:
            w_in = w_a[j, : 3 * head_cols, :]
            first = vf_all[place.source(j)]
        else:
            w_in = jnp.concatenate(
                [
                    w_a[j * per + u, i * head_cols : (i + 1) * head_cols, :]
                    for i in range(3)
                    for u in range(per)
                ],
                axis=0,
            )
            first = jnp.concatenate([vf_all[place.source(j * per + u)] for u in range(per)], axis=1)
        half = length // 2
        for part_at in range(2):
            at = slice(part_at * half, (part_at + 1) * half)
            project = dot_nt(h_one[at, :], w_in)
            cosine, sine_part = cos_ref[at, :], sin_ref[at, :]
            q_raw, k_raw = project[:, :LANES], project[:, LANES : 2 * LANES]
            q_out[j, at, :] = ((q_raw * cosine + swap_halves(q_raw) * sine_part) * 0.125).astype(BF16)
            k_out[j, at, :] = (k_raw * cosine + swap_halves(k_raw) * sine_part).astype(BF16)
            v_out[j, at, :] = (0.5 * project[:, 2 * LANES :] + 0.5 * first[at].astype(F32)).astype(BF16)
        pump(1)
        v_turned = v_out[j].T
        for step in range(length // BLOCK):
            begin, keys = step * BLOCK, (step + 1) * BLOCK
            low = first_key(begin, length)
            queries = two_heads(q_out[j, begin:keys, :])
            scores = dot_nt(k_out[j, low:keys, :], queries)
            scores = jnp.where(seen(first_ref, begin, low, keys - low), scores, -1e30)
            top = jnp.max(scores, axis=0, keepdims=True)
            exps = jnp.exp(scores - top)
            total = jnp.sum(exps, axis=0, keepdims=True)
            chances = (exps * (1.0 / total)).astype(BF16)
            attended = dot_nn(v_turned[:, low:keys], chances)
            att_out[begin:keys, lanes(j, LANES)] = one_pair(attended, BLOCK).astype(BF16)
            log_total = top + jnp.log(total)
            lse_out[j, 0:1, begin:keys] = log_total[:, :BLOCK]
            lse_out[j, 1:2, begin:keys] = log_total[:, BLOCK:]
            if step % (length // BLOCK // 4) == 0:
                pump(2 + step // (length // BLOCK // 4))
        pump(6)
        return carry

    lax.fori_loop(0, pairs, one_pair_of_heads, 0)
    for name in ("q", "k", "v", "att", "a"):
        result(name).start()

    w_o = w_a[:, 3 * head_cols :, :].reshape(slots * head_cols, width)

    def away_copy(p, j):
        return remote(("away", p, j), away.at[j - 1, p], back.at[j - 1, p],
                      place.device(rank=(place.rank + j) % ranks))

    for p in range(slots):
        for j in range(1, ranks):
            at = position(p, (place.rank + j) % ranks)
            away[j - 1, p] = dot_nn(att_out[at, :], w_o).astype(BF16)
            away_copy(p, j).start()
    for p in range(slots):
        middle[p] = x_out[p].astype(F32) + dot_nn(att_out[position(p, place.rank), :], w_o)
    for p in range(slots):
        value = middle[p]
        for j in range(1, ranks):
            away_copy(p, j).wait_recv()
            value = value + back[j - 1, p].astype(F32)
        middle[p] = value
        normed = value * lax.rsqrt(jnp.mean(value * value, axis=-1, keepdims=True) + EPSILON)
        h_two[position(p, place.rank), :] = (normed * gains_ref[1:2, :]).astype(BF16)
        for j in range(1, ranks):
            share("h2", h_two, p, j).start()
    result("mid").start()
    for p in range(slots):
        for j in range(1, ranks):
            share("h2", h_two, p, j).wait_recv()
    result("h2").start()

    units = (w_b.shape[1]) // 3
    strip = length // 2

    def feed(k):
        def strips(n, carry):
            at = pl.ds(pl.multiple_of(n * strip, strip), strip)
            gate = dot_nt(h_two[at, :], w_b[k, :units, :])
            up = dot_nt(h_two[at, :], w_b[k, units : 2 * units, :])
            hid = (gate * (1.0 / (1.0 + jnp.exp(-gate))) * up).astype(BF16)
            out = dot_nn(hid, w_b[k, 2 * units :, :])
            if k == 0:
                ffn[at, :] = out
            else:
                ffn[at, :] += out
            return carry

        lax.fori_loop(0, length // strip, strips, 0)

    own[2].wait()
    for step in range(slots - 1):
        done_event("b", step)
        result(("b", step)).start()
        if early:
            feed(step)
        if step == 1 and place.line:
            xy_event("b", 3)
    if not early:
        ffn[0:8, :] = jnp.zeros((8, width), F32)
    result("ffn").start()
    own[4].wait()
    for k in range(1, slots):
        g_copy(k).wait_recv()
    result("g").start()
    for p in range(slots):
        e_all[position(p, place.rank), :] = (g_out[p].astype(F32) * live_ref[...]).astype(BF16)
        for j in range(1, ranks):
            share("e", e_all, p, j).start()
    for p in range(slots):
        for j in range(1, ranks):
            share("e", e_all, p, j).wait_recv()
            share("e", e_all, p, j).wait_send()
    result("e").start()
    done_event("b", slots - 1)
    result(("b", slots - 1)).start()
    for name in results:
        result(name).wait()
    for p in range(slots):
        for j in range(1, ranks):
            share("h1", h_one, p, j).wait_send()
            share("h2", h_two, p, j).wait_send()
            away_copy(p, j).wait_send()
    for k in range(1, slots):
        x_copy(k).wait_send()
        v_copy(k).wait_send()
        g_copy(k).wait_send()
    for sec in ("a", "b"):
        z_own_sends(sec)
        for step in range(slots):
            for copy in near_copy(sec, step):
                copy.wait_send()
            if place.line:
                for which in range(2):
                    far_copy(sec, step, which).wait_send()
                if step > 0:
                    @pl.when(inner == 1)
                    def _(sec=sec, step=step):
                        z_relay(sec, step).wait_send()


def forward_part(
    n_seq, n_head, head_cols, head_dim, layer_input, values_first, out_grad, weights, gains,
    segments, counts, early,
):
    slots, rows, width = layer_input.shape
    part = weights[0].shape[1]
    all_rows = 4 * head_cols + 3 * weights[1].shape[1]
    ranks = n_head // slots
    length = slots * ranks * rows
    rows_a = 4 * head_cols
    pairs = slots * head_cols // LANES
    count = 3 * (slots - 1) + 2 * (2 + 4 * slots + slots * n_seq) + 4 * slots * ranks
    any_space = pl.BlockSpec(memory_space=pl.ANY)
    vmem = pl.BlockSpec(memory_space=pltpu.VMEM)
    shape = jax.ShapeDtypeStruct
    heads = shape((pairs, length, LANES), BF16)
    return pl.pallas_call(
        functools.partial(forward_kernel, n_seq, n_head, head_cols, head_dim, early),
        in_specs=[any_space] * 3 + [vmem] * 7,
        out_specs=[vmem] * 4 + [any_space] * 6 + [vmem] + [any_space] * 7,
        out_shape=[
            shape((length, LANES), F32),
            shape((length, LANES), F32),
            shape((1, length), jnp.int32),
            shape((1, width), F32),
            shape(layer_input.shape, BF16),
            shape((length, width), BF16),
            heads, heads, heads,
            shape((length, slots * head_cols), BF16),
            shape((pairs, 2, length), F32),
            shape((slots, rows_a, width), BF16),
            shape((slots, all_rows - rows_a, width), BF16),
            shape(layer_input.shape, F32),
            shape((length, width), BF16),
            shape(layer_input.shape, BF16),
            shape((length, width), BF16),
            shape((length if early else 8, width), F32),
        ],
        scratch_shapes=[
            pltpu.VMEM(layer_input.shape, BF16),
            pltpu.VMEM((length, width), BF16),
            pltpu.VMEM(heads.shape, BF16),
            pltpu.VMEM(heads.shape, BF16),
            pltpu.VMEM(heads.shape, BF16),
            pltpu.VMEM((length, slots * head_cols), BF16),
            pltpu.VMEM((slots, rows_a, width), BF16),
            pltpu.VMEM(layer_input.shape, F32),
            pltpu.VMEM((length, width), BF16),
            pltpu.VMEM(layer_input.shape, BF16),
            pltpu.VMEM((length, width), BF16),
            pltpu.VMEM(values_first.shape, BF16),
            pltpu.VMEM((ranks - 1, slots, rows, width), BF16),
            pltpu.VMEM((ranks - 1, slots, rows, width), BF16),
            pltpu.VMEM((slots, all_rows - rows_a, width), BF16),
            pltpu.VMEM((length if early else 8, width), F32),
            pltpu.VMEM((all_rows, part), BF16),
            pltpu.SemaphoreType.DMA((2, count)),
            pltpu.SemaphoreType.DMA((2, slots)),
            pltpu.SemaphoreType.DMA((slots,)),
            pltpu.SemaphoreType.DMA((5,)),
            pltpu.SemaphoreType.DMA((12 + slots,)),
        ],
        compiler_params=pltpu.CompilerParams(
            collective_id=0, has_side_effects=True, vmem_limit_bytes=60 << 20
        ),
    )(
        layer_input, values_first, out_grad, *weights, gains, segments, counts.reshape(1, 1)
    )


def backward_kernel(
    n_seq, n_head, head_cols,
    wa_ref, wb_ref, h_one_ref, h_two_ref, x_ref, mid_ref, g_ref, q_ref, k_ref, v_ref, att_ref, e_ref,
    ffn_ref, root_ref, head_root, unit_root,
    lse_ref, gains_ref, cos_ref, sin_ref, first_ref, live_ref,
    block_out, input_out, first_out, gains_out, sum_a, sum_b, full_a_out, full_b_out, step_a, step_b,
    w_a, w_b, normed_all, e_all, x_own, middle, g_own, q_all, k_all, v_all, att_all,
    acc_one, acc_two, hidden, d_gate, d_project, away, back, delta_own,
    full_a, full_b, head_buf, unit_buf, near_a, near_b, next_a, next_b, far_a, far_b,
    gain_sum, gain_seq, gain_slot, gain_rank,
    sems, near_sems, next_sems, far_sems, first_sems, load_sems, own_sems, step_sems, credit,
):
    slots, rows_b, width = w_b.shape
    rows_a = w_a.shape[1]
    ffn_cols = rows_b // 3
    ranks = n_head // slots
    rows = x_own.shape[1]
    length = slots * ranks * rows
    part = width // n_seq
    place = Place(n_seq, n_head, slots)
    slot = place.slot
    beside, across = place.beside, place.across
    corner = 3 - place.seq
    mine = lanes(place.seq, part)
    other = 1 - place.rank
    elsewhere = place.device(seq=beside)
    ids = {}
    sections = {
        "a": (0, w_a, near_a, next_a, far_a, sum_a, full_a, 128),
        "b": (1, w_b, near_b, next_b, far_b, sum_b, full_b, rows_b // 6),
    }

    def remote(name, src, dst, device, send=None, recv=None):
        if send is None:
            i = ids.setdefault(name, len(ids))
            send, recv = sems.at[0, i], sems.at[1, i]
        return pltpu.make_async_remote_copy(
            src_ref=src, dst_ref=dst, send_sem=send, recv_sem=recv,
            device_id=device, device_id_type=MESH,
        )

    def position(p, rank):
        return pl.ds(pl.multiple_of((p * ranks + rank) * rows, rows), rows)

    def halves(sec):
        half = sections[sec][1].shape[1] // 2
        return pl.ds(0, half), pl.ds(half, half)

    def near_copies(sec, k):
        i, grads, near = sections[sec][:3]
        upper, lower = halves(sec)
        plan = (
            (upper, beside, beside), (upper, corner, beside),
            (lower, across, across), (lower, corner, across),
        )
        return [
            remote(None, grads.at[k, cut, lanes(quarter, part)], near.at[k, n],
                   place.device(seq=to), near_sems.at[0, i, k, n], near_sems.at[1, i, k, n])
            for n, (cut, quarter, to) in enumerate(plan)
        ]

    def next_copies(sec, k):
        i, grads, _, then = sections[sec][:4]
        upper, lower = halves(sec)
        plan = ((upper, across), (lower, beside))
        return [
            remote(None, grads.at[k, cut, lanes(to, part)], then.at[k, n],
                   place.device(seq=to), next_sems.at[0, i, k, n], next_sems.at[1, i, k, n])
            for n, (cut, to) in enumerate(plan)
        ]

    upper = slot // 2
    inner = (slot + upper) % 2
    toward = 1 - 2 * upper

    def far_copy(sec, k):
        i, grads = sections[sec][:2]
        far = sections[sec][4]
        to = slot + toward * (1 - 2 * inner * (1 - k // 2))
        landing = inner * (4 - 3 * (k // 3)) + (1 - inner) * ((k // 2) * k)
        return remote(None, grads.at[k, :, mine], far.at[landing], place.device(slot=to),
                      far_sems.at[0, i, k], far_sems.at[1, i, landing])

    def far_wait(sec, landing):
        i, grads = sections[sec][:2]
        far = sections[sec][4]
        remote(None, grads.at[0, :, mine], far.at[landing], elsewhere,
               far_sems.at[0, i, 0], far_sems.at[1, i, landing]).wait_recv()

    def add_rows(sec, k, begin, where, addend):
        grads, strip = sections[sec][1], sections[sec][7]

        def one(i, carry):
            at = pl.ds(pl.multiple_of(begin + i * strip, 16), strip)
            value = grads[k, at, where].astype(F32)
            value = value + addend[pl.ds(pl.multiple_of(i * strip, 16), strip), :].astype(F32)
            grads[k, at, where] = value.astype(BF16)
            return carry

        lax.fori_loop(0, addend.shape[0] // strip, one, 0)

    def launch(sec, k):
        for copy in near_copies(sec, k):
            copy.start()

    def second(sec, k):
        near = sections[sec][2]
        half = near.shape[2]
        came = near_copies(sec, k)
        onward = next_copies(sec, k)
        came[1].wait_recv()
        add_rows(sec, k, 0, lanes(across, part), near.at[k, 1])
        onward[0].start()
        came[3].wait_recv()
        add_rows(sec, k, half, lanes(beside, part), near.at[k, 3])
        onward[1].start()
        came[0].wait_recv()
        add_rows(sec, k, 0, mine, near.at[k, 0])
        came[2].wait_recv()
        add_rows(sec, k, half, mine, near.at[k, 2])

    def third(sec, k, sends):
        then = sections[sec][3]
        half = then.shape[2]
        for n, copy in enumerate(next_copies(sec, k)):
            copy.wait_recv()
            add_rows(sec, k, n * half, mine, then.at[k, n])
        if sends:
            @pl.when(inner == 0)
            def _():
                far_copy(sec, k).start()

    def fourth(sec, k):
        @pl.when(inner == 1)
        def _():
            far_wait(sec, k)
            add_rows(sec, k, 0, mine, sections[sec][4].at[k])
            far_copy(sec, k).start()

    def gather_copies(sec):
        total, full = sections[sec][5:7]
        half = total.shape[0] // 2
        near = [
            remote(("full", sec, n), total, full.at[:, mine], place.device(seq=to))
            for n, to in enumerate((beside, across))
        ]
        far = []
        for n, (source, to) in enumerate(((beside, across), (across, beside))):
            where = full.at[pl.ds(n * half, half), lanes(source, part)]
            far.append(remote(("relay", sec, n), where, where, place.device(seq=to)))
        return near, far

    def own_copy(sec):
        i = sections[sec][0]
        return pltpu.make_async_copy(
            sections[sec][5], sections[sec][6].at[:, mine], own_sems.at[3 + i]
        )

    def finish(sec):
        grads = sections[sec][1]
        far, total, _, strip = sections[sec][4:]

        @pl.when(inner == 1)
        def _():
            far_wait(sec, 0)
            add_rows(sec, 0, 0, mine, far.at[0])

        far_wait(sec, 4)

        def one(r, carry):
            at = pl.ds(pl.multiple_of(r * strip, 16), strip)
            value = grads[0, at, mine].astype(F32) + far[4, at, :].astype(F32)
            total[at, :] = value.astype(BF16)
            return carry

        lax.fori_loop(0, total.shape[0] // strip, one, 0)
        own_copy(sec).start()
        for copy in gather_copies(sec)[0]:
            copy.start()

    def relay(sec):
        near, far = gather_copies(sec)
        for n in range(2):
            near[n].wait_recv()
            far[n].start()

    loads = {
        "h2": (h_two_ref, normed_all), "e": (e_ref, e_all), "h1": (h_one_ref, normed_all),
        "ffn": (ffn_ref, acc_one),
        "a": (wa_ref, w_a), "x": (x_ref, x_own), "mid": (mid_ref, middle),
        "g": (g_ref, g_own), "q": (q_ref, q_all), "k": (k_ref, k_all), "v": (v_ref, v_all),
        "att": (att_ref, att_all),
    }

    def load(name):
        src, dst = loads[name]
        return pltpu.make_async_copy(src, dst, load_sems.at[slots + list(loads).index(name)])

    def load_b(k):
        return pltpu.make_async_copy(wb_ref.at[k], w_b.at[k], load_sems.at[k])

    load_b(slots - 1).start()
    load("h2").start()
    load("e").start()
    load("ffn").start()
    load("x").start()
    load("mid").start()
    for k in reversed(range(slots - 1)):
        load_b(k).start()
    for name in loads:
        if name not in ("h1", "h2", "e", "ffn", "x", "mid"):
            load(name).start()
    place.greet(True)
    load("h2").wait()
    load("e").wait()
    load("ffn").wait()

    strip = length // 2
    key_sum, value_sum = acc_two.at[:, :LANES], acc_two.at[:, LANES : 2 * LANES]

    def away_copy(n, p):
        return remote(("away", n, p), away.at[p], back.at[p], place.device(rank=other))

    def swap(name, src, dst):
        return [
            remote((name, j), src.at[place.at_slot(j)], dst.at[slot],
                   place.device(slot=place.at_slot(j)))
            for j in (2, 3, 1)
        ]

    def keep(n, src, dst):
        return pltpu.make_async_copy(src, dst.at[slot], own_sems.at[n])

    def send_away(n, acc):
        if n > 0:
            pl.semaphore_wait(credit, 1)
        for p in range(slots):
            if n > 0:
                away_copy(n - 1, p).wait_send()
            away[p] = acc[position(p, other), :].astype(BF16)
            away_copy(n, p).start()

    def taken():
        pl.semaphore_signal(credit, inc=1, device_id=place.device(rank=other), device_id_type=MESH)

    live = live_ref[...]

    def block_delta():
        load("x").wait()
        load("mid").wait()
        for p in range(slots):
            away_copy(0, p).wait_recv()
            out = acc_one[position(p, place.rank), :] + back[p].astype(F32)
            delta_own[p] = ((middle[p] - x_own[p].astype(F32) + out) * live).astype(BF16)
        taken()
        for copy in swap("block", delta_own, block_out):
            copy.start()
        keep(0, delta_own.at[slot], block_out).start()

    def pump(schedule, i, point):
        for (turn, at), acts in schedule.items():
            if at == point:
                @pl.when(i == turn)
                def _(acts=acts):
                    for act in acts:
                        act()

    unit_events = {
        (2, 0): [lambda: second("b", 3)],
        (3, 0): [lambda: second("b", 2)],
    }
    head_events = {
        (0, 0): [lambda: third("b", 3, True)],
        (0, 2): [lambda: second("b", 1)],
        (1, 1): [lambda: third("b", 2, True)],
        (2, 1): [lambda: fourth("b", 3)],
        (2, 2): [lambda: second("b", 0)],
    }

    def units(i, carry):
        k = slots - 1 - i
        load_b(k).wait()

        def strips(n, carry):
            at = pl.ds(pl.multiple_of(n * strip, strip), strip)
            inner = normed_all[at, :]
            gate = dot_nt(inner, w_b[k, :ffn_cols, :])
            up = dot_nt(inner, w_b[k, ffn_cols : 2 * ffn_cols, :])
            sigmoid_gate = 1.0 / (1.0 + jnp.exp(-gate))
            activated = gate * sigmoid_gate
            hid = (activated * up).astype(BF16)
            hidden[at, :] = hid
            d_hidden = dot_nt(e_all[at, :], w_b[k, 2 * ffn_cols :, :])
            dg = (d_hidden * up * sigmoid_gate * (1.0 + gate * (1.0 - sigmoid_gate))).astype(BF16)
            du = (d_hidden * activated).astype(BF16)
            d_gate[at, :] = dg
            d_project[at, :ffn_cols] = du
            d_in = dot_nn(dg, w_b[k, :ffn_cols, :]) + dot_nn(du, w_b[k, ffn_cols : 2 * ffn_cols, :])

            @pl.when(i == 0)
            def _():
                acc_one[at, :] += dot_nn(hid, w_b[k, 2 * ffn_cols :, :])
                acc_two[at, :] = d_in

            @pl.when(i > 0)
            def _():
                acc_two[at, :] += d_in

            return carry

        lax.fori_loop(0, length // strip, strips, 0)
        pump(unit_events, i, 0)
        w_b[k, 2 * ffn_cols :, :] = dot_tn(hidden[...], e_all[...]).astype(BF16)
        w_b[k, :ffn_cols, :] = dot_tn(d_gate[...], normed_all[...]).astype(BF16)
        w_b[k, ffn_cols : 2 * ffn_cols, :] = dot_tn(d_project[:, :ffn_cols], normed_all[...]).astype(BF16)
        launch("b", k)

        @pl.when(i == 0)
        def _():
            send_away(0, acc_one)

        @pl.when(i == 1)
        def _():
            block_delta()

        return carry

    lax.fori_loop(0, slots, units, 0)
    load("h1").start()

    def share(p):
        where = e_all.at[position(p, place.rank), :]
        return remote(("share", p), where, where, place.device(rank=other))

    send_away(1, acc_two)
    load("g").wait()
    gain_sum[...] = jnp.zeros_like(gain_sum)
    for p in range(slots):
        value = middle[p]
        inverse = lax.rsqrt(jnp.mean(value * value, axis=-1, keepdims=True) + EPSILON)
        normed = value * inverse
        away_copy(1, p).wait_recv()
        d_normed = acc_two[position(p, place.rank), :] + back[p].astype(F32)
        gain_sum[1:2, :] += jnp.sum(normed * d_normed, axis=0, keepdims=True)
        delta = norm_back(d_normed * gains_ref[1:2, :], normed, inverse)
        middle[p] = delta
        e_all[position(p, place.rank), :] = (g_own[p].astype(F32) * live + delta).astype(BF16)
        share(p).start()
    taken()

    for name in ("a", "h1", "q", "k", "v", "att"):
        load(name).wait()
    for p in range(slots):
        share(p).wait_recv()

    def first_copy(k):
        return remote(None, v_all.at[k], first_out.at[slot],
                      place.device(slot=place.source(k)),
                      first_sems.at[0, k], first_sems.at[1, slot])

    def heads(i, carry):
        k = slots - 1 - i
        lane = lanes(k, LANES)
        pump(head_events, i, 0)
        d_att = dot_nt(e_all[...], w_a[k, 3 * head_cols :, :]).astype(BF16)
        product = (d_att.astype(F32) * att_all[:, lane].astype(F32)).T
        inner = [
            jnp.sum(product[:64], axis=0, keepdims=True),
            jnp.sum(product[64:], axis=0, keepdims=True),
        ]
        key_sum[...] = jnp.zeros_like(key_sum)
        value_sum[...] = jnp.zeros_like(value_sum)
        k_turned = k_all[k].T
        for step in range(length // BLOCK):
            begin, keys = step * BLOCK, (step + 1) * BLOCK
            low = first_key(begin, length)
            queries = two_heads(q_all[k, begin:keys, :])
            d_out = two_heads(d_att[begin:keys, :])
            scores = dot_nt(k_all[k, low:keys, :], queries)
            log_total = jnp.concatenate(
                [lse_ref[k, 0:1, begin:keys], lse_ref[k, 1:2, begin:keys]], axis=1
            )
            chances = jnp.where(seen(first_ref, begin, low, keys - low), jnp.exp(scores - log_total), 0.0)
            d_chances = dot_nt(v_all[k, low:keys, :], d_out)
            rest = jnp.concatenate([inner[0][:, begin:keys], inner[1][:, begin:keys]], axis=1)
            d_scores = (chances * (d_chances - rest)).astype(BF16)
            key_sum[low:keys, :] += dot_nn(d_scores, queries)
            value_sum[low:keys, :] += dot_nn(chances.astype(BF16), d_out)
            d_query = one_pair(dot_nn(k_turned[:, low:keys], d_scores), BLOCK) * 0.125
            d_project[begin:keys, :LANES] = (
                d_query * cos_ref[begin:keys, :] - swap_halves(d_query) * sin_ref[begin:keys, :]
            ).astype(BF16)
        pump(head_events, i, 1)
        d_key = key_sum[...]
        d_project[:, LANES : 2 * LANES] = (
            d_key * cos_ref[...] - swap_halves(d_key) * sin_ref[...]
        ).astype(BF16)
        d_value = (0.5 * value_sum[...]).astype(BF16)
        d_project[:, 2 * LANES :] = d_value
        v_all[k] = d_value

        @pl.when(k > 0)
        def _():
            first_copy(k).start()

        @pl.when(k == 0)
        def _():
            keep(2, v_all.at[0], first_out).start()

        for n in range(2):
            at = pl.ds(n * strip, strip)
            d_in = dot_nn(d_project[at, :], w_a[k, : 3 * head_cols, :])

            @pl.when(i == 0)
            def _():
                acc_one[at, :] = d_in

            @pl.when(i > 0)
            def _():
                acc_one[at, :] += d_in

        w_a[k, : 3 * head_cols, :] = dot_tn(d_project[...], normed_all[...]).astype(BF16)
        w_a[k, 3 * head_cols :, :] = dot_tn(att_all[:, lane], e_all[...]).astype(BF16)
        launch("a", k)

        pump(head_events, i, 2)
        return carry

    lax.fori_loop(0, slots, heads, 0)

    for copy in swap("block", delta_own, block_out):
        copy.wait_send()
    keep(0, delta_own.at[slot], block_out).wait()
    send_away(2, acc_one)
    for p in range(slots):
        value = x_own[p].astype(F32)
        inverse = lax.rsqrt(jnp.mean(value * value, axis=-1, keepdims=True) + EPSILON)
        normed = value * inverse
        away_copy(2, p).wait_recv()
        d_normed = acc_one[position(p, place.rank), :] + back[p].astype(F32)
        gain_sum[0:1, :] += jnp.sum(normed * d_normed, axis=0, keepdims=True)
        delta = norm_back(d_normed * gains_ref[0:1, :], normed, inverse)
        delta_own[p] = ((middle[p] + delta) * live).astype(BF16)
    input_copies = swap("input", delta_own, input_out)
    input_copies[0].start()
    keep(1, delta_own.at[slot], input_out).start()

    def gain_copies(level):
        if level == 0:
            return [
                remote(("gain", 0, d), gain_seq.at[place.seq], gain_seq.at[place.seq],
                       place.device(seq=place.at_seq(d)))
                for d in range(1, n_seq)
            ]
        if level == 1:
            return [
                remote(("gain", 1, j), gain_slot.at[slot], gain_slot.at[slot],
                       place.device(slot=place.at_slot(j)))
                for j in range(1, slots)
            ]
        return [
            remote(("gain", 2, 0), gain_rank.at[place.rank], gain_rank.at[place.rank],
                   place.device(rank=other))
        ]

    def gain_step(level):
        value = gain_sum[...]
        if level > 0:
            for copy in gain_copies(level - 1):
                copy.wait_recv()
            held = (gain_seq, gain_slot, gain_rank)[level - 1]
            value = held[0]
            for j in range(1, held.shape[0]):
                value = value + held[j]
        if level == 3:
            gains_out[...] = value
            return
        target = (gain_seq, gain_slot, gain_rank)[level]
        target[(place.seq, slot, place.rank)[level]] = value
        for copy in gain_copies(level):
            copy.start()

    blocks = root_ref.shape[1]
    jobs = [("b", m, b) for m in range(3) for b in range(blocks)]
    jobs += [("a", m, b) for m in range(4) for b in range(blocks)]
    members = {"a": (0, 1, 2, 5), "b": (3, 4, 6)}
    small = {"a": (head_root, head_buf, step_a), "b": (unit_root, unit_buf, step_b)}
    depth = 8

    def job_root(n):
        acc = (acc_two, acc_one)[n % depth // 4]
        return acc.at[pl.ds(n % 4 * part, part)]

    def job_loads(n):
        sec, m, b = jobs[n]
        root_in, held, _ = small[sec]
        pairs = ((root_ref.at[members[sec][m], b], job_root(n)), (root_in.at[m, b], held.at[n % depth]))
        return [
            pltpu.make_async_copy(src, dst, step_sems.at[0, n % depth, i])
            for i, (src, dst) in enumerate(pairs)
        ]

    def job_store(n):
        sec, m, b = jobs[n]
        _, held, step = small[sec]
        high = held.shape[1]
        return pltpu.make_async_copy(
            job_root(n).at[pl.ds(0, high), pl.ds(0, part)],
            step.at[pl.ds((m * blocks + b) * high, high)], step_sems.at[1, n % depth, 0],
        )

    def run_jobs(first, last):
        for n in range(first, last):
            sec, m, b = jobs[n]
            root = job_root(n)
            held = small[sec][1]
            high = held.shape[1]
            for copy in job_loads(n):
                copy.wait()
            grad = sections[sec][6][pl.ds((m * blocks + b) * high, high), :]
            turned = dot_nn(held[n % depth].astype(BF16), grad).astype(BF16)
            turned = dot_nt(turned, root[...].astype(BF16))
            scale = lax.rsqrt(jnp.mean(turned * turned, axis=0, keepdims=True) + EPSILON)
            root[pl.ds(0, high), pl.ds(0, part)] = turned * scale
            job_store(n).start()
            if n > 0 and n - 1 + depth < len(jobs):
                job_store(n - 1).wait()
                for copy in job_loads(n - 1 + depth):
                    copy.start()

    def full_copy(sec):
        i = sections[sec][0]
        return pltpu.make_async_copy(
            sections[sec][6], (full_a_out, full_b_out)[i], step_sems.at[1, i, 1]
        )

    for n in range(depth):
        for copy in job_loads(n):
            copy.start()
    gain_step(0)
    third("b", 1, True)
    second("a", 3)
    second("a", 2)
    fourth("b", 2)
    input_copies[1].start()
    fourth("b", 1)
    input_copies[2].start()
    second("a", 1)
    gain_step(1)
    third("b", 0, False)
    second("a", 0)
    finish("b")
    third("a", 3, True)
    third("a", 2, True)
    fourth("a", 3)
    third("a", 1, True)
    fourth("a", 2)
    relay("b")
    gain_step(2)
    third("a", 0, False)
    fourth("a", 1)
    gain_step(3)
    finish("a")
    for copy in gather_copies("b")[1]:
        copy.wait_recv()
    own_copy("b").wait()
    full_copy("b").start()
    run_jobs(0, 6)
    relay("a")
    for copy in gather_copies("a")[1]:
        copy.wait_recv()
    own_copy("a").wait()
    full_copy("a").start()
    run_jobs(6, len(jobs))
    for n in range(len(jobs) - depth, len(jobs)):
        job_store(n).wait()
    full_copy("a").wait()
    full_copy("b").wait()
    for sec in ("b", "a"):
        near, far = gather_copies(sec)
        for copy in far:
            copy.wait_send()
        for copy in near:
            copy.wait_send()
        for k in range(slots):
            for copy in near_copies(sec, k) + next_copies(sec, k):
                copy.wait_send()
            if k > 0:
                far_copy(sec, k).wait_send()
    for copy in swap("block", delta_own, block_out):
        copy.wait_recv()
    for copy in swap("input", delta_own, input_out):
        copy.wait()
    for j in range(1, slots):
        source = place.at_slot(j)
        remote(None, v_all.at[0], first_out.at[source], elsewhere,
               first_sems.at[0, 0], first_sems.at[1, source]).wait_recv()
        first_copy(j).wait_send()
    for p in range(slots):
        away_copy(2, p).wait_send()
        share(p).wait_send()
    for level in range(3):
        for copy in gain_copies(level):
            copy.wait_send()
    keep(1, delta_own.at[slot], input_out).wait()
    keep(2, v_all.at[0], first_out).wait()


def backward_part(n_seq, n_head, head_cols, saved, gains, tables, live, roots):
    (
        x_own, h_one, q_rot, k_rot, v_mix, attended, log_total, weights_a, weights_b, middle, h_two,
        grad_own, e_all, ffn,
    ) = saved
    cos_wide, sin_wide, first_pos = tables
    _, roots_head, roots_unit = roots
    slots, rows, width = x_own.shape
    length = h_one.shape[0]
    rows_a, rows_b = weights_a.shape[1], weights_b.shape[1]
    part = width // n_seq
    ranks = n_head // slots
    any_space = pl.BlockSpec(memory_space=pl.ANY)
    vmem = pl.BlockSpec(memory_space=pltpu.VMEM)
    shape = jax.ShapeDtypeStruct
    like = lambda value: pltpu.VMEM(value.shape, value.dtype)
    count = 2 * 4 + 3 * slots + slots + 2 * (slots - 1) + n_seq + slots + 4
    sem = pltpu.SemaphoreType.DMA
    return pl.pallas_call(
        functools.partial(backward_kernel, n_seq, n_head, head_cols),
        in_specs=[any_space] * 16 + [vmem] * 6,
        out_specs=[any_space] * 3 + [vmem] * 3 + [any_space] * 4,
        out_shape=[
            shape(x_own.shape, BF16),
            shape(x_own.shape, BF16),
            shape((slots, length, head_cols), BF16),
            shape((8, width), F32),
            shape((rows_a, part), BF16),
            shape((rows_b, part), BF16),
            shape((rows_a, width), BF16),
            shape((rows_b, width), BF16),
            shape((rows_a, part), F32),
            shape((rows_b, part), F32),
        ],
        scratch_shapes=[
            like(weights_a), like(weights_b), like(h_two), like(e_all), like(x_own), like(middle),
            like(grad_own),
            like(q_rot), like(k_rot), like(v_mix), like(attended),
            pltpu.VMEM((length, width), F32),
            pltpu.VMEM((length, width), F32),
            pltpu.VMEM((length, rows_b // 3), BF16),
            pltpu.VMEM((length, rows_b // 3), BF16),
            pltpu.VMEM((length, 3 * LANES), BF16),
            like(x_own), like(x_own), like(x_own),
            pltpu.VMEM((rows_a, width), BF16),
            pltpu.VMEM((rows_b, width), BF16),
            pltpu.VMEM((8,) + roots_head.shape[2:], F32),
            pltpu.VMEM((8,) + roots_unit.shape[2:], F32),
            pltpu.VMEM((slots, 4, rows_a // 2, part), BF16),
            pltpu.VMEM((slots, 4, rows_b // 2, part), BF16),
            pltpu.VMEM((slots, 2, rows_a // 2, part), BF16),
            pltpu.VMEM((slots, 2, rows_b // 2, part), BF16),
            pltpu.VMEM((slots + 1, rows_a, part), BF16),
            pltpu.VMEM((slots + 1, rows_b, part), BF16),
            pltpu.VMEM((8, width), F32),
            pltpu.VMEM((n_seq, 8, width), F32),
            pltpu.VMEM((slots, 8, width), F32),
            pltpu.VMEM((ranks, 8, width), F32),
            sem((2, count)),
            sem((2, 2, slots, 4)),
            sem((2, 2, slots, 2)),
            sem((2, 2, slots + 1)),
            sem((2, slots)),
            sem((slots + 12,)),
            sem((5,)),
            sem((2, 8, 2)),
            pltpu.SemaphoreType.REGULAR,
        ],
        compiler_params=pltpu.CompilerParams(
            collective_id=2, has_side_effects=True, vmem_limit_bytes=64 << 20
        ),
    )(
        weights_a, weights_b, h_one, h_two, x_own, middle, grad_own, q_rot, k_rot, v_mix, attended,
        e_all, ffn, *roots, log_total, gains, cos_wide, sin_wide, first_pos[None, :], live,
    )


def reduce_kernel(
    n_seq, n_head, chunks,
    block_ref, input_ref, first_ref, gains_ref, grads_a, grads_b,
    block_out, input_out, first_out, gains_out, sum_a, sum_b, full_a, full_b,
    near_a, near_b, turn_a, turn_b, far_a, far_b, gain_seq, gain_slot, gain_rank,
    send_sems, recv_sems, own_sems, far_recv, first_recv,
):
    slots = block_ref.shape[0]
    place = Place(n_seq, n_head, slots)
    place.greet(True)
    sender = Sender(send_sems, recv_sems)
    part = sum_a.shape[1]
    mine = lanes(place.seq, part)
    order = [2, 3, 1, 0]
    parts = ((grads_b, sum_b, full_b, near_b, turn_b, far_b, chunks[1]),
             (grads_a, sum_a, full_a, near_a, turn_a, far_a, chunks[0]))
    copies, received = [], []

    def arrive(copy):
        copy.wait_recv()
        received.append(copy)

    def swap(src, dst):
        return [
            sender.start(
                src.at[place.at_slot(k)], dst.at[place.slot], place.device(slot=place.at_slot(k))
            )
            for k in (2, 3, 1)
        ]

    gain_seq[place.seq] = gains_ref[...]
    small = [
        sender.start(gain_seq.at[place.seq], gain_seq.at[place.seq],
                     place.device(seq=place.at_seq(d)))
        for d in range(1, n_seq)
    ]
    copies += small

    def to_seqs(grads, near, k):
        return [
            sender.start(
                grads.at[k, :, lanes(place.at_seq(d), part)],
                near.at[k, d - 1],
                place.device(seq=place.at_seq(d)),
            )
            for d in range(1, n_seq)
        ]

    sent = {}
    units = [(which, k) for which in range(2) for k in order]

    def launch(unit):
        which, k = unit
        sent[unit] = to_seqs(parts[which][0], parts[which][3], k)
        copies.extend(sent[unit])

    own = [
        pltpu.make_async_copy(src, dst.at[place.slot], own_sems.at[i])
        for i, (src, dst) in enumerate(
            (
                (block_ref.at[place.slot], block_out),
                (input_ref.at[place.slot], input_out),
                (first_ref.at[0], first_out),
            )
        )
    ]
    for copy in own:
        copy.start()
    launch(units[0])
    launch(units[1])
    copies += swap(block_ref, block_out)
    for copy in small:
        arrive(copy)
    total = gain_seq[0]
    for i in range(1, n_seq):
        total = total + gain_seq[i]
    gain_slot[place.slot] = total
    small = [
        sender.start(gain_slot.at[place.slot], gain_slot.at[place.slot],
                     place.device(slot=place.at_slot(k)))
        for k in range(1, slots)
    ]
    copies += small
    elsewhere = place.device(seq=place.at_seq(1))
    for index, unit in enumerate(units):
        which, k = unit
        grads, _, _, near, turn, far, chunk = parts[which]
        if index + 2 < len(units):
            launch(units[index + 2])
        for copy in sent[unit]:
            arrive(copy)

        def add(i, carry, grads=grads, near=near, turn=turn, k=k, chunk=chunk):
            rows = pl.ds(pl.multiple_of(i * chunk, chunk), chunk)
            value = grads[k, rows, mine].astype(F32)
            for d in range(n_seq - 1):
                value = value + near[k, d, rows, :].astype(F32)
            turn[k, rows, :] = value.astype(BF16)
            return carry

        lax.fori_loop(0, grads.shape[1] // chunk, add, 0)
        if k != 0:
            copy = sender.start(
                turn.at[k], far.at[place.slot], place.device(slot=place.source(k)),
                far_recv.at[which, place.slot],
            )
            copies.append(copy)
            received.append(copy)
        if index == 1:
            for j in range(1, slots):
                copy = sender.start(
                    first_ref.at[j], first_out.at[place.slot],
                    place.device(slot=place.source(j)), first_recv.at[place.slot],
                )
                copies.append(copy)
                received.append(copy)
        if index == 4:
            copies += swap(input_ref, input_out)
            for copy in small:
                arrive(copy)
            total = gain_slot[0]
            for i in range(1, slots):
                total = total + gain_slot[i]
            gain_rank[place.rank] = total
            small = [
                sender.start(gain_rank.at[place.rank], gain_rank.at[place.rank],
                             place.device(rank=(place.rank + j) % place.ranks))
                for j in range(1, place.ranks)
            ]
            copies += small
        if k == 0:
            for j in range(1, slots):
                source = place.at_slot(j)
                pltpu.make_async_remote_copy(
                    src_ref=turn.at[0], dst_ref=far.at[source], send_sem=send_sems.at[0],
                    recv_sem=far_recv.at[which, source], device_id=elsewhere, device_id_type=MESH,
                ).wait_recv()
            _, total_ref, full, _, _, _, _ = parts[which]

            def finish(i, carry, turn=turn, far=far, total_ref=total_ref, full=full, chunk=chunk):
                rows = pl.ds(pl.multiple_of(i * chunk, chunk), chunk)
                value = turn[0, rows, :].astype(F32)
                for j in range(1, slots):
                    value = value + far[place.at_slot(j), rows, :].astype(F32)
                value = value.astype(BF16)
                total_ref[rows, :] = value
                full[rows, mine] = value
                return carry

            lax.fori_loop(0, grads.shape[1] // chunk, finish, 0)
            copies += [
                sender.start(total_ref, full.at[:, mine], place.device(seq=place.at_seq(d)))
                for d in range(1, n_seq)
            ]
    for copy in small:
        arrive(copy)
    total = gain_rank[0]
    for i in range(1, place.ranks):
        total = total + gain_rank[i]
    gains_out[...] = total
    for copy in copies:
        if all(copy is not other for other in received):
            copy.wait_recv()
    for j in range(1, slots):
        source = place.at_slot(j)
        pltpu.make_async_remote_copy(
            src_ref=first_ref.at[0], dst_ref=first_out.at[source], send_sem=send_sems.at[0],
            recv_sem=first_recv.at[source], device_id=elsewhere, device_id_type=MESH,
        ).wait_recv()
    for copy in copies:
        copy.wait_send()
    for copy in own:
        copy.wait()


def reduce_grads(n_seq, n_head, chunks, block_delta, input_delta, first_delta, gains, grads_a, grads_b):
    slots = block_delta.shape[0]
    part = grads_a.shape[2] // n_seq
    rows = (grads_a.shape[1], grads_b.shape[1])
    ranks = n_head // slots
    count = (
        3 * (slots - 1) + 2 * (slots * (n_seq - 1) + (slots - 1) + (n_seq - 1))
        + (n_seq - 1) + (slots - 1) + (ranks - 1)
    )
    any_space = pl.BlockSpec(memory_space=pl.ANY)
    vmem = pl.BlockSpec(memory_space=pltpu.VMEM)
    like = lambda value: jax.ShapeDtypeStruct(value.shape, value.dtype)
    return pl.pallas_call(
        functools.partial(reduce_kernel, n_seq, n_head, chunks),
        in_specs=[any_space] * 3 + [vmem] * 3,
        out_specs=[any_space] * 3 + [vmem] * 5,
        out_shape=[like(block_delta), like(input_delta), like(first_delta), like(gains)]
        + [jax.ShapeDtypeStruct((r, part), BF16) for r in rows]
        + [jax.ShapeDtypeStruct((r, part * n_seq), BF16) for r in rows],
        scratch_shapes=[pltpu.VMEM((slots, n_seq - 1, r, part), BF16) for r in rows]
        + [pltpu.VMEM((slots, r, part), BF16) for r in rows]
        + [pltpu.VMEM((slots, r, part), BF16) for r in rows]
        + [pltpu.VMEM((n,) + gains.shape, F32) for n in (n_seq, slots, ranks)]
        + [
            pltpu.SemaphoreType.DMA((count,)),
            pltpu.SemaphoreType.DMA((count,)),
            pltpu.SemaphoreType.DMA((3,)),
            pltpu.SemaphoreType.DMA((2, slots)),
            pltpu.SemaphoreType.DMA((slots,)),
        ],
        compiler_params=pltpu.CompilerParams(
            collective_id=1, has_side_effects=True, vmem_limit_bytes=56 << 20
        ),
    )(block_delta, input_delta, first_delta, gains, grads_a, grads_b)


def shampoo_kernel(
    stat_ref, root_ref, head_stat, head_root, unit_stat, unit_root, full_a, sum_a, full_b, sum_b,
    wide_ref, out_right_ref, new_head, new_unit, step_a, step_b,
):
    step = pl.program_id(0)
    blocks = stat_ref.shape[1]

    def one(member, width, small_stat, small_root, full, total, big_out, small_out, step_out):
        for b in range(blocks):
            rows = pl.ds(pl.multiple_of((member * blocks + b) * width, 16), width)
            grad, own = full[rows, :], total[rows, :]
            big_out[0, b] = STAT_DECAY * stat_ref[0, b] + (1.0 - STAT_DECAY) * dot_tn(own, grad)
            small_out[member, b] = STAT_DECAY * small_stat[member, b] + (
                1.0 - STAT_DECAY
            ) * dot_nt(grad, grad)
            turned = dot_nn(small_root[member, b].astype(BF16), grad).astype(BF16)
            turned = dot_nt(turned, root_ref[0, b].astype(BF16))
            scale = lax.rsqrt(jnp.mean(turned * turned, axis=0, keepdims=True) + EPSILON)
            step_out[rows, :] = turned * scale

    head_width, unit_width = head_stat.shape[2], unit_stat.shape[2]
    head_args = (head_width, head_stat, head_root, full_a, sum_a)
    unit_args = (unit_width, unit_stat, unit_root, full_b, sum_b)

    @pl.when(step < 3)
    def _():
        one(step, *head_args, wide_ref, new_head, step_a)

    @pl.when((step >= 3) & (step < 6))
    def _():
        one(step - 3, *unit_args, wide_ref, new_unit, step_b)

    @pl.when(step == 6)
    def _():
        one(3, *head_args, out_right_ref, new_head, step_a)


def shampoo(stats_wide, roots_wide, stats_head, roots_head, stats_unit, roots_unit, full_a, sum_a, full_b, sum_b):
    members, blocks, part, width = stats_wide.shape
    member = lambda i: (jnp.where(i == 5, 6, jnp.where(i == 6, 5, i)), 0, 0, 0)
    wide = pl.BlockSpec((1, blocks, part, width), member)
    vmem = pl.BlockSpec(memory_space=pltpu.VMEM)
    return pl.pallas_call(
        shampoo_kernel,
        grid=(members,),
        in_specs=[wide, wide] + [vmem] * 8,
        out_specs=[
            pl.BlockSpec((1, blocks, part, width), lambda i: (jnp.minimum(i, 5), 0, 0, 0)),
            pl.BlockSpec((1, blocks, part, width), lambda i: (0, 0, 0, 0)),
            vmem, vmem, vmem, vmem,
        ],
        out_shape=[
            jax.ShapeDtypeStruct((members - 1, blocks, part, width), F32),
            jax.ShapeDtypeStruct((1, blocks, part, width), F32),
            jax.ShapeDtypeStruct(stats_head.shape, F32),
            jax.ShapeDtypeStruct(stats_unit.shape, F32),
            jax.ShapeDtypeStruct(sum_a.shape, F32),
            jax.ShapeDtypeStruct(sum_b.shape, F32),
        ],
        compiler_params=pltpu.CompilerParams(vmem_limit_bytes=48 << 20),
    )(stats_wide, roots_wide, stats_head, roots_head, stats_unit, roots_unit, full_a, sum_a, full_b, sum_b)


def finish_kernel(
    blocks, stat_ref, head_stat, unit_stat, full_a, sum_a, full_b, sum_b, step_a, step_b,
    w_qkv, w_gate_up, w_out, w_down, gains_ref, norm_ref,
    block_got, x_ref, input_got, g_ref, first_got,
    wide_ref, right_ref, new_head, new_unit, grad_qkv, grad_gate_up, grad_out, grad_down,
    new_qkv, new_gate_up, new_out, new_down, grad_gains, new_gains, block_out, input_out, first_out,
):
    step = pl.program_id(0)
    member, b = step // blocks, step % blocks

    def one(m, small_stat, full, total, big_out, small_out):
        width = small_stat.shape[2]
        rows = pl.ds(pl.multiple_of((m * blocks + b) * width, 16), width)
        grad, own = full[rows, :], total[rows, :]
        big_out[0, 0] = STAT_DECAY * stat_ref[0, 0] + (1.0 - STAT_DECAY) * dot_tn(own, grad)
        small_out[m, b] = STAT_DECAY * small_stat[m, b] + (1.0 - STAT_DECAY) * dot_nt(grad, grad)

    head_args, unit_args = (head_stat, full_a, sum_a), (unit_stat, full_b, sum_b)

    @pl.when(member < 3)
    def _():
        one(member, *head_args, wide_ref, new_head)

    @pl.when((member >= 3) & (member < 6))
    def _():
        one(member - 3, *unit_args, wide_ref, new_unit)

    @pl.when(member == 6)
    def _():
        one(3, *head_args, right_ref, new_head)

    @pl.when(step % 4 == 0)
    def _():
        block_out[...] = x_ref[...].astype(F32) + block_got[...].astype(F32)

    @pl.when(step % 4 == 1)
    def _():
        input_out[...] = g_ref[...].astype(F32) + input_got[...].astype(F32)

    @pl.when(step % 4 == 2)
    def _():
        first_out[...] = first_got[...].astype(F32)

    def stepped(i, at, total, steps, old, grad_ref, new_ref, turn):
        grad, change = total[at, :].astype(F32), STEP_RATE * steps[at, :]
        grad_ref[i] = grad.T if turn else grad
        new_ref[i] = old[i] - (change.T if turn else change)

    high = w_qkv.shape[2]
    for i in range(3):
        @pl.when(step == i)
        def _(i=i):
            stepped(i, pl.ds(i * high, high), sum_a, step_a, w_qkv, grad_qkv, new_qkv, True)

    tall = w_gate_up.shape[1]
    for i in range(2):
        @pl.when(step == 3 + i)
        def _(i=i):
            stepped(
                i, pl.ds(i * tall, tall), sum_b, step_b, w_gate_up, grad_gate_up, new_gate_up, False
            )

    @pl.when(step == 5)
    def _():
        at = pl.ds(3 * high, high)
        grad_out[...] = sum_a[at, :].astype(F32)
        new_out[...] = w_out[...] - OUT_RATE * step_a[at, :]

    @pl.when(step == 6)
    def _():
        at = pl.ds(2 * tall, tall)
        grad_down[...] = sum_b[at, :].astype(F32)
        new_down[...] = w_down[...] - STEP_RATE * step_b[at, :]

    @pl.when(step == 7)
    def _():
        gains = gains_ref[0:2, :]
        grad_gains[...] = gains
        scale = lax.rsqrt(jnp.mean(gains * gains, axis=-1, keepdims=True) + EPSILON)
        new_gains[...] = norm_ref[...] - GAIN_RATE * gains * scale


def finish(
    stats_wide, stats_head, stats_unit, full_a, sum_a, full_b, sum_b, step_a, step_b,
    w_qkv, w_gate_up, w_out, w_down, gains, norm_gains,
    block_got, layer_input, input_got, out_grad, first_got,
):
    members, blocks, part, width = stats_wide.shape
    slots, rows, _ = layer_input.shape
    length, head_cols = first_got.shape[1:]
    steps = 4 * slots

    def source(i):
        m = jnp.minimum(i // blocks, members - 1)
        return jnp.where(m == 5, 6, jnp.where(m == 6, 5, m)), i % blocks, 0, 0

    last = (members - 1) * blocks
    block = (1, 1, part, width)

    def right(i):
        return 0, jnp.clip(i - last, 0, blocks - 1), 0, 0

    def wide(i):
        at = jnp.minimum(i, last - 1)
        return at // blocks, at % blocks, 0, 0

    vmem = pl.BlockSpec(memory_space=pltpu.VMEM)
    tokens = pl.BlockSpec((1, rows, width), lambda i: (i // 4, 0, 0))
    firsts = pl.BlockSpec((1, length, head_cols), lambda i: (i // 4, 0, 0))
    like = lambda *values: [jax.ShapeDtypeStruct(v.shape, F32) for v in values]
    weights = (w_qkv, w_gate_up, w_out, w_down)
    return pl.pallas_call(
        functools.partial(finish_kernel, blocks),
        grid=(steps,),
        in_specs=[pl.BlockSpec(block, source)] + [vmem] * 14 + [tokens] * 4 + [firsts],
        out_specs=[pl.BlockSpec(block, wide), pl.BlockSpec(block, right)] + [vmem] * 12
        + [tokens, tokens, firsts],
        out_shape=[
            jax.ShapeDtypeStruct((members - 1, blocks, part, width), F32),
            jax.ShapeDtypeStruct((1, blocks, part, width), F32),
        ]
        + like(stats_head, stats_unit, *weights, *weights, norm_gains, norm_gains, layer_input, out_grad, first_got),
        compiler_params=pltpu.CompilerParams(vmem_limit_bytes=60 << 20),
    )(
        stats_wide, stats_head, stats_unit, full_a, sum_a, full_b, sum_b, step_a, step_b,
        w_qkv, w_gate_up, w_out, w_down, gains, norm_gains,
        block_got, layer_input, input_got, out_grad, first_got,
    )


class Links:
    def __init__(self, n_seq, n_head, slots):
        self.n_seq, self.n_head, self.slots = n_seq, n_head, slots
        self.ranks = n_head // slots
        self.slot = lax.axis_index("head") // self.ranks
        self.rank = lax.axis_index("head") % self.ranks

    def permute(self, value, partner):
        pairs = []
        for s in range(self.n_seq):
            for h in range(self.n_head):
                to_s, to_h = partner(s, h)
                pairs.append((s * self.n_head + h, to_s * self.n_head + to_h))
        return lax.ppermute(value, AXES, pairs)

    def swap_slots(self, value):
        got = [lax.dynamic_index_in_dim(value, self.slot, 0, keepdims=False)]
        for step in range(1, self.slots):
            piece = lax.dynamic_index_in_dim(value, self.slot ^ step, 0, keepdims=False)
            got.append(self.permute(piece, lambda s, h: (s, h ^ (step * self.ranks))))
        got = jnp.stack(got)
        return jnp.stack(
            [lax.dynamic_index_in_dim(got, self.slot ^ q, 0, keepdims=False) for q in range(self.slots)]
        )

    def gather_ranks(self, value):
        got = [value] + [
            self.permute(value, lambda s, h: (s, h ^ step)) for step in range(1, self.ranks)
        ]
        got = jnp.stack(got)
        return jnp.stack(
            [lax.dynamic_index_in_dim(got, self.rank ^ r, 0, keepdims=False) for r in range(self.ranks)]
        )

    def sum_ranks(self, value):
        total = lax.dynamic_index_in_dim(value, self.rank, 0, keepdims=False)
        for step in range(1, self.ranks):
            piece = lax.dynamic_index_in_dim(value, self.rank ^ step, 0, keepdims=False)
            got = self.permute(piece.astype(BF16), lambda s, h: (s, h ^ step))
            total = total + got.astype(F32)
        return total

    def whole_sequence(self, own):
        both = self.gather_ranks(own)
        return jnp.swapaxes(both, 0, 1).reshape(-1, own.shape[-1])

    def own_sum(self, full):
        rows = full.shape[0] // (self.slots * self.ranks)
        parts = full.reshape(self.slots, self.ranks, rows, full.shape[-1])
        return self.sum_ranks(jnp.swapaxes(parts, 0, 1)).reshape(-1, full.shape[-1])


def backward_plain(n_seq, n_head, head_cols, ffn_cols, links, saved, gains, tables, is_live):
    (
        x_bf16, h_one, q_rot, k_rot, v_mix, attended, log_total, weights_a, weights_b, middle,
        h_two, grad_own, d_ffn, _,
    ) = saved
    cos_wide, sin_wide, first_pos = tables
    slots, rows, width = x_bf16.shape
    length = h_one.shape[0]
    rows_a, rows_b = weights_a.shape[1], weights_b.shape[1]
    pairs = slots * head_cols // LANES
    per = LANES // head_cols

    def pair_major(value):
        n = value.shape[2]
        value = value.reshape(pairs, per, length, n, head_cols)
        return value.transpose(0, 2, 3, 1, 4).reshape(pairs, length, n, LANES)

    def slot_major(value):
        n = value.shape[2]
        value = value.reshape(pairs, length, n, per, head_cols)
        return value.transpose(0, 3, 1, 2, 4).reshape(slots, length, n, head_cols)

    w_in, w_o = weights_a[:, : 3 * head_cols], weights_a[:, 3 * head_cols :]
    w_gu, w_d = weights_b[:, : 2 * ffn_cols], weights_b[:, 2 * ffn_cols :]
    x_own = x_bf16.reshape(slots * rows, width).astype(F32)
    middle = middle.reshape(slots * rows, width)
    ein = functools.partial(jnp.einsum, preferred_element_type=F32)
    inverse_one = lax.rsqrt(jnp.mean(x_own * x_own, axis=-1, keepdims=True) + EPSILON)
    normed_one = x_own * inverse_one
    inverse_two = lax.rsqrt(jnp.mean(middle * middle, axis=-1, keepdims=True) + EPSILON)
    normed_two = middle * inverse_two
    saved = (q_rot, k_rot, v_mix, attended, log_total)
    attended = jnp.swapaxes(attended.reshape(length, slots, head_cols), 0, 1)
    gate_up = ein("ld,qfd->qlf", h_two, w_gu)
    gate, up = gate_up[..., :ffn_cols], gate_up[..., ffn_cols:]
    sigmoid_gate = jax.nn.sigmoid(gate)
    activated = gate * sigmoid_gate
    hidden = (activated * up).astype(BF16)
    ffn_out = links.own_sum(ein("qlf,qfd->ld", hidden, w_d))
    block_delta = jnp.where(is_live, middle - x_own + ffn_out, 0.0).astype(BF16)

    d_own = jnp.where(is_live, grad_own, jnp.zeros_like(grad_own))
    d_out = d_own.reshape(slots * rows, width).astype(F32)
    g_down = ein("qlf,ld->qfd", hidden, d_ffn)
    d_hidden = ein("ld,qfd->qlf", d_ffn, w_d)
    d_gate = (
        d_hidden * up * sigmoid_gate * (1.0 + gate * (1.0 - sigmoid_gate))
    ).astype(BF16)
    d_up = (d_hidden * activated).astype(BF16)
    d_gate_up = jnp.concatenate([d_gate, d_up], axis=2)
    d_normed_two = links.own_sum(ein("qlf,qfd->ld", d_gate_up, w_gu))
    g_gate_up = ein("qlf,ld->qfd", d_gate_up, h_two)
    grads_b = jnp.concatenate([g_gate_up.astype(BF16), g_down.astype(BF16)], axis=1)
    gain_two = jnp.sum(normed_two * d_normed_two, axis=0)
    middle_delta = norm_back(d_normed_two * gains[1], normed_two, inverse_two)
    d_middle = d_out + middle_delta
    d_attn = links.whole_sequence(d_middle.astype(BF16).reshape(slots, rows, width))
    d_attended = ein("ld,qcd->qlc", d_attn, w_o).astype(BF16)
    if per > 1:
        d_attended = pair_major(d_attended[:, :, None])[:, :, 0]
    d_project = jnp.concatenate(
        attend_back(saved, d_attended, cos_wide, sin_wide, first_pos), axis=2
    )
    if per > 1:
        d_project = slot_major(d_project.reshape(pairs, length, 3, LANES)).reshape(
            slots, length, 3 * head_cols
        )
    d_value = d_project[:, :, 2 * head_cols :]
    g_out = ein("qlc,ld->qcd", attended, d_attn)
    g_qkv = ein("qlc,ld->qcd", d_project, h_one)
    grads_a = jnp.concatenate([g_qkv.astype(BF16), g_out.astype(BF16)], axis=1)
    d_normed_one = links.own_sum(ein("qlc,qcd->ld", d_project, w_in))
    gain_one = jnp.sum(normed_one * d_normed_one, axis=0)
    input_delta = middle_delta + norm_back(d_normed_one * gains[0], normed_one, inverse_one)
    input_delta = jnp.where(is_live, input_delta, 0.0).astype(BF16)
    gain_rows = jnp.concatenate([gain_one.reshape(8, -1), gain_two.reshape(8, -1)], axis=0)

    return reduce_grads(
        n_seq,
        n_head,
        (LANES, unit_chunk(rows_b)),
        block_delta.reshape(slots, rows, width),
        input_delta.reshape(slots, rows, width),
        d_value,
        gain_rows,
        grads_a,
        grads_b,
    )


def shards(
    n_seq,
    n_head,
    layer_input,
    values_first,
    w_qkv,
    w_gate_up,
    w_out,
    w_down,
    norm_gains,
    out_grad,
    segments,
    counts,
    stats_wide,
    roots_wide,
    stats_head,
    roots_head,
    stats_unit,
    roots_unit,
):
    slots, rows, width = layer_input.shape
    length = segments.shape[1]
    row_part, head_cols, ffn_cols = w_qkv.shape[1], w_qkv.shape[2], w_gate_up.shape[2]
    head_dim = stats_head.shape[2]
    links = Links(n_seq, n_head, slots)
    is_live = links.slot < counts[0]
    pairs = slots * head_cols // LANES
    per = LANES // head_cols
    rows_a, rows_b = 4 * head_cols, 3 * ffn_cols

    fused = n_seq == 4 and slots == 4 and links.ranks == 2 and head_cols == LANES
    cos_wide, sin_wide, first_pos, live, *saved = forward_part(
        n_seq, n_head, head_cols, head_dim, layer_input, values_first, out_grad,
        (w_qkv, jnp.swapaxes(w_gate_up, 1, 2), w_out, w_down), norm_gains, segments, counts, fused,
    )
    first_pos = first_pos[0]
    tables = (cos_wide, sin_wide, first_pos)
    if fused:
        (
            block_got, input_got, first_got, gains, sum_a, sum_b, full_a, full_b, step_a, step_b
        ) = backward_part(
            n_seq, n_head, head_cols, saved, norm_gains, tables, live,
            (roots_wide, roots_head, roots_unit),
        )
        (
            wide, out_right, new_head, new_unit, grad_qkv, grad_gate_up, grad_out, grad_down,
            new_qkv, new_gate_up, new_out, new_down, grad_gains, new_gains,
            block_out, input_grad, first_grad,
        ) = finish(
            stats_wide, stats_head, stats_unit, full_a, sum_a, full_b, sum_b, step_a, step_b,
            w_qkv, jnp.swapaxes(w_gate_up, 1, 2), w_out, w_down, gains, norm_gains,
            block_got, layer_input, input_got, out_grad, first_got,
        )
        return (
            block_out, input_grad, first_grad, grad_qkv, jnp.swapaxes(grad_gate_up, 1, 2),
            grad_out, grad_down, grad_gains, new_qkv, jnp.swapaxes(new_gate_up, 1, 2), new_out, new_down, new_gains,
            wide, out_right[0], new_head, new_unit,
        )
    else:
        block_got, input_got, first_got, gains, sum_a, sum_b, full_a, full_b = backward_plain(
            n_seq, n_head, head_cols, ffn_cols, links, saved, norm_gains, tables, is_live
        )
        gains = gains.reshape(2, width)
        wide, out_right, new_head, new_unit, step_a, step_b = shampoo(
            stats_wide, roots_wide, stats_head, roots_head, stats_unit, roots_unit,
            full_a, sum_a, full_b, sum_b,
        )
        out_right = out_right[0]
    block_out = layer_input.astype(F32) + block_got.astype(F32)
    input_grad = out_grad.astype(F32) + input_got.astype(F32)
    first_grad = first_got.astype(F32)
    grad_gains = gains
    new_gains = norm_gains - GAIN_RATE * grad_gains * lax.rsqrt(
        jnp.mean(grad_gains * grad_gains, axis=-1, keepdims=True) + EPSILON
    )

    cut = 3 * head_cols
    turned = lambda value, n: jnp.swapaxes(value.reshape(n, -1, row_part), 1, 2)
    return (
        block_out,
        input_grad,
        first_grad,
        turned(sum_a[:cut], 3).astype(F32),
        turned(sum_b[: 2 * ffn_cols], 2).astype(F32),
        sum_a[cut:].astype(F32),
        sum_b[2 * ffn_cols :].astype(F32),
        grad_gains,
        w_qkv - STEP_RATE * turned(step_a[:cut], 3),
        w_gate_up - STEP_RATE * turned(step_b[: 2 * ffn_cols], 2),
        w_out - OUT_RATE * step_a[cut:],
        w_down - STEP_RATE * step_b[2 * ffn_cols :],
        new_gains,
        wide,
        out_right,
        new_head,
        new_unit,
    )


def unit_chunk(rows):
    return max(c for c in range(16, 177, 16) if rows % c == 0)


def solution(mesh):
    return jax.shard_map(
        functools.partial(shards, mesh.shape["seq"], mesh.shape["head"]),
        mesh=mesh,
        in_specs=(
            P("seq", "head", None),
            P("seq", None, "head"),
            P(None, "seq", "head"),
            P(None, "seq", "head"),
            P("head", "seq"),
            P("head", "seq"),
            P(),
            P("seq", "head", None),
            P("seq", None),
            P("seq"),
            P(None, "head", "seq", None),
            P(None, "head", "seq", None),
            P(None, "head", None, None),
            P(None, "head", None, None),
            P(None, "head", None, None),
            P(None, "head", None, None),
        ),
        out_specs=(
            P("seq", "head", None),
            P("seq", "head", None),
            P("seq", None, "head"),
            P(None, "seq", "head"),
            P(None, "seq", "head"),
            P("head", "seq"),
            P("head", "seq"),
            P(),
            P(None, "seq", "head"),
            P(None, "seq", "head"),
            P("head", "seq"),
            P("head", "seq"),
            P(),
            P(None, "head", "seq", None),
            P("head", "seq", None),
            P(None, "head", None, None),
            P(None, "head", None, None),
        ),
        check_vma=False,
    )
```
